32 devices in a mesh: dp: 16 (over z, y, x), rep: 2 (over core).
Axes of the slice: x: 2, y: 2, z: 4, core: 2. Of those that a mesh axis runs over, the one named last changes fastest.
Arguments:
- media: bfloat16 [32, 5, 256, 1024], P(('dp', 'rep')), may hold values from -6 to 6
- latents: bfloat16 [32, 5, 64, 1024], P(('dp', 'rep')), may hold values from -6 to 6
- image_counts: int32 [32], P(('dp', 'rep')), may hold values from 1 to 5, as said below
- grad_out: bfloat16 [32, 5, 64, 1024], P(('dp', 'rep')), may hold values from -6 to 6
- media_gain: bfloat16 [1024], P('dp'), may hold values from 0.25 to 1.75
- media_bias: bfloat16 [1024], P('dp'), may hold values from -3 to 3
- latent_gain: bfloat16 [1024], P('dp'), may hold values from 0.25 to 1.75
- latent_bias: bfloat16 [1024], P('dp'), may hold values from -3 to 3
- feed_gain: bfloat16 [1024], P('dp'), may hold values from 0.25 to 1.75
- feed_bias: bfloat16 [1024], P('dp'), may hold values from -3 to 3
- query_weight: bfloat16 [1024, 512], P('dp'), may hold values from -0.1875 to 0.1875
- context_weight: bfloat16 [1024, 1024], P('dp'), may hold values from -0.1875 to 0.1875
- output_weight: bfloat16 [512, 1024], P('dp'), may hold values from -1.5 to 1.5
- up_weight: bfloat16 [1024, 4096], P('dp'), may hold values from -0.1875 to 0.1875
- down_weight: bfloat16 [4096, 1024], P('dp'), may hold values from -0.09375 to 0.09375
Outputs:
- latents_out: bfloat16 [32, 5, 64, 1024], P(('dp', 'rep'))
- grad_media: bfloat16 [32, 5, 256, 1024], P(('dp', 'rep'))
- grad_latents: bfloat16 [32, 5, 64, 1024], P(('dp', 'rep'))
- grad_media_gain: float32 [1024], P('dp')
- grad_media_bias: float32 [1024], P('dp')
- grad_latent_gain: float32 [1024], P('dp')
- grad_latent_bias: float32 [1024], P('dp')
- grad_feed_gain: float32 [1024], P('dp')
- grad_feed_bias: float32 [1024], P('dp')
- grad_query: float32 [1024, 512], P('dp')
- grad_context: float32 [1024, 1024], P('dp')
- grad_output: float32 [512, 1024], P('dp')
- grad_up: float32 [1024, 4096], P('dp')
- grad_down: float32 [4096, 1024], P('dp')
The draws below stay inside these ranges and needn't reach their ends.
Inputs may be any that keep to these rules, and one draw needn't show every extreme that they name: Slot j of sample s holds an image where j < image_counts[s]; the other slots are empty. Some sample holds 5 images and some holds one.
All inputs are finite; a program needn't handle non-finite values.
Results may differ from the reference program's by a relative error of at most 0.014.
Values may be sent and summed in bfloat16 or wider, within the bound.
A program may use at most 192 MiB of HBM per device.

```python
import jax
import jax.numpy as jnp
from jax import lax

D = 1024
HEADS = 8
HEAD_DIM = 64
INNER = 512
FF = 4096
LAT = 64
PATCHES = 256
SLOTS = 5
SAMPLES = 32


def draw_image_counts(key, part):
    key = jax.random.fold_in(key, 11)
    key_counts, key_ranking = jax.random.split(key, 2)
    counts = jax.random.randint(key_counts, (SAMPLES,), 1, SLOTS + 1, dtype=jnp.int32)
    ranking = jax.random.permutation(key_ranking, SAMPLES)
    counts = counts.at[ranking[0]].set(SLOTS)
    counts = counts.at[ranking[1]].set(1)
    return counts


def strengthened(result, stream_key, source, target, parts, factor):
    owner, partner = [(jnp.arange(result.shape[position]) // (result.shape[position] // parts)).reshape([-1 if axis == position else 1 for axis in range(result.ndim)]) for position in (source, target)]
    chosen = jax.random.permutation(stream_key, parts)[partner]
    strong = (owner == chosen) | (owner == (partner + parts // 2) % parts)
    return jnp.where(strong, factor * result, result)


def levels(rng, dims, pieces, smallest, top_value):
    loudness = 1.0
    for position, blocks in pieces:
        heights = jax.random.uniform(jax.random.fold_in(jax.random.fold_in(rng, 6), position), (blocks,), jnp.float32, smallest / len(pieces), top_value / len(pieces))
        loudness = loudness * jnp.repeat(jnp.exp(heights), dims[position] // blocks).reshape((-1,) + (1,) * (len(dims) - 1 - position))
    return loudness


def normal_values(own_key, extent, width, most, pieces=(), held_as=jnp.bfloat16):
    drawn = width * jax.random.normal(own_key, extent, jnp.float32)
    if pieces:
        drawn = drawn * levels(own_key, extent, pieces, -0.22, 0.18)
    return jnp.clip(drawn, -most, most).astype(held_as)


def heavy_noise(rng, dims, scale, limit, cuts, heavy, kind=jnp.bfloat16):
    values = scale * jax.random.normal(rng, dims, jnp.float32)
    if cuts:
        values = values * levels(rng, dims, cuts, -0.22, 0.18)
    return jnp.clip(strengthened(values, jax.random.fold_in(rng, 3), *heavy), -limit, limit).astype(kind)


def setup_inputs(seed: int = 0) -> dict:
    keys = jax.random.split(jax.random.key(seed), 16)
    return {
        "media": heavy_noise(keys[0], (SAMPLES, SLOTS, PATCHES, D), 1.0, 6.0, ((0, 32),), (0, 3, 32, 2.75)),
        "latents": normal_values(keys[1], (SAMPLES, SLOTS, LAT, D), 1.0, 6.0, ((0, 32),)),
        "image_counts": draw_image_counts(jax.random.fold_in(keys[15], 71), 0),
        "grad_out": heavy_noise(keys[3], (SAMPLES, SLOTS, LAT, D), 1.0, 6.0, ((0, 32),), (0, 3, 32, 2.75)),
        "media_gain": jnp.clip(1.0 + 0.15 * jax.random.normal(keys[4], (D,), jnp.float32), 0.25, 1.75).astype(jnp.bfloat16),
        "media_bias": normal_values(keys[5], (D,), 0.5, 3.0, ((0, 16),)),
        "latent_gain": jnp.clip(1.0 + 0.15 * jax.random.normal(keys[6], (D,), jnp.float32), 0.25, 1.75).astype(jnp.bfloat16),
        "latent_bias": normal_values(keys[7], (D,), 0.5, 3.0, ((0, 16),)),
        "feed_gain": jnp.clip(1.0 + 0.15 * jax.random.normal(keys[8], (D,), jnp.float32), 0.25, 1.75).astype(jnp.bfloat16),
        "feed_bias": normal_values(keys[9], (D,), 0.5, 3.0, ((0, 16),)),
        "query_weight": normal_values(keys[10], (D, INNER), D ** -0.5, 0.1875, ((0, 16),)),
        "context_weight": normal_values(keys[11], (D, 2 * INNER), D ** -0.5, 0.1875, ((0, 16),)),
        "output_weight": normal_values(keys[12], (INNER, D), (INNER // 32) ** -0.5, 1.5, ((0, 16),)),
        "up_weight": normal_values(keys[13], (D, FF), D ** -0.5, 0.1875, ((0, 16),)),
        "down_weight": normal_values(keys[14], (FF, D), FF ** -0.5, 0.09375, ((0, 16),)),
    }


epsilon = 1e-05
highest = lax.Precision.HIGHEST
per_group = 2

@jax.custom_vjp
def low(v):
    return lax.optimization_barrier(v.astype(jnp.bfloat16)).astype(jnp.float32)

@jax.custom_vjp
def low_back(v):
    return v

def low_keep(v):
    return (low(v), None)

def low_pass(kept, grad):
    return (grad,)

def back_keep(v):
    return (v, None)

def back_low(kept, grad):
    return (low(grad),)
low.defvjp(low_keep, low_pass)
low_back.defvjp(back_keep, back_low)

def layer_norm(values, gain, offset):
    centre = lax.optimization_barrier(jnp.mean(values, axis=-1, keepdims=True))
    shifted = values - centre
    spread = lax.optimization_barrier(jnp.mean(shifted * shifted, axis=-1, keepdims=True))
    return shifted * lax.rsqrt(spread + epsilon) * gain + offset

def gelu_exact(values):
    return 0.5 * values * (1.0 + jax.scipy.special.erf(values * 0.7071067811865476))

def product(left, right):
    return jnp.matmul(left, right, precision=highest)

def forward(params, media, latents, slot_mask):
    media_gain, media_bias, latent_gain, latent_bias, feed_gain, feed_bias, query_weight, context_weight, output_weight, up_weight, down_weight = params
    blocks = media.shape[0] * media.shape[1]
    key_count = PATCHES + LAT
    media_rows = media.reshape(blocks, PATCHES, D)
    latent_rows = latents.reshape(blocks, LAT, D)
    media_normed = low(layer_norm(media_rows, media_gain, media_bias))
    latent_normed = low(layer_norm(latent_rows, latent_gain, latent_bias))
    queries = low(low_back(product(latent_normed, query_weight) * HEAD_DIM ** (-0.5)))
    context = jnp.concatenate([media_normed, latent_normed], axis=1)
    key_value = low(low_back(product(context, context_weight)))
    query_heads = queries.reshape(blocks, LAT, HEADS, HEAD_DIM)
    key_heads = key_value[:, :, :INNER].reshape(blocks, key_count, HEADS, HEAD_DIM)
    value_heads = key_value[:, :, INNER:].reshape(blocks, key_count, HEADS, HEAD_DIM)
    scores = low_back(jnp.einsum('bqhd,bkhd->bhqk', query_heads, key_heads, precision=highest))
    row_max = lax.optimization_barrier(jnp.max(scores, axis=-1, keepdims=True))
    exponent = jnp.exp(scores - row_max)
    attention_weights = low(exponent / lax.optimization_barrier(jnp.sum(exponent, axis=-1, keepdims=True)))
    attended = low(low_back(jnp.einsum('bhqk,bkhd->bqhd', attention_weights, value_heads, precision=highest)))
    attended = attended.reshape(blocks, LAT, INNER)
    after_attention = latent_rows + low_back(product(attended, output_weight))
    feed_input = low(layer_norm(after_attention, feed_gain, feed_bias))
    hidden = low_back(product(feed_input, up_weight))
    activated = low(gelu_exact(hidden))
    after_feed = after_attention + low_back(product(activated, down_weight))
    return after_feed.reshape(latents.shape) * slot_mask[:, :, None, None]

def reference(media, latents, image_counts, grad_out, media_gain, media_bias, latent_gain, latent_bias, feed_gain, feed_bias, query_weight, context_weight, output_weight, up_weight, down_weight):
    params = tuple((element.astype(jnp.float32) for element in (media_gain, media_bias, latent_gain, latent_bias, feed_gain, feed_bias, query_weight, context_weight, output_weight, up_weight, down_weight)))
    slot_mask = (jnp.arange(SLOTS, dtype=jnp.int32)[None, :] < image_counts[:, None].astype(jnp.int32)).astype(jnp.float32)
    group_count = SAMPLES // per_group

    def regroup(array):
        return array.reshape((group_count, per_group) + array.shape[1:])

    def one_group(totals, inputs):
        media_group, latent_group, mask_group, cotangent = inputs

        def local_forward(weights_in, media_in, latent_in):
            return forward(weights_in, media_in, latent_in, mask_group)
        outputs, pullback = jax.vjp(local_forward, params, media_group.astype(jnp.float32), latent_group.astype(jnp.float32))
        grad_params, media_grads, latent_grads = pullback(cotangent.astype(jnp.float32))
        totals = tuple((earlier + added for earlier, added in zip(totals, grad_params)))
        return (totals, (outputs.astype(jnp.bfloat16), media_grads.astype(jnp.bfloat16), latent_grads.astype(jnp.bfloat16)))
    initial = tuple((jnp.zeros(element.shape, jnp.float32) for element in params))
    totals, stacked = lax.scan(one_group, initial, (regroup(media), regroup(latents), regroup(slot_mask), regroup(grad_out)))
    latents_out = stacked[0].reshape((SAMPLES,) + stacked[0].shape[2:])
    grad_media = stacked[1].reshape((SAMPLES,) + stacked[1].shape[2:])
    grad_latents = stacked[2].reshape((SAMPLES,) + stacked[2].shape[2:])
    return (latents_out, grad_media, grad_latents, totals[0], totals[1], totals[2], totals[3], totals[4], totals[5], totals[6], totals[7], totals[8], totals[9], totals[10])
```

```python
import functools

import jax
import jax.numpy as jnp
from jax import lax
from jax.experimental import pallas as pl
from jax.experimental.pallas import tpu as pltpu
from jax.sharding import PartitionSpec as P

HEAD_DIM = 64


epsilon = 1e-05

MESH = pl.DeviceIdType.MESH
ALL = slice(None)


class Links:
    def __init__(self, length):
        self.length = length
        self.dp = lax.axis_index("dp")
        self.rep = lax.axis_index("rep")
        self.z = lax.div(self.dp, 4)
        self.y = lax.rem(lax.div(self.dp, 2), 2)
        self.x = lax.rem(self.dp, 2)

    def device(self, axis, way=0):
        if axis == "core":
            return (self.dp, 1 - self.rep)
        if axis == "x":
            return (self.dp + 1 - 2 * self.x, self.rep)
        if axis == "y":
            return (self.dp + 2 - 4 * self.y, self.rep)
        return (self.dp + 4 * way, self.rep)

    def greet(self):
        barrier = pltpu.get_barrier_semaphore()
        for axis in ("core", "x", "y"):
            pl.semaphore_signal(barrier, inc=1, device_id=self.device(axis), device_id_type=MESH)

        @pl.when(self.z > 0)
        def _():
            pl.semaphore_signal(barrier, inc=1, device_id=self.device("z", -1), device_id_type=MESH)

        @pl.when(self.z < self.length - 1)
        def _():
            pl.semaphore_signal(barrier, inc=1, device_id=self.device("z", 1), device_id_type=MESH)

        inside = jnp.where(self.z > 0, 1, 0) + jnp.where(self.z < self.length - 1, 1, 0)
        pl.semaphore_wait(barrier, 3 + inside)


class Move:
    def __init__(self, send, recv, slot, device, source, target, landing, gives=None, takes=None):
        self.out = pltpu.make_async_remote_copy(
            src_ref=source, dst_ref=target, send_sem=send.at[slot], recv_sem=recv.at[slot],
            device_id=device, device_id_type=MESH)
        self.into = pltpu.make_async_remote_copy(
            src_ref=landing, dst_ref=landing, send_sem=send.at[slot], recv_sem=recv.at[slot],
            device_id=device, device_id_type=MESH)
        self.gives, self.takes = gives, takes

    def start(self):
        guarded(self.gives, self.out.start)

    def wait(self, then=None):
        def both():
            self.into.wait_recv()
            if then is not None:
                then()

        guarded(self.takes, both)

    def drain(self):
        guarded(self.gives, self.out.wait_send)


def guarded(condition, action):
    if condition is None:
        action()
    else:
        pl.when(condition)(action)


class Slots:
    def __init__(self, send, recv):
        self.send, self.recv, self.used = send, recv, 0

    def take(self):
        self.used += 1
        return self.used - 1

    def move(self, *args, **kwargs):
        return Move(self.send, self.recv, self.take(), *args, **kwargs)


class Gather:
    def __init__(self, links, slots, view, order, halved):
        self.moves = []
        z, y, x, length = links.z, links.y, links.x, links.length
        here = {"z": z, "y": y, "x": x}
        for hop in range(1, length):
            up = view(z - hop + 1, y, x)
            down = view(z + hop - 1, y, x)
            self.moves.append([
                slots.move(links.device("z", 1), up, up, view(z - hop, y, x),
                           gives=(z < length - 1) & (z >= hop - 1), takes=z >= hop),
                slots.move(links.device("z", -1), down, down, view(z + hop, y, x),
                           gives=(z > 0) & (z + hop <= length), takes=z + hop < length),
            ])
        here["z"] = ALL
        for axis in order:
            mine = view(here["z"], here["y"], here["x"])
            other = dict(here)
            other[axis] = 1 - here[axis]
            self.moves.append([
                slots.move(links.device(axis), mine, mine, view(other["z"], other["y"], other["x"]))])
            here[axis] = ALL
        if halved:
            mine = view(ALL, ALL, ALL)
            self.moves.append([
                slots.move(links.device("core"), mine, mine, view(ALL, ALL, ALL, 1 - links.rep))])

    def step(self, number):
        if 0 < number <= len(self.moves):
            for move in self.moves[number - 1]:
                move.wait()
        if number < len(self.moves):
            for move in self.moves[number]:
                move.start()

    def drain(self):
        for group in self.moves:
            for move in group:
                move.drain()


class Reduce:
    def __init__(self, links, slots, own, order, lands_b, lands_a, lands_z, finish):
        self.own, self.order, self.links, self.finish = own, order, links, finish
        self.moves, self.adds = [], []
        z, y, x, length = links.z, links.y, links.x, links.length
        here = {"z": ALL, "y": ALL, "x": ALL}
        for axis, lands in zip(order, (lands_b, lands_a)):
            away, home = dict(here), dict(here)
            place = {"y": y, "x": x}[axis]
            away[axis], home[axis] = 1 - place, place
            self.moves.append([slots.move(
                links.device(axis), own(away["z"], away["y"], away["x"]), lands, lands)])
            here = home
            self.adds.append([functools.partial(add_into, own(home["z"], home["y"], home["x"]), lands)])
        for hop in range(1, length):
            above, below = z + length - hop, z - length + hop
            from_below, from_above = lands_z.at[0, hop - 1], lands_z.at[1, hop - 1]
            last = hop == length - 1
            self.moves.append([
                slots.move(links.device("z", 1), own(above, y, x), from_below, from_below,
                           gives=(z < length - 1) & (z < hop), takes=(z > 0) & (z <= hop)),
                slots.move(links.device("z", -1), own(below, y, x), from_above, from_above,
                           gives=(z > 0) & (z >= length - hop),
                           takes=(z < length - 1) & (z >= length - 1 - hop)),
            ])
            if last:
                self.adds.append([None, None])
            else:
                self.adds.append([
                    functools.partial(add_into, own(above - 1, y, x), from_below),
                    functools.partial(add_into, own(below + 1, y, x), from_above)])
        self.lands_z = lands_z

    def step(self, number):
        if 0 < number <= len(self.moves):
            for move, add in zip(self.moves[number - 1], self.adds[number - 1]):
                move.wait(add)
            if number == len(self.moves):
                self.end()
        if number < len(self.moves):
            for move in self.moves[number]:
                move.start()

    def end(self):
        links, length = self.links, self.links.length
        block = self.own(links.z, links.y, links.x)

        def total(below, above):
            value = block[...].astype(jnp.float32)
            if below:
                value = value + self.lands_z[0, length - 2].astype(jnp.float32)
            if above:
                value = value + self.lands_z[1, length - 2].astype(jnp.float32)
            self.finish(value)

        pl.when(links.z == 0)(lambda: total(False, True))
        pl.when(links.z == length - 1)(lambda: total(True, False))
        pl.when((links.z > 0) & (links.z < length - 1))(lambda: total(True, True))

    def drain(self):
        for group in self.moves:
            for move in group:
                move.drain()


def add_into(target, arrived):
    lead = target.shape[:-2]
    if not lead:
        target[...] = (target[...].astype(jnp.float32) + arrived[...].astype(jnp.float32)).astype(target.dtype)
        return
    count = 1
    for size in lead:
        count *= size

    @pl.loop(0, count)
    def _(flat):
        index = []
        for size in reversed(lead):
            index.insert(0, lax.rem(flat, size))
            flat = lax.div(flat, size)
        index = tuple(index)
        target[index] = (target[index].astype(jnp.float32) + arrived[index].astype(jnp.float32)).astype(target.dtype)


def gather_kernel(length, *refs):
    names = 5
    shards, packed = refs[:names], refs[names]
    outs, packed_out = refs[names + 1:2 * names + 1], refs[2 * names + 1]
    send, recv, local = refs[2 * names + 2:]
    links = Links(length)
    z, y, x, rep = links.z, links.y, links.x, links.rep
    staged = []
    for number, (shard, out) in enumerate(zip(shards, outs)):
        rows = out.shape[-2]
        staged.append(pltpu.make_async_copy(
            shard.at[pl.ds(pl.multiple_of(rep * rows, 16), rows)], out.at[z, y, x, rep], local.at[number]))
    staged.append(pltpu.make_async_copy(packed, packed_out.at[z, y, x], local.at[names]))
    for copy in staged:
        copy.start()
    links.greet()
    slots = Slots(send, recv)
    items = []

    def window(out, begin, width):
        def view(zi, yi, xi, half=rep):
            return out.at[zi, yi, xi, half, :, pl.ds(begin, width)]

        return view

    def pair(out, begin, width):
        return [Gather(links, slots, window(out, begin, width), ("x", "y"), True),
                Gather(links, slots, window(out, begin + width, width), ("y", "x"), True)]

    query, context, output, up, down = outs
    items.append([Gather(links, slots, lambda zi, yi, xi: packed_out.at[zi, yi, xi], ("x", "y"), False)]
                 + pair(context, 0, context.shape[-1] // 2))
    items.append(pair(query, 0, query.shape[-1] // 2) + pair(output, 0, output.shape[-1] // 2))
    quarter = up.shape[-1] // 4
    items.append(pair(up, 0, quarter))
    items.append(pair(up, 2 * quarter, quarter))
    quarter = down.shape[-1] // 4
    items.append(pair(down, 0, quarter))
    items.append(pair(down, 2 * quarter, quarter))
    for copy in staged:
        copy.wait()
    depth = length + 3
    for tick in range(len(items) + depth - 1):
        for number in range(len(items)):
            step = tick - number
            if 0 <= step < depth:
                for gather in items[number]:
                    gather.step(step)
    for item in items:
        for gather in item:
            gather.drain()


def reduce_kernel(length, grads, vectors, outs, vectors_out, own, lands_c, lands_b, lands_a, lands_z, result,
                  vector_lands, send, recv, local):
    links = Links(length)
    z, y, x, rep = links.z, links.y, links.x, links.rep
    loads = []
    for number, (grad, mine) in enumerate(zip(grads, own)):
        loads.append(pltpu.make_async_copy(grad.at[:, :, :, rep], mine, local.at[number]))
        loads[-1].start()
    links.greet()
    slots = Slots(send, recv)
    siblings = [slots.move(links.device("core"), grad.at[:, :, :, 1 - rep], land, land)
                for grad, land in zip(grads, lands_c)]
    steps = []

    def pair(number, begin, width):
        made = []
        for order, first in ((("y", "x"), begin), (("x", "y"), begin + width)):
            window = pl.ds(first, width)

            def view(zi, yi, xi, window=window):
                return own[number].at[zi, yi, xi, :, window]

            def finish(value, window=window):
                result[number][:, window] = value

            made.append(Reduce(
                links, slots, view, order, lands_b[number].at[:, :, :, window], lands_a[number].at[:, :, window],
                lands_z[number].at[:, :, :, window], finish))
        return made

    order = (4, 3, 1, 0, 2)
    for number in order:
        siblings[number].start()
    items = []
    for number in order:
        width = own[number].shape[-1]
        parts = 2 if number >= 3 else 1
        width //= 2 * parts
        for part in range(parts):
            items.append((number, part == 0, pair(number, 2 * part * width, width)))
    vectors_out[...] = vectors[...]
    for axis in ("core", "x", "y"):
        number = ("core", "x", "y").index(axis)
        mine, land = vector_lands.at[2 * number], vector_lands.at[2 * number + 1]
        mine[...] = vectors_out[...]
        move = slots.move(links.device(axis), mine, land, land)
        move.start()
        move.wait()
        vectors_out[...] = mine[...] + land[...]
        move.drain()
    base = 6
    running = vector_lands.at[base]
    running[...] = vectors_out[...]
    line = []
    for hop in range(1, length):
        mine_up, mine_down = vector_lands.at[base + 4 * hop - 3], vector_lands.at[base + 4 * hop - 2]
        below, above = vector_lands.at[base + 4 * hop - 1], vector_lands.at[base + 4 * hop]
        if hop == 1:
            mine_up[...] = running[...]
            mine_down[...] = running[...]
        else:
            mine_up[...] = vector_lands[base + 4 * hop - 5]
            mine_down[...] = vector_lands[base + 4 * hop - 4]
        moves = [
            slots.move(links.device("z", 1), mine_up, below, below,
                       gives=(z < length - 1) & (z >= hop - 1), takes=z >= hop),
            slots.move(links.device("z", -1), mine_down, above, above,
                       gives=(z > 0) & (z + hop <= length), takes=z + hop < length)]
        for move in moves:
            move.start()

        def take(land):
            vectors_out[...] = vectors_out[...] + land[...]

        moves[0].wait(functools.partial(take, below))
        moves[1].wait(functools.partial(take, above))
        line += moves
    depth = length + 2
    for tick in range(len(items) + depth - 1):
        for place, (number, first, halves) in enumerate(items):
            step = tick - place
            if step == 0 and first:
                loads[number].wait()
                siblings[number].wait()
                add_into(own[number], lands_c[number])
            if 0 <= step < depth:
                for half in halves:
                    half.step(step)
    finals = []
    for number, (total, out) in enumerate(zip(result, outs)):
        keep = pltpu.make_async_copy(total, out.at[rep], local.at[number])
        keep.start()
        move = slots.move(links.device("core"), total, out.at[rep], out.at[1 - rep])
        move.start()
        finals.append((keep, move))
    for keep, move in finals:
        keep.wait()
        move.wait()
        move.drain()
    for move in siblings + line:
        move.drain()
    for number, first, halves in items:
        for half in halves:
            half.drain()


def gather_parameters(shards, packed, length):
    blocks = (length, 2, 2)
    anywhere = pl.BlockSpec(memory_space=pl.ANY)
    out_shape = [jax.ShapeDtypeStruct(blocks + (2, s.shape[0] // 2, s.shape[1]), s.dtype) for s in shards]
    out_shape.append(jax.ShapeDtypeStruct(blocks + packed.shape, packed.dtype))
    made = pl.pallas_call(
        functools.partial(gather_kernel, length),
        out_shape=out_shape,
        in_specs=[anywhere] * (len(shards) + 1),
        out_specs=[anywhere] * (len(shards) + 1),
        scratch_shapes=[
            pltpu.SemaphoreType.DMA((160,)),
            pltpu.SemaphoreType.DMA((160,)),
            pltpu.SemaphoreType.DMA((8,)),
        ],
        compiler_params=pltpu.CompilerParams(collective_id=0, has_side_effects=True),
        name="gather_parameters",
    )(*shards, packed)
    return [m.reshape(-1, m.shape[-1]) for m in made[:-1]], made[-1]


def reduce_gradients(grads, vectors, length):
    blocks = (length, 2, 2)
    anywhere = pl.BlockSpec(memory_space=pl.ANY)
    count = len(grads)
    folded = []
    for grad in grads:
        rows = grad.shape[0] // (8 * length)
        folded.append(grad.reshape(blocks + (2, rows, grad.shape[1])))
    halves = [f.shape[4:] for f in folded]
    bf16 = jnp.bfloat16
    scratch = [
        [pltpu.VMEM(blocks + h, bf16) for h in halves],
        [pltpu.VMEM(blocks + h, bf16) for h in halves],
        [pltpu.VMEM((length, 2) + h, bf16) for h in halves],
        [pltpu.VMEM((length,) + h, bf16) for h in halves],
        [pltpu.VMEM((2, length - 1) + h, bf16) for h in halves],
        [pltpu.VMEM(h, jnp.float32) for h in halves],
        pltpu.VMEM((6 + 4 * length,) + vectors.shape, jnp.float32),
        pltpu.SemaphoreType.DMA((200,)),
        pltpu.SemaphoreType.DMA((200,)),
        pltpu.SemaphoreType.DMA((8,)),
    ]
    vmem = pl.BlockSpec(memory_space=pltpu.VMEM)
    outs, vectors_out = pl.pallas_call(
        functools.partial(reduce_kernel, length),
        out_shape=([jax.ShapeDtypeStruct((2,) + h, jnp.float32) for h in halves],
                   jax.ShapeDtypeStruct(vectors.shape, jnp.float32)),
        in_specs=[[anywhere] * count, vmem],
        out_specs=([anywhere] * count, vmem),
        scratch_shapes=scratch,
        compiler_params=pltpu.CompilerParams(
            collective_id=1, has_side_effects=True, vmem_limit_bytes=56 * 2 ** 20),
        name="reduce_gradients",
    )(folded, vectors)
    return [o.reshape(-1, o.shape[-1]) for o in outs], vectors_out

def layer_norm(values, gain, offset):
    centre = jnp.mean(values, axis=-1, keepdims=True)
    shifted = values - centre
    spread = jnp.mean(shifted * shifted, axis=-1, keepdims=True)
    return shifted * lax.rsqrt(spread + epsilon) * gain + offset


def gelu_exact(values):
    return 0.5 * values * (1.0 + jax.scipy.special.erf(values * 0.7071067811865476))


def matmul(left, right):
    return jnp.dot(left, right, preferred_element_type=jnp.float32)


def matmul_left(left, right):
    return lax.dot_general(
        left, right, (((0,), (0,)), ((), ())), preferred_element_type=jnp.float32
    )


def matmul_right(left, right):
    return lax.dot_general(
        left, right, (((1,), (1,)), ((), ())), preferred_element_type=jnp.float32
    )


def head_scores(first_heads, second_heads):
    return jnp.einsum(
        "bqhd,bkhd->bhqk", first_heads, second_heads, preferred_element_type=jnp.float32
    )


def body(
    media,
    latents,
    image_counts,
    grad_out,
    media_gain,
    media_bias,
    latent_gain,
    latent_bias,
    feed_gain,
    feed_bias,
    query_weight,
    context_weight,
    output_weight,
    up_weight,
    down_weight,
):
    samples, slots, patches, model_width = media.shape
    latent_count = latents.shape[2]
    inner_width = query_weight.shape[1]
    head_count = inner_width // HEAD_DIM
    blocks = samples * slots
    key_count = patches + latent_count
    latent_total = blocks * latent_count
    scaling = HEAD_DIM ** (-0.5)
    vector_shards = (media_gain, media_bias, latent_gain, latent_bias, feed_gain, feed_bias)
    weight_shards = (query_weight, context_weight, output_weight, up_weight, down_weight)
    chips = lax.axis_size("dp")
    tiled = chips % 4 == 0 and chips > 4 and all(s.shape[0] % 32 == 0 for s in weight_shards)
    if tiled:
        packed = jnp.pad(jnp.stack(vector_shards), ((0, 10), (0, 128 - media_gain.shape[0])))
        matrices, packed = gather_parameters(weight_shards, packed, chips // 4)
        packed = packed.reshape(chips, 16, 128)[:, :6, :media_gain.shape[0]]
        gathered = tuple(packed.transpose(1, 0, 2).reshape(6, model_width)) + tuple(matrices)
    else:
        gathered = tuple(
            lax.all_gather(s, "dp", axis=0, tiled=True) for s in vector_shards + weight_shards)
    vectors = [element.astype(jnp.float32) for element in gathered[:6]]
    media_rows = media.reshape(blocks * patches, model_width).astype(jnp.float32)
    latent_rows = latents.reshape(latent_total, model_width).astype(jnp.float32)
    media_normed = layer_norm(media_rows, vectors[0], vectors[1]).astype(jnp.bfloat16)
    latent_normed = layer_norm(latent_rows, vectors[2], vectors[3]).astype(jnp.bfloat16)
    queries = (matmul(latent_normed, gathered[6]) * scaling).astype(jnp.bfloat16)
    context = jnp.concatenate(
        [
            media_normed.reshape(blocks, patches, model_width),
            latent_normed.reshape(blocks, latent_count, model_width),
        ],
        axis=1,
    ).reshape(blocks * key_count, model_width)
    key_value = (
        matmul(context, gathered[7])
        .astype(jnp.bfloat16)
        .reshape(blocks, key_count, 2 * inner_width)
    )
    query_heads = queries.reshape(blocks, latent_count, head_count, HEAD_DIM)
    key_heads = key_value[:, :, :inner_width].reshape(blocks, key_count, head_count, HEAD_DIM)
    value_heads = key_value[:, :, inner_width:].reshape(blocks, key_count, head_count, HEAD_DIM)
    scores = head_scores(query_heads, key_heads)
    row_max = jnp.max(scores, axis=-1, keepdims=True)
    exponent = jnp.exp(scores - row_max)
    row_total = jnp.sum(exponent, axis=-1, keepdims=True)
    log_total = row_max + jnp.log(row_total)
    attention_weights = (exponent / row_total).astype(jnp.bfloat16)
    attended = (
        jnp.einsum(
            "bhqk,bkhd->bqhd", attention_weights, value_heads, preferred_element_type=jnp.float32
        )
        .astype(jnp.bfloat16)
        .reshape(latent_total, inner_width)
    )
    after_attention = latent_rows + matmul(attended, gathered[8])
    feed_input = layer_norm(after_attention, vectors[4], vectors[5]).astype(jnp.bfloat16)
    hidden = matmul(feed_input, gathered[9])
    activated = gelu_exact(hidden).astype(jnp.bfloat16)
    after_feed = after_attention + matmul(activated, gathered[10])
    slot_mask = (
        lax.broadcasted_iota(jnp.int32, (samples, slots), 1) < image_counts[:, None]
    ).astype(jnp.float32)
    row_mask = jnp.broadcast_to(slot_mask[:, :, None], (samples, slots, latent_count)).reshape(
        latent_total, 1
    )
    latents_out = (after_feed * row_mask).astype(jnp.bfloat16).reshape(latents.shape)
    backward_set = gathered
    back_vectors = [element.astype(jnp.float32) for element in backward_set[:6]]
    d_after = grad_out.reshape(latent_total, model_width).astype(jnp.float32) * row_mask
    d_branch = d_after.astype(jnp.bfloat16)
    grad_down = matmul_left(activated, d_branch)
    d_activated = matmul_right(d_branch, backward_set[10])
    d_hidden = jax.vjp(gelu_exact, hidden)[1](d_activated)[0].astype(jnp.bfloat16)
    grad_up = matmul_left(feed_input, d_hidden)
    d_feed = matmul_right(d_hidden, backward_set[9])
    d_feed_norm, grad_feed_gain, grad_feed_bias = jax.vjp(
        layer_norm, after_attention, back_vectors[4], back_vectors[5]
    )[1](d_feed)
    d_middle = d_after + d_feed_norm
    d_out_branch = d_middle.astype(jnp.bfloat16)
    grad_output = matmul_left(attended, d_out_branch)
    d_attended = (
        matmul_right(d_out_branch, backward_set[8])
        .astype(jnp.bfloat16)
        .reshape(blocks, latent_count, head_count, HEAD_DIM)
    )
    recomputed = jnp.exp(head_scores(query_heads, key_heads) - log_total)
    d_weights = head_scores(d_attended, value_heads)
    d_scores = (
        recomputed * (d_weights - jnp.sum(recomputed * d_weights, axis=-1, keepdims=True))
    ).astype(jnp.bfloat16)
    d_queries = (
        jnp.einsum(
            "bhqk,bkhd->bqhd", d_scores, key_heads, preferred_element_type=jnp.float32
        ).astype(jnp.bfloat16)
        * scaling
    ).reshape(latent_total, inner_width)
    d_keys = jnp.einsum(
        "bhqk,bqhd->bkhd", d_scores, query_heads, preferred_element_type=jnp.float32
    ).astype(jnp.bfloat16)
    d_values = jnp.einsum(
        "bhqk,bqhd->bkhd",
        recomputed.astype(jnp.bfloat16),
        d_attended,
        preferred_element_type=jnp.float32,
    ).astype(jnp.bfloat16)
    d_key_value = jnp.concatenate(
        [
            d_keys.reshape(blocks, key_count, inner_width),
            d_values.reshape(blocks, key_count, inner_width),
        ],
        axis=-1,
    ).reshape(blocks * key_count, 2 * inner_width)
    grad_query = matmul_left(latent_normed, d_queries)
    grad_context = matmul_left(context, d_key_value)
    d_context = matmul_right(d_key_value, backward_set[7]).reshape(blocks, key_count, model_width)
    d_latent_normed = matmul_right(d_queries, backward_set[6]) + d_context[:, patches:, :].reshape(
        latent_total, model_width
    )
    d_media_normed = d_context[:, :patches, :].reshape(blocks * patches, model_width)
    d_latent_norm, grad_latent_gain, grad_latent_bias = jax.vjp(
        layer_norm, latent_rows, back_vectors[2], back_vectors[3]
    )[1](d_latent_normed)
    grad_latents = (d_middle + d_latent_norm).astype(jnp.bfloat16).reshape(latents.shape)
    d_media, grad_media_gain, grad_media_bias = jax.vjp(
        layer_norm, media_rows, back_vectors[0], back_vectors[1]
    )[1](d_media_normed)
    grad_media = d_media.astype(jnp.bfloat16).reshape(media.shape)
    vector_grads = jnp.stack([
        grad_media_gain, grad_media_bias, grad_latent_gain, grad_latent_bias, grad_feed_gain, grad_feed_bias])
    weight_grads = [
        g.astype(jnp.bfloat16) for g in (grad_query, grad_context, grad_output, grad_up, grad_down)]
    if tiled:
        summed, vector_sums = reduce_gradients(weight_grads, jnp.pad(vector_grads, ((0, 2), (0, 0))), chips // 4)
        width = media_gain.shape[0]
        mine = lax.dynamic_slice(vector_sums, (0, lax.axis_index("dp") * width), (6, width))
        owned = tuple(mine) + tuple(summed)
    else:
        vector_sums = lax.psum_scatter(vector_grads, "dp", scatter_dimension=1, tiled=True)
        summed = [lax.psum_scatter(g, "dp", scatter_dimension=0, tiled=True) for g in weight_grads]
        owned = tuple(lax.psum(vector_sums, "rep")) + tuple(
            lax.psum(s, "rep").astype(jnp.float32) for s in summed)
    return (
        latents_out,
        grad_media,
        grad_latents,
        owned[0],
        owned[1],
        owned[2],
        owned[3],
        owned[4],
        owned[5],
        owned[6],
        owned[7],
        owned[8],
        owned[9],
        owned[10],
    )


def solution(mesh):
    return jax.shard_map(
        body,
        mesh=mesh,
        in_specs=(
            P(("dp", "rep"), None, None, None),
            P(("dp", "rep"), None, None, None),
            P(("dp", "rep")),
            P(("dp", "rep"), None, None, None),
            P("dp"),
            P("dp"),
            P("dp"),
            P("dp"),
            P("dp"),
            P("dp"),
            P("dp", None),
            P("dp", None),
            P("dp", None),
            P("dp", None),
            P("dp", None),
        ),
        out_specs=(
            P(("dp", "rep"), None, None, None),
            P(("dp", "rep"), None, None, None),
            P(("dp", "rep"), None, None, None),
            P("dp"),
            P("dp"),
            P("dp"),
            P("dp"),
            P("dp"),
            P("dp"),
            P("dp", None),
            P("dp", None),
            P("dp", None),
            P("dp", None),
            P("dp", None),
        ),
        check_vma=False,
    )
```

```python
import functools

import jax
import jax.numpy as jnp
from jax import lax
from jax.experimental import pallas as pl
from jax.experimental.pallas import tpu as pltpu
from jax.sharding import PartitionSpec as P

HEAD_DIM = 64
GROUP = 256

epsilon = 1e-05

MESH = pl.DeviceIdType.MESH
ALL = slice(None)
F32 = jnp.float32
BF16 = jnp.bfloat16


class Links:
    def __init__(self, length):
        self.length = length
        self.dp = lax.axis_index("dp")
        self.rep = lax.axis_index("rep")
        self.z = lax.div(self.dp, 4)
        self.y = lax.rem(lax.div(self.dp, 2), 2)
        self.x = lax.rem(self.dp, 2)

    def device(self, axis, way=0):
        if axis == "core":
            return (self.dp, 1 - self.rep)
        if axis == "x":
            return (self.dp + 1 - 2 * self.x, self.rep)
        if axis == "y":
            return (self.dp + 2 - 4 * self.y, self.rep)
        return (self.dp + 4 * (self.along(way) - self.z), self.rep)

    def along(self, way):
        return lax.rem(self.z + way + self.length, self.length)

    def greet(self):
        barrier = pltpu.get_barrier_semaphore()
        peers = [("core", 0), ("x", 0), ("y", 0)] + [("z", way) for way in range(1, self.length)]
        for axis, way in peers:
            pl.semaphore_signal(barrier, inc=1, device_id=self.device(axis, way), device_id_type=MESH)
        pl.semaphore_wait(barrier, len(peers))


class Move:
    def __init__(self, send, recv, slot, device, source, target, landing):
        self.out = pltpu.make_async_remote_copy(
            src_ref=source, dst_ref=target, send_sem=send.at[slot], recv_sem=recv.at[slot],
            device_id=device, device_id_type=MESH)
        self.into = pltpu.make_async_remote_copy(
            src_ref=landing, dst_ref=landing, send_sem=send.at[slot], recv_sem=recv.at[slot],
            device_id=device, device_id_type=MESH)

    def start(self):
        self.out.start()

    def wait(self):
        self.into.wait_recv()

    def drain(self):
        self.out.wait_send()


class Slots:
    def __init__(self, send, recv):
        self.send, self.recv, self.made = send, recv, []

    def move(self, *args):
        self.made.append(Move(self.send, self.recv, len(self.made), *args))
        return self.made[-1]

    def drain(self):
        for move in self.made:
            move.drain()


class Locals:
    def __init__(self, semaphores):
        self.semaphores, self.made = semaphores, []

    def copy(self, source, target):
        self.made.append(pltpu.make_async_copy(source, target, self.semaphores.at[len(self.made)]))
        self.made[-1].start()
        return self.made[-1]


class Gather:
    def __init__(self, links, slots, view, order, halved):
        z, y, x, length = links.z, links.y, links.x, links.length
        here = {"z": z, "y": y, "x": x}
        mine = view(z, y, x)
        self.moves = [[
            slots.move(links.device("z", way), mine, mine, view(links.along(-way), y, x))
            for way in range(1, length)]]
        here["z"] = ALL
        for axis in order:
            mine = view(here["z"], here["y"], here["x"])
            other = dict(here)
            other[axis] = 1 - here[axis]
            self.moves.append([
                slots.move(links.device(axis), mine, mine, view(other["z"], other["y"], other["x"]))])
            here[axis] = ALL
        if halved:
            mine = view(ALL, ALL, ALL)
            self.moves.append([
                slots.move(links.device("core"), mine, mine, view(ALL, ALL, ALL, 1 - links.rep))])

    def step(self, number):
        if 0 < number <= len(self.moves):
            for move in self.moves[number - 1]:
                move.wait()
        if 0 <= number < len(self.moves):
            for move in self.moves[number]:
                move.start()


class Reduce:
    def __init__(self, links, slots, own, order, lands_b, lands_a, lands_z, finish):
        self.own, self.links, self.finish, self.lands_z = own, links, finish, lands_z
        self.moves, self.adds = [], []
        z, y, x, length = links.z, links.y, links.x, links.length
        here = {"z": ALL, "y": ALL, "x": ALL}
        for axis, lands in zip(order, (lands_b, lands_a)):
            away, home = dict(here), dict(here)
            place = {"y": y, "x": x}[axis]
            away[axis], home[axis] = 1 - place, place
            self.moves.append([slots.move(
                links.device(axis), own(away["z"], away["y"], away["x"]), lands, lands)])
            here = home
            self.adds.append(functools.partial(add_into, own(home["z"], home["y"], home["x"]), lands))
        self.moves.append([
            slots.move(links.device("z", way), own(links.along(way), y, x), lands_z.at[way - 1], lands_z.at[way - 1])
            for way in range(1, length)])
        self.adds.append(self.end)

    def step(self, number):
        if 0 < number <= len(self.moves):
            for move in self.moves[number - 1]:
                move.wait()
            self.adds[number - 1]()
        if 0 <= number < len(self.moves):
            for move in self.moves[number]:
                move.start()

    def end(self):
        links = self.links
        total = self.own(links.z, links.y, links.x)[...].astype(F32)
        for way in range(1, links.length):
            total = total + self.lands_z[way - 1].astype(F32)
        self.finish(total)


def add_into(target, arrived):
    lead = target.shape[:-2]
    count = 1
    for size in lead:
        count *= size

    @pl.loop(0, count)
    def _(flat):
        index = []
        for size in reversed(lead):
            index.insert(0, lax.rem(flat, size))
            flat = lax.div(flat, size)
        index = tuple(index)
        target[index] = (target[index].astype(F32) + arrived[index].astype(F32)).astype(target.dtype)


def run(items, depth, tick):
    for number, item in enumerate(items):
        if 0 <= tick - number < depth:
            for part in item:
                part.step(tick - number)


def matmul(left, right):
    return jnp.dot(left, right, preferred_element_type=F32)


def matmul_left(left, right):
    return lax.dot_general(left, right, (((0,), (0,)), ((), ())), preferred_element_type=F32)


def matmul_right(left, right):
    return lax.dot_general(left, right, (((1,), (1,)), ((), ())), preferred_element_type=F32)


def layer_norm(values, gain, offset):
    centre = jnp.mean(values, axis=-1, keepdims=True)
    shifted = values - centre
    spread = jnp.mean(shifted * shifted, axis=-1, keepdims=True)
    return shifted * lax.rsqrt(spread + epsilon) * gain + offset


def layer_norm_back(values, gain, upstream):
    centre = jnp.mean(values, axis=-1, keepdims=True)
    shifted = values - centre
    spread = jnp.mean(shifted * shifted, axis=-1, keepdims=True)
    rate = lax.rsqrt(spread + epsilon)
    normed = shifted * rate
    scaled = upstream * gain
    first = jnp.mean(scaled, axis=-1, keepdims=True)
    second = jnp.mean(scaled * normed, axis=-1, keepdims=True)
    return rate * (scaled - first - normed * second), upstream * normed


def gelu_exact(values):
    return 0.5 * values * (1.0 + jax.scipy.special.erf(values * 0.7071067811865476))


def gelu_parts(values):
    cumulative = 0.5 * (1.0 + lax.erf(values * 0.7071067811865476))
    density = 0.3989422804014327 * jnp.exp(-0.5 * values * values)
    return values * cumulative, cumulative + values * density


def tiles(count, size, action):
    @pl.loop(0, count)
    def _(number):
        action(pl.multiple_of(number * size, size))


def head_mask(rows, columns):
    heads = columns // HEAD_DIM
    row = lax.broadcasted_iota(jnp.int32, (rows * heads, columns), 0)
    column = lax.broadcasted_iota(jnp.int32, (rows * heads, columns), 1)
    head_row = jnp.zeros_like(row)
    head_column = jnp.zeros_like(row)
    for head in range(1, heads):
        head_row = head_row + jnp.where(row >= head * rows, 1, 0)
        head_column = head_column + jnp.where(column >= head * HEAD_DIM, 1, 0)
    return jnp.where(head_row == head_column, 1.0, 0.0)


def spread_heads(rows, mask):
    return jnp.concatenate([rows] * (mask.shape[0] // rows.shape[0]), axis=0) * mask


def pick_heads(stacked, mask, rows):
    kept = stacked * mask
    total = kept[:rows]
    for head in range(1, stacked.shape[0] // rows):
        total = total + kept[head * rows:(head + 1) * rows]
    return total


def softmax(scores):
    exponent = jnp.exp(scores - jnp.max(scores, axis=-1, keepdims=True))
    return exponent / jnp.sum(exponent, axis=-1, keepdims=True)


def forward_kernel(length, scaling, counts, media, latents, grad_out, packed, query_shard, context_shard,
                   output_shard, up_shard, down_shard, context_out, key_value_out, query_out, attended_out,
                   after_out, d_feed_out, latents_out, grad_up_out, grad_down_out, vectors_out, query_weight_out,
                   context_weight_out, output_weight_out, query_all, context_all, output_all, up_all, down_all,
                   packed_all, vectors, media_in, latents_in, grad_in, context, key_value, query, attended, after,
                   feed, feed_t, branch, branch_t, d_active, active, d_hidden, after_feed, d_feed, after_lands,
                   d_feed_lands, out_stage, grad_up, grad_down, mask, send, recv, local):
    links = Links(length)
    z, y, x, rep = links.z, links.y, links.x, links.rep
    slots, locals_ = Slots(send, recv), Locals(local)
    slot_count, patches, width = media.shape
    latent_count = latents.shape[1]
    key_count = patches + latent_count
    rows = slot_count * latent_count
    inner = query.shape[-1]
    chunk = d_active.shape[-1]
    chunks = d_active.shape[0]

    staged = [locals_.copy(packed, packed_all.at[z, y, x])]
    for shard, whole in ((context_shard, context_all), (query_shard, query_all), (output_shard, output_all)):
        half = whole.shape[-2]
        staged.append(locals_.copy(shard.at[pl.ds(pl.multiple_of(rep * half, 16), half)], whole.at[z, y, x, rep]))
    grad_load = locals_.copy(grad_out, grad_in)
    half = down_all.shape[-2]
    staged.append(locals_.copy(down_shard.at[pl.ds(pl.multiple_of(rep * half, 16), half)], down_all.at[z, y, x]))
    for block in range(up_all.shape[-1] // half):
        begin = pl.multiple_of((2 * block + rep) * half, half)
        staged.append(locals_.copy(
            up_shard.at[:, pl.ds(begin, half)], up_all.at[z, y, x, :, pl.ds(block * half, half)]))
    latents_load = locals_.copy(latents, latents_in)
    media_load = [locals_.copy(media.at[j], media_in.at[j]) for j in range(slot_count)]
    links.greet()
    for copy in staged:
        copy.wait()

    def halves(whole, begin, size, order):
        def view(zi, yi, xi, half=rep):
            return whole.at[zi, yi, xi, half, :, pl.ds(begin, size)]

        return Gather(links, slots, view, order, True)

    def columns(whole, begin, size, order):
        return Gather(links, slots, lambda zi, yi, xi: whole.at[zi, yi, xi, :, pl.ds(begin, size)], order, False)

    xy, yx = ("x", "y"), ("y", "x")
    items = [
        [Gather(links, slots, lambda zi, yi, xi: packed_all.at[zi, yi, xi], xy, False),
         halves(context_all, 0, width // 2, xy), halves(context_all, width // 2, width // 2, yx)],
        [halves(query_all, 0, inner, xy), halves(output_all, 0, width, yx)],
    ]
    for whole in (down_all, up_all):
        part = whole.shape[-1] // (2 * chunks)
        for number in range(chunks):
            items.append([columns(whole, 2 * number * part, part, xy), columns(whole, (2 * number + 1) * part, part, yx)])
    depth = length + 1

    def pump(tick):
        run(items, 5, tick)

    pump(0)
    grad_load.wait()
    count = counts[0]
    for j in range(slot_count):
        keep = jnp.where(j < count, 1.0, 0.0)
        branch[pl.ds(j * latent_count, latent_count)] = (grad_in[j].astype(F32) * keep).astype(BF16)
    branch_move = slots.move(links.device("core"), branch.at[pl.ds(0, rows)], branch.at[pl.ds(rows, rows)],
                             branch.at[pl.ds(rows, rows)])
    branch_move.start()
    mask[...] = head_mask(latent_count, GROUP)
    pump(1)
    latents_load.wait()
    for copy in media_load:
        copy.wait()
    pump(2)
    pump(3)
    lane = packed_all.shape[-1]
    for zi in range(length):
        for yi in range(2):
            place = (zi * 2 + yi) * lane
            vectors[:, place:place + lane] = (packed_all[zi, yi, 0] + packed_all[zi, yi, 1]).astype(F32)[:8]

    step = 32
    for j in range(slot_count):
        def media_tile(at, j=j):
            context[j, pl.ds(at, step)] = layer_norm(
                media_in[j, pl.ds(at, step)].astype(F32), vectors[0:1], vectors[1:2]).astype(BF16)

        def latent_tile(at, j=j):
            context[j, pl.ds(patches + at, step)] = layer_norm(
                latents_in[j, pl.ds(at, step)].astype(F32), vectors[2:3], vectors[3:4]).astype(BF16)

        tiles(patches // step, step, media_tile)
        tiles(latent_count // step, step, latent_tile)
    pump(4)

    weight_step = 256

    def key_value_slot(j):
        def body(at):
            weight = context_all[:, :, :, :, :, pl.ds(at, weight_step)].reshape(width, weight_step)
            key_value[j, :, pl.ds(at, weight_step)] = matmul(context[j], weight).astype(BF16)

        tiles(width // weight_step, weight_step, body)

    pl.loop(0, slot_count)(key_value_slot)
    pump(5)

    latent_normed = context[:, patches:, :].reshape(rows, width)
    query[...] = (matmul(latent_normed, query_all[...].reshape(width, inner)) * scaling).astype(BF16).reshape(
        slot_count, latent_count, inner)

    def attention_slot(j):
        for begin in range(0, inner, GROUP):
            stacked = spread_heads(query[j, :, begin:begin + GROUP], mask[...].astype(BF16))
            probs = softmax(matmul_right(stacked, key_value[j, :, begin:begin + GROUP])).astype(BF16)
            result = matmul(probs, key_value[j, :, inner + begin:inner + begin + GROUP])
            attended[j, :, begin:begin + GROUP] = pick_heads(result, mask[...], latent_count).astype(BF16)

    pl.loop(0, slot_count)(attention_slot)
    pump(6)

    def output_tile(at):
        weight = output_all[:, :, :, :, :, pl.ds(at, weight_step)].reshape(inner, weight_step)
        after[:, pl.ds(at, weight_step)] = latents_in[:, :, pl.ds(at, weight_step)].reshape(
            rows, weight_step).astype(F32) + matmul(attended[...].reshape(rows, inner), weight)

    tiles(width // weight_step, weight_step, output_tile)

    def feed_tile(at):
        feed[pl.ds(at, step)] = layer_norm(after[pl.ds(at, step)], vectors[4:5], vectors[5:6]).astype(BF16)

    tiles(rows // step, step, feed_tile)
    feed_move = slots.move(links.device("core"), feed.at[pl.ds(0, rows)], feed.at[pl.ds(rows, rows)],
                           feed.at[pl.ds(rows, rows)])
    feed_move.start()
    written = [
        locals_.copy(context, context_out), locals_.copy(key_value, key_value_out), locals_.copy(query, query_out),
        locals_.copy(attended, attended_out), locals_.copy(after, after_out),
        locals_.copy(query_all, query_weight_out), locals_.copy(context_all, context_weight_out),
        locals_.copy(output_all, output_weight_out), locals_.copy(vectors, vectors_out)]
    pump(7)
    branch_move.wait()

    def turn(source, target):
        def body(at):
            target[pl.ds(at, weight_step)] = source[:, pl.ds(at, weight_step)].T

        tiles(width // weight_step, weight_step, body)

    turn(branch, branch_t)
    feed_move.wait()
    turn(feed, feed_t)
    pump(8)
    both = 2 * rows
    tall = rows

    for c in range(chunks):
        def d_active_tile(at, c=c):
            weight = down_all[c].reshape(chunk, width)
            d_active[c, pl.ds(at, tall)] = matmul_right(branch[pl.ds(at, tall)], weight).astype(BF16)

        tiles(both // tall, tall, d_active_tile)
    for c in range(chunks):
        pump(9 + c)
        begin = c * chunk
        short = 128

        def hidden_tile(at, c=c, begin=begin):
            weight = up_all[:, :, :, :, begin:begin + chunk].reshape(width, chunk)
            value, slope = gelu_parts(matmul(feed[pl.ds(at, short)], weight))
            active[pl.ds(at, short)] = value.astype(BF16)
            d_hidden[pl.ds(at, short)] = (d_active[c, pl.ds(at, short)].astype(F32) * slope).astype(BF16)

        tiles(both // short, short, hidden_tile)

        def forward_tile(at, c=c):
            value = matmul(active[pl.ds(at, tall)], down_all[c].reshape(chunk, width))
            after_feed[pl.ds(at, tall)] = value if c == 0 else after_feed[pl.ds(at, tall)] + value

        def back_tile(at, c=c, begin=begin):
            weight = up_all[:, :, :, :, begin:begin + chunk].reshape(width, chunk)
            value = matmul_right(d_hidden[pl.ds(at, tall)], weight)
            d_feed[pl.ds(at, tall)] = value if c == 0 else d_feed[pl.ds(at, tall)] + value

        tiles(both // tall, tall, forward_tile)
        tiles(both // tall, tall, back_tile)
        if c == chunks - 1:
            after_move = slots.move(links.device("core"), after_feed.at[pl.ds(rows, rows)], after_lands, after_lands)
            d_feed_move = slots.move(links.device("core"), d_feed.at[pl.ds(rows, rows)], d_feed_lands, d_feed_lands)
            d_feed_move.start()
            after_move.start()

        def grad_tile(zi, begin=begin, c=c):
            place = pl.multiple_of(zi * (width // length), width // length)
            up = matmul(feed_t[pl.ds(place, width // length)], d_hidden[...]).astype(BF16)
            grad_up[zi, :, :, :, begin:begin + chunk] = up.reshape(2, 2, width // (4 * length), chunk)
            down = matmul(branch_t[pl.ds(place, width // length)], active[...]).astype(BF16)
            block = chunk // 4
            for number in range(4):
                grad_down[c, number // 2, number % 2, pl.ds(place, width // length)] = down[
                    :, number * block:(number + 1) * block]

        pl.loop(0, length)(grad_tile)
        written.append(locals_.copy(
            grad_up.at[:, :, :, :, pl.ds(begin, chunk)], grad_up_out.at[:, :, :, :, pl.ds(begin, chunk)]))
        written.append(locals_.copy(grad_down.at[c], grad_down_out.at[c]))
    d_feed_move.wait()

    def d_feed_tile(at):
        d_feed[pl.ds(at, step)] = d_feed[pl.ds(at, step)] + d_feed_lands[pl.ds(at, step)]

    tiles(rows // step, step, d_feed_tile)
    written.append(locals_.copy(d_feed.at[pl.ds(0, rows)], d_feed_out))
    after_move.wait()
    for j in range(slot_count):
        keep = jnp.where(j < count, 1.0, 0.0)
        own = pl.ds(j * latent_count, latent_count)
        out_stage[j] = ((after[own] + after_feed[own] + after_lands[own]) * keep).astype(BF16)
    written.append(locals_.copy(out_stage, latents_out))
    for copy in written:
        copy.wait()
    slots.drain()


def forward(length, counts, media, latents, grad_out, packed, shards):
    query_shard, context_shard, output_shard, up_shard, down_shard = shards
    slot_count, patches, width = media.shape
    latent_count = latents.shape[1]
    key_count = patches + latent_count
    rows = slot_count * latent_count
    inner = query_shard.shape[1]
    hidden = up_shard.shape[1] // 2
    chunk = hidden // length
    blocks = (length, 2, 2)

    def halved(shard):
        return blocks + (2, shard.shape[0] // 2, shard.shape[1])

    grad_up_shape = blocks + (up_shard.shape[0], hidden)
    grad_down_shape = blocks + (width, down_shard.shape[0] // 2)
    anywhere = pl.BlockSpec(memory_space=pl.ANY)
    outs = [
        ((slot_count, key_count, width), BF16),
        ((slot_count, key_count, 2 * inner), BF16),
        ((slot_count, latent_count, inner), BF16),
        ((slot_count, latent_count, inner), BF16),
        ((rows, width), F32),
        ((rows, width), F32),
        (latents.shape, BF16),
        (grad_up_shape, BF16),
        (grad_down_shape, BF16),
        ((8, width), F32),
        (halved(query_shard), BF16),
        (halved(context_shard), BF16),
        (halved(output_shard), BF16),
    ]
    scratch = [
        pltpu.VMEM(halved(query_shard), BF16),
        pltpu.VMEM(halved(context_shard), BF16),
        pltpu.VMEM(halved(output_shard), BF16),
        pltpu.VMEM(grad_up_shape, BF16),
        pltpu.VMEM(blocks + (down_shard.shape[0] // 2, width), BF16),
        pltpu.VMEM(blocks + packed.shape, BF16),
        pltpu.VMEM((8, width), F32),
        pltpu.VMEM(media.shape, BF16),
        pltpu.VMEM(latents.shape, BF16),
        pltpu.VMEM(grad_out.shape, BF16),
        pltpu.VMEM((slot_count, key_count, width), BF16),
        pltpu.VMEM((slot_count, key_count, 2 * inner), BF16),
        pltpu.VMEM((slot_count, latent_count, inner), BF16),
        pltpu.VMEM((slot_count, latent_count, inner), BF16),
        pltpu.VMEM((rows, width), F32),
        pltpu.VMEM((2 * rows, width), BF16),
        pltpu.VMEM((width, 2 * rows), BF16),
        pltpu.VMEM((2 * rows, width), BF16),
        pltpu.VMEM((width, 2 * rows), BF16),
        pltpu.VMEM((length, 2 * rows, chunk), BF16),
        pltpu.VMEM((2 * rows, chunk), BF16),
        pltpu.VMEM((2 * rows, chunk), BF16),
        pltpu.VMEM((2 * rows, width), F32),
        pltpu.VMEM((2 * rows, width), F32),
        pltpu.VMEM((rows, width), F32),
        pltpu.VMEM((rows, width), F32),
        pltpu.VMEM(latents.shape, BF16),
        pltpu.VMEM(grad_up_shape, BF16),
        pltpu.VMEM(grad_down_shape, BF16),
        pltpu.VMEM((latent_count * (GROUP // HEAD_DIM), GROUP), F32),
        pltpu.SemaphoreType.DMA((140,)),
        pltpu.SemaphoreType.DMA((140,)),
        pltpu.SemaphoreType.DMA((64,)),
    ]
    return pl.pallas_call(
        functools.partial(forward_kernel, length, HEAD_DIM ** (-0.5)),
        out_shape=[jax.ShapeDtypeStruct(*o) for o in outs],
        in_specs=[pl.BlockSpec(memory_space=pltpu.SMEM)] + [anywhere] * 9,
        out_specs=[anywhere] * len(outs),
        scratch_shapes=scratch,
        compiler_params=pltpu.CompilerParams(
            collective_id=0, has_side_effects=True, vmem_limit_bytes=60 * 2 ** 20),
        name="forward_and_feed",
    )(counts, media, latents, grad_out, packed, query_shard, context_shard, output_shard, up_shard, down_shard)


def reduce_kernel(length, grads, vectors, outs, vectors_out, own, lands_c, lands_b, lands_a, lands_z, result,
                  vector_lands, send, recv, local):
    links = Links(length)
    rep = links.rep
    slots, locals_ = Slots(send, recv), Locals(local)
    loads, siblings = [], []
    for grad, mine, land in zip(grads, own, lands_c):
        loads.append(locals_.copy(grad.at[:, :, :, rep] if land is not None else grad, mine))
    links.greet()
    for grad, land in zip(grads, lands_c):
        siblings.append(None if land is None else slots.move(
            links.device("core"), grad.at[:, :, :, 1 - rep], land, land))

    def half(number, rows, columns, order):
        def finish(value):
            result[number][rows, columns] = value

        return Reduce(
            links, slots, lambda zi, yi, xi: own[number].at[zi, yi, xi, rows, columns], order,
            lands_b[number].at[:, :, rows, columns], lands_a[number].at[:, rows, columns],
            lands_z[number].at[:, rows, columns], finish)

    xy, yx = ("x", "y"), ("y", "x")
    items, firsts = [], []
    for number in (3, 4, 2, 0, 1):
        height, width = own[number].shape[-2:]
        wide = number != 4
        size = width if wide else height
        parts = length if lands_c[number] is None else 1
        size //= 2 * parts
        for part in range(parts):
            windows = [pl.ds((2 * part + which) * size, size) for which in range(2)]
            whole = pl.ds(0, height if wide else width)
            items.append([half(number, whole if wide else w, w if wide else whole, order)
                          for w, order in zip(windows, (yx, xy))])
            firsts.append(number if part == 0 else None)
    for move in siblings:
        if move is not None:
            move.start()
    vectors_out[...] = vectors[...]
    for number, axis in enumerate(("core", "x", "y")):
        mine, land = vector_lands.at[2 * number], vector_lands.at[2 * number + 1]
        mine[...] = vectors_out[...]
        move = slots.move(links.device(axis), mine, land, land)
        move.start()
        move.wait()
        vectors_out[...] = mine[...] + land[...]
    mine = vector_lands.at[6]
    mine[...] = vectors_out[...]
    line = [slots.move(links.device("z", way), mine, vector_lands.at[6 + way], vector_lands.at[6 + way])
            for way in range(1, length)]
    for move in line:
        move.start()
    depth = 4
    for tick in range(len(items) + depth - 1):
        if tick < len(items) and firsts[tick] is not None:
            number = firsts[tick]
            loads[number].wait()
            if siblings[number] is not None:
                siblings[number].wait()
                add_into(own[number], lands_c[number])
        run(items, depth, tick)
    for way, move in enumerate(line):
        move.wait()
        vectors_out[...] = vectors_out[...] + vector_lands[7 + way]
    kept = []
    for total, out in zip(result, outs):
        kept.append(locals_.copy(total, out.at[rep]))
        move = slots.move(links.device("core"), total, out.at[rep], out.at[1 - rep])
        move.start()
        kept.append(move)
    for copy in kept:
        copy.wait()
    slots.drain()


def reduce_gradients(grads, vectors, length):
    blocks = (length, 2, 2)
    anywhere = pl.BlockSpec(memory_space=pl.ANY)
    count = len(grads)
    halves = [g.shape[-2:] for g in grads]
    halved = [len(g.shape) == 6 for g in grads]
    scratch = [
        [pltpu.VMEM(blocks + h, BF16) for h in halves],
        [pltpu.VMEM(blocks + h, BF16) if two else None for h, two in zip(halves, halved)],
        [pltpu.VMEM((length, 2) + h, BF16) for h in halves],
        [pltpu.VMEM((length,) + h, BF16) for h in halves],
        [pltpu.VMEM((length - 1,) + h, BF16) for h in halves],
        [pltpu.VMEM(h, F32) for h in halves],
        pltpu.VMEM((7 + length,) + vectors.shape, F32),
        pltpu.SemaphoreType.DMA((200,)),
        pltpu.SemaphoreType.DMA((200,)),
        pltpu.SemaphoreType.DMA((16,)),
    ]
    vmem = pl.BlockSpec(memory_space=pltpu.VMEM)
    return pl.pallas_call(
        functools.partial(reduce_kernel, length),
        out_shape=([jax.ShapeDtypeStruct((2,) + h, F32) for h in halves],
                   jax.ShapeDtypeStruct(vectors.shape, F32)),
        in_specs=[[anywhere] * count, vmem],
        out_specs=([anywhere] * count, vmem),
        scratch_shapes=scratch,
        compiler_params=pltpu.CompilerParams(
            collective_id=1, has_side_effects=True, vmem_limit_bytes=56 * 2 ** 20),
        name="reduce_gradients",
    )(grads, vectors)


def head_scores(first_heads, second_heads):
    return jnp.einsum(
        "bqhd,bkhd->bhqk", first_heads, second_heads, preferred_element_type=jnp.float32
    )


def collective_body(
    media,
    latents,
    image_counts,
    grad_out,
    media_gain,
    media_bias,
    latent_gain,
    latent_bias,
    feed_gain,
    feed_bias,
    query_weight,
    context_weight,
    output_weight,
    up_weight,
    down_weight,
):
    samples, slots, patches, model_width = media.shape
    latent_count = latents.shape[2]
    inner_width = query_weight.shape[1]
    head_count = inner_width // HEAD_DIM
    blocks = samples * slots
    key_count = patches + latent_count
    latent_total = blocks * latent_count
    scaling = HEAD_DIM ** (-0.5)
    vector_shards = (media_gain, media_bias, latent_gain, latent_bias, feed_gain, feed_bias)
    weight_shards = (query_weight, context_weight, output_weight, up_weight, down_weight)
    gathered = tuple(lax.all_gather(s, "dp", axis=0, tiled=True) for s in vector_shards + weight_shards)
    vectors = [element.astype(jnp.float32) for element in gathered[:6]]
    media_rows = media.reshape(blocks * patches, model_width).astype(jnp.float32)
    latent_rows = latents.reshape(latent_total, model_width).astype(jnp.float32)
    media_normed = layer_norm(media_rows, vectors[0], vectors[1]).astype(jnp.bfloat16)
    latent_normed = layer_norm(latent_rows, vectors[2], vectors[3]).astype(jnp.bfloat16)
    queries = (matmul(latent_normed, gathered[6]) * scaling).astype(jnp.bfloat16)
    context = jnp.concatenate(
        [
            media_normed.reshape(blocks, patches, model_width),
            latent_normed.reshape(blocks, latent_count, model_width),
        ],
        axis=1,
    ).reshape(blocks * key_count, model_width)
    key_value = (
        matmul(context, gathered[7])
        .astype(jnp.bfloat16)
        .reshape(blocks, key_count, 2 * inner_width)
    )
    query_heads = queries.reshape(blocks, latent_count, head_count, HEAD_DIM)
    key_heads = key_value[:, :, :inner_width].reshape(blocks, key_count, head_count, HEAD_DIM)
    value_heads = key_value[:, :, inner_width:].reshape(blocks, key_count, head_count, HEAD_DIM)
    scores = head_scores(query_heads, key_heads)
    row_max = jnp.max(scores, axis=-1, keepdims=True)
    exponent = jnp.exp(scores - row_max)
    row_total = jnp.sum(exponent, axis=-1, keepdims=True)
    log_total = row_max + jnp.log(row_total)
    attention_weights = (exponent / row_total).astype(jnp.bfloat16)
    attended = (
        jnp.einsum(
            "bhqk,bkhd->bqhd", attention_weights, value_heads, preferred_element_type=jnp.float32
        )
        .astype(jnp.bfloat16)
        .reshape(latent_total, inner_width)
    )
    after_attention = latent_rows + matmul(attended, gathered[8])
    feed_input = layer_norm(after_attention, vectors[4], vectors[5]).astype(jnp.bfloat16)
    hidden = matmul(feed_input, gathered[9])
    activated = gelu_exact(hidden).astype(jnp.bfloat16)
    after_feed = after_attention + matmul(activated, gathered[10])
    slot_mask = (
        lax.broadcasted_iota(jnp.int32, (samples, slots), 1) < image_counts[:, None]
    ).astype(jnp.float32)
    row_mask = jnp.broadcast_to(slot_mask[:, :, None], (samples, slots, latent_count)).reshape(
        latent_total, 1
    )
    latents_out = (after_feed * row_mask).astype(jnp.bfloat16).reshape(latents.shape)
    backward_set = gathered
    back_vectors = [element.astype(jnp.float32) for element in backward_set[:6]]
    d_after = grad_out.reshape(latent_total, model_width).astype(jnp.float32) * row_mask
    d_branch = d_after.astype(jnp.bfloat16)
    grad_down = matmul_left(activated, d_branch)
    d_activated = matmul_right(d_branch, backward_set[10])
    d_hidden = jax.vjp(gelu_exact, hidden)[1](d_activated)[0].astype(jnp.bfloat16)
    grad_up = matmul_left(feed_input, d_hidden)
    d_feed = matmul_right(d_hidden, backward_set[9])
    d_feed_norm, grad_feed_gain, grad_feed_bias = jax.vjp(
        layer_norm, after_attention, back_vectors[4], back_vectors[5]
    )[1](d_feed)
    d_middle = d_after + d_feed_norm
    d_out_branch = d_middle.astype(jnp.bfloat16)
    grad_output = matmul_left(attended, d_out_branch)
    d_attended = (
        matmul_right(d_out_branch, backward_set[8])
        .astype(jnp.bfloat16)
        .reshape(blocks, latent_count, head_count, HEAD_DIM)
    )
    recomputed = jnp.exp(head_scores(query_heads, key_heads) - log_total)
    d_weights = head_scores(d_attended, value_heads)
    d_scores = (
        recomputed * (d_weights - jnp.sum(recomputed * d_weights, axis=-1, keepdims=True))
    ).astype(jnp.bfloat16)
    d_queries = (
        jnp.einsum(
            "bhqk,bkhd->bqhd", d_scores, key_heads, preferred_element_type=jnp.float32
        ).astype(jnp.bfloat16)
        * scaling
    ).reshape(latent_total, inner_width)
    d_keys = jnp.einsum(
        "bhqk,bqhd->bkhd", d_scores, query_heads, preferred_element_type=jnp.float32
    ).astype(jnp.bfloat16)
    d_values = jnp.einsum(
        "bhqk,bqhd->bkhd",
        recomputed.astype(jnp.bfloat16),
        d_attended,
        preferred_element_type=jnp.float32,
    ).astype(jnp.bfloat16)
    d_key_value = jnp.concatenate(
        [
            d_keys.reshape(blocks, key_count, inner_width),
            d_values.reshape(blocks, key_count, inner_width),
        ],
        axis=-1,
    ).reshape(blocks * key_count, 2 * inner_width)
    grad_query = matmul_left(latent_normed, d_queries)
    grad_context = matmul_left(context, d_key_value)
    d_context = matmul_right(d_key_value, backward_set[7]).reshape(blocks, key_count, model_width)
    d_latent_normed = matmul_right(d_queries, backward_set[6]) + d_context[:, patches:, :].reshape(
        latent_total, model_width
    )
    d_media_normed = d_context[:, :patches, :].reshape(blocks * patches, model_width)
    d_latent_norm, grad_latent_gain, grad_latent_bias = jax.vjp(
        layer_norm, latent_rows, back_vectors[2], back_vectors[3]
    )[1](d_latent_normed)
    grad_latents = (d_middle + d_latent_norm).astype(jnp.bfloat16).reshape(latents.shape)
    d_media, grad_media_gain, grad_media_bias = jax.vjp(
        layer_norm, media_rows, back_vectors[0], back_vectors[1]
    )[1](d_media_normed)
    grad_media = d_media.astype(jnp.bfloat16).reshape(media.shape)
    vector_grads = jnp.stack([
        grad_media_gain, grad_media_bias, grad_latent_gain, grad_latent_bias, grad_feed_gain, grad_feed_bias])
    weight_grads = [
        g.astype(jnp.bfloat16) for g in (grad_query, grad_context, grad_output, grad_up, grad_down)]
    vector_sums = lax.psum_scatter(vector_grads, "dp", scatter_dimension=1, tiled=True)
    summed = [lax.psum_scatter(g, "dp", scatter_dimension=0, tiled=True) for g in weight_grads]
    owned = tuple(lax.psum(vector_sums, "rep")) + tuple(
        lax.psum(s, "rep").astype(jnp.float32) for s in summed)
    return (
        latents_out,
        grad_media,
        grad_latents,
        owned[0],
        owned[1],
        owned[2],
        owned[3],
        owned[4],
        owned[5],
        owned[6],
        owned[7],
        owned[8],
        owned[9],
        owned[10],
    )


def body(media, latents, image_counts, grad_out, *parameters):
    chips = lax.axis_size("dp")
    weight_shards = parameters[6:]
    tiled = (media.shape[0] == 1 and chips % 4 == 0 and chips > 4 and parameters[0].shape[0] == 64
             and all(s.shape[0] % 32 == 0 for s in weight_shards))
    if not tiled:
        return collective_body(media, latents, image_counts, grad_out, *parameters)
    length = chips // 4
    slots, patches, model_width = media.shape[1:]
    latent_count = latents.shape[2]
    inner_width = weight_shards[0].shape[1]
    head_count = inner_width // HEAD_DIM
    key_count = patches + latent_count
    latent_total = slots * latent_count
    scaling = HEAD_DIM ** (-0.5)
    side = lax.rem(lax.axis_index("dp"), 2)
    stacked = jnp.stack(parameters[:6])
    packed = jnp.pad(
        jnp.concatenate([jnp.where(side == 0, stacked, 0), jnp.where(side == 0, 0, stacked)], axis=1), ((0, 10), (0, 0)))
    (context, key_value, queries, attended, after_attention, d_feed, latents_out, grad_up, grad_down, vectors,
     query_weight, context_weight, output_weight) = forward(
        length, image_counts, media[0], latents[0], grad_out[0], packed, weight_shards)
    query_weight = query_weight.reshape(model_width, inner_width)
    context_weight = context_weight.reshape(model_width, 2 * inner_width)
    output_weight = output_weight.reshape(inner_width, model_width)
    media_rows = media.reshape(slots * patches, model_width).astype(F32)
    latent_rows = latents.reshape(latent_total, model_width).astype(F32)
    attended = attended.reshape(latent_total, inner_width)
    latent_normed = context[:, patches:].reshape(latent_total, model_width)
    row_mask = jnp.repeat((jnp.arange(slots) < image_counts[0]).astype(F32), latent_count)[:, None]
    d_after = grad_out.reshape(latent_total, model_width).astype(F32) * row_mask
    d_norm, gain_terms = layer_norm_back(after_attention, vectors[4], d_feed)
    grad_feed_gain, grad_feed_bias = jnp.sum(gain_terms, axis=0), jnp.sum(d_feed, axis=0)
    d_middle = d_after + d_norm
    d_out_branch = d_middle.astype(BF16)
    grad_output = matmul_left(attended, d_out_branch).astype(BF16)
    d_attended = matmul_right(d_out_branch, output_weight).astype(BF16).reshape(
        slots, latent_count, head_count, HEAD_DIM)
    query_heads = queries.reshape(slots, latent_count, head_count, HEAD_DIM)
    key_heads = key_value[:, :, :inner_width].reshape(slots, key_count, head_count, HEAD_DIM)
    value_heads = key_value[:, :, inner_width:].reshape(slots, key_count, head_count, HEAD_DIM)
    recomputed = softmax(head_scores(query_heads, key_heads))
    d_weights = head_scores(d_attended, value_heads)
    d_scores = (
        recomputed * (d_weights - jnp.sum(recomputed * d_weights, axis=-1, keepdims=True))).astype(BF16)
    d_queries = (jnp.einsum("bhqk,bkhd->bqhd", d_scores, key_heads, preferred_element_type=F32).astype(BF16)
                 * scaling).reshape(latent_total, inner_width)
    d_keys = jnp.einsum("bhqk,bqhd->bkhd", d_scores, query_heads, preferred_element_type=F32).astype(BF16)
    d_values = jnp.einsum(
        "bhqk,bqhd->bkhd", recomputed.astype(BF16), d_attended, preferred_element_type=F32).astype(BF16)
    d_key_value = jnp.concatenate(
        [d_keys.reshape(slots, key_count, inner_width), d_values.reshape(slots, key_count, inner_width)],
        axis=-1).reshape(slots * key_count, 2 * inner_width)
    grad_query = matmul_left(latent_normed, d_queries).astype(BF16)
    grad_context = matmul_left(context.reshape(slots * key_count, model_width), d_key_value).astype(BF16)
    d_context = matmul_right(d_key_value, context_weight).reshape(slots, key_count, model_width)
    d_latent_normed = matmul_right(d_queries, query_weight) + d_context[:, patches:].reshape(
        latent_total, model_width)
    d_media_normed = d_context[:, :patches].reshape(slots * patches, model_width)
    d_latent_norm, gain_terms = layer_norm_back(latent_rows, vectors[2], d_latent_normed)
    grad_latent_gain, grad_latent_bias = jnp.sum(gain_terms, axis=0), jnp.sum(d_latent_normed, axis=0)
    grad_latents = (d_middle + d_latent_norm).astype(BF16).reshape(latents.shape)
    d_media, gain_terms = layer_norm_back(media_rows, vectors[0], d_media_normed)
    grad_media_gain, grad_media_bias = jnp.sum(gain_terms, axis=0), jnp.sum(d_media_normed, axis=0)
    grad_media = d_media.astype(BF16).reshape(media.shape)
    zeros = jnp.zeros_like(grad_media_gain)
    vector_grads = jnp.stack([
        grad_media_gain, grad_media_bias, grad_latent_gain, grad_latent_bias, grad_feed_gain, grad_feed_bias,
        zeros, zeros])

    def halved(grad):
        return grad.reshape(length, 2, 2, 2, grad.shape[0] // (8 * length), grad.shape[1])

    summed, vector_sums = reduce_gradients(
        [halved(grad_query), halved(grad_context), halved(grad_output), grad_up, grad_down], vector_grads, length)
    sums = [s.reshape(-1, s.shape[-1]) for s in summed[:3]]
    rows, hidden = summed[3].shape[1:]
    half = summed[4].shape[-1]
    sums.append(summed[3].reshape(2, rows, hidden // half, half).transpose(1, 2, 0, 3).reshape(rows, 2 * hidden))
    sums.append(summed[4].transpose(0, 2, 1).reshape(2 * half, model_width))
    width = parameters[0].shape[0]
    mine = lax.dynamic_slice(vector_sums, (0, lax.axis_index("dp") * width), (6, width))
    return (latents_out[None], grad_media, grad_latents) + tuple(mine) + tuple(sums)


def solution(mesh):
    return jax.shard_map(
        body,
        mesh=mesh,
        in_specs=(
            P(("dp", "rep"), None, None, None),
            P(("dp", "rep"), None, None, None),
            P(("dp", "rep")),
            P(("dp", "rep"), None, None, None),
            P("dp"),
            P("dp"),
            P("dp"),
            P("dp"),
            P("dp"),
            P("dp"),
            P("dp", None),
            P("dp", None),
            P("dp", None),
            P("dp", None),
            P("dp", None),
        ),
        out_specs=(
            P(("dp", "rep"), None, None, None),
            P(("dp", "rep"), None, None, None),
            P(("dp", "rep"), None, None, None),
            P("dp"),
            P("dp"),
            P("dp"),
            P("dp"),
            P("dp"),
            P("dp"),
            P("dp", None),
            P("dp", None),
            P("dp", None),
            P("dp", None),
            P("dp", None),
        ),
        check_vma=False,
    )
```

```python
import functools

import jax
import jax.numpy as jnp
from jax import lax
from jax.experimental import pallas as pl
from jax.experimental.pallas import tpu as pltpu
from jax.sharding import PartitionSpec as P

HEAD_DIM = 64
GROUP = 256

epsilon = 1e-05

MESH = pl.DeviceIdType.MESH
ALL = slice(None)
F32 = jnp.float32
BF16 = jnp.bfloat16


class Links:
    def __init__(self, length):
        self.length = length
        self.dp = lax.axis_index("dp")
        self.rep = lax.axis_index("rep")
        self.z = lax.div(self.dp, 4)
        self.y = lax.rem(lax.div(self.dp, 2), 2)
        self.x = lax.rem(self.dp, 2)

    def device(self, axis, way=0):
        if axis == "core":
            return (self.dp, 1 - self.rep)
        if axis == "x":
            return (self.dp + 1 - 2 * self.x, self.rep)
        if axis == "y":
            return (self.dp + 2 - 4 * self.y, self.rep)
        return (self.dp + 4 * (self.along(way) - self.z), self.rep)

    def along(self, way):
        return lax.rem(self.z + way + self.length, self.length)

    def greet(self):
        barrier = pltpu.get_barrier_semaphore()
        peers = [("core", 0), ("x", 0), ("y", 0)] + [("z", way) for way in range(1, self.length)]
        for axis, way in peers:
            pl.semaphore_signal(barrier, inc=1, device_id=self.device(axis, way), device_id_type=MESH)
        pl.semaphore_wait(barrier, len(peers))


class Move:
    def __init__(self, send, recv, slot, device, source, target, landing):
        self.out = pltpu.make_async_remote_copy(
            src_ref=source, dst_ref=target, send_sem=send.at[slot], recv_sem=recv.at[slot],
            device_id=device, device_id_type=MESH)
        self.into = pltpu.make_async_remote_copy(
            src_ref=landing, dst_ref=landing, send_sem=send.at[slot], recv_sem=recv.at[slot],
            device_id=device, device_id_type=MESH)

    def start(self):
        self.out.start()

    def wait(self):
        self.into.wait_recv()

    def drain(self):
        self.out.wait_send()


class Slots:
    def __init__(self, send, recv):
        self.send, self.recv, self.made = send, recv, []

    def move(self, *args):
        self.made.append(Move(self.send, self.recv, len(self.made), *args))
        return self.made[-1]

    def drain(self):
        for move in self.made:
            move.drain()


class Locals:
    def __init__(self, semaphores):
        self.semaphores, self.made = semaphores, []

    def copy(self, source, target):
        self.made.append(pltpu.make_async_copy(source, target, self.semaphores.at[len(self.made)]))
        self.made[-1].start()
        return self.made[-1]


class Gather:
    def __init__(self, links, slots, view, order, halved):
        z, y, x, length = links.z, links.y, links.x, links.length
        here = {"z": z, "y": y, "x": x}
        mine = view(z, y, x)
        self.moves = [[
            slots.move(links.device("z", way), mine, mine, view(links.along(-way), y, x))
            for way in range(1, length)]]
        here["z"] = ALL
        for axis in order:
            mine = view(here["z"], here["y"], here["x"])
            other = dict(here)
            other[axis] = 1 - here[axis]
            self.moves.append([
                slots.move(links.device(axis), mine, mine, view(other["z"], other["y"], other["x"]))])
            here[axis] = ALL
        if halved:
            mine = view(ALL, ALL, ALL)
            self.moves.append([
                slots.move(links.device("core"), mine, mine, view(ALL, ALL, ALL, 1 - links.rep))])

    def step(self, number):
        if 0 < number <= len(self.moves):
            for move in self.moves[number - 1]:
                move.wait()
        if 0 <= number < len(self.moves):
            for move in self.moves[number]:
                move.start()


class Reduce:
    def __init__(self, links, slots, own, order, lands_b, lands_a, lands_z, finish):
        self.own, self.links, self.finish, self.lands_z = own, links, finish, lands_z
        self.moves, self.adds = [], []
        z, y, x, length = links.z, links.y, links.x, links.length
        here = {"z": ALL, "y": ALL, "x": ALL}
        for axis, lands in zip(order, (lands_b, lands_a)):
            away, home = dict(here), dict(here)
            place = {"y": y, "x": x}[axis]
            away[axis], home[axis] = 1 - place, place
            self.moves.append([slots.move(
                links.device(axis), own(away["z"], away["y"], away["x"]), lands, lands)])
            here = home
            self.adds.append(functools.partial(add_into, own(home["z"], home["y"], home["x"]), lands))
        self.moves.append([
            slots.move(links.device("z", way), own(links.along(way), y, x), lands_z.at[way - 1], lands_z.at[way - 1])
            for way in range(1, length)])
        self.adds.append(self.end)

    def step(self, number):
        if 0 < number <= len(self.moves):
            for move in self.moves[number - 1]:
                move.wait()
            self.adds[number - 1]()
        if 0 <= number < len(self.moves):
            for move in self.moves[number]:
                move.start()

    def end(self):
        links = self.links
        total = self.own(links.z, links.y, links.x)[...].astype(F32)
        for way in range(1, links.length):
            total = total + self.lands_z[way - 1].astype(F32)
        self.finish(total)


def add_into(target, arrived):
    lead = target.shape[:-2]
    count = 1
    for size in lead:
        count *= size

    @pl.loop(0, count)
    def _(flat):
        index = []
        for size in reversed(lead):
            index.insert(0, lax.rem(flat, size))
            flat = lax.div(flat, size)
        index = tuple(index)
        target[index] = (target[index].astype(F32) + arrived[index].astype(F32)).astype(target.dtype)


def run(items, depth, tick):
    for number, item in enumerate(items):
        if 0 <= tick - number < depth:
            for part in item:
                part.step(tick - number)


def matmul(left, right):
    return jnp.dot(left, right, preferred_element_type=F32)


def matmul_left(left, right):
    return lax.dot_general(left, right, (((0,), (0,)), ((), ())), preferred_element_type=F32)


def matmul_right(left, right):
    return lax.dot_general(left, right, (((1,), (1,)), ((), ())), preferred_element_type=F32)


def layer_norm(values, gain, offset):
    centre = jnp.mean(values, axis=-1, keepdims=True)
    shifted = values - centre
    spread = jnp.mean(shifted * shifted, axis=-1, keepdims=True)
    return shifted * lax.rsqrt(spread + epsilon) * gain + offset


def layer_norm_back(values, gain, upstream):
    centre = jnp.mean(values, axis=-1, keepdims=True)
    shifted = values - centre
    spread = jnp.mean(shifted * shifted, axis=-1, keepdims=True)
    rate = lax.rsqrt(spread + epsilon)
    normed = shifted * rate
    scaled = upstream * gain
    first = jnp.mean(scaled, axis=-1, keepdims=True)
    second = jnp.mean(scaled * normed, axis=-1, keepdims=True)
    return rate * (scaled - first - normed * second), upstream * normed


def gelu_exact(values):
    return 0.5 * values * (1.0 + jax.scipy.special.erf(values * 0.7071067811865476))


def gelu_parts(values):
    cumulative = 0.5 * (1.0 + lax.erf(values * 0.7071067811865476))
    density = 0.3989422804014327 * jnp.exp(-0.5 * values * values)
    return values * cumulative, cumulative + values * density


def tiles(count, size, action):
    @pl.loop(0, count)
    def _(number):
        action(pl.multiple_of(number * size, size))


def head_mask(rows, columns):
    heads = columns // HEAD_DIM
    row = lax.broadcasted_iota(jnp.int32, (rows * heads, columns), 0)
    column = lax.broadcasted_iota(jnp.int32, (rows * heads, columns), 1)
    head_row = jnp.zeros_like(row)
    head_column = jnp.zeros_like(row)
    for head in range(1, heads):
        head_row = head_row + jnp.where(row >= head * rows, 1, 0)
        head_column = head_column + jnp.where(column >= head * HEAD_DIM, 1, 0)
    return jnp.where(head_row == head_column, 1.0, 0.0)


def spread_heads(rows, mask):
    return jnp.concatenate([rows] * (mask.shape[0] // rows.shape[0]), axis=0) * mask


def pick_heads(stacked, mask, rows):
    kept = stacked * mask
    total = kept[:rows]
    for head in range(1, stacked.shape[0] // rows):
        total = total + kept[head * rows:(head + 1) * rows]
    return total


def softmax(scores):
    exponent = jnp.exp(scores - jnp.max(scores, axis=-1, keepdims=True))
    return exponent / jnp.sum(exponent, axis=-1, keepdims=True)


class VectorSum:
    def __init__(self, links, slots, total, stage, lands):
        self.total, self.stage, self.lands, self.length = total, stage, lands, links.length
        self.moves = [[slots.move(links.device(axis), stage.at[number], lands.at[number], lands.at[number])]
                      for number, axis in enumerate(("core", "x", "y"))]
        self.moves.append([
            slots.move(links.device("z", way), stage.at[3], lands.at[2 + way], lands.at[2 + way])
            for way in range(1, links.length)])

    def step(self, number):
        if 0 < number <= 4:
            for move in self.moves[number - 1]:
                move.wait()
            for land in ([number - 1] if number < 4 else range(3, 2 + self.length)):
                self.total[...] = self.total[...] + self.lands[land]
        if number < 4:
            self.stage[number] = self.total[...]
            for move in self.moves[number]:
                move.start()


def layer_kernel(length, scaling, counts, media, latents, grad_out, packed, query_shard, context_shard,
                 output_shard, up_shard, down_shard, latents_out, media_grad_out, latents_grad_out, sums_out, grads_out,
                 query_all, context_all, output_all, up_all, down_all,
                 packed_all, vectors, media_in, latents_in, grad_in, context, key_value, query, attended, after,
                 feed, feed_t, branch, branch_t, pool, active, after_feed, d_feed, after_lands,
                 d_feed_lands, out_stage, grad_up, grad_down, mask, sums, total, total_stage, total_lands,
                 lands_b, lands_a, lands_z, result, send, recv, local):
    links = Links(length)
    z, y, x, rep = links.z, links.y, links.x, links.rep
    slots, locals_ = Slots(send, recv), Locals(local)
    slot_count, patches, width = media.shape
    latent_count = latents.shape[1]
    key_count = patches + latent_count
    rows = slot_count * latent_count
    both = 2 * rows
    inner = query.shape[-1]
    chunk = pool.shape[-1]
    chunks = length
    xy, yx = ("x", "y"), ("y", "x")

    staged = [locals_.copy(packed, packed_all.at[z, y, x])]
    for shard, whole in ((context_shard, context_all), (query_shard, query_all), (output_shard, output_all)):
        half = whole.shape[-2]
        staged.append(locals_.copy(shard.at[pl.ds(pl.multiple_of(rep * half, 16), half)], whole.at[z, y, x, rep]))
    grad_load = locals_.copy(grad_out, grad_in)
    half = down_all.shape[-2]
    staged.append(locals_.copy(down_shard.at[pl.ds(pl.multiple_of(rep * half, 16), half)], down_all.at[z, y, x]))
    for block in range(up_all.shape[-1] // half):
        begin = pl.multiple_of((2 * block + rep) * half, half)
        staged.append(locals_.copy(
            up_shard.at[:, pl.ds(begin, half)], up_all.at[z, y, x, :, pl.ds(block * half, half)]))
    latents_load = locals_.copy(latents, latents_in)
    media_load = locals_.copy(media, media_in)
    links.greet()
    for copy in staged:
        copy.wait()

    def halves(whole, begin, size, order):
        def view(zi, yi, xi, half=rep):
            return whole.at[zi, yi, xi, half, :, pl.ds(begin, size)]

        return Gather(links, slots, view, order, True)

    def columns(whole, begin, size, order):
        return Gather(links, slots, lambda zi, yi, xi: whole.at[zi, yi, xi, :, pl.ds(begin, size)], order, False)

    gathers = [
        [Gather(links, slots, lambda zi, yi, xi: packed_all.at[zi, yi, xi], xy, False),
         halves(context_all, 0, width // 2, xy), halves(context_all, width // 2, width // 2, yx)],
        [halves(query_all, 0, inner, xy), halves(output_all, 0, width, yx)],
    ]
    for whole in (down_all, up_all):
        part = whole.shape[-1] // (2 * chunks)
        for number in range(chunks):
            gathers.append(
                [columns(whole, 2 * number * part, part, xy), columns(whole, (2 * number + 1) * part, part, yx)])
    gathered = len(slots.made)

    def pump(tick):
        run(gathers, 5, tick)

    pump(0)
    grad_load.wait()
    count = counts[0]

    def keep(j):
        return jnp.where(j < count, 1.0, 0.0)

    for j in range(slot_count):
        branch[pl.ds(j * latent_count, latent_count)] = (grad_in[j].astype(F32) * keep(j)).astype(BF16)
    branch_move = slots.move(links.device("core"), branch.at[pl.ds(0, rows)], branch.at[pl.ds(rows, rows)],
                             branch.at[pl.ds(rows, rows)])
    branch_move.start()
    mask[...] = head_mask(latent_count, GROUP)
    sums[...] = jnp.zeros_like(sums)
    pump(1)
    latents_load.wait()
    media_load.wait()
    pump(2)
    pump(3)
    lane = packed_all.shape[-1]
    for zi in range(length):
        for yi in range(2):
            place = (zi * 2 + yi) * lane
            vectors[:, place:place + lane] = (packed_all[zi, yi, 0] + packed_all[zi, yi, 1]).astype(F32)[:8]

    step = 32

    def normalise_slot(j):
        def media_tile(at):
            context[j, pl.ds(at, step)] = layer_norm(
                media_in[j, pl.ds(at, step)].astype(F32), vectors[0:1], vectors[1:2]).astype(BF16)

        def latent_tile(at):
            context[j, pl.ds(patches + at, step)] = layer_norm(
                latents_in[j, pl.ds(at, step)].astype(F32), vectors[2:3], vectors[3:4]).astype(BF16)

        tiles(patches // step, step, media_tile)
        tiles(latent_count // step, step, latent_tile)

    pl.loop(0, slot_count)(normalise_slot)
    pump(4)

    weight_step = 256

    def key_value_slot(j):
        def body(at):
            weight = context_all[:, :, :, :, :, pl.ds(at, weight_step)].reshape(width, weight_step)
            key_value[j, :, pl.ds(at, weight_step)] = matmul(context[j], weight).astype(BF16)

        tiles(width // weight_step, weight_step, body)

    pl.loop(0, slot_count)(key_value_slot)
    pump(5)

    latent_normed = context[:, patches:, :].reshape(rows, width)
    query[...] = (matmul(latent_normed, query_all[...].reshape(width, inner)) * scaling).astype(BF16).reshape(
        slot_count, latent_count, inner)

    def attention_slot(j):
        for begin in range(0, inner, GROUP):
            stacked = spread_heads(query[j, :, begin:begin + GROUP], mask[...].astype(BF16))
            probs = softmax(matmul_right(stacked, key_value[j, :, begin:begin + GROUP])).astype(BF16)
            value = matmul(probs, key_value[j, :, inner + begin:inner + begin + GROUP])
            attended[j, :, begin:begin + GROUP] = pick_heads(value, mask[...], latent_count).astype(BF16)

    pl.loop(0, slot_count)(attention_slot)
    pump(6)

    def output_tile(at):
        weight = output_all[:, :, :, :, :, pl.ds(at, weight_step)].reshape(inner, weight_step)
        after[:, pl.ds(at, weight_step)] = latents_in[:, :, pl.ds(at, weight_step)].reshape(
            rows, weight_step).astype(F32) + matmul(attended[...].reshape(rows, inner), weight)

    tiles(width // weight_step, weight_step, output_tile)

    def feed_tile(at):
        feed[pl.ds(at, step)] = layer_norm(after[pl.ds(at, step)], vectors[4:5], vectors[5:6]).astype(BF16)

    tiles(rows // step, step, feed_tile)
    feed_move = slots.move(links.device("core"), feed.at[pl.ds(0, rows)], feed.at[pl.ds(rows, rows)],
                           feed.at[pl.ds(rows, rows)])
    feed_move.start()
    pump(7)
    branch_move.wait()

    def turn(source, target):
        def body(at):
            target[pl.ds(at, weight_step)] = source[:, pl.ds(at, weight_step)].T

        tiles(width // weight_step, weight_step, body)

    turn(branch, branch_t)
    feed_move.wait()
    turn(feed, feed_t)
    pump(8)
    tall = rows
    short = 128

    def reduction(own, lands, windows, order, keep_total):
        return Reduce(links, slots, own, order, lands[0].at[(ALL, ALL) + windows], lands[1].at[(ALL,) + windows],
                      lands[2].at[(ALL,) + windows], keep_total)

    def halved_reduction(own, lands, target, height, begin, size, along_rows):
        made = []
        for which, order in enumerate((yx, xy)):
            window = pl.ds(begin + which * size, size)
            windows = (window, pl.ds(0, target.shape[1])) if along_rows else (pl.ds(0, height), window)

            def finish(value, windows=windows):
                target[windows] = value

            made.append(reduction(lambda zi, yi, xi, windows=windows: own(zi, yi, xi, *windows), lands, windows, order, finish))
        return made

    up_lands, down_lands, query_lands, context_lands, output_lands = zip(lands_b, lands_a, lands_z)
    up_result, down_result, query_result, context_result, output_result = result
    reductions = []

    def send_off(tick):
        run(reductions, 4, tick)

    for c in range(chunks):
        def d_active_tile(at, c=c):
            weight = down_all[c].reshape(chunk, width)
            pool[pl.ds(c * both + at, tall)] = matmul_right(branch[pl.ds(at, tall)], weight).astype(BF16)

        tiles(both // tall, tall, d_active_tile)
    d_hidden = pool.at[pl.ds(chunks * both, both)]
    for c in range(chunks):
        pump(9 + c)
        begin = c * chunk

        def hidden_tile(at, c=c, begin=begin):
            weight = up_all[:, :, :, :, begin:begin + chunk].reshape(width, chunk)
            value, slope = gelu_parts(matmul(feed[pl.ds(at, short)], weight))
            active[pl.ds(at, short)] = value.astype(BF16)
            d_hidden[pl.ds(at, short)] = (pool[pl.ds(c * both + at, short)].astype(F32) * slope).astype(BF16)

        tiles(both // short, short, hidden_tile)

        def forward_tile(at, c=c):
            value = matmul(active[pl.ds(at, tall)], down_all[c].reshape(chunk, width))
            after_feed[pl.ds(at, tall)] = value if c == 0 else after_feed[pl.ds(at, tall)] + value

        def back_tile(at, c=c, begin=begin):
            weight = up_all[:, :, :, :, begin:begin + chunk].reshape(width, chunk)
            value = matmul_right(d_hidden[pl.ds(at, tall)], weight)
            d_feed[pl.ds(at, tall)] = value if c == 0 else d_feed[pl.ds(at, tall)] + value

        tiles(both // tall, tall, forward_tile)
        tiles(both // tall, tall, back_tile)
        if c == chunks - 1:
            for move in slots.made[:gathered]:
                move.drain()
            d_feed_move = slots.move(links.device("core"), d_feed.at[pl.ds(rows, rows)], d_feed_lands, d_feed_lands)
            after_move = slots.move(links.device("core"), after_feed.at[pl.ds(rows, rows)], after_lands, after_lands)
            d_feed_move.start()
            after_move.start()

        def grad_tile(zi, begin=begin, c=c):
            place = pl.multiple_of(zi * (width // length), width // length)
            up = matmul(feed_t[pl.ds(place, width // length)], d_hidden[...]).astype(BF16)
            grad_up[zi, :, :, :, begin:begin + chunk] = up.reshape(2, 2, width // (4 * length), chunk)
            down = matmul(branch_t[pl.ds(place, width // length)], active[...]).astype(BF16)
            block = chunk // 4
            for number in range(4):
                grad_down[c, number // 2, number % 2, pl.ds(place, width // length)] = down[
                    :, number * block:(number + 1) * block]

        pl.loop(0, length)(grad_tile)
        reductions.append(halved_reduction(
            lambda zi, yi, xi, *w: grad_up.at[(zi, yi, xi) + w], up_lands, up_result, up_result.shape[0],
            begin, chunk // 2, False))
        send_off(c)
    part = width // chunks
    for number in range(chunks):
        reductions.append(halved_reduction(
            lambda zi, yi, xi, *w: grad_down.at[(zi, yi, xi) + w], down_lands, down_result, width,
            number * part, part // 2, True))

    d_feed_move.wait()
    feed_move.drain()

    def fold(terms):
        return jnp.sum(terms.reshape(-1, 8, width), axis=0)

    def middle_slot(j):
        def body(at):
            own = pl.ds(pl.multiple_of(j * latent_count + at, step), step)
            upstream = d_feed[own] + d_feed_lands[own]
            d_norm, gain_terms = layer_norm_back(after[own], vectors[4:5], upstream)
            sums[4] = sums[4] + fold(gain_terms)
            sums[5] = sums[5] + fold(upstream)
            d_middle = grad_in[j, pl.ds(at, step)].astype(F32) * keep(j) + d_norm
            d_feed[own] = d_middle
            feed[own] = d_middle.astype(BF16)

        tiles(latent_count // step, step, body)

    pl.loop(0, slot_count)(middle_slot)
    send_off(4)
    after_move.wait()
    for j in range(slot_count):
        own = pl.ds(j * latent_count, latent_count)
        out_stage[j] = ((after[own] + after_feed[own] + after_lands[own]) * keep(j)).astype(BF16)
    written = [locals_.copy(out_stage, latents_out)]

    output_rows, context_rows = output_all.shape[-2], context_all.shape[-2]
    output_at = 3 * down_all.shape[-2] // 4

    def output_own(zi, yi, xi, half, *w):
        return down_all.at[zi, yi, xi, pl.ds(pl.multiple_of(output_at + half * output_rows, 16), output_rows), w[1]]

    def context_own(zi, yi, xi, half, *w):
        return up_all.at[zi, yi, xi, pl.ds(pl.multiple_of(half * context_rows, 16), context_rows), w[1]]

    def query_own(zi, yi, xi, half, *w):
        moved = pl.ds(2 * inner + w[1].start, w[1].size)
        return up_all.at[zi, yi, xi, pl.ds(pl.multiple_of(half * context_rows, 16), context_rows), moved]

    sibling_lands = {
        "context": down_all.at[:, :, :, pl.ds(0, context_rows)],
        "query": down_all.at[:, :, :, pl.ds(context_rows, context_rows), pl.ds(0, inner)],
        "output": down_all.at[:, :, :, pl.ds(2 * context_rows, output_rows)],
    }

    def to_sibling(own, name, size):
        whole = (None, pl.ds(0, size))
        move = slots.move(links.device("core"), own(ALL, ALL, ALL, 1 - rep, *whole), sibling_lands[name],
                          sibling_lands[name])
        move.start()

        def settle():
            move.wait()
            add_into(own(ALL, ALL, ALL, rep, *whole), sibling_lands[name])

        return settle

    d_branch = feed.at[pl.ds(0, rows)]
    output_block = inner // length

    def output_grad_tile(zi):
        place = pl.multiple_of(zi * output_block, output_block)
        turned = attended[:, :, pl.ds(place, output_block)].reshape(rows, output_block).T
        value = matmul(turned, d_branch[...]).astype(BF16)
        down_all[zi, :, :, output_at:] = value.reshape(2, 2, output_block // 4, width)

    pl.loop(0, length)(output_grad_tile)
    settle_output = to_sibling(output_own, "output", width)
    d_attended, d_query = active.at[pl.ds(0, rows)], active.at[pl.ds(rows, rows)]
    d_attended[...] = matmul_right(d_branch[...], output_all[...].reshape(inner, width)).astype(BF16)
    send_off(5)

    def attention_back_slot(j):
        own = pl.ds(pl.multiple_of(j * latent_count, latent_count), latent_count)
        for begin in range(0, inner, GROUP):
            keys = key_value[j, :, begin:begin + GROUP]
            values = key_value[j, :, inner + begin:inner + begin + GROUP]
            low_mask = mask[...].astype(BF16)
            stacked = spread_heads(query[j, :, begin:begin + GROUP], low_mask)
            upstream = spread_heads(d_attended[own, begin:begin + GROUP], low_mask)
            probs = softmax(matmul_right(stacked, keys))
            d_probs = matmul_right(upstream, values)
            d_scores = (probs * (d_probs - jnp.sum(probs * d_probs, axis=-1, keepdims=True))).astype(BF16)
            d_query[own, begin:begin + GROUP] = (
                pick_heads(matmul(d_scores, keys), mask[...], latent_count).astype(BF16).astype(F32) * scaling
            ).astype(BF16)
            at = pl.multiple_of(j * 2 * key_count, 16)
            pool[pl.ds(at, key_count), begin:begin + GROUP] = matmul_left(d_scores, stacked).astype(BF16)
            pool[pl.ds(at + key_count, key_count), begin:begin + GROUP] = matmul_left(
                probs.astype(BF16), upstream).astype(BF16)

    pl.loop(0, 2)(attention_back_slot)
    send_off(6)
    pl.loop(2, slot_count)(attention_back_slot)
    send_off(7)

    block = width // length

    def query_grad_tile(zi):
        place = pl.multiple_of(zi * block, block)
        turned = context[:, patches:, pl.ds(place, block)].reshape(rows, block).T
        value = matmul(turned, d_query[...]).astype(BF16)
        up_all[zi, :, :, :, 2 * inner:3 * inner] = value.reshape(2, 2, block // 4, inner)

    pl.loop(0, length)(query_grad_tile)
    settle_query = to_sibling(query_own, "query", inner)

    def context_grad_tile(zi):
        place = pl.multiple_of(zi * block, block)
        for which in range(2):
            value = None
            for j in range(slot_count):
                turned = context[j, :, pl.ds(place, block)].T
                at = (2 * j + which) * key_count
                term = matmul(turned, pool[at:at + key_count])
                value = term if value is None else value + term
            up_all[zi, :, :, :, which * inner:(which + 1) * inner] = value.astype(BF16).reshape(
                2, 2, block // 4, inner)

    pl.loop(0, length)(context_grad_tile)
    settle_context = to_sibling(context_own, "context", width)
    settle_output()
    settle_query()
    reductions.append(
        halved_reduction(lambda zi, yi, xi, *w: output_own(zi, yi, xi, rep, *w), output_lands, output_result,
                         output_rows, 0, width // 2, False)
        + halved_reduction(lambda zi, yi, xi, *w: query_own(zi, yi, xi, rep, *w), query_lands, query_result,
                           context_rows, 0, inner // 2, False))
    send_off(8)
    settle_context()
    reductions.append(halved_reduction(
        lambda zi, yi, xi, *w: context_own(zi, yi, xi, rep, *w), context_lands, context_result, context_rows,
        0, width // 2, False))
    send_off(9)

    upstream_rows = d_feed_lands

    def input_slot(j):
        at = pl.multiple_of(j * 2 * key_count, 16)

        def upstream_tile(number):
            weight = context_all[number].reshape(block, 2 * inner)
            place = pl.ds(pl.multiple_of(number * block, block), block)
            upstream_rows[:, place] = (matmul_right(pool[pl.ds(at, key_count)], weight[:, :inner])
                                       + matmul_right(pool[pl.ds(at + key_count, key_count)], weight[:, inner:]))
            own = pl.ds(pl.multiple_of(j * latent_count, latent_count), latent_count)
            upstream_rows[patches:, place] = upstream_rows[patches:, place] + matmul_right(
                d_query[own], query_all[number].reshape(block, inner))

        pl.loop(0, length)(upstream_tile)

        def media_tile(at):
            own = pl.ds(at, step)
            upstream = upstream_rows[own]
            value, gain_terms = layer_norm_back(media_in[j, own].astype(F32), vectors[0:1], upstream)
            sums[0] = sums[0] + fold(gain_terms)
            sums[1] = sums[1] + fold(upstream)
            media_in[j, own] = value.astype(BF16)

        def latent_tile(at):
            own = pl.ds(at, step)
            upstream = upstream_rows[pl.ds(patches + at, step)]
            value, gain_terms = layer_norm_back(latents_in[j, own].astype(F32), vectors[2:3], upstream)
            sums[2] = sums[2] + fold(gain_terms)
            sums[3] = sums[3] + fold(upstream)
            d_middle = d_feed[pl.ds(pl.multiple_of(j * latent_count + at, step), step)]
            latents_in[j, own] = (d_middle + value).astype(BF16)

        tiles(patches // step, step, media_tile)
        tiles(latent_count // step, step, latent_tile)

    pl.loop(0, 2)(input_slot)
    send_off(10)
    pl.loop(2, slot_count)(input_slot)
    written.append(locals_.copy(media_in, media_grad_out))
    written.append(locals_.copy(latents_in, latents_grad_out))
    total[...] = jnp.zeros_like(total)
    for number in range(6):
        total[number:number + 1] = jnp.sum(sums[number], axis=0, keepdims=True)
    vector_sum = VectorSum(links, slots, total, total_stage, total_lands)
    vector_sum.step(0)
    send_off(11)
    vector_sum.step(1)
    send_off(12)
    for number in range(2, 5):
        vector_sum.step(number)
    sums_out[...] = total[...]
    for value, out in zip(result, grads_out):
        written.append(locals_.copy(value, out.at[rep]))
        move = slots.move(links.device("core"), value, out.at[rep], out.at[1 - rep])
        move.start()
        written.append(move)
    for copy in written:
        copy.wait()
    drained = slots.made[gathered:]
    for move in drained:
        if move is not feed_move:
            move.drain()


def layer(length, counts, media, latents, grad_out, packed, shards):
    query_shard, context_shard, output_shard, up_shard, down_shard = shards
    slot_count, patches, width = media.shape
    latent_count = latents.shape[1]
    key_count = patches + latent_count
    rows = slot_count * latent_count
    inner = query_shard.shape[1]
    hidden = up_shard.shape[1] // 2
    chunk = hidden // length
    blocks = (length, 2, 2)

    def halved(shard):
        return blocks + (2, shard.shape[0] // 2, shard.shape[1])

    grad_up_shape = blocks + (up_shard.shape[0], hidden)
    grad_down_shape = blocks + (width, down_shard.shape[0] // 2)
    results = [grad_up_shape[3:], grad_down_shape[3:]] + [halved(s)[4:] for s in shards[:3]]
    anywhere = pl.BlockSpec(memory_space=pl.ANY)
    vmem = pl.BlockSpec(memory_space=pltpu.VMEM)
    sums_shape = (8, width)
    scratch = [
        pltpu.VMEM(halved(query_shard), BF16),
        pltpu.VMEM(halved(context_shard), BF16),
        pltpu.VMEM(halved(output_shard), BF16),
        pltpu.VMEM(grad_up_shape, BF16),
        pltpu.VMEM(blocks + (down_shard.shape[0] // 2, width), BF16),
        pltpu.VMEM(blocks + packed.shape, BF16),
        pltpu.VMEM((8, width), F32),
        pltpu.VMEM(media.shape, BF16),
        pltpu.VMEM(latents.shape, BF16),
        pltpu.VMEM(grad_out.shape, BF16),
        pltpu.VMEM((slot_count, key_count, width), BF16),
        pltpu.VMEM((slot_count, key_count, 2 * inner), BF16),
        pltpu.VMEM((slot_count, latent_count, inner), BF16),
        pltpu.VMEM((slot_count, latent_count, inner), BF16),
        pltpu.VMEM((rows, width), F32),
        pltpu.VMEM((2 * rows, width), BF16),
        pltpu.VMEM((width, 2 * rows), BF16),
        pltpu.VMEM((2 * rows, width), BF16),
        pltpu.VMEM((width, 2 * rows), BF16),
        pltpu.VMEM((max((length + 1) * 2 * rows, 2 * slot_count * key_count), chunk), BF16),
        pltpu.VMEM((2 * rows, chunk), BF16),
        pltpu.VMEM((2 * rows, width), F32),
        pltpu.VMEM((2 * rows, width), F32),
        pltpu.VMEM((rows, width), F32),
        pltpu.VMEM((rows, width), F32),
        pltpu.VMEM(latents.shape, BF16),
        pltpu.VMEM(grad_up_shape, BF16),
        pltpu.VMEM(grad_down_shape, BF16),
        pltpu.VMEM((latent_count * (GROUP // HEAD_DIM), GROUP), F32),
        pltpu.VMEM((6, 8, width), F32),
        pltpu.VMEM(sums_shape, F32),
        pltpu.VMEM((4,) + sums_shape, F32),
        pltpu.VMEM((2 + length,) + sums_shape, F32),
        [pltpu.VMEM((length, 2) + r, BF16) for r in results],
        [pltpu.VMEM((length,) + r, BF16) for r in results],
        [pltpu.VMEM((length - 1,) + r, BF16) for r in results],
        [pltpu.VMEM(r, F32) for r in results],
        pltpu.SemaphoreType.DMA((240,)),
        pltpu.SemaphoreType.DMA((240,)),
        pltpu.SemaphoreType.DMA((64,)),
    ]
    out_shape = (
        jax.ShapeDtypeStruct(latents.shape, BF16), jax.ShapeDtypeStruct(media.shape, BF16),
        jax.ShapeDtypeStruct(latents.shape, BF16), jax.ShapeDtypeStruct(sums_shape, F32),
        [jax.ShapeDtypeStruct((2,) + r, F32) for r in results])
    return pl.pallas_call(
        functools.partial(layer_kernel, length, HEAD_DIM ** (-0.5)),
        out_shape=out_shape,
        in_specs=[pl.BlockSpec(memory_space=pltpu.SMEM)] + [anywhere] * 9,
        out_specs=(anywhere, anywhere, anywhere, vmem, [anywhere] * 5),
        scratch_shapes=scratch,
        compiler_params=pltpu.CompilerParams(
            collective_id=0, has_side_effects=True, vmem_limit_bytes=63 * 2 ** 20),
        name="resampler_layer",
    )(counts, media, latents, grad_out, packed, query_shard, context_shard, output_shard, up_shard, down_shard)


def head_scores(first_heads, second_heads):
    return jnp.einsum(
        "bqhd,bkhd->bhqk", first_heads, second_heads, preferred_element_type=jnp.float32
    )


def collective_body(
    media,
    latents,
    image_counts,
    grad_out,
    media_gain,
    media_bias,
    latent_gain,
    latent_bias,
    feed_gain,
    feed_bias,
    query_weight,
    context_weight,
    output_weight,
    up_weight,
    down_weight,
):
    samples, slots, patches, model_width = media.shape
    latent_count = latents.shape[2]
    inner_width = query_weight.shape[1]
    head_count = inner_width // HEAD_DIM
    blocks = samples * slots
    key_count = patches + latent_count
    latent_total = blocks * latent_count
    scaling = HEAD_DIM ** (-0.5)
    vector_shards = (media_gain, media_bias, latent_gain, latent_bias, feed_gain, feed_bias)
    weight_shards = (query_weight, context_weight, output_weight, up_weight, down_weight)
    gathered = tuple(lax.all_gather(s, "dp", axis=0, tiled=True) for s in vector_shards + weight_shards)
    vectors = [element.astype(jnp.float32) for element in gathered[:6]]
    media_rows = media.reshape(blocks * patches, model_width).astype(jnp.float32)
    latent_rows = latents.reshape(latent_total, model_width).astype(jnp.float32)
    media_normed = layer_norm(media_rows, vectors[0], vectors[1]).astype(jnp.bfloat16)
    latent_normed = layer_norm(latent_rows, vectors[2], vectors[3]).astype(jnp.bfloat16)
    queries = (matmul(latent_normed, gathered[6]) * scaling).astype(jnp.bfloat16)
    context = jnp.concatenate(
        [
            media_normed.reshape(blocks, patches, model_width),
            latent_normed.reshape(blocks, latent_count, model_width),
        ],
        axis=1,
    ).reshape(blocks * key_count, model_width)
    key_value = (
        matmul(context, gathered[7])
        .astype(jnp.bfloat16)
        .reshape(blocks, key_count, 2 * inner_width)
    )
    query_heads = queries.reshape(blocks, latent_count, head_count, HEAD_DIM)
    key_heads = key_value[:, :, :inner_width].reshape(blocks, key_count, head_count, HEAD_DIM)
    value_heads = key_value[:, :, inner_width:].reshape(blocks, key_count, head_count, HEAD_DIM)
    scores = head_scores(query_heads, key_heads)
    row_max = jnp.max(scores, axis=-1, keepdims=True)
    exponent = jnp.exp(scores - row_max)
    row_total = jnp.sum(exponent, axis=-1, keepdims=True)
    log_total = row_max + jnp.log(row_total)
    attention_weights = (exponent / row_total).astype(jnp.bfloat16)
    attended = (
        jnp.einsum(
            "bhqk,bkhd->bqhd", attention_weights, value_heads, preferred_element_type=jnp.float32
        )
        .astype(jnp.bfloat16)
        .reshape(latent_total, inner_width)
    )
    after_attention = latent_rows + matmul(attended, gathered[8])
    feed_input = layer_norm(after_attention, vectors[4], vectors[5]).astype(jnp.bfloat16)
    hidden = matmul(feed_input, gathered[9])
    activated = gelu_exact(hidden).astype(jnp.bfloat16)
    after_feed = after_attention + matmul(activated, gathered[10])
    slot_mask = (
        lax.broadcasted_iota(jnp.int32, (samples, slots), 1) < image_counts[:, None]
    ).astype(jnp.float32)
    row_mask = jnp.broadcast_to(slot_mask[:, :, None], (samples, slots, latent_count)).reshape(
        latent_total, 1
    )
    latents_out = (after_feed * row_mask).astype(jnp.bfloat16).reshape(latents.shape)
    backward_set = gathered
    back_vectors = [element.astype(jnp.float32) for element in backward_set[:6]]
    d_after = grad_out.reshape(latent_total, model_width).astype(jnp.float32) * row_mask
    d_branch = d_after.astype(jnp.bfloat16)
    grad_down = matmul_left(activated, d_branch)
    d_activated = matmul_right(d_branch, backward_set[10])
    d_hidden = jax.vjp(gelu_exact, hidden)[1](d_activated)[0].astype(jnp.bfloat16)
    grad_up = matmul_left(feed_input, d_hidden)
    d_feed = matmul_right(d_hidden, backward_set[9])
    d_feed_norm, grad_feed_gain, grad_feed_bias = jax.vjp(
        layer_norm, after_attention, back_vectors[4], back_vectors[5]
    )[1](d_feed)
    d_middle = d_after + d_feed_norm
    d_out_branch = d_middle.astype(jnp.bfloat16)
    grad_output = matmul_left(attended, d_out_branch)
    d_attended = (
        matmul_right(d_out_branch, backward_set[8])
        .astype(jnp.bfloat16)
        .reshape(blocks, latent_count, head_count, HEAD_DIM)
    )
    recomputed = jnp.exp(head_scores(query_heads, key_heads) - log_total)
    d_weights = head_scores(d_attended, value_heads)
    d_scores = (
        recomputed * (d_weights - jnp.sum(recomputed * d_weights, axis=-1, keepdims=True))
    ).astype(jnp.bfloat16)
    d_queries = (
        jnp.einsum(
            "bhqk,bkhd->bqhd", d_scores, key_heads, preferred_element_type=jnp.float32
        ).astype(jnp.bfloat16)
        * scaling
    ).reshape(latent_total, inner_width)
    d_keys = jnp.einsum(
        "bhqk,bqhd->bkhd", d_scores, query_heads, preferred_element_type=jnp.float32
    ).astype(jnp.bfloat16)
    d_values = jnp.einsum(
        "bhqk,bqhd->bkhd",
        recomputed.astype(jnp.bfloat16),
        d_attended,
        preferred_element_type=jnp.float32,
    ).astype(jnp.bfloat16)
    d_key_value = jnp.concatenate(
        [
            d_keys.reshape(blocks, key_count, inner_width),
            d_values.reshape(blocks, key_count, inner_width),
        ],
        axis=-1,
    ).reshape(blocks * key_count, 2 * inner_width)
    grad_query = matmul_left(latent_normed, d_queries)
    grad_context = matmul_left(context, d_key_value)
    d_context = matmul_right(d_key_value, backward_set[7]).reshape(blocks, key_count, model_width)
    d_latent_normed = matmul_right(d_queries, backward_set[6]) + d_context[:, patches:, :].reshape(
        latent_total, model_width
    )
    d_media_normed = d_context[:, :patches, :].reshape(blocks * patches, model_width)
    d_latent_norm, grad_latent_gain, grad_latent_bias = jax.vjp(
        layer_norm, latent_rows, back_vectors[2], back_vectors[3]
    )[1](d_latent_normed)
    grad_latents = (d_middle + d_latent_norm).astype(jnp.bfloat16).reshape(latents.shape)
    d_media, grad_media_gain, grad_media_bias = jax.vjp(
        layer_norm, media_rows, back_vectors[0], back_vectors[1]
    )[1](d_media_normed)
    grad_media = d_media.astype(jnp.bfloat16).reshape(media.shape)
    vector_grads = jnp.stack([
        grad_media_gain, grad_media_bias, grad_latent_gain, grad_latent_bias, grad_feed_gain, grad_feed_bias])
    weight_grads = [
        g.astype(jnp.bfloat16) for g in (grad_query, grad_context, grad_output, grad_up, grad_down)]
    vector_sums = lax.psum_scatter(vector_grads, "dp", scatter_dimension=1, tiled=True)
    summed = [lax.psum_scatter(g, "dp", scatter_dimension=0, tiled=True) for g in weight_grads]
    owned = tuple(lax.psum(vector_sums, "rep")) + tuple(
        lax.psum(s, "rep").astype(jnp.float32) for s in summed)
    return (
        latents_out,
        grad_media,
        grad_latents,
        owned[0],
        owned[1],
        owned[2],
        owned[3],
        owned[4],
        owned[5],
        owned[6],
        owned[7],
        owned[8],
        owned[9],
        owned[10],
    )


def body(media, latents, image_counts, grad_out, *parameters):
    chips = lax.axis_size("dp")
    weight_shards = parameters[6:]
    tiled = (media.shape[0] == 1 and chips % 4 == 0 and chips > 4 and parameters[0].shape[0] == 64
             and all(s.shape[0] % 32 == 0 for s in weight_shards))
    if not tiled:
        return collective_body(media, latents, image_counts, grad_out, *parameters)
    side = lax.rem(lax.axis_index("dp"), 2)
    stacked = jnp.stack(parameters[:6])
    packed = jnp.pad(
        jnp.concatenate([jnp.where(side == 0, stacked, 0), jnp.where(side == 0, 0, stacked)], axis=1), ((0, 10), (0, 0)))
    latents_out, grad_media, grad_latents, vector_sums, summed = layer(
        chips // 4, image_counts, media[0], latents[0], grad_out[0], packed, weight_shards)
    sums = [s.reshape(-1, s.shape[-1]) for s in summed[2:]]
    rows, hidden = summed[0].shape[1:]
    half = summed[1].shape[-1]
    sums.append(summed[0].reshape(2, rows, hidden // half, half).transpose(1, 2, 0, 3).reshape(rows, 2 * hidden))
    sums.append(summed[1].transpose(0, 2, 1).reshape(2 * half, -1))
    width = parameters[0].shape[0]
    mine = lax.dynamic_slice(vector_sums, (0, lax.axis_index("dp") * width), (6, width))
    return (latents_out[None], grad_media[None], grad_latents[None]) + tuple(mine) + tuple(sums)


def solution(mesh):
    return jax.shard_map(
        body,
        mesh=mesh,
        in_specs=(
            P(("dp", "rep"), None, None, None),
            P(("dp", "rep"), None, None, None),
            P(("dp", "rep")),
            P(("dp", "rep"), None, None, None),
            P("dp"),
            P("dp"),
            P("dp"),
            P("dp"),
            P("dp"),
            P("dp"),
            P("dp", None),
            P("dp", None),
            P("dp", None),
            P("dp", None),
            P("dp", None),
        ),
        out_specs=(
            P(("dp", "rep"), None, None, None),
            P(("dp", "rep"), None, None, None),
            P(("dp", "rep"), None, None, None),
            P("dp"),
            P("dp"),
            P("dp"),
            P("dp"),
            P("dp"),
            P("dp"),
            P("dp", None),
            P("dp", None),
            P("dp", None),
            P("dp", None),
            P("dp", None),
        ),
        check_vma=False,
    )
```

```python
import functools

import jax
import jax.numpy as jnp
from jax import lax
from jax.experimental import pallas as pl
from jax.experimental.pallas import tpu as pltpu
from jax.sharding import PartitionSpec as P

HEAD_DIM = 64
GROUP = 256

epsilon = 1e-05

MESH = pl.DeviceIdType.MESH
ALL = slice(None)
F32 = jnp.float32
BF16 = jnp.bfloat16


class Links:
    def __init__(self, length):
        self.length = length
        self.dp = lax.axis_index("dp")
        self.rep = lax.axis_index("rep")
        self.z = lax.div(self.dp, 4)
        self.y = lax.rem(lax.div(self.dp, 2), 2)
        self.x = lax.rem(self.dp, 2)

    def device(self, axis, way=0):
        if axis == "core":
            return (self.dp, 1 - self.rep)
        if axis == "x":
            return (self.dp + 1 - 2 * self.x, self.rep)
        if axis == "y":
            return (self.dp + 2 - 4 * self.y, self.rep)
        return (self.dp + 4 * (self.along(way) - self.z), self.rep)

    def along(self, way):
        return lax.rem(self.z + way + self.length, self.length)

    def greet(self):
        barrier = pltpu.get_barrier_semaphore()
        peers = [("core", 0), ("x", 0), ("y", 0)] + [("z", way) for way in range(1, self.length)]
        for axis, way in peers:
            pl.semaphore_signal(barrier, inc=1, device_id=self.device(axis, way), device_id_type=MESH)
        pl.semaphore_wait(barrier, len(peers))


class Move:
    def __init__(self, send, recv, slot, device, source, target, landing):
        self.out = pltpu.make_async_remote_copy(
            src_ref=source, dst_ref=target, send_sem=send.at[slot], recv_sem=recv.at[slot],
            device_id=device, device_id_type=MESH)
        self.into = pltpu.make_async_remote_copy(
            src_ref=landing, dst_ref=landing, send_sem=send.at[slot], recv_sem=recv.at[slot],
            device_id=device, device_id_type=MESH)

    def start(self):
        self.out.start()

    def wait(self):
        self.into.wait_recv()

    drained = False

    def drain(self):
        self.drained = True
        self.out.wait_send()


class Slots:
    def __init__(self, send, recv):
        self.send, self.recv, self.made = send, recv, []

    def move(self, *args):
        self.made.append(Move(self.send, self.recv, len(self.made), *args))
        return self.made[-1]


class Locals:
    def __init__(self, semaphores):
        self.semaphores, self.made = semaphores, []

    def copy(self, source, target):
        self.made.append(pltpu.make_async_copy(source, target, self.semaphores.at[len(self.made)]))
        self.made[-1].start()
        return self.made[-1]


class Gather:
    def __init__(self, links, slots, view, axes, halved):
        here = {"z": links.z, "y": links.y, "x": links.x}
        self.moves = []
        for axis in axes:
            mine = view(here["z"], here["y"], here["x"])
            if axis == "z":
                self.moves.append([
                    slots.move(links.device("z", way), mine, mine, view(links.along(-way), here["y"], here["x"]))
                    for way in range(1, links.length)])
            else:
                other = dict(here)
                other[axis] = 1 - here[axis]
                self.moves.append([
                    slots.move(links.device(axis), mine, mine, view(other["z"], other["y"], other["x"]))])
            here[axis] = ALL
        if halved:
            mine = view(ALL, ALL, ALL)
            self.moves.append([
                slots.move(links.device("core"), mine, mine, view(ALL, ALL, ALL, 1 - links.rep))])

    def step(self, number):
        if 0 < number <= len(self.moves):
            for move in self.moves[number - 1]:
                move.wait()
        if 0 <= number < len(self.moves):
            for move in self.moves[number]:
                move.start()


class Reduce:
    def __init__(self, links, slots, own, axes, lands, lands_z, finish):
        self.own, self.links, self.finish, self.lands_z = own, links, finish, lands_z
        self.moves, self.adds = [], []
        z, y, x = links.z, links.y, links.x
        here = {"z": ALL, "y": ALL, "x": ALL}
        for axis, land in zip(axes, lands):
            away, home = dict(here), dict(here)
            place = {"y": y, "x": x}[axis]
            away[axis], home[axis] = 1 - place, place
            self.moves.append([slots.move(
                links.device(axis), own(away["z"], away["y"], away["x"]), land, land)])
            here = home
            self.adds.append(functools.partial(add_into, own(home["z"], home["y"], home["x"]), land))
        self.moves.append([
            slots.move(links.device("z", way), own(links.along(way), here["y"], here["x"]), lands_z.at[way - 1],
                       lands_z.at[way - 1])
            for way in range(1, links.length)])
        self.mine = own(z, here["y"], here["x"])
        self.adds.append(self.end)

    def step(self, number):
        if 0 < number <= len(self.moves):
            for move in self.moves[number - 1]:
                move.wait()
            self.adds[number - 1]()
        if 0 <= number < len(self.moves):
            for move in self.moves[number]:
                move.start()

    def end(self):
        total = self.mine[...].astype(F32)
        for way in range(1, self.links.length):
            total = total + self.lands_z[way - 1].astype(F32)
        self.finish(total)


def add_into(target, arrived):
    lead = target.shape[:-2]
    count = 1
    for size in lead:
        count *= size

    @pl.loop(0, count)
    def _(flat):
        index = []
        for size in reversed(lead):
            index.insert(0, lax.rem(flat, size))
            flat = lax.div(flat, size)
        index = tuple(index)
        target[index] = (target[index].astype(F32) + arrived[index].astype(F32)).astype(target.dtype)


def run(table, tick):
    for item, first, stride in table:
        late = tick - first
        if late >= 0 and late % stride == 0:
            item.step(late // stride)


def matmul(left, right):
    return jnp.dot(left, right, preferred_element_type=F32)


def matmul_left(left, right):
    return lax.dot_general(left, right, (((0,), (0,)), ((), ())), preferred_element_type=F32)


def matmul_right(left, right):
    return lax.dot_general(left, right, (((1,), (1,)), ((), ())), preferred_element_type=F32)


def layer_norm(values, gain, offset):
    centre = jnp.mean(values, axis=-1, keepdims=True)
    shifted = values - centre
    spread = jnp.mean(shifted * shifted, axis=-1, keepdims=True)
    return shifted * lax.rsqrt(spread + epsilon) * gain + offset


def layer_norm_back(values, gain, upstream):
    centre = jnp.mean(values, axis=-1, keepdims=True)
    shifted = values - centre
    spread = jnp.mean(shifted * shifted, axis=-1, keepdims=True)
    rate = lax.rsqrt(spread + epsilon)
    normed = shifted * rate
    scaled = upstream * gain
    first = jnp.mean(scaled, axis=-1, keepdims=True)
    second = jnp.mean(scaled * normed, axis=-1, keepdims=True)
    return rate * (scaled - first - normed * second), upstream * normed


def gelu_exact(values):
    return 0.5 * values * (1.0 + jax.scipy.special.erf(values * 0.7071067811865476))


def gelu_parts(values):
    cumulative = 0.5 * (1.0 + lax.erf(values * 0.7071067811865476))
    density = 0.3989422804014327 * jnp.exp(-0.5 * values * values)
    return values * cumulative, cumulative + values * density


def tiles(count, size, action):
    @pl.loop(0, count)
    def _(number):
        action(pl.multiple_of(number * size, size))


def head_mask(rows, columns):
    heads = columns // HEAD_DIM
    row = lax.broadcasted_iota(jnp.int32, (rows * heads, columns), 0)
    column = lax.broadcasted_iota(jnp.int32, (rows * heads, columns), 1)
    head_row = jnp.zeros_like(row)
    head_column = jnp.zeros_like(row)
    for head in range(1, heads):
        head_row = head_row + jnp.where(row >= head * rows, 1, 0)
        head_column = head_column + jnp.where(column >= head * HEAD_DIM, 1, 0)
    return jnp.where(head_row == head_column, 1.0, 0.0)


def spread_heads(rows, mask):
    return jnp.concatenate([rows] * (mask.shape[0] // rows.shape[0]), axis=0) * mask


def pick_heads(stacked, mask, rows):
    kept = stacked * mask
    total = kept[:rows]
    for head in range(1, stacked.shape[0] // rows):
        total = total + kept[head * rows:(head + 1) * rows]
    return total


def softmax(scores):
    exponent = jnp.exp(scores - jnp.max(scores, axis=-1, keepdims=True))
    return exponent / jnp.sum(exponent, axis=-1, keepdims=True)


class VectorSum:
    def __init__(self, links, slots, total, stage, lands):
        self.total, self.stage, self.lands, self.length = total, stage, lands, links.length
        self.moves = [[slots.move(links.device(axis), stage.at[number], lands.at[number], lands.at[number])]
                      for number, axis in enumerate(("core", "x", "y"))]
        self.moves.append([
            slots.move(links.device("z", way), stage.at[3], lands.at[2 + way], lands.at[2 + way])
            for way in range(1, links.length)])

    def step(self, number):
        if 0 < number <= 4:
            for move in self.moves[number - 1]:
                move.wait()
            for land in ([number - 1] if number < 4 else range(3, 2 + self.length)):
                self.total[...] = self.total[...] + self.lands[land]
        if number < 4:
            self.stage[number] = self.total[...]
            for move in self.moves[number]:
                move.start()


class Rows:
    def __init__(self, links, slots, buffer, count, parts):
        self.moves, self.passed = [], []
        for begin, size in parts:
            def place(owner, begin=begin, size=size):
                return buffer.at[pl.ds(owner * count + begin, size)]

            self.moves.append([
                slots.move(links.device("x"), place(0), place(2), place(2)),
                slots.move(links.device("core"), place(0), place(1), place(1))])
            self.passed.append(slots.move(links.device("core"), place(2), place(3), place(3)))

    def send(self, part):
        for move in self.moves[part]:
            move.start()

    def near(self, part):
        self.moves[part][1].wait()

    def forward(self, part):
        self.moves[part][0].wait()
        self.passed[part].start()

    def far(self, part):
        self.passed[part].wait()

    def drain(self):
        for move in [m for pair in self.moves for m in pair] + self.passed:
            move.drain()


class Partials:
    def __init__(self, links, slots, stage, lands, count):
        def place(owner):
            return stage.at[pl.ds(owner * count, count)]

        self.place, self.lands = place, lands
        self.far = slots.move(links.device("core"), place(3), lands.at[0], lands.at[0])
        self.near = slots.move(links.device("core"), place(1), lands.at[1], lands.at[1])
        self.across = slots.move(links.device("x"), place(2), lands.at[2], lands.at[2])


def layer_kernel(length, scaling, counts, media, latents, grad_out, packed, query_shard, context_shard,
                 output_shard, up_shard, down_shard, latents_out, media_grad_out, latents_grad_out, sums_out, grads_out,
                 query_all, context_all, output_all, up_all, up_stage, down_all,
                 packed_all, vectors, media_in, latents_in, grad_in, context, key_value, query, attended, after,
                 feed, feed_t, branch, branch_t, pool, totals, after_lands, d_feed_lands, upstream_rows,
                 grad_up, grad_down, grad_query, grad_output, mask, sums, total, total_stage, total_lands,
                 own_rows_send, own_rows_land, lands_c, lands_b, lands_a, lands_z, result, send, recv, local):
    links = Links(length)
    z, y, x, rep = links.z, links.y, links.x, links.rep
    slots, locals_ = Slots(send, recv), Locals(local)
    slot_count, patches, width = media.shape
    latent_count = latents.shape[1]
    key_count = patches + latent_count
    rows = slot_count * latent_count
    inner = query.shape[-1]
    chunks = length
    hidden = up_all.shape[-1]
    chunk = hidden // chunks
    unit = down_all.shape[-2]
    xy, yx = ("z", "x", "y"), ("z", "y", "x")

    def unit_columns(half, number):
        return pl.ds(pl.multiple_of(((2 * number + half) * 2 + rep) * unit, unit), unit)

    staged = [locals_.copy(packed, packed_all.at[z, y, x])]
    for shard, whole in ((context_shard, context_all), (query_shard, query_all), (output_shard, output_all)):
        half = whole.shape[-2]
        staged.append(locals_.copy(shard.at[pl.ds(pl.multiple_of(rep * half, 16), half)], whole.at[z, y, x, rep]))
    later = []
    for number in range(hidden // unit):
        window = pl.ds(number * unit, unit)
        later.append(locals_.copy(up_shard.at[:, unit_columns(1 - x, number)], up_stage.at[:, window]))
        later.append(locals_.copy(up_shard.at[:, unit_columns(x, number)], up_all.at[z, y, x, :, window]))
    later.append(locals_.copy(down_shard.at[pl.ds(pl.multiple_of(rep * unit, 16), unit)], down_all.at[z, y]))
    grad_load = locals_.copy(grad_out, grad_in)
    latents_load = locals_.copy(latents, latents_in)
    media_load = locals_.copy(media, media_in)
    links.greet()

    def halves(whole, begin, size, order):
        def view(zi, yi, xi, half=rep):
            return whole.at[zi, yi, xi, half, :, pl.ds(begin, size)]

        return Gather(links, slots, view, order, True)

    gathers = [
        (Gather(links, slots, lambda zi, yi, xi: packed_all.at[zi, yi, xi], xy, False), 0, 1),
        (halves(context_all, 0, width // 2, xy), 0, 1), (halves(context_all, width // 2, width // 2, yx), 0, 1),
        (halves(query_all, 0, inner, xy), 1, 1), (halves(output_all, 0, width, yx), 1, 1),
    ]
    for number in range(chunks):
        window = pl.ds(number * (width // chunks), width // chunks)
        gathers.append((Gather(links, slots, lambda zi, yi, xi, window=window: down_all.at[zi, yi, :, window],
                               ("z", "y"), False), 2 + number, 2))
    for number in range(chunks):
        window = pl.ds(number * chunk, chunk)
        gathers.append((Gather(links, slots, lambda zi, yi, xi, window=window: up_all.at[zi, yi, ALL, :, window],
                               ("z", "y"), False), 2 + chunks + number, 2))
    up_across = slots.move(links.device("x"), up_stage, up_all.at[z, y, x], up_all.at[z, y, 1 - x])
    gathered = len(slots.made)
    parts = [(0, 2 * latent_count), (2 * latent_count, rows - 2 * latent_count)]
    branch_rows = Rows(links, slots, branch, rows, [(0, rows)])
    feed_rows = Rows(links, slots, feed, rows, parts)

    def pump(tick):
        run(gathers, tick)

    for copy in staged:
        copy.wait()
    pump(0)
    grad_load.wait()
    count = counts[0]

    def keep(j):
        return jnp.where(j < count, 1.0, 0.0)

    for j in range(slot_count):
        branch[pl.ds(j * latent_count, latent_count)] = (grad_in[j].astype(F32) * keep(j)).astype(BF16)
    mask[...] = head_mask(latent_count, GROUP)
    sums[...] = jnp.zeros_like(sums)
    for copy in later:
        copy.wait()
    pump(1)
    up_across.start()
    pump(2)
    latents_load.wait()
    media_load.wait()
    pump(3)
    lane = packed_all.shape[-1]
    for zi in range(length):
        for yi in range(2):
            place = (zi * 2 + yi) * lane
            vectors[:, place:place + lane] = (packed_all[zi, yi, 0] + packed_all[zi, yi, 1]).astype(F32)[:8]

    step = 32

    def normalise_slot(j):
        def media_tile(at):
            context[j, pl.ds(at, step)] = layer_norm(
                media_in[j, pl.ds(at, step)].astype(F32), vectors[0:1], vectors[1:2]).astype(BF16)

        def latent_tile(at):
            context[j, pl.ds(patches + at, step)] = layer_norm(
                latents_in[j, pl.ds(at, step)].astype(F32), vectors[2:3], vectors[3:4]).astype(BF16)

        tiles(patches // step, step, media_tile)
        tiles(latent_count // step, step, latent_tile)

    pl.loop(0, slot_count)(normalise_slot)
    pump(4)
    branch_rows.send(0)

    def key_value_slot(j):
        key_value[j] = matmul(context[j], context_all[...].reshape(width, 2 * inner)).astype(BF16)

    pl.loop(0, 3)(key_value_slot)
    pump(5)
    pl.loop(3, slot_count)(key_value_slot)
    latent_normed = context[:, patches:, :].reshape(rows, width)
    query[...] = (matmul(latent_normed, query_all[...].reshape(width, inner)) * scaling).astype(BF16).reshape(
        slot_count, latent_count, inner)
    up_across.wait()
    pump(6)

    def attention_slot(j):
        for begin in range(0, inner, GROUP):
            stacked = spread_heads(query[j, :, begin:begin + GROUP], mask[...].astype(BF16))
            probs = softmax(matmul_right(stacked, key_value[j, :, begin:begin + GROUP])).astype(BF16)
            value = matmul(probs, key_value[j, :, inner + begin:inner + begin + GROUP])
            attended[j, :, begin:begin + GROUP] = pick_heads(value, mask[...], latent_count).astype(BF16)

    def feed_tile(at):
        feed[pl.ds(at, step)] = layer_norm(after[pl.ds(at, step)], vectors[4:5], vectors[5:6]).astype(BF16)

    for part, (begin, size) in enumerate(parts):
        first, last = begin // latent_count, (begin + size) // latent_count
        pl.loop(first, last)(attention_slot)
        after[begin:begin + size] = latents_in[first:last].reshape(size, width).astype(F32) + matmul(
            attended[first:last].reshape(size, inner), output_all[...].reshape(inner, width))
        pl.loop(begin // step, (begin + size) // step)(lambda n: feed_tile(pl.multiple_of(n * step, step)))
        feed_rows.send(part)
        pump(7 + part)
    branch_rows.near(0)
    branch_rows.forward(0)
    pump(9)
    branch_rows.far(0)

    def turn(source, target, owner):
        def body(at):
            target[pl.ds(at, 256), pl.ds(owner * rows, 2 * rows)] = source[
                pl.ds(owner * rows, 2 * rows), pl.ds(at, 256)].T

        tiles(width // 256, 256, body)

    tall = rows
    d_active, active, d_hidden = [pool.at[pl.ds(n * 4 * rows, 4 * rows)] for n in range(3)]

    def d_active_tile(at):
        d_active[pl.ds(at, tall)] = matmul_right(
            branch[pl.ds(at, tall)], down_all[...].reshape(hidden, width)).astype(BF16)

    tiles(4, tall, d_active_tile)
    turn(branch, branch_t, 0)
    turn(branch, branch_t, 2)
    pump(10)
    feed_rows.forward(0)
    feed_rows.near(0)
    feed_rows.near(1)

    def hidden_tile(at, begin):
        window = pl.ds(begin, chunk)
        weight = up_all[:, :, :, :, window].reshape(width, chunk)
        value, slope = gelu_parts(matmul(feed[pl.ds(at, tall)], weight))
        active[pl.ds(at, tall), window] = value.astype(BF16)
        d_hidden[pl.ds(at, tall), window] = (d_active[pl.ds(at, tall), window].astype(F32) * slope).astype(BF16)

    for c in range(chunks):
        tiles(2, tall, lambda at, c=c: hidden_tile(at, c * chunk))
        if c == 0:
            feed_rows.forward(1)
            turn(feed, feed_t, 0)
        pump(11 + c)
    feed_rows.far(0)
    feed_rows.far(1)
    for move in slots.made[:gathered]:
        move.drain()
    feed_rows.drain()
    branch_rows.drain()
    d_feed_back = Partials(links, slots, feed, d_feed_lands, rows)
    after_back = Partials(links, slots, branch, after_lands, rows)
    turn(feed, feed_t, 2)

    def far_tile(at):
        pl.loop(0, chunks)(lambda c: hidden_tile(pl.multiple_of(2 * rows + at, tall), pl.multiple_of(c * chunk, chunk)))

    tiles(2, tall, far_tile)

    def d_feed_of(owner):
        return matmul_right(d_hidden[pl.ds(owner * rows, rows)], up_all[...].reshape(width, hidden))

    def after_feed_of(owner):
        return matmul(active[pl.ds(owner * rows, rows)], down_all[...].reshape(hidden, width))

    def rounded(buffer, owner, value):
        buffer[pl.ds(owner * rows, rows)] = value.astype(BF16)

    rounded(feed, 3, d_feed_of(3))
    d_feed_back.far.start()
    totals[1] = d_feed_of(2)
    d_feed_back.far.wait()

    def across_tile(back, buffer):
        def body(at):
            here = pl.ds(at, step)
            buffer[pl.ds(2 * rows + at, step)] = (totals[1, here] + back.lands[0, here].astype(F32)).astype(BF16)

        tiles(rows // step, step, body)

    across_tile(d_feed_back, feed)
    d_feed_back.across.start()
    rounded(feed, 1, d_feed_of(1))
    d_feed_back.near.start()
    totals[0] = d_feed_of(0)

    up_result, down_result, query_result, context_result, output_result = result
    reductions = []

    def send_off(tick):
        run(reductions, tick)

    def plane_reduction(own, lands_y, lands, finish):
        return Reduce(links, slots, own, ("y",), [lands_y], lands, finish)

    def keep_up(value, window):
        up_result[0, :, window] = jnp.where(x == 0, value[0], value[1])
        own_rows_send[:, window] = jnp.where(x == 0, value[1], value[0]).astype(BF16)

    for c in range(chunks):
        begin = c * chunk
        window = pl.ds(begin, chunk)

        def grad_tile(number, window=window, c=c):
            size = width // 2
            place = pl.multiple_of(number * size, size)
            up = matmul(feed_t[pl.ds(place, size)], d_hidden[:, window]).astype(BF16)
            grad_up[pl.ds(number * (length // 2), length // 2), :, :, :, window] = up.reshape(
                length // 2, 2, 2, size // (2 * length), chunk)
            down = matmul(branch_t[pl.ds(place, size)], active[:, window]).astype(BF16)
            for owner in range(2):
                grad_down[c, owner, pl.ds(place, size)] = down[:, owner * unit:(owner + 1) * unit]

        pl.loop(0, 2)(grad_tile)
        reductions.append((plane_reduction(
            lambda zi, yi, xi, window=window: grad_up.at[zi, yi, ALL, :, window],
            lands_b[0].at[:, :, :, window], lands_z[0].at[:, :, :, window],
            functools.partial(keep_up, window=window)), c, 2))
        send_off(c)
    part_size = width // chunks
    for number in range(chunks):
        window = pl.ds(number * part_size, part_size)

        def keep_down(value, window=window):
            down_result[window] = value

        reductions.append((plane_reduction(
            lambda zi, yi, xi, window=window: grad_down.at[zi, yi, window],
            lands_b[1].at[:, window], lands_z[1].at[:, window], keep_down), chunks + number, 2))

    rounded(branch, 3, after_feed_of(3))
    after_back.far.start()
    d_feed_back.near.wait()
    d_feed_back.across.wait()
    send_off(4)

    def fold(terms):
        return jnp.sum(terms.reshape(-1, 8, width), axis=0)

    d_feed = totals.at[0]
    d_feed_back.far.drain()
    d_feed_back.near.drain()
    d_feed_back.across.drain()

    def middle_slot(j):
        def body(at):
            own = pl.ds(pl.multiple_of(j * latent_count + at, step), step)
            upstream = d_feed[own] + d_feed_lands[1, own].astype(F32) + d_feed_lands[2, own].astype(F32)
            d_norm, gain_terms = layer_norm_back(after[own], vectors[4:5], upstream)
            sums[4] = sums[4] + fold(gain_terms)
            sums[5] = sums[5] + fold(upstream)
            d_middle = grad_in[j, pl.ds(at, step)].astype(F32) * keep(j) + d_norm
            d_feed[own] = d_middle
            feed[own] = d_middle.astype(BF16)

        tiles(latent_count // step, step, body)

    pl.loop(0, slot_count)(middle_slot)
    totals[1] = after_feed_of(2)
    after_back.far.wait()
    across_tile(after_back, branch)
    after_back.across.start()
    rounded(branch, 1, after_feed_of(1))
    after_back.near.start()
    after[...] = after[...] + after_feed_of(0)
    send_off(5)

    context_rows, output_rows = context_all.shape[-2], output_all.shape[-2]

    def context_own(zi, yi, xi, half):
        return up_all.at[zi, yi, xi, pl.ds(pl.multiple_of(half * context_rows, 16), context_rows)]

    def query_own(zi, yi, xi, half):
        return grad_query.at[zi, yi, xi, half]

    def output_own(zi, yi, xi, half):
        return grad_output.at[zi, yi, xi, half]

    def to_sibling(own, land):
        move = slots.move(links.device("core"), own(ALL, ALL, ALL, 1 - rep), land, land)
        move.start()

        def settle():
            move.wait()
            add_into(own(ALL, ALL, ALL, rep), land)

        return settle

    def halved_reduction(own, number, target, first):
        made = []
        size = target.shape[-1] // 2
        for which, order in enumerate((("y", "x"), ("x", "y"))):
            window = pl.ds(which * size, size)

            def finish(value, window=window):
                target[:, window] = value

            made.append((Reduce(
                links, slots, lambda zi, yi, xi, window=window: own(zi, yi, xi, rep).at[..., window], order,
                [lands_b[number].at[:, :, :, window], lands_a[number].at[:, :, window]],
                lands_z[number].at[:, :, window], finish), first, 1))
        return made

    d_branch = feed.at[pl.ds(0, rows)]
    output_block = inner // 2

    def output_grad_tile(number):
        place = pl.multiple_of(number * output_block, output_block)
        turned = attended[:, :, pl.ds(place, output_block)].reshape(rows, output_block).T
        value = matmul(turned, d_branch[...]).astype(BF16)
        grad_output[pl.ds(number * (length // 2), length // 2)] = value.reshape(
            length // 2, 2, 2, 2, output_rows, width)

    pl.loop(0, 2)(output_grad_tile)
    settle_output = to_sibling(output_own, lands_c[2])
    d_attended, d_query = upstream_rows[0], upstream_rows[1]
    d_attended[...] = matmul_right(d_branch[...], output_all[...].reshape(inner, width)).astype(BF16)
    send_off(6)

    def attention_back_slot(j):
        own = pl.ds(pl.multiple_of(j * latent_count, latent_count), latent_count)
        for begin in range(0, inner, GROUP):
            keys = key_value[j, :, begin:begin + GROUP]
            values = key_value[j, :, inner + begin:inner + begin + GROUP]
            low_mask = mask[...].astype(BF16)
            stacked = spread_heads(query[j, :, begin:begin + GROUP], low_mask)
            upstream = spread_heads(d_attended[own, begin:begin + GROUP], low_mask)
            probs = softmax(matmul_right(stacked, keys))
            d_probs = matmul_right(upstream, values)
            d_scores = (probs * (d_probs - jnp.sum(probs * d_probs, axis=-1, keepdims=True))).astype(BF16)
            d_query[own, begin:begin + GROUP] = (
                pick_heads(matmul(d_scores, keys), mask[...], latent_count).astype(BF16).astype(F32) * scaling
            ).astype(BF16)
            at = pl.ds(pl.multiple_of(j * key_count, 16), key_count)
            pool[at, begin:begin + GROUP] = matmul_left(d_scores, stacked).astype(BF16)
            pool[at, inner + begin:inner + begin + GROUP] = matmul_left(probs.astype(BF16), upstream).astype(BF16)

    pl.loop(0, 2)(attention_back_slot)
    send_off(7)
    pl.loop(2, slot_count)(attention_back_slot)
    send_off(8)
    block = width // length

    def query_grad_tile(zi):
        place = pl.multiple_of(zi * block, block)
        turned = context[:, patches:, pl.ds(place, block)].reshape(rows, block).T
        value = matmul(turned, d_query[...]).astype(BF16)
        grad_query[zi] = value.reshape(2, 2, 2, context_rows, inner)

    pl.loop(0, length)(query_grad_tile)
    settle_query = to_sibling(query_own, lands_c[0])

    def context_grad_tile(zi):
        place = pl.multiple_of(zi * block, block)
        value = None
        for j in range(slot_count):
            turned = context[j, :, pl.ds(place, block)].T
            term = matmul(turned, pool[j * key_count:(j + 1) * key_count])
            value = term if value is None else value + term
        up_all[zi] = value.astype(BF16).reshape(2, 2, block // 4, 2 * inner)

    pl.loop(0, 2)(context_grad_tile)
    send_off(9)
    pl.loop(2, length)(context_grad_tile)
    settle_context = to_sibling(context_own, lands_c[1])
    settle_output()
    settle_query()
    first = 2 * chunks + 2
    reductions.extend(halved_reduction(output_own, 4, output_result, first))
    reductions.extend(halved_reduction(query_own, 2, query_result, first))
    send_off(10)
    settle_context()
    reductions.extend(halved_reduction(context_own, 3, context_result, first + 1))
    send_off(11)
    own_rows_move = slots.move(links.device("x"), own_rows_send, own_rows_land, own_rows_land)
    own_rows_move.start()
    after_back.near.wait()
    after_back.across.wait()
    for move in (after_back.far, after_back.near, after_back.across):
        move.drain()
    for j in range(slot_count):
        own = pl.ds(j * latent_count, latent_count)
        branch[own] = ((after[own] + after_lands[1, own].astype(F32) + after_lands[2, own].astype(F32))
                       * keep(j)).astype(BF16)
    written = [locals_.copy(branch.at[pl.ds(j * latent_count, latent_count)], latents_out.at[j])
               for j in range(slot_count)]

    context_up = totals.at[1]

    def input_slot(j):
        at = pl.ds(pl.multiple_of(j * key_count, 16), key_count)
        own = pl.ds(pl.multiple_of(j * latent_count, latent_count), latent_count)
        context_up[...] = matmul_right(pool[at], context_all[...].reshape(width, 2 * inner))
        context_up[patches:] = context_up[patches:] + matmul_right(d_query[own], query_all[...].reshape(width, inner))

        def media_tile(at):
            own = pl.ds(at, step)
            upstream = context_up[own]
            value, gain_terms = layer_norm_back(media_in[j, own].astype(F32), vectors[0:1], upstream)
            sums[0] = sums[0] + fold(gain_terms)
            sums[1] = sums[1] + fold(upstream)
            media_in[j, own] = value.astype(BF16)

        def latent_tile(at):
            own = pl.ds(at, step)
            upstream = context_up[pl.ds(patches + at, step)]
            value, gain_terms = layer_norm_back(latents_in[j, own].astype(F32), vectors[2:3], upstream)
            sums[2] = sums[2] + fold(gain_terms)
            sums[3] = sums[3] + fold(upstream)
            d_middle = d_feed[pl.ds(pl.multiple_of(j * latent_count + at, step), step)]
            latents_in[j, own] = (d_middle + value).astype(BF16)

        tiles(patches // step, step, media_tile)
        tiles(latent_count // step, step, latent_tile)

    pl.loop(0, 2)(input_slot)
    send_off(12)
    own_rows_move.wait()
    up_result[1] = own_rows_land[...].astype(F32)
    pl.loop(2, 3)(input_slot)
    send_off(13)
    pl.loop(3, slot_count)(input_slot)
    send_off(14)
    written.append(locals_.copy(media_in, media_grad_out))
    written.append(locals_.copy(latents_in, latents_grad_out))
    total[...] = jnp.zeros_like(total)
    for number in range(6):
        total[number:number + 1] = jnp.sum(sums[number], axis=0, keepdims=True)
    vector_sum = VectorSum(links, slots, total, total_stage, total_lands)
    vector_sum.step(0)
    send_off(15)
    for value, out in zip(result, grads_out):
        written.append(locals_.copy(value, out.at[rep]))
        move = slots.move(links.device("core"), value, out.at[rep], out.at[1 - rep])
        move.start()
        written.append(move)
    for number in range(1, 5):
        vector_sum.step(number)
    sums_out[...] = total[...]
    for copy in written:
        copy.wait()
    for move in slots.made:
        if not move.drained:
            move.drain()


def layer(length, counts, media, latents, grad_out, packed, shards):
    query_shard, context_shard, output_shard, up_shard, down_shard = shards
    slot_count, patches, width = media.shape
    latent_count = latents.shape[1]
    key_count = patches + latent_count
    rows = slot_count * latent_count
    inner = query_shard.shape[1]
    unit = down_shard.shape[0] // 2
    hidden = up_shard.shape[1] // 4
    blocks = (length, 2, 2)

    def halved(shard):
        return blocks + (2, shard.shape[0] // 2, shard.shape[1])

    up_shape = blocks + (up_shard.shape[0], hidden)
    down_shape = (length, 2, unit, width)
    halves = [halved(s)[4:] for s in shards[:3]]
    results = [(2,) + up_shape[3:], (width, unit)] + halves
    anywhere = pl.BlockSpec(memory_space=pl.ANY)
    vmem = pl.BlockSpec(memory_space=pltpu.VMEM)
    sums_shape = (8, width)
    scratch = [
        pltpu.VMEM(halved(query_shard), BF16),
        pltpu.VMEM(halved(context_shard), BF16),
        pltpu.VMEM(halved(output_shard), BF16),
        pltpu.VMEM(up_shape, BF16),
        pltpu.VMEM(up_shape[3:], BF16),
        pltpu.VMEM(down_shape, BF16),
        pltpu.VMEM(blocks + packed.shape, BF16),
        pltpu.VMEM((8, width), F32),
        pltpu.VMEM(media.shape, BF16),
        pltpu.VMEM(latents.shape, BF16),
        pltpu.VMEM(grad_out.shape, BF16),
        pltpu.VMEM((slot_count, key_count, width), BF16),
        pltpu.VMEM((slot_count, key_count, 2 * inner), BF16),
        pltpu.VMEM((slot_count, latent_count, inner), BF16),
        pltpu.VMEM((slot_count, latent_count, inner), BF16),
        pltpu.VMEM((rows, width), F32),
        pltpu.VMEM((4 * rows, width), BF16),
        pltpu.VMEM((width, 4 * rows), BF16),
        pltpu.VMEM((4 * rows, width), BF16),
        pltpu.VMEM((width, 4 * rows), BF16),
        pltpu.VMEM((max(12 * rows, slot_count * key_count), hidden), BF16),
        pltpu.VMEM((2, rows, width), F32),
        pltpu.VMEM((3, rows, width), BF16),
        pltpu.VMEM((3, rows, width), BF16),
        [pltpu.VMEM((rows, inner), BF16)] * 2,
        pltpu.VMEM(up_shape, BF16),
        pltpu.VMEM((length, 2, width, unit), BF16),
        pltpu.VMEM(halved(query_shard), BF16),
        pltpu.VMEM(halved(output_shard), BF16),
        pltpu.VMEM((latent_count * (GROUP // HEAD_DIM), GROUP), F32),
        pltpu.VMEM((6, 8, width), F32),
        pltpu.VMEM(sums_shape, F32),
        pltpu.VMEM((4,) + sums_shape, F32),
        pltpu.VMEM((2 + length,) + sums_shape, F32),
        pltpu.VMEM(up_shape[3:], BF16),
        pltpu.VMEM(up_shape[3:], BF16),
        [pltpu.VMEM(blocks + h, BF16) for h in halves],
        [pltpu.VMEM((length, 2) + up_shape[3:], BF16), pltpu.VMEM((length, width, unit), BF16)]
        + [pltpu.VMEM((length, 2) + h, BF16) for h in halves],
        [None, None] + [pltpu.VMEM((length,) + h, BF16) for h in halves],
        [pltpu.VMEM((length - 1, 2) + up_shape[3:], BF16), pltpu.VMEM((length - 1, width, unit), BF16)]
        + [pltpu.VMEM((length - 1,) + h, BF16) for h in halves],
        [pltpu.VMEM(r, F32) for r in results],
        pltpu.SemaphoreType.DMA((200,)),
        pltpu.SemaphoreType.DMA((200,)),
        pltpu.SemaphoreType.DMA((64,)),
    ]
    out_shape = (
        jax.ShapeDtypeStruct(latents.shape, BF16), jax.ShapeDtypeStruct(media.shape, BF16),
        jax.ShapeDtypeStruct(latents.shape, BF16), jax.ShapeDtypeStruct(sums_shape, F32),
        [jax.ShapeDtypeStruct((2,) + r, F32) for r in results])
    return pl.pallas_call(
        functools.partial(layer_kernel, length, HEAD_DIM ** (-0.5)),
        out_shape=out_shape,
        in_specs=[pl.BlockSpec(memory_space=pltpu.SMEM)] + [anywhere] * 9,
        out_specs=(anywhere, anywhere, anywhere, vmem, [anywhere] * 5),
        scratch_shapes=scratch,
        compiler_params=pltpu.CompilerParams(
            collective_id=0, has_side_effects=True, vmem_limit_bytes=63 * 2 ** 20),
        name="resampler_layer",
    )(counts, media, latents, grad_out, packed, query_shard, context_shard, output_shard, up_shard, down_shard)


def head_scores(first_heads, second_heads):
    return jnp.einsum(
        "bqhd,bkhd->bhqk", first_heads, second_heads, preferred_element_type=jnp.float32
    )


def collective_body(
    media,
    latents,
    image_counts,
    grad_out,
    media_gain,
    media_bias,
    latent_gain,
    latent_bias,
    feed_gain,
    feed_bias,
    query_weight,
    context_weight,
    output_weight,
    up_weight,
    down_weight,
):
    samples, slots, patches, model_width = media.shape
    latent_count = latents.shape[2]
    inner_width = query_weight.shape[1]
    head_count = inner_width // HEAD_DIM
    blocks = samples * slots
    key_count = patches + latent_count
    latent_total = blocks * latent_count
    scaling = HEAD_DIM ** (-0.5)
    vector_shards = (media_gain, media_bias, latent_gain, latent_bias, feed_gain, feed_bias)
    weight_shards = (query_weight, context_weight, output_weight, up_weight, down_weight)
    gathered = tuple(lax.all_gather(s, "dp", axis=0, tiled=True) for s in vector_shards + weight_shards)
    vectors = [element.astype(jnp.float32) for element in gathered[:6]]
    media_rows = media.reshape(blocks * patches, model_width).astype(jnp.float32)
    latent_rows = latents.reshape(latent_total, model_width).astype(jnp.float32)
    media_normed = layer_norm(media_rows, vectors[0], vectors[1]).astype(jnp.bfloat16)
    latent_normed = layer_norm(latent_rows, vectors[2], vectors[3]).astype(jnp.bfloat16)
    queries = (matmul(latent_normed, gathered[6]) * scaling).astype(jnp.bfloat16)
    context = jnp.concatenate(
        [
            media_normed.reshape(blocks, patches, model_width),
            latent_normed.reshape(blocks, latent_count, model_width),
        ],
        axis=1,
    ).reshape(blocks * key_count, model_width)
    key_value = (
        matmul(context, gathered[7])
        .astype(jnp.bfloat16)
        .reshape(blocks, key_count, 2 * inner_width)
    )
    query_heads = queries.reshape(blocks, latent_count, head_count, HEAD_DIM)
    key_heads = key_value[:, :, :inner_width].reshape(blocks, key_count, head_count, HEAD_DIM)
    value_heads = key_value[:, :, inner_width:].reshape(blocks, key_count, head_count, HEAD_DIM)
    scores = head_scores(query_heads, key_heads)
    row_max = jnp.max(scores, axis=-1, keepdims=True)
    exponent = jnp.exp(scores - row_max)
    row_total = jnp.sum(exponent, axis=-1, keepdims=True)
    log_total = row_max + jnp.log(row_total)
    attention_weights = (exponent / row_total).astype(jnp.bfloat16)
    attended = (
        jnp.einsum(
            "bhqk,bkhd->bqhd", attention_weights, value_heads, preferred_element_type=jnp.float32
        )
        .astype(jnp.bfloat16)
        .reshape(latent_total, inner_width)
    )
    after_attention = latent_rows + matmul(attended, gathered[8])
    feed_input = layer_norm(after_attention, vectors[4], vectors[5]).astype(jnp.bfloat16)
    hidden = matmul(feed_input, gathered[9])
    activated = gelu_exact(hidden).astype(jnp.bfloat16)
    after_feed = after_attention + matmul(activated, gathered[10])
    slot_mask = (
        lax.broadcasted_iota(jnp.int32, (samples, slots), 1) < image_counts[:, None]
    ).astype(jnp.float32)
    row_mask = jnp.broadcast_to(slot_mask[:, :, None], (samples, slots, latent_count)).reshape(
        latent_total, 1
    )
    latents_out = (after_feed * row_mask).astype(jnp.bfloat16).reshape(latents.shape)
    backward_set = gathered
    back_vectors = [element.astype(jnp.float32) for element in backward_set[:6]]
    d_after = grad_out.reshape(latent_total, model_width).astype(jnp.float32) * row_mask
    d_branch = d_after.astype(jnp.bfloat16)
    grad_down = matmul_left(activated, d_branch)
    d_activated = matmul_right(d_branch, backward_set[10])
    d_hidden = jax.vjp(gelu_exact, hidden)[1](d_activated)[0].astype(jnp.bfloat16)
    grad_up = matmul_left(feed_input, d_hidden)
    d_feed = matmul_right(d_hidden, backward_set[9])
    d_feed_norm, grad_feed_gain, grad_feed_bias = jax.vjp(
        layer_norm, after_attention, back_vectors[4], back_vectors[5]
    )[1](d_feed)
    d_middle = d_after + d_feed_norm
    d_out_branch = d_middle.astype(jnp.bfloat16)
    grad_output = matmul_left(attended, d_out_branch)
    d_attended = (
        matmul_right(d_out_branch, backward_set[8])
        .astype(jnp.bfloat16)
        .reshape(blocks, latent_count, head_count, HEAD_DIM)
    )
    recomputed = jnp.exp(head_scores(query_heads, key_heads) - log_total)
    d_weights = head_scores(d_attended, value_heads)
    d_scores = (
        recomputed * (d_weights - jnp.sum(recomputed * d_weights, axis=-1, keepdims=True))
    ).astype(jnp.bfloat16)
    d_queries = (
        jnp.einsum(
            "bhqk,bkhd->bqhd", d_scores, key_heads, preferred_element_type=jnp.float32
        ).astype(jnp.bfloat16)
        * scaling
    ).reshape(latent_total, inner_width)
    d_keys = jnp.einsum(
        "bhqk,bqhd->bkhd", d_scores, query_heads, preferred_element_type=jnp.float32
    ).astype(jnp.bfloat16)
    d_values = jnp.einsum(
        "bhqk,bqhd->bkhd",
        recomputed.astype(jnp.bfloat16),
        d_attended,
        preferred_element_type=jnp.float32,
    ).astype(jnp.bfloat16)
    d_key_value = jnp.concatenate(
        [
            d_keys.reshape(blocks, key_count, inner_width),
            d_values.reshape(blocks, key_count, inner_width),
        ],
        axis=-1,
    ).reshape(blocks * key_count, 2 * inner_width)
    grad_query = matmul_left(latent_normed, d_queries)
    grad_context = matmul_left(context, d_key_value)
    d_context = matmul_right(d_key_value, backward_set[7]).reshape(blocks, key_count, model_width)
    d_latent_normed = matmul_right(d_queries, backward_set[6]) + d_context[:, patches:, :].reshape(
        latent_total, model_width
    )
    d_media_normed = d_context[:, :patches, :].reshape(blocks * patches, model_width)
    d_latent_norm, grad_latent_gain, grad_latent_bias = jax.vjp(
        layer_norm, latent_rows, back_vectors[2], back_vectors[3]
    )[1](d_latent_normed)
    grad_latents = (d_middle + d_latent_norm).astype(jnp.bfloat16).reshape(latents.shape)
    d_media, grad_media_gain, grad_media_bias = jax.vjp(
        layer_norm, media_rows, back_vectors[0], back_vectors[1]
    )[1](d_media_normed)
    grad_media = d_media.astype(jnp.bfloat16).reshape(media.shape)
    vector_grads = jnp.stack([
        grad_media_gain, grad_media_bias, grad_latent_gain, grad_latent_bias, grad_feed_gain, grad_feed_bias])
    weight_grads = [
        g.astype(jnp.bfloat16) for g in (grad_query, grad_context, grad_output, grad_up, grad_down)]
    vector_sums = lax.psum_scatter(vector_grads, "dp", scatter_dimension=1, tiled=True)
    summed = [lax.psum_scatter(g, "dp", scatter_dimension=0, tiled=True) for g in weight_grads]
    owned = tuple(lax.psum(vector_sums, "rep")) + tuple(
        lax.psum(s, "rep").astype(jnp.float32) for s in summed)
    return (
        latents_out,
        grad_media,
        grad_latents,
        owned[0],
        owned[1],
        owned[2],
        owned[3],
        owned[4],
        owned[5],
        owned[6],
        owned[7],
        owned[8],
        owned[9],
        owned[10],
    )


def body(media, latents, image_counts, grad_out, *parameters):
    chips = lax.axis_size("dp")
    weight_shards = parameters[6:]
    tiled = (media.shape[0] == 1 and chips % 4 == 0 and chips > 4 and parameters[0].shape[0] == 64
             and all(s.shape[0] % 32 == 0 for s in weight_shards))
    if not tiled:
        return collective_body(media, latents, image_counts, grad_out, *parameters)
    side = lax.rem(lax.axis_index("dp"), 2)
    stacked = jnp.stack(parameters[:6])
    packed = jnp.pad(
        jnp.concatenate([jnp.where(side == 0, stacked, 0), jnp.where(side == 0, 0, stacked)], axis=1), ((0, 10), (0, 0)))
    latents_out, grad_media, grad_latents, vector_sums, summed = layer(
        chips // 4, image_counts, media[0], latents[0], grad_out[0], packed, weight_shards)
    sums = [s.reshape(-1, s.shape[-1]) for s in summed[2:]]
    rows, hidden = summed[0].shape[2:]
    unit = summed[1].shape[-1]
    planes = jnp.where(lax.rem(lax.axis_index("dp"), 2) == 0, summed[0], summed[0][:, ::-1])
    sums.append(planes.reshape(2, 2, rows, hidden // unit, unit).transpose(2, 3, 1, 0, 4).reshape(rows, 4 * hidden))
    sums.append(summed[1].transpose(0, 2, 1).reshape(2 * unit, -1))
    width = parameters[0].shape[0]
    mine = lax.dynamic_slice(vector_sums, (0, lax.axis_index("dp") * width), (6, width))
    return (latents_out[None], grad_media[None], grad_latents[None]) + tuple(mine) + tuple(sums)


def solution(mesh):
    return jax.shard_map(
        body,
        mesh=mesh,
        in_specs=(
            P(("dp", "rep"), None, None, None),
            P(("dp", "rep"), None, None, None),
            P(("dp", "rep")),
            P(("dp", "rep"), None, None, None),
            P("dp"),
            P("dp"),
            P("dp"),
            P("dp"),
            P("dp"),
            P("dp"),
            P("dp", None),
            P("dp", None),
            P("dp", None),
            P("dp", None),
            P("dp", None),
        ),
        out_specs=(
            P(("dp", "rep"), None, None, None),
            P(("dp", "rep"), None, None, None),
            P(("dp", "rep"), None, None, None),
            P("dp"),
            P("dp"),
            P("dp"),
            P("dp"),
            P("dp"),
            P("dp"),
            P("dp", None),
            P("dp", None),
            P("dp", None),
            P("dp", None),
            P("dp", None),
        ),
        check_vma=False,
    )
```

```python
import functools

import jax
import jax.numpy as jnp
from jax import lax
from jax.experimental import pallas as pl
from jax.experimental.pallas import tpu as pltpu
from jax.sharding import PartitionSpec as P

HEAD_DIM = 64
GROUP = 256

epsilon = 1e-05

MESH = pl.DeviceIdType.MESH
ALL = slice(None)
F32 = jnp.float32
BF16 = jnp.bfloat16


class Links:
    def __init__(self, length):
        self.length = length
        self.dp = lax.axis_index("dp")
        self.rep = lax.axis_index("rep")
        self.z = lax.div(self.dp, 4)
        self.y = lax.rem(lax.div(self.dp, 2), 2)
        self.x = lax.rem(self.dp, 2)

    def device(self, axis, way=0):
        if axis == "core":
            return (self.dp, 1 - self.rep)
        if axis == "x":
            return (self.dp + 1 - 2 * self.x, self.rep)
        if axis == "y":
            return (self.dp + 2 - 4 * self.y, self.rep)
        return (self.dp + 4 * (self.along(way) - self.z), self.rep)

    def along(self, way):
        return lax.rem(self.z + way + self.length, self.length)

    def greet(self):
        barrier = pltpu.get_barrier_semaphore()
        peers = [("core", 0), ("x", 0), ("y", 0)] + [("z", way) for way in range(1, self.length)]
        for axis, way in peers:
            pl.semaphore_signal(barrier, inc=1, device_id=self.device(axis, way), device_id_type=MESH)
        pl.semaphore_wait(barrier, len(peers))


class Move:
    def __init__(self, send, recv, slot, device, source, target, landing):
        self.out = pltpu.make_async_remote_copy(
            src_ref=source, dst_ref=target, send_sem=send.at[slot], recv_sem=recv.at[slot],
            device_id=device, device_id_type=MESH)
        self.into = pltpu.make_async_remote_copy(
            src_ref=landing, dst_ref=landing, send_sem=send.at[slot], recv_sem=recv.at[slot],
            device_id=device, device_id_type=MESH)

    def start(self):
        self.out.start()

    def wait(self):
        self.into.wait_recv()

    drained = False

    def drain(self):
        self.drained = True
        self.out.wait_send()


class Slots:
    def __init__(self, send, recv):
        self.send, self.recv, self.made = send, recv, []

    def move(self, *args):
        self.made.append(Move(self.send, self.recv, len(self.made), *args))
        return self.made[-1]


class Locals:
    def __init__(self, semaphores):
        self.semaphores, self.made = semaphores, []

    def copy(self, source, target):
        self.made.append(pltpu.make_async_copy(source, target, self.semaphores.at[len(self.made)]))
        self.made[-1].start()
        return self.made[-1]


class Gather:
    def __init__(self, links, slots, view, axes, halved):
        here = {"z": links.z, "y": links.y, "x": links.x}
        self.moves = []
        for axis in axes:
            mine = view(here["z"], here["y"], here["x"])
            if axis == "z":
                self.moves.append([
                    slots.move(links.device("z", way), mine, mine, view(links.along(-way), here["y"], here["x"]))
                    for way in range(1, links.length)])
            else:
                other = dict(here)
                other[axis] = 1 - here[axis]
                self.moves.append([
                    slots.move(links.device(axis), mine, mine, view(other["z"], other["y"], other["x"]))])
            here[axis] = ALL
        if halved:
            mine = view(ALL, ALL, ALL)
            self.moves.append([
                slots.move(links.device("core"), mine, mine, view(ALL, ALL, ALL, 1 - links.rep))])

    def step(self, number):
        if 0 < number <= len(self.moves):
            for move in self.moves[number - 1]:
                move.wait()
        if 0 <= number < len(self.moves):
            for move in self.moves[number]:
                move.start()


class Reduce:
    def __init__(self, links, slots, own, axes, lands, lands_z, finish):
        self.own, self.links, self.finish, self.lands_z = own, links, finish, lands_z
        self.moves, self.adds = [], []
        z, y, x = links.z, links.y, links.x
        here = {"z": ALL, "y": ALL, "x": ALL}
        for axis, land in zip(axes, lands):
            away, home = dict(here), dict(here)
            place = {"y": y, "x": x}[axis]
            away[axis], home[axis] = 1 - place, place
            self.moves.append([slots.move(
                links.device(axis), own(away["z"], away["y"], away["x"]), land, land)])
            here = home
            self.adds.append(functools.partial(add_into, own(home["z"], home["y"], home["x"]), land))
        self.moves.append([
            slots.move(links.device("z", way), own(links.along(way), here["y"], here["x"]), lands_z.at[way - 1],
                       lands_z.at[way - 1])
            for way in range(1, links.length)])
        self.mine = own(z, here["y"], here["x"])
        self.adds.append(self.end)

    def step(self, number):
        if 0 < number <= len(self.moves):
            for move in self.moves[number - 1]:
                move.wait()
            self.adds[number - 1]()
        if 0 <= number < len(self.moves):
            for move in self.moves[number]:
                move.start()

    def end(self):
        total = self.mine[...].astype(F32)
        for way in range(1, self.links.length):
            total = total + self.lands_z[way - 1].astype(F32)
        self.finish(total)


def add_into(target, arrived):
    @pl.loop(0, target.shape[0])
    def _(number):
        target[number] = (target[number].astype(F32) + arrived[number].astype(F32)).astype(target.dtype)


def run(table, tick):
    for item, ticks in table:
        if tick in ticks:
            item.step(ticks.index(tick))


def matmul(left, right):
    return jnp.dot(left, right, preferred_element_type=F32)


def matmul_left(left, right):
    return lax.dot_general(left, right, (((0,), (0,)), ((), ())), preferred_element_type=F32)


def matmul_right(left, right):
    return lax.dot_general(left, right, (((1,), (1,)), ((), ())), preferred_element_type=F32)


def layer_norm(values, gain, offset):
    centre = jnp.mean(values, axis=-1, keepdims=True)
    shifted = values - centre
    spread = jnp.mean(shifted * shifted, axis=-1, keepdims=True)
    return shifted * lax.rsqrt(spread + epsilon) * gain + offset


def layer_norm_back(values, gain, upstream):
    centre = jnp.mean(values, axis=-1, keepdims=True)
    shifted = values - centre
    spread = jnp.mean(shifted * shifted, axis=-1, keepdims=True)
    rate = lax.rsqrt(spread + epsilon)
    normed = shifted * rate
    scaled = upstream * gain
    first = jnp.mean(scaled, axis=-1, keepdims=True)
    second = jnp.mean(scaled * normed, axis=-1, keepdims=True)
    return rate * (scaled - first - normed * second), upstream * normed


def gelu_exact(values):
    return 0.5 * values * (1.0 + jax.scipy.special.erf(values * 0.7071067811865476))


def gelu_parts(values):
    cumulative = 0.5 * (1.0 + lax.erf(values * 0.7071067811865476))
    density = 0.3989422804014327 * jnp.exp(-0.5 * values * values)
    return values * cumulative, cumulative + values * density


def tiles(count, size, action):
    @pl.loop(0, count)
    def _(number):
        action(pl.multiple_of(number * size, size))


def head_mask(rows, columns):
    heads = columns // HEAD_DIM
    row = lax.broadcasted_iota(jnp.int32, (rows * heads, columns), 0)
    column = lax.broadcasted_iota(jnp.int32, (rows * heads, columns), 1)
    head_row = jnp.zeros_like(row)
    head_column = jnp.zeros_like(row)
    for head in range(1, heads):
        head_row = head_row + jnp.where(row >= head * rows, 1, 0)
        head_column = head_column + jnp.where(column >= head * HEAD_DIM, 1, 0)
    return jnp.where(head_row == head_column, 1.0, 0.0)


def spread_heads(rows, mask):
    return jnp.concatenate([rows] * (mask.shape[0] // rows.shape[0]), axis=0) * mask


def pick_heads(stacked, mask, rows):
    kept = stacked * mask
    total = kept[:rows]
    for head in range(1, stacked.shape[0] // rows):
        total = total + kept[head * rows:(head + 1) * rows]
    return total


def softmax(scores):
    exponent = jnp.exp(scores - jnp.max(scores, axis=-1, keepdims=True))
    return exponent / jnp.sum(exponent, axis=-1, keepdims=True)


class VectorSum:
    def __init__(self, links, slots, total, stage, lands):
        self.total, self.stage, self.lands, self.length = total, stage, lands, links.length
        self.moves = [[slots.move(links.device(axis), stage.at[number], lands.at[number], lands.at[number])]
                      for number, axis in enumerate(("core", "x", "y"))]
        self.moves.append([
            slots.move(links.device("z", way), stage.at[3], lands.at[2 + way], lands.at[2 + way])
            for way in range(1, links.length)])

    def step(self, number):
        if 0 < number <= 4:
            for move in self.moves[number - 1]:
                move.wait()
            for land in ([number - 1] if number < 4 else range(3, 2 + self.length)):
                self.total[...] = self.total[...] + self.lands[land]
        if number < 4:
            self.stage[number] = self.total[...]
            for move in self.moves[number]:
                move.start()


class Rows:
    def __init__(self, links, slots, buffer, count, parts):
        self.moves, self.passed = [], []
        for begin, size in parts:
            def place(owner, begin=begin, size=size):
                return buffer.at[pl.ds(owner * count + begin, size)]

            self.moves.append([
                slots.move(links.device("x"), place(0), place(2), place(2)),
                slots.move(links.device("core"), place(0), place(1), place(1))])
            self.passed.append(slots.move(links.device("core"), place(2), place(3), place(3)))

    def send(self, part):
        for move in self.moves[part]:
            move.start()

    def near(self, part):
        self.moves[part][1].wait()

    def forward(self, part):
        self.moves[part][0].wait()
        self.passed[part].start()

    def far(self, part):
        self.passed[part].wait()

    def drain(self):
        for move in [m for pair in self.moves for m in pair] + self.passed:
            move.drain()


class Partials:
    def __init__(self, links, slots, stage, lands, count):
        def place(owner):
            return stage.at[pl.ds(owner * count, count)]

        self.place, self.lands = place, lands
        self.far = slots.move(links.device("core"), place(3), lands.at[0], lands.at[0])
        self.near = slots.move(links.device("core"), place(1), lands.at[1], lands.at[1])
        self.across = slots.move(links.device("x"), place(2), lands.at[2], lands.at[2])


def layer_kernel(length, scaling, counts, media, latents, grad_out, packed, query_shard, context_shard,
                 output_shard, up_shard, down_shard, latents_out, media_grad_out, latents_grad_out, sums_out, grads_out,
                 query_all, context_all, output_all, up_all, up_stage, down_all,
                 packed_all, vectors, media_in, latents_in, grad_in, context, key_value, query, attended, after,
                 feed, feed_t, branch, branch_t, pool, totals, after_lands, d_feed_lands, upstream_rows,
                 grad_up, grad_down, grad_query, grad_output, mask, sums, total, total_stage, total_lands,
                 own_rows_send, own_rows_land, lands_c, lands_b, lands_a, lands_z, result, send, recv, local):
    links = Links(length)
    z, y, x, rep = links.z, links.y, links.x, links.rep
    slots, locals_ = Slots(send, recv), Locals(local)
    slot_count, patches, width = media.shape
    latent_count = latents.shape[1]
    key_count = patches + latent_count
    rows = slot_count * latent_count
    inner = query.shape[-1]
    chunks = length
    hidden = up_all.shape[-1]
    chunk = hidden // chunks
    unit = down_all.shape[-2]
    xy, yx = ("z", "x", "y"), ("z", "y", "x")

    def unit_columns(half, number):
        return pl.ds(pl.multiple_of(((2 * number + half) * 2 + rep) * unit, unit), unit)

    staged = [locals_.copy(packed, packed_all.at[z, y, x])]
    for shard, whole in ((context_shard, context_all), (query_shard, query_all), (output_shard, output_all)):
        half = whole.shape[-2]
        staged.append(locals_.copy(shard.at[pl.ds(pl.multiple_of(rep * half, 16), half)], whole.at[z, y, x, rep]))
    later = []
    for number in range(hidden // unit):
        window = pl.ds(number * unit, unit)
        later.append(locals_.copy(up_shard.at[:, unit_columns(1 - x, number)], up_stage.at[:, window]))
        later.append(locals_.copy(up_shard.at[:, unit_columns(x, number)], up_all.at[z, y, x, :, window]))
    later.append(locals_.copy(down_shard.at[pl.ds(pl.multiple_of(rep * unit, 16), unit)], down_all.at[z, y]))
    grad_load = locals_.copy(grad_out, grad_in)
    latents_load = locals_.copy(latents, latents_in)
    media_load = locals_.copy(media, media_in)
    links.greet()

    def halves(whole, begin, size, order):
        def view(zi, yi, xi, half=rep):
            return whole.at[zi, yi, xi, half, :, pl.ds(begin, size)]

        return Gather(links, slots, view, order, True)

    vector_gather = Gather(links, slots, lambda zi, yi, xi: packed_all.at[zi, yi, xi], xy, False)
    gathers = [
        (halves(context_all, 0, width // 2, xy), (0, 1, 2, 3, 4)),
        (halves(context_all, width // 2, width // 2, yx), (0, 1, 2, 3, 4)),
        (halves(query_all, 0, inner, xy), (1, 2, 3, 4, 5)), (halves(output_all, 0, width, yx), (1, 2, 3, 4, 5)),
    ]
    for number in range(2 * chunks):
        window = pl.ds(number % chunks * chunk, chunk)
        if number < chunks:
            def view(zi, yi, xi, window=window):
                return down_all.at[zi, yi, :, window]
        else:
            def view(zi, yi, xi, window=window):
                return up_all.at[zi, yi, ALL, :, window]
        gathers.append((Gather(links, slots, view, ("z", "y"), False), (number, number + 3, number + 5)))
    up_across = slots.move(links.device("x"), up_stage, up_all.at[z, y, x], up_all.at[z, y, 1 - x])
    gathered = len(slots.made)
    parts = [(0, 2 * latent_count), (2 * latent_count, rows - 2 * latent_count)]
    branch_rows = Rows(links, slots, branch, rows, [(0, rows)])
    feed_rows = Rows(links, slots, feed, rows, parts)

    def pump(tick):
        run(gathers, tick)

    for copy in staged + later:
        copy.wait()
    vector_gather.step(0)
    pump(0)
    up_across.start()
    grad_load.wait()
    kept = jnp.where(lax.broadcasted_iota(jnp.int32, (rows, 1), 0) < counts[0] * latent_count, 1.0, 0.0)
    branch[:rows] = (grad_in[...].reshape(rows, width).astype(F32) * kept).astype(BF16)
    vector_gather.step(1)
    mask[...] = head_mask(latent_count, GROUP)
    sums[...] = jnp.zeros_like(sums)
    vector_gather.step(2)
    latents_load.wait()
    media_load.wait()
    pump(1)
    vector_gather.step(3)
    lane = packed_all.shape[-1]
    for zi in range(length):
        for yi in range(2):
            place = (zi * 2 + yi) * lane
            vectors[:, place:place + lane] = (packed_all[zi, yi, 0] + packed_all[zi, yi, 1]).astype(F32)[:8]

    def normalise_slot(j):
        context[j, :patches] = layer_norm(media_in[j].astype(F32), vectors[0:1], vectors[1:2]).astype(BF16)
        context[j, patches:] = layer_norm(latents_in[j].astype(F32), vectors[2:3], vectors[3:4]).astype(BF16)

    pl.loop(0, slot_count)(normalise_slot)
    pump(2)
    pump(3)
    up_across.wait()
    pump(4)
    branch_rows.send(0)

    def key_value_slot(j):
        key_value[j] = matmul(context[j], context_all[...].reshape(width, 2 * inner)).astype(BF16)

    pl.loop(0, 3)(key_value_slot)
    pump(5)
    pl.loop(3, slot_count)(key_value_slot)
    latent_normed = context[:, patches:, :].reshape(rows, width)
    query[...] = (matmul(latent_normed, query_all[...].reshape(width, inner)) * scaling).astype(BF16).reshape(
        slot_count, latent_count, inner)
    pump(6)

    def attention_slot(j):
        for begin in range(0, inner, GROUP):
            stacked = spread_heads(query[j, :, begin:begin + GROUP], mask[...].astype(BF16))
            probs = softmax(matmul_right(stacked, key_value[j, :, begin:begin + GROUP])).astype(BF16)
            value = matmul(probs, key_value[j, :, inner + begin:inner + begin + GROUP])
            attended[j, :, begin:begin + GROUP] = pick_heads(value, mask[...], latent_count).astype(BF16)

    for part, (begin, size) in enumerate(parts):
        first, last = begin // latent_count, (begin + size) // latent_count
        pl.loop(first, last)(attention_slot)
        after[begin:begin + size] = latents_in[first:last].reshape(size, width).astype(F32) + matmul(
            attended[first:last].reshape(size, inner), output_all[...].reshape(inner, width))
        feed[begin:begin + size] = layer_norm(
            after[begin:begin + size], vectors[4:5], vectors[5:6]).astype(BF16)
        feed_rows.send(part)
        pump(7 + part)
    branch_rows.near(0)
    branch_rows.forward(0)

    def turn(source, target, owner):
        def body(at):
            target[pl.ds(at, 256), pl.ds(owner * rows, 2 * rows)] = source[
                pl.ds(owner * rows, 2 * rows), pl.ds(at, 256)].T

        tiles(width // 256, 256, body)

    turn(branch, branch_t, 0)
    branch_rows.far(0)
    tall = rows
    d_active, active, d_hidden = [pool.at[pl.ds(n * 4 * rows, 4 * rows)] for n in range(3)]

    def d_active_tile(at):
        d_active[pl.ds(at, tall)] = matmul_right(
            branch[pl.ds(at, tall)], down_all[...].reshape(hidden, width)).astype(BF16)

    tiles(4, tall, d_active_tile)
    turn(branch, branch_t, 2)
    pump(9)

    def hidden_tile(at, begin):
        window = pl.ds(begin, chunk)
        weight = up_all[:, :, :, :, window].reshape(width, chunk)
        value, slope = gelu_parts(matmul(feed[pl.ds(at, tall)], weight))
        active[pl.ds(at, tall), window] = value.astype(BF16)
        d_hidden[pl.ds(at, tall), window] = (d_active[pl.ds(at, tall), window].astype(F32) * slope).astype(BF16)

    def d_feed_of(owner):
        return matmul_right(d_hidden[pl.ds(owner * rows, rows)], up_all[...].reshape(width, hidden))

    def after_feed_of(owner):
        return matmul(active[pl.ds(owner * rows, rows)], down_all[...].reshape(hidden, width))

    def rounded(buffer, owner, value):
        buffer[pl.ds(owner * rows, rows)] = value.astype(BF16)

    def across_tile(back, buffer):
        rounded(buffer, 2, totals[1] + back.lands[0].astype(F32))

    up_result, down_result, query_result, context_result, output_result = result
    reductions = []

    def send_off(tick):
        run(reductions, tick)

    def plane_reduction(own, lands_y, lands, finish):
        return Reduce(links, slots, own, ("y",), [lands_y], lands, finish)

    def keep_up(value, window):
        up_result[0, :, window] = jnp.where(x == 0, value[0], value[1])
        own_rows_send[:, window] = jnp.where(x == 0, value[1], value[0]).astype(BF16)

    feed_rows.near(0)
    feed_rows.near(1)
    for c in range(chunks):
        begin = c * chunk
        window = pl.ds(begin, chunk)
        tiles(2, tall, lambda at, begin=begin: hidden_tile(at, begin))
        if c == 0:
            pump(10)
            turn(feed, feed_t, 0)
            feed_rows.forward(0)
            feed_rows.forward(1)
            feed_rows.far(0)
            feed_rows.far(1)
            turn(feed, feed_t, 2)
        tiles(2, tall, lambda at, begin=begin: hidden_tile(pl.multiple_of(2 * rows + at, tall), begin))
        if c == chunks - 1:
            for move in slots.made[:gathered]:
                move.drain()
            feed_rows.drain()
            branch_rows.drain()
            d_feed_back = Partials(links, slots, feed, d_feed_lands, rows)
            after_back = Partials(links, slots, branch, after_lands, rows)
            rounded(feed, 3, d_feed_of(3))
            d_feed_back.far.start()
            totals[1] = d_feed_of(2)
            d_feed_back.far.wait()
            across_tile(d_feed_back, feed)
            d_feed_back.across.start()

        def grad_tile(number, window=window, c=c):
            size = width // 2
            place = pl.multiple_of(number * size, size)
            up = matmul(feed_t[pl.ds(place, size)], d_hidden[:, window]).astype(BF16)
            grad_up[pl.ds(number * (length // 2), length // 2), :, :, :, window] = up.reshape(
                length // 2, 2, 2, size // (2 * length), chunk)
            down = matmul(branch_t[pl.ds(place, size)], active[:, window]).astype(BF16)
            for owner in range(2):
                grad_down[c, owner, pl.ds(place, size)] = down[:, owner * unit:(owner + 1) * unit]

        pl.loop(0, 2)(grad_tile)
        reductions.append((plane_reduction(
            lambda zi, yi, xi, window=window: grad_up.at[zi, yi, ALL, :, window],
            lands_b[0].at[:, :, :, window], lands_z[0].at[:, :, :, window],
            functools.partial(keep_up, window=window)), (c, c + 2, c + 4)))
        if c < chunks - 1:
            pump(10 + c + (1 if c > 0 else 1))
        send_off(c)
    part_size = width // chunks
    for number in range(chunks):
        window = pl.ds(number * part_size, part_size)

        def keep_down(value, window=window):
            down_result[window] = value

        reductions.append((plane_reduction(
            lambda zi, yi, xi, window=window: grad_down.at[zi, yi, window],
            lands_b[1].at[:, window], lands_z[1].at[:, window], keep_down),
            (chunks, chunks + 2 + number, chunks + 4 + number)))
    send_off(4)
    rounded(feed, 1, d_feed_of(1))
    d_feed_back.near.start()
    totals[0] = d_feed_of(0)

    rounded(branch, 3, after_feed_of(3))
    after_back.far.start()
    totals[1] = after_feed_of(2)
    after_back.far.wait()
    across_tile(after_back, branch)
    send_off(5)
    rounded(branch, 1, after_feed_of(1))
    after_back.near.start()
    d_feed_back.near.wait()
    d_feed_back.across.wait()
    after_back.across.start()
    for move in (d_feed_back.far, d_feed_back.near, d_feed_back.across):
        move.drain()

    def fold(terms):
        return jnp.sum(terms.reshape(-1, 8, width), axis=0)

    d_feed = totals.at[0]
    flat_grad = lambda at, size: grad_in[pl.ds(lax.div(at, latent_count), size // latent_count)].reshape(size, width)

    def middle_tile(at, size=latent_count):
        own = pl.ds(at, size)
        upstream = d_feed[own] + d_feed_lands[1, own].astype(F32) + d_feed_lands[2, own].astype(F32)
        d_norm, gain_terms = layer_norm_back(after[own], vectors[4:5], upstream)
        sums[4] = sums[4] + fold(gain_terms)
        sums[5] = sums[5] + fold(upstream)
        row = lax.broadcasted_iota(jnp.int32, (size, 1), 0) + at
        keep = jnp.where(row < counts[0] * latent_count, 1.0, 0.0)
        d_middle = flat_grad(at, size).astype(F32) * keep + d_norm
        d_feed[own] = d_middle
        feed[own] = d_middle.astype(BF16)

    tiles(slot_count, latent_count, middle_tile)
    send_off(6)
    after[...] = after[...] + after_feed_of(0)

    context_rows, output_rows = context_all.shape[-2], output_all.shape[-2]

    def context_own(zi, yi, xi, half):
        return up_all.at[zi, yi, xi, pl.ds(pl.multiple_of(half * context_rows, 16), context_rows)]

    def query_own(zi, yi, xi, half):
        return grad_query.at[zi, yi, xi, half]

    def output_own(zi, yi, xi, half):
        return grad_output.at[zi, yi, xi, half]

    def to_sibling(own, land):
        move = slots.move(links.device("core"), own(ALL, ALL, ALL, 1 - rep), land, land)
        move.start()

        def settle():
            move.wait()
            add_into(own(ALL, ALL, ALL, rep), land)

        return settle

    def halved_reduction(own, number, target, first):
        made = []
        size = target.shape[-1] // 2
        for which, order in enumerate((("y", "x"), ("x", "y"))):
            window = pl.ds(which * size, size)

            def finish(value, window=window):
                target[:, window] = value

            made.append((Reduce(
                links, slots, lambda zi, yi, xi, window=window: own(zi, yi, xi, rep).at[..., window], order,
                [lands_b[number].at[:, :, :, window], lands_a[number].at[:, :, window]],
                lands_z[number].at[:, :, window], finish), (first, first + 1, first + 2, first + 3)))
        return made

    d_branch = feed.at[pl.ds(0, rows)]
    output_block = inner // 2

    def output_grad_tile(number):
        place = pl.multiple_of(number * output_block, output_block)
        turned = attended[:, :, pl.ds(place, output_block)].reshape(rows, output_block).T
        value = matmul(turned, d_branch[...]).astype(BF16)
        grad_output[pl.ds(number * (length // 2), length // 2)] = value.reshape(
            length // 2, 2, 2, 2, output_rows, width)

    pl.loop(0, 2)(output_grad_tile)
    settle_output = to_sibling(output_own, lands_c[2])
    d_attended, d_query = upstream_rows[0], upstream_rows[1]
    d_attended[...] = matmul_right(d_branch[...], output_all[...].reshape(inner, width)).astype(BF16)
    send_off(7)

    def attention_back_slot(j):
        own = pl.ds(pl.multiple_of(j * latent_count, latent_count), latent_count)
        for begin in range(0, inner, GROUP):
            keys = key_value[j, :, begin:begin + GROUP]
            values = key_value[j, :, inner + begin:inner + begin + GROUP]
            low_mask = mask[...].astype(BF16)
            stacked = spread_heads(query[j, :, begin:begin + GROUP], low_mask)
            upstream = spread_heads(d_attended[own, begin:begin + GROUP], low_mask)
            probs = softmax(matmul_right(stacked, keys))
            d_probs = matmul_right(upstream, values)
            d_scores = (probs * (d_probs - jnp.sum(probs * d_probs, axis=-1, keepdims=True))).astype(BF16)
            d_query[own, begin:begin + GROUP] = (
                pick_heads(matmul(d_scores, keys), mask[...], latent_count).astype(BF16).astype(F32) * scaling
            ).astype(BF16)
            at = pl.ds(pl.multiple_of(j * key_count, 16), key_count)
            pool[at, begin:begin + GROUP] = matmul_left(d_scores, stacked).astype(BF16)
            pool[at, inner + begin:inner + begin + GROUP] = matmul_left(probs.astype(BF16), upstream).astype(BF16)

    pl.loop(0, 3)(attention_back_slot)
    send_off(8)
    pl.loop(3, slot_count)(attention_back_slot)
    send_off(9)
    block = width // length

    def query_grad_tile(zi):
        place = pl.multiple_of(zi * block, block)
        turned = context[:, patches:, pl.ds(place, block)].reshape(rows, block).T
        value = matmul(turned, d_query[...]).astype(BF16)
        grad_query[zi] = value.reshape(2, 2, 2, context_rows, inner)

    pl.loop(0, length)(query_grad_tile)
    settle_query = to_sibling(query_own, lands_c[0])

    def context_grad_tile(zi):
        place = pl.multiple_of(zi * block, block)
        value = None
        for j in range(slot_count):
            turned = context[j, :, pl.ds(place, block)].T
            term = matmul(turned, pool[j * key_count:(j + 1) * key_count])
            value = term if value is None else value + term
        up_all[zi] = value.astype(BF16).reshape(2, 2, block // 4, 2 * inner)

    pl.loop(0, length)(context_grad_tile)
    settle_context = to_sibling(context_own, lands_c[1])
    settle_output()
    settle_query()
    first = 2 * chunks + 2
    reductions.extend(halved_reduction(output_own, 4, output_result, first))
    reductions.extend(halved_reduction(query_own, 2, query_result, first))
    send_off(10)
    settle_context()
    reductions.extend(halved_reduction(context_own, 3, context_result, first + 1))
    send_off(11)
    own_rows_move = slots.move(links.device("x"), own_rows_send, own_rows_land, own_rows_land)
    own_rows_move.start()
    after_back.near.wait()
    after_back.across.wait()
    for move in (after_back.far, after_back.near, after_back.across):
        move.drain()
    branch[:rows] = ((after[...] + after_lands[1].astype(F32) + after_lands[2].astype(F32)) * kept).astype(BF16)
    written = [locals_.copy(branch.at[pl.ds(j * latent_count, latent_count)], latents_out.at[j])
               for j in range(slot_count)]

    context_up = totals.at[1]

    def input_slot(j):
        at = pl.ds(pl.multiple_of(j * key_count, 16), key_count)
        own = pl.ds(pl.multiple_of(j * latent_count, latent_count), latent_count)
        context_up[...] = matmul_right(pool[at], context_all[...].reshape(width, 2 * inner))
        context_up[patches:] = context_up[patches:] + matmul_right(d_query[own], query_all[...].reshape(width, inner))

        def media_tile(at, size=patches // 2):
            tile = pl.ds(at, size)
            upstream = context_up[tile]
            value, gain_terms = layer_norm_back(media_in[j, tile].astype(F32), vectors[0:1], upstream)
            sums[0] = sums[0] + fold(gain_terms)
            sums[1] = sums[1] + fold(upstream)
            media_in[j, tile] = value.astype(BF16)

        tiles(2, patches // 2, media_tile)
        upstream = context_up[patches:]
        value, gain_terms = layer_norm_back(latents_in[j].astype(F32), vectors[2:3], upstream)
        sums[2] = sums[2] + fold(gain_terms)
        sums[3] = sums[3] + fold(upstream)
        latents_in[j] = (d_feed[own] + value).astype(BF16)

    pl.loop(0, 2)(input_slot)
    send_off(12)
    own_rows_move.wait()
    up_result[1] = own_rows_land[...].astype(F32)
    pl.loop(2, 3)(input_slot)
    send_off(13)
    pl.loop(3, slot_count)(input_slot)
    send_off(14)
    written.append(locals_.copy(media_in, media_grad_out))
    written.append(locals_.copy(latents_in, latents_grad_out))
    total[...] = jnp.zeros_like(total)
    for number in range(6):
        total[number:number + 1] = jnp.sum(sums[number], axis=0, keepdims=True)
    vector_sum = VectorSum(links, slots, total, total_stage, total_lands)
    vector_sum.step(0)
    send_off(15)
    for value, out in zip(result, grads_out):
        written.append(locals_.copy(value, out.at[rep]))
        move = slots.move(links.device("core"), value, out.at[rep], out.at[1 - rep])
        move.start()
        written.append(move)
    for number in range(1, 5):
        vector_sum.step(number)
    sums_out[...] = total[...]
    for copy in written:
        copy.wait()
    for move in slots.made:
        if not move.drained:
            move.drain()


def layer(length, counts, media, latents, grad_out, packed, shards):
    query_shard, context_shard, output_shard, up_shard, down_shard = shards
    slot_count, patches, width = media.shape
    latent_count = latents.shape[1]
    key_count = patches + latent_count
    rows = slot_count * latent_count
    inner = query_shard.shape[1]
    unit = down_shard.shape[0] // 2
    hidden = up_shard.shape[1] // 4
    blocks = (length, 2, 2)

    def halved(shard):
        return blocks + (2, shard.shape[0] // 2, shard.shape[1])

    up_shape = blocks + (up_shard.shape[0], hidden)
    down_shape = (length, 2, unit, width)
    halves = [halved(s)[4:] for s in shards[:3]]
    results = [(2,) + up_shape[3:], (width, unit)] + halves
    anywhere = pl.BlockSpec(memory_space=pl.ANY)
    vmem = pl.BlockSpec(memory_space=pltpu.VMEM)
    sums_shape = (8, width)
    scratch = [
        pltpu.VMEM(halved(query_shard), BF16),
        pltpu.VMEM(halved(context_shard), BF16),
        pltpu.VMEM(halved(output_shard), BF16),
        pltpu.VMEM(up_shape, BF16),
        pltpu.VMEM(up_shape[3:], BF16),
        pltpu.VMEM(down_shape, BF16),
        pltpu.VMEM(blocks + packed.shape, BF16),
        pltpu.VMEM((8, width), F32),
        pltpu.VMEM(media.shape, BF16),
        pltpu.VMEM(latents.shape, BF16),
        pltpu.VMEM(grad_out.shape, BF16),
        pltpu.VMEM((slot_count, key_count, width), BF16),
        pltpu.VMEM((slot_count, key_count, 2 * inner), BF16),
        pltpu.VMEM((slot_count, latent_count, inner), BF16),
        pltpu.VMEM((slot_count, latent_count, inner), BF16),
        pltpu.VMEM((rows, width), F32),
        pltpu.VMEM((4 * rows, width), BF16),
        pltpu.VMEM((width, 4 * rows), BF16),
        pltpu.VMEM((4 * rows, width), BF16),
        pltpu.VMEM((width, 4 * rows), BF16),
        pltpu.VMEM((max(12 * rows, slot_count * key_count), hidden), BF16),
        pltpu.VMEM((2, rows, width), F32),
        pltpu.VMEM((3, rows, width), BF16),
        pltpu.VMEM((3, rows, width), BF16),
        [pltpu.VMEM((rows, inner), BF16)] * 2,
        pltpu.VMEM(up_shape, BF16),
        pltpu.VMEM((length, 2, width, unit), BF16),
        pltpu.VMEM(halved(query_shard), BF16),
        pltpu.VMEM(halved(output_shard), BF16),
        pltpu.VMEM((latent_count * (GROUP // HEAD_DIM), GROUP), F32),
        pltpu.VMEM((6, 8, width), F32),
        pltpu.VMEM(sums_shape, F32),
        pltpu.VMEM((4,) + sums_shape, F32),
        pltpu.VMEM((2 + length,) + sums_shape, F32),
        pltpu.VMEM(up_shape[3:], BF16),
        pltpu.VMEM(up_shape[3:], BF16),
        [pltpu.VMEM(blocks + h, BF16) for h in halves],
        [pltpu.VMEM((length, 2) + up_shape[3:], BF16), pltpu.VMEM((length, width, unit), BF16)]
        + [pltpu.VMEM((length, 2) + h, BF16) for h in halves],
        [None, None] + [pltpu.VMEM((length,) + h, BF16) for h in halves],
        [pltpu.VMEM((length - 1, 2) + up_shape[3:], BF16), pltpu.VMEM((length - 1, width, unit), BF16)]
        + [pltpu.VMEM((length - 1,) + h, BF16) for h in halves],
        [pltpu.VMEM(r, F32) for r in results],
        pltpu.SemaphoreType.DMA((200,)),
        pltpu.SemaphoreType.DMA((200,)),
        pltpu.SemaphoreType.DMA((64,)),
    ]
    out_shape = (
        jax.ShapeDtypeStruct(latents.shape, BF16), jax.ShapeDtypeStruct(media.shape, BF16),
        jax.ShapeDtypeStruct(latents.shape, BF16), jax.ShapeDtypeStruct(sums_shape, F32),
        [jax.ShapeDtypeStruct((2,) + r, F32) for r in results])
    return pl.pallas_call(
        functools.partial(layer_kernel, length, HEAD_DIM ** (-0.5)),
        out_shape=out_shape,
        in_specs=[pl.BlockSpec(memory_space=pltpu.SMEM)] + [anywhere] * 9,
        out_specs=(anywhere, anywhere, anywhere, vmem, [anywhere] * 5),
        scratch_shapes=scratch,
        compiler_params=pltpu.CompilerParams(
            collective_id=0, has_side_effects=True, vmem_limit_bytes=63 * 2 ** 20),
        name="resampler_layer",
    )(counts, media, latents, grad_out, packed, query_shard, context_shard, output_shard, up_shard, down_shard)


def head_scores(first_heads, second_heads):
    return jnp.einsum(
        "bqhd,bkhd->bhqk", first_heads, second_heads, preferred_element_type=jnp.float32
    )


def collective_body(
    media,
    latents,
    image_counts,
    grad_out,
    media_gain,
    media_bias,
    latent_gain,
    latent_bias,
    feed_gain,
    feed_bias,
    query_weight,
    context_weight,
    output_weight,
    up_weight,
    down_weight,
):
    samples, slots, patches, model_width = media.shape
    latent_count = latents.shape[2]
    inner_width = query_weight.shape[1]
    head_count = inner_width // HEAD_DIM
    blocks = samples * slots
    key_count = patches + latent_count
    latent_total = blocks * latent_count
    scaling = HEAD_DIM ** (-0.5)
    vector_shards = (media_gain, media_bias, latent_gain, latent_bias, feed_gain, feed_bias)
    weight_shards = (query_weight, context_weight, output_weight, up_weight, down_weight)
    gathered = tuple(lax.all_gather(s, "dp", axis=0, tiled=True) for s in vector_shards + weight_shards)
    vectors = [element.astype(jnp.float32) for element in gathered[:6]]
    media_rows = media.reshape(blocks * patches, model_width).astype(jnp.float32)
    latent_rows = latents.reshape(latent_total, model_width).astype(jnp.float32)
    media_normed = layer_norm(media_rows, vectors[0], vectors[1]).astype(jnp.bfloat16)
    latent_normed = layer_norm(latent_rows, vectors[2], vectors[3]).astype(jnp.bfloat16)
    queries = (matmul(latent_normed, gathered[6]) * scaling).astype(jnp.bfloat16)
    context = jnp.concatenate(
        [
            media_normed.reshape(blocks, patches, model_width),
            latent_normed.reshape(blocks, latent_count, model_width),
        ],
        axis=1,
    ).reshape(blocks * key_count, model_width)
    key_value = (
        matmul(context, gathered[7])
        .astype(jnp.bfloat16)
        .reshape(blocks, key_count, 2 * inner_width)
    )
    query_heads = queries.reshape(blocks, latent_count, head_count, HEAD_DIM)
    key_heads = key_value[:, :, :inner_width].reshape(blocks, key_count, head_count, HEAD_DIM)
    value_heads = key_value[:, :, inner_width:].reshape(blocks, key_count, head_count, HEAD_DIM)
    scores = head_scores(query_heads, key_heads)
    row_max = jnp.max(scores, axis=-1, keepdims=True)
    exponent = jnp.exp(scores - row_max)
    row_total = jnp.sum(exponent, axis=-1, keepdims=True)
    log_total = row_max + jnp.log(row_total)
    attention_weights = (exponent / row_total).astype(jnp.bfloat16)
    attended = (
        jnp.einsum(
            "bhqk,bkhd->bqhd", attention_weights, value_heads, preferred_element_type=jnp.float32
        )
        .astype(jnp.bfloat16)
        .reshape(latent_total, inner_width)
    )
    after_attention = latent_rows + matmul(attended, gathered[8])
    feed_input = layer_norm(after_attention, vectors[4], vectors[5]).astype(jnp.bfloat16)
    hidden = matmul(feed_input, gathered[9])
    activated = gelu_exact(hidden).astype(jnp.bfloat16)
    after_feed = after_attention + matmul(activated, gathered[10])
    slot_mask = (
        lax.broadcasted_iota(jnp.int32, (samples, slots), 1) < image_counts[:, None]
    ).astype(jnp.float32)
    row_mask = jnp.broadcast_to(slot_mask[:, :, None], (samples, slots, latent_count)).reshape(
        latent_total, 1
    )
    latents_out = (after_feed * row_mask).astype(jnp.bfloat16).reshape(latents.shape)
    backward_set = gathered
    back_vectors = [element.astype(jnp.float32) for element in backward_set[:6]]
    d_after = grad_out.reshape(latent_total, model_width).astype(jnp.float32) * row_mask
    d_branch = d_after.astype(jnp.bfloat16)
    grad_down = matmul_left(activated, d_branch)
    d_activated = matmul_right(d_branch, backward_set[10])
    d_hidden = jax.vjp(gelu_exact, hidden)[1](d_activated)[0].astype(jnp.bfloat16)
    grad_up = matmul_left(feed_input, d_hidden)
    d_feed = matmul_right(d_hidden, backward_set[9])
    d_feed_norm, grad_feed_gain, grad_feed_bias = jax.vjp(
        layer_norm, after_attention, back_vectors[4], back_vectors[5]
    )[1](d_feed)
    d_middle = d_after + d_feed_norm
    d_out_branch = d_middle.astype(jnp.bfloat16)
    grad_output = matmul_left(attended, d_out_branch)
    d_attended = (
        matmul_right(d_out_branch, backward_set[8])
        .astype(jnp.bfloat16)
        .reshape(blocks, latent_count, head_count, HEAD_DIM)
    )
    recomputed = jnp.exp(head_scores(query_heads, key_heads) - log_total)
    d_weights = head_scores(d_attended, value_heads)
    d_scores = (
        recomputed * (d_weights - jnp.sum(recomputed * d_weights, axis=-1, keepdims=True))
    ).astype(jnp.bfloat16)
    d_queries = (
        jnp.einsum(
            "bhqk,bkhd->bqhd", d_scores, key_heads, preferred_element_type=jnp.float32
        ).astype(jnp.bfloat16)
        * scaling
    ).reshape(latent_total, inner_width)
    d_keys = jnp.einsum(
        "bhqk,bqhd->bkhd", d_scores, query_heads, preferred_element_type=jnp.float32
    ).astype(jnp.bfloat16)
    d_values = jnp.einsum(
        "bhqk,bqhd->bkhd",
        recomputed.astype(jnp.bfloat16),
        d_attended,
        preferred_element_type=jnp.float32,
    ).astype(jnp.bfloat16)
    d_key_value = jnp.concatenate(
        [
            d_keys.reshape(blocks, key_count, inner_width),
            d_values.reshape(blocks, key_count, inner_width),
        ],
        axis=-1,
    ).reshape(blocks * key_count, 2 * inner_width)
    grad_query = matmul_left(latent_normed, d_queries)
    grad_context = matmul_left(context, d_key_value)
    d_context = matmul_right(d_key_value, backward_set[7]).reshape(blocks, key_count, model_width)
    d_latent_normed = matmul_right(d_queries, backward_set[6]) + d_context[:, patches:, :].reshape(
        latent_total, model_width
    )
    d_media_normed = d_context[:, :patches, :].reshape(blocks * patches, model_width)
    d_latent_norm, grad_latent_gain, grad_latent_bias = jax.vjp(
        layer_norm, latent_rows, back_vectors[2], back_vectors[3]
    )[1](d_latent_normed)
    grad_latents = (d_middle + d_latent_norm).astype(jnp.bfloat16).reshape(latents.shape)
    d_media, grad_media_gain, grad_media_bias = jax.vjp(
        layer_norm, media_rows, back_vectors[0], back_vectors[1]
    )[1](d_media_normed)
    grad_media = d_media.astype(jnp.bfloat16).reshape(media.shape)
    vector_grads = jnp.stack([
        grad_media_gain, grad_media_bias, grad_latent_gain, grad_latent_bias, grad_feed_gain, grad_feed_bias])
    weight_grads = [
        g.astype(jnp.bfloat16) for g in (grad_query, grad_context, grad_output, grad_up, grad_down)]
    vector_sums = lax.psum_scatter(vector_grads, "dp", scatter_dimension=1, tiled=True)
    summed = [lax.psum_scatter(g, "dp", scatter_dimension=0, tiled=True) for g in weight_grads]
    owned = tuple(lax.psum(vector_sums, "rep")) + tuple(
        lax.psum(s, "rep").astype(jnp.float32) for s in summed)
    return (
        latents_out,
        grad_media,
        grad_latents,
        owned[0],
        owned[1],
        owned[2],
        owned[3],
        owned[4],
        owned[5],
        owned[6],
        owned[7],
        owned[8],
        owned[9],
        owned[10],
    )


def body(media, latents, image_counts, grad_out, *parameters):
    chips = lax.axis_size("dp")
    weight_shards = parameters[6:]
    tiled = (media.shape[0] == 1 and chips % 4 == 0 and chips > 4 and parameters[0].shape[0] == 64
             and all(s.shape[0] % 32 == 0 for s in weight_shards))
    if not tiled:
        return collective_body(media, latents, image_counts, grad_out, *parameters)
    side = lax.rem(lax.axis_index("dp"), 2)
    stacked = jnp.stack(parameters[:6])
    packed = jnp.pad(
        jnp.concatenate([jnp.where(side == 0, stacked, 0), jnp.where(side == 0, 0, stacked)], axis=1), ((0, 10), (0, 0)))
    latents_out, grad_media, grad_latents, vector_sums, summed = layer(
        chips // 4, image_counts, media[0], latents[0], grad_out[0], packed, weight_shards)
    sums = [s.reshape(-1, s.shape[-1]) for s in summed[2:]]
    rows, hidden = summed[0].shape[2:]
    unit = summed[1].shape[-1]
    planes = jnp.where(lax.rem(lax.axis_index("dp"), 2) == 0, summed[0], summed[0][:, ::-1])
    sums.append(planes.reshape(2, 2, rows, hidden // unit, unit).transpose(2, 3, 1, 0, 4).reshape(rows, 4 * hidden))
    sums.append(summed[1].transpose(0, 2, 1).reshape(2 * unit, -1))
    width = parameters[0].shape[0]
    mine = lax.dynamic_slice(vector_sums, (0, lax.axis_index("dp") * width), (6, width))
    return (latents_out[None], grad_media[None], grad_latents[None]) + tuple(mine) + tuple(sums)


def solution(mesh):
    return jax.shard_map(
        body,
        mesh=mesh,
        in_specs=(
            P(("dp", "rep"), None, None, None),
            P(("dp", "rep"), None, None, None),
            P(("dp", "rep")),
            P(("dp", "rep"), None, None, None),
            P("dp"),
            P("dp"),
            P("dp"),
            P("dp"),
            P("dp"),
            P("dp"),
            P("dp", None),
            P("dp", None),
            P("dp", None),
            P("dp", None),
            P("dp", None),
        ),
        out_specs=(
            P(("dp", "rep"), None, None, None),
            P(("dp", "rep"), None, None, None),
            P(("dp", "rep"), None, None, None),
            P("dp"),
            P("dp"),
            P("dp"),
            P("dp"),
            P("dp"),
            P("dp"),
            P("dp", None),
            P("dp", None),
            P("dp", None),
            P("dp", None),
            P("dp", None),
        ),
        check_vma=False,
    )
```

```python
import functools

import jax
import jax.numpy as jnp
from jax import lax
from jax.experimental import pallas as pl
from jax.experimental.pallas import tpu as pltpu
from jax.sharding import PartitionSpec as P

HEAD_DIM = 64
GROUP = 256

epsilon = 1e-05

MESH = pl.DeviceIdType.MESH
ALL = slice(None)
F32 = jnp.float32
BF16 = jnp.bfloat16


class Links:
    def __init__(self, length):
        self.length = length
        self.dp = lax.axis_index("dp")
        self.rep = lax.axis_index("rep")
        self.z = lax.div(self.dp, 4)
        self.y = lax.rem(lax.div(self.dp, 2), 2)
        self.x = lax.rem(self.dp, 2)

    def device(self, axis, way=0):
        if axis == "core":
            return (self.dp, 1 - self.rep)
        if axis == "x":
            return (self.dp + 1 - 2 * self.x, self.rep)
        if axis == "y":
            return (self.dp + 2 - 4 * self.y, self.rep)
        return (self.dp + 4 * (self.along(way) - self.z), self.rep)

    def along(self, way):
        return lax.rem(self.z + way + self.length, self.length)

    def greet(self):
        barrier = pltpu.get_barrier_semaphore()
        peers = [("core", 0), ("x", 0), ("y", 0)] + [("z", way) for way in range(1, self.length)]
        for axis, way in peers:
            pl.semaphore_signal(barrier, inc=1, device_id=self.device(axis, way), device_id_type=MESH)
        pl.semaphore_wait(barrier, len(peers))


class Move:
    def __init__(self, slots, copies, landing):
        send, recv = slots.send.at[slots.group], slots.recv.at[slots.made]
        slots.made += 1
        self.slots, self.group, self.copies = slots, slots.group, [
            pltpu.make_async_remote_copy(
                src_ref=source, dst_ref=target, send_sem=send, recv_sem=recv,
                device_id=device, device_id_type=MESH)
            for device, source, target in copies]
        self.bytes = 0
        for _, source, _ in copies:
            size = jnp.dtype(source.dtype).itemsize
            for extent in source.shape:
                size *= extent
            self.bytes += size
        self.into = pltpu.make_async_remote_copy(
            src_ref=landing, dst_ref=landing, send_sem=send, recv_sem=recv,
            device_id=copies[0][0], device_id_type=MESH)

    def start(self):
        for copy in self.copies:
            copy.start()
        self.slots.sent[self.group] += self.bytes

    def wait(self):
        self.into.wait_recv()


class Slots:
    def __init__(self, send, recv, ruler):
        self.send, self.recv, self.ruler, self.made, self.group = send, recv, ruler, 0, 0
        self.sent = [0] * send.shape[0]

    def move(self, device, source, target, landing):
        return Move(self, [(device, source, target)], landing)

    def drain(self, group, ruler=None):
        ruler = self.ruler if ruler is None else ruler
        row = ruler.shape[-1] * jnp.dtype(ruler.dtype).itemsize
        rows, rest = divmod(self.sent[group], row)
        assert rest == 0 and rows % 16 == 0 and rows <= ruler.shape[0]
        whole = ruler.at[pl.ds(0, rows)]
        pltpu.make_async_copy(whole, whole, self.send.at[group]).wait()


class Locals:
    def __init__(self, semaphores):
        self.semaphores, self.made = semaphores, 0

    def copy(self, source, target):
        return self.fill([(source, target)], target)

    def fill(self, copies, whole):
        semaphore = self.semaphores.at[self.made]
        self.made += 1
        for source, target in copies:
            pltpu.make_async_copy(source, target, semaphore).start()
        return pltpu.make_async_copy(whole, whole, semaphore)


class Gather:
    def __init__(self, links, slots, view, axes, halved):
        here = {"z": links.z, "y": links.y, "x": links.x}
        self.moves = []
        for axis in axes:
            mine = view(here["z"], here["y"], here["x"])
            if axis == "z":
                self.moves.append(Move(
                    slots, [(links.device("z", way), mine, mine) for way in range(1, links.length)],
                    view(pl.ds(0, links.length - 1), here["y"], here["x"])))
            else:
                other = dict(here)
                other[axis] = 1 - here[axis]
                self.moves.append(
                    slots.move(links.device(axis), mine, mine, view(other["z"], other["y"], other["x"])))
            here[axis] = ALL
        if halved:
            mine = view(ALL, ALL, ALL)
            self.moves.append(
                slots.move(links.device("core"), mine, mine, view(ALL, ALL, ALL, 1 - links.rep)))

    def step(self, number):
        if 0 < number <= len(self.moves):
            self.moves[number - 1].wait()
        if 0 <= number < len(self.moves):
            self.moves[number].start()


class Reduce:
    def __init__(self, links, slots, own, axes, lands, lands_z, finish):
        self.own, self.links, self.finish, self.lands_z = own, links, finish, lands_z
        self.moves, self.adds = [], []
        z, y, x = links.z, links.y, links.x
        here = {"z": ALL, "y": ALL, "x": ALL}
        for axis, land in zip(axes, lands):
            away, home = dict(here), dict(here)
            place = {"y": y, "x": x}[axis]
            away[axis], home[axis] = 1 - place, place
            self.moves.append(slots.move(
                links.device(axis), own(away["z"], away["y"], away["x"]), land, land))
            here = home
            self.adds.append(functools.partial(add_into, own(home["z"], home["y"], home["x"]), land))
        self.moves.append(Move(
            slots, [(links.device("z", way), own(links.along(way), here["y"], here["x"]), lands_z.at[way - 1])
                    for way in range(1, links.length)], lands_z))
        self.mine = own(z, here["y"], here["x"])
        self.adds.append(self.end)

    def step(self, number):
        if 0 < number <= len(self.moves):
            self.moves[number - 1].wait()
            self.adds[number - 1]()
        if 0 <= number < len(self.moves):
            self.moves[number].start()

    def end(self):
        total = self.mine[...].astype(F32)
        for way in range(1, self.links.length):
            total = total + self.lands_z[way - 1].astype(F32)
        self.finish(total)


def add_into(target, arrived):
    @pl.loop(0, target.shape[0])
    def _(number):
        target[number] = (target[number].astype(F32) + arrived[number].astype(F32)).astype(target.dtype)


def run(table, tick):
    for item, ticks in table:
        if tick in ticks:
            item.step(ticks.index(tick))


def matmul(left, right):
    return jnp.dot(left, right, preferred_element_type=F32)


def matmul_left(left, right):
    return lax.dot_general(left, right, (((0,), (0,)), ((), ())), preferred_element_type=F32)


def matmul_right(left, right):
    return lax.dot_general(left, right, (((1,), (1,)), ((), ())), preferred_element_type=F32)


def layer_norm(values, gain, offset):
    centre = jnp.mean(values, axis=-1, keepdims=True)
    shifted = values - centre
    spread = jnp.mean(shifted * shifted, axis=-1, keepdims=True)
    return shifted * lax.rsqrt(spread + epsilon) * gain + offset


def layer_norm_back(values, gain, upstream):
    centre = jnp.mean(values, axis=-1, keepdims=True)
    shifted = values - centre
    spread = jnp.mean(shifted * shifted, axis=-1, keepdims=True)
    rate = lax.rsqrt(spread + epsilon)
    normed = shifted * rate
    scaled = upstream * gain
    first = jnp.mean(scaled, axis=-1, keepdims=True)
    second = jnp.mean(scaled * normed, axis=-1, keepdims=True)
    return rate * (scaled - first - normed * second), upstream * normed


def gelu_exact(values):
    return 0.5 * values * (1.0 + jax.scipy.special.erf(values * 0.7071067811865476))


def gelu_parts(values):
    cumulative = 0.5 * (1.0 + lax.erf(values * 0.7071067811865476))
    density = 0.3989422804014327 * jnp.exp(-0.5 * values * values)
    return values * cumulative, cumulative + values * density


def tiles(count, size, action):
    @pl.loop(0, count)
    def _(number):
        action(pl.multiple_of(number * size, size))


def head_mask(rows, columns):
    heads = columns // HEAD_DIM
    row = lax.broadcasted_iota(jnp.int32, (rows * heads, columns), 0)
    column = lax.broadcasted_iota(jnp.int32, (rows * heads, columns), 1)
    head_row = jnp.zeros_like(row)
    head_column = jnp.zeros_like(row)
    for head in range(1, heads):
        head_row = head_row + jnp.where(row >= head * rows, 1, 0)
        head_column = head_column + jnp.where(column >= head * HEAD_DIM, 1, 0)
    return jnp.where(head_row == head_column, 1.0, 0.0)


def spread_heads(rows, mask):
    return jnp.concatenate([rows] * (mask.shape[0] // rows.shape[0]), axis=0) * mask


def pick_heads(stacked, mask, rows):
    kept = stacked * mask
    total = kept[:rows]
    for head in range(1, stacked.shape[0] // rows):
        total = total + kept[head * rows:(head + 1) * rows]
    return total


def softmax(scores):
    exponent = jnp.exp(scores - jnp.max(scores, axis=-1, keepdims=True))
    return exponent / jnp.sum(exponent, axis=-1, keepdims=True)


class VectorSum:
    def __init__(self, links, slots, total, stage, lands):
        self.total, self.stage, self.lands, self.length = total, stage, lands, links.length
        self.moves = [slots.move(links.device(axis), stage.at[number], lands.at[number], lands.at[number])
                      for number, axis in enumerate(("core", "x", "y"))]
        self.moves.append(Move(
            slots, [(links.device("z", way), stage.at[3], lands.at[2 + way]) for way in range(1, links.length)],
            lands.at[pl.ds(3, links.length - 1)]))

    def step(self, number):
        if 0 < number <= 4:
            self.moves[number - 1].wait()
            for land in ([number - 1] if number < 4 else range(3, 2 + self.length)):
                self.total[...] = self.total[...] + self.lands[land]
        if number < 4:
            self.stage[number] = self.total[...]
            self.moves[number].start()


class Rows:
    def __init__(self, links, slots, buffer, count, parts):
        self.moves, self.passed = [], []
        for begin, size in parts:
            def place(owner, begin=begin, size=size):
                return buffer.at[pl.ds(owner * count + begin, size)]

            self.moves.append([
                slots.move(links.device("x"), place(0), place(2), place(2)),
                slots.move(links.device("core"), place(0), place(1), place(1))])
            self.passed.append(slots.move(links.device("core"), place(2), place(3), place(3)))

    def send(self, part):
        for move in self.moves[part]:
            move.start()

    def near(self, part):
        self.moves[part][1].wait()

    def forward(self, part):
        self.moves[part][0].wait()
        self.passed[part].start()

    def far(self, part):
        self.passed[part].wait()


class Partials:
    def __init__(self, links, slots, stage, lands, count):
        def place(owner):
            return stage.at[pl.ds(owner * count, count)]

        self.place, self.lands = place, lands
        self.far = slots.move(links.device("core"), place(3), lands.at[0], lands.at[0])
        self.near = slots.move(links.device("core"), place(1), lands.at[1], lands.at[1])
        self.across = slots.move(links.device("x"), place(2), lands.at[2], lands.at[2])


def layer_kernel(length, scaling, counts, media, latents, grad_out, packed, query_shard, context_shard,
                 output_shard, up_shard, down_shard, latents_out, media_grad_out, latents_grad_out, sums_out, grads_out,
                 query_all, context_all, output_all, up_all, up_stage, down_all,
                 packed_all, vectors, media_in, latents_in, grad_in, context, key_value, query, attended, after,
                 feed, feed_t, branch, branch_t, pool, totals, after_lands, d_feed_lands, upstream_rows,
                 grad_up, grad_down, grad_query, grad_output, mask, sums, total, total_stage, total_lands,
                 own_rows_send, own_rows_land, lands_c, lands_b, lands_a, lands_z, result, send, recv, local):
    links = Links(length)
    z, y, x, rep = links.z, links.y, links.x, links.rep
    slots, locals_ = Slots(send, recv, pool), Locals(local)
    slot_count, patches, width = media.shape
    latent_count = latents.shape[1]
    key_count = patches + latent_count
    rows = slot_count * latent_count
    inner = query.shape[-1]
    chunks = length
    hidden = up_all.shape[-1]
    chunk = hidden // chunks
    unit = down_all.shape[-2]
    xy, yx = ("z", "x", "y"), ("z", "y", "x")

    def unit_columns(half, number):
        return pl.ds(pl.multiple_of(((2 * number + half) * 2 + rep) * unit, unit), unit)

    staged = [locals_.copy(packed, packed_all.at[z, y, x])]
    for shard, whole in ((context_shard, context_all), (query_shard, query_all), (output_shard, output_all)):
        half = whole.shape[-2]
        staged.append(locals_.copy(shard.at[pl.ds(pl.multiple_of(rep * half, 16), half)], whole.at[z, y, x, rep]))
    units = range(hidden // unit)
    staged.append(locals_.fill(
        [(up_shard.at[:, unit_columns(1 - x, n)], up_stage.at[:, pl.ds(n * unit, unit)]) for n in units], up_stage))
    staged.append(locals_.fill(
        [(up_shard.at[:, unit_columns(x, n)], up_all.at[z, y, x, :, pl.ds(n * unit, unit)]) for n in units],
        up_all.at[z, y, x]))
    staged.append(locals_.copy(down_shard.at[pl.ds(pl.multiple_of(rep * unit, 16), unit)], down_all.at[z, y]))
    grad_load = locals_.copy(grad_out, grad_in)
    latents_load = locals_.copy(latents, latents_in)
    media_load = locals_.copy(media, media_in)
    links.greet()

    def halves(whole, begin, size, order):
        def view(zi, yi, xi, half=rep):
            return whole.at[zi, yi, xi, half, :, pl.ds(begin, size)]

        return Gather(links, slots, view, order, True)

    slots.group = 0
    vector_gather = Gather(links, slots, lambda zi, yi, xi: packed_all.at[zi, yi, xi], xy, False)
    slots.group = 1
    gathers = [
        (halves(context_all, 0, width // 2, xy), (0, 1, 2, 3, 4)),
        (halves(context_all, width // 2, width // 2, yx), (0, 1, 2, 3, 4)),
        (halves(query_all, 0, inner, yx), (0, 2, 3, 4, 5)), (halves(output_all, 0, width, yx), (0, 2, 3, 4, 5)),
    ]
    slots.group = 2
    for number in range(2 * chunks):
        window = pl.ds(number % chunks * chunk, chunk)
        if number < chunks:
            def view(zi, yi, xi, window=window):
                return down_all.at[zi, yi, :, window]
        else:
            def view(zi, yi, xi, window=window):
                return up_all.at[zi, yi, ALL, :, window]
        if number == chunks - 1:
            gathers.append((Gather(links, slots, view, ("y", "z"), False), (0, 2, 7)))
        else:
            ticks = (max(number - 1, 0), number + 2, number + 4)
            gathers.append((Gather(links, slots, view, ("z", "y"), False), ticks))
    up_across = slots.move(links.device("x"), up_stage, up_all.at[z, y, x], up_all.at[z, y, 1 - x])
    slots.group = 3
    parts = [(0, 2 * latent_count), (2 * latent_count, rows - 2 * latent_count)]
    branch_rows = Rows(links, slots, branch, rows, [(0, rows)])
    feed_rows = Rows(links, slots, feed, rows, parts)

    def pump(tick):
        run(gathers, tick)

    for copy in staged:
        copy.wait()
    vector_gather.step(0)
    pump(0)
    up_across.start()
    grad_load.wait()
    kept = jnp.where(lax.broadcasted_iota(jnp.int32, (rows, 1), 0) < counts[0] * latent_count, 1.0, 0.0)
    branch[:rows] = (grad_in[...].reshape(rows, width).astype(F32) * kept).astype(BF16)
    vector_gather.step(1)
    mask[...] = head_mask(latent_count, GROUP)
    sums[...] = jnp.zeros_like(sums)
    vector_gather.step(2)
    latents_load.wait()
    media_load.wait()
    pump(1)
    vector_gather.step(3)
    lane = packed_all.shape[-1]
    for zi in range(length):
        for yi in range(2):
            place = (zi * 2 + yi) * lane
            vectors[:, place:place + lane] = (packed_all[zi, yi, 0] + packed_all[zi, yi, 1]).astype(F32)[:8]

    def normalise_slot(j):
        context[j, :patches] = layer_norm(media_in[j].astype(F32), vectors[0:1], vectors[1:2]).astype(BF16)
        context[j, patches:] = layer_norm(latents_in[j].astype(F32), vectors[2:3], vectors[3:4]).astype(BF16)

    pl.loop(0, slot_count)(normalise_slot)
    pump(2)
    up_across.wait()
    pump(3)
    pump(4)
    branch_rows.send(0)

    def key_value_slot(j):
        key_value[j] = matmul(context[j], context_all[...].reshape(width, 2 * inner)).astype(BF16)

    pl.loop(0, 3)(key_value_slot)
    pump(5)
    pl.loop(3, slot_count)(key_value_slot)
    latent_normed = context[:, patches:, :].reshape(rows, width)
    query[...] = (matmul(latent_normed, query_all[...].reshape(width, inner)) * scaling).astype(BF16).reshape(
        slot_count, latent_count, inner)
    pump(6)

    def attention_slot(j):
        for begin in range(0, inner, GROUP):
            stacked = spread_heads(query[j, :, begin:begin + GROUP], mask[...].astype(BF16))
            probs = softmax(matmul_right(stacked, key_value[j, :, begin:begin + GROUP])).astype(BF16)
            value = matmul(probs, key_value[j, :, inner + begin:inner + begin + GROUP])
            attended[j, :, begin:begin + GROUP] = pick_heads(value, mask[...], latent_count).astype(BF16)

    for part, (begin, size) in enumerate(parts):
        first, last = begin // latent_count, (begin + size) // latent_count
        pl.loop(first, last)(attention_slot)
        after[begin:begin + size] = latents_in[first:last].reshape(size, width).astype(F32) + matmul(
            attended[first:last].reshape(size, inner), output_all[...].reshape(inner, width))
        feed[begin:begin + size] = layer_norm(
            after[begin:begin + size], vectors[4:5], vectors[5:6]).astype(BF16)
        feed_rows.send(part)
        pump(7 + part)
    slots.drain(0, grad_down.at[0, 0])
    branch_rows.near(0)
    branch_rows.forward(0)

    def turn(source, target, owner):
        def body(at):
            target[pl.ds(at, 256), pl.ds(owner * rows, 2 * rows)] = source[
                pl.ds(owner * rows, 2 * rows), pl.ds(at, 256)].T

        tiles(width // 256, 256, body)

    turn(branch, branch_t, 0)
    branch_rows.far(0)
    tall = rows
    d_active, active, d_hidden = [pool.at[pl.ds(n * 4 * rows, 4 * rows)] for n in range(3)]

    def d_active_tile(at):
        d_active[pl.ds(at, tall)] = matmul_right(
            branch[pl.ds(at, tall)], down_all[...].reshape(hidden, width)).astype(BF16)

    tiles(4, tall, d_active_tile)
    turn(branch, branch_t, 2)

    def hidden_tile(at, begin):
        window = pl.ds(begin, chunk)
        weight = up_all[:, :, :, :, window].reshape(width, chunk)
        value, slope = gelu_parts(matmul(feed[pl.ds(at, tall)], weight))
        active[pl.ds(at, tall), window] = value.astype(BF16)
        d_hidden[pl.ds(at, tall), window] = (d_active[pl.ds(at, tall), window].astype(F32) * slope).astype(BF16)

    def d_feed_of(owner):
        return matmul_right(d_hidden[pl.ds(owner * rows, rows)], up_all[...].reshape(width, hidden))

    def after_feed_of(owner):
        return matmul(active[pl.ds(owner * rows, rows)], down_all[...].reshape(hidden, width))

    def rounded(buffer, owner, value):
        buffer[pl.ds(owner * rows, rows)] = value.astype(BF16)

    def across_tile(back, buffer):
        rounded(buffer, 2, totals[1] + back.lands[0].astype(F32))

    up_result, down_result, query_result, context_result, output_result = result
    reductions = []

    def send_off(tick):
        run(reductions, tick)

    def plane_reduction(own, lands_y, lands, finish):
        return Reduce(links, slots, own, ("y",), [lands_y], lands, finish)

    def keep_up(value, window):
        up_result[0, :, window] = jnp.where(x == 0, value[0], value[1])
        own_rows_send[:, window] = jnp.where(x == 0, value[1], value[0]).astype(BF16)

    feed_rows.near(0)
    feed_rows.near(1)
    slots.group = 6
    for c in range(chunks):
        begin = c * chunk
        window = pl.ds(begin, chunk)
        tiles(2, tall, lambda at, begin=begin: hidden_tile(at, begin))
        if c == 0:
            pump(9)
            turn(feed, feed_t, 0)
            feed_rows.forward(0)
            feed_rows.forward(1)
            feed_rows.far(0)
            feed_rows.far(1)
            turn(feed, feed_t, 2)
        tiles(2, tall, lambda at, begin=begin: hidden_tile(pl.multiple_of(2 * rows + at, tall), begin))
        if c == chunks - 1:
            for group in range(1, 4):
                slots.drain(group)
            slots.group = 4
            d_feed_back = Partials(links, slots, feed, d_feed_lands, rows)
            slots.group = 5
            after_back = Partials(links, slots, branch, after_lands, rows)
            slots.group = 6
            rounded(feed, 3, d_feed_of(3))
            d_feed_back.far.start()
            totals[1] = d_feed_of(2)
            d_feed_back.far.wait()
            across_tile(d_feed_back, feed)
            d_feed_back.across.start()

        def grad_tile(number, window=window, c=c):
            size = width // 2
            place = pl.multiple_of(number * size, size)
            up = matmul(feed_t[pl.ds(place, size)], d_hidden[:, window]).astype(BF16)
            grad_up[pl.ds(number * (length // 2), length // 2), :, :, :, window] = up.reshape(
                length // 2, 2, 2, size // (2 * length), chunk)
            down = matmul(branch_t[pl.ds(place, size)], active[:, window]).astype(BF16)
            for owner in range(2):
                grad_down[c, owner, pl.ds(place, size)] = down[:, owner * unit:(owner + 1) * unit]

        pl.loop(0, 2)(grad_tile)
        reductions.append((plane_reduction(
            lambda zi, yi, xi, window=window: grad_up.at[zi, yi, ALL, :, window],
            lands_b[0].at[:, :, :, window], lands_z[0].at[:, :, :, window],
            functools.partial(keep_up, window=window)), (c, c + 2, c + 4)))
        if c == 0:
            pump(10)
        if c == chunks - 2:
            pump(11)
        send_off(c)
    part_size = width // chunks
    for number in range(chunks):
        window = pl.ds(number * part_size, part_size)

        def keep_down(value, window=window):
            down_result[:, window] = value.T

        reductions.append((plane_reduction(
            lambda zi, yi, xi, window=window: grad_down.at[zi, yi, window],
            lands_b[1].at[:, window], lands_z[1].at[:, window], keep_down),
            (chunks, chunks + 2 + number, chunks + 4 + number)))
    send_off(4)
    rounded(feed, 1, d_feed_of(1))
    d_feed_back.near.start()
    totals[0] = d_feed_of(0)

    rounded(branch, 3, after_feed_of(3))
    after_back.far.start()
    totals[1] = after_feed_of(2)
    after_back.far.wait()
    across_tile(after_back, branch)
    send_off(5)
    rounded(branch, 1, after_feed_of(1))
    after_back.near.start()
    d_feed_back.near.wait()
    d_feed_back.across.wait()
    after_back.across.start()
    slots.drain(4)

    def fold(terms):
        return jnp.sum(terms.reshape(-1, 8, width), axis=0)

    d_feed = totals.at[0]
    flat_grad = lambda at, size: grad_in[pl.ds(lax.div(at, latent_count), size // latent_count)].reshape(size, width)

    def middle_tile(at, size=latent_count):
        own = pl.ds(at, size)
        upstream = d_feed[own] + d_feed_lands[1, own].astype(F32) + d_feed_lands[2, own].astype(F32)
        d_norm, gain_terms = layer_norm_back(after[own], vectors[4:5], upstream)
        sums[4] = sums[4] + fold(gain_terms)
        sums[5] = sums[5] + fold(upstream)
        row = lax.broadcasted_iota(jnp.int32, (size, 1), 0) + at
        keep = jnp.where(row < counts[0] * latent_count, 1.0, 0.0)
        d_middle = flat_grad(at, size).astype(F32) * keep + d_norm
        d_feed[own] = d_middle
        feed[own] = d_middle.astype(BF16)

    tiles(slot_count, latent_count, middle_tile)
    send_off(6)
    after[...] = after[...] + after_feed_of(0)

    context_rows, output_rows = context_all.shape[-2], output_all.shape[-2]

    def context_own(zi, yi, xi, half):
        return up_all.at[zi, yi, xi, pl.ds(pl.multiple_of(half * context_rows, 16), context_rows)]

    def query_own(zi, yi, xi, half):
        return grad_query.at[zi, yi, xi, half]

    def output_own(zi, yi, xi, half):
        return grad_output.at[zi, yi, xi, half]

    def to_sibling(own, land):
        move = slots.move(links.device("core"), own(ALL, ALL, ALL, 1 - rep), land, land)
        move.start()

        def settle():
            move.wait()
            add_into(own(ALL, ALL, ALL, rep), land)

        return settle

    def halved_reduction(own, number, target, begin, size, *ticks):
        made = []
        for which, order in enumerate((("y", "x"), ("x", "y"))):
            window = pl.ds(begin + which * (size // 2), size // 2)

            def finish(value, window=window):
                target[:, window] = value

            made.append((Reduce(
                links, slots, lambda zi, yi, xi, window=window: own(zi, yi, xi, rep).at[..., window], order,
                [lands_b[number].at[:, :, :, window], lands_a[number].at[:, :, window]],
                lands_z[number].at[:, :, window], finish), ticks))
        return made

    d_branch = feed.at[pl.ds(0, rows)]
    output_block = inner // 2

    def output_grad_tile(number):
        place = pl.multiple_of(number * output_block, output_block)
        turned = attended[:, :, pl.ds(place, output_block)].reshape(rows, output_block).T
        value = matmul(turned, d_branch[...]).astype(BF16)
        grad_output[pl.ds(number * (length // 2), length // 2)] = value.reshape(
            length // 2, 2, 2, 2, output_rows, width)

    pl.loop(0, 2)(output_grad_tile)
    settle_output = to_sibling(output_own, lands_c[2])
    d_attended, d_query = upstream_rows[0], upstream_rows[1]
    d_attended[...] = matmul_right(d_branch[...], output_all[...].reshape(inner, width)).astype(BF16)
    send_off(7)

    def attention_back_slot(j):
        own = pl.ds(pl.multiple_of(j * latent_count, latent_count), latent_count)
        for begin in range(0, inner, GROUP):
            keys = key_value[j, :, begin:begin + GROUP]
            values = key_value[j, :, inner + begin:inner + begin + GROUP]
            low_mask = mask[...].astype(BF16)
            stacked = spread_heads(query[j, :, begin:begin + GROUP], low_mask)
            upstream = spread_heads(d_attended[own, begin:begin + GROUP], low_mask)
            probs = softmax(matmul_right(stacked, keys))
            d_probs = matmul_right(upstream, values)
            d_scores = (probs * (d_probs - jnp.sum(probs * d_probs, axis=-1, keepdims=True))).astype(BF16)
            d_query[own, begin:begin + GROUP] = (
                pick_heads(matmul(d_scores, keys), mask[...], latent_count).astype(BF16).astype(F32) * scaling
            ).astype(BF16)
            at = pl.ds(pl.multiple_of(j * key_count, 16), key_count)
            pool[at, begin:begin + GROUP] = matmul_left(d_scores, stacked).astype(BF16)
            pool[at, inner + begin:inner + begin + GROUP] = matmul_left(probs.astype(BF16), upstream).astype(BF16)

    pl.loop(0, 3)(attention_back_slot)
    settle_output()
    reductions.extend(halved_reduction(output_own, 4, output_result, 0, width, 8, 9, 10, 11))
    send_off(8)
    pl.loop(3, slot_count)(attention_back_slot)
    send_off(9)
    block = width // length

    def query_grad_tile(zi):
        place = pl.multiple_of(zi * block, block)
        turned = context[:, patches:, pl.ds(place, block)].reshape(rows, block).T
        value = matmul(turned, d_query[...]).astype(BF16)
        grad_query[zi] = value.reshape(2, 2, 2, context_rows, inner)

    pl.loop(0, length)(query_grad_tile)
    settle_query = to_sibling(query_own, lands_c[0])

    def context_grad_tile(zi):
        place = pl.multiple_of(zi * block, block)
        value = None
        for j in range(slot_count):
            turned = context[j, :, pl.ds(place, block)].T
            term = matmul(turned, pool[j * key_count:(j + 1) * key_count])
            value = term if value is None else value + term
        up_all[zi] = value.astype(BF16).reshape(2, 2, block // 4, 2 * inner)

    pl.loop(0, length)(context_grad_tile)
    settle_context = to_sibling(context_own, lands_c[1])
    settle_query()
    reductions.extend(halved_reduction(query_own, 2, query_result, 0, inner, 10, 11, 12, 13))
    settle_context()
    reductions.extend(halved_reduction(context_own, 3, context_result, 0, inner, 10, 11, 12, 13))
    reductions.extend(halved_reduction(context_own, 3, context_result, inner, inner, 10, 12, 13, 14))
    send_off(10)
    slots.group = 7
    own_rows_move = slots.move(links.device("x"), own_rows_send, own_rows_land, own_rows_land)
    own_rows_move.start()
    after_back.near.wait()
    after_back.across.wait()
    slots.drain(5)
    branch[:rows] = ((after[...] + after_lands[1].astype(F32) + after_lands[2].astype(F32)) * kept).astype(BF16)
    written = [locals_.fill(
        [(branch.at[pl.ds(j * latent_count, latent_count)], latents_out.at[j]) for j in range(slot_count)], latents_out)]

    context_up = totals.at[1]

    def input_slot(j):
        at = pl.ds(pl.multiple_of(j * key_count, 16), key_count)
        own = pl.ds(pl.multiple_of(j * latent_count, latent_count), latent_count)
        context_up[...] = matmul_right(pool[at], context_all[...].reshape(width, 2 * inner))
        context_up[patches:] = context_up[patches:] + matmul_right(d_query[own], query_all[...].reshape(width, inner))

        def media_tile(at, size=patches // 2):
            tile = pl.ds(at, size)
            upstream = context_up[tile]
            value, gain_terms = layer_norm_back(media_in[j, tile].astype(F32), vectors[0:1], upstream)
            sums[0] = sums[0] + fold(gain_terms)
            sums[1] = sums[1] + fold(upstream)
            media_in[j, tile] = value.astype(BF16)

        tiles(2, patches // 2, media_tile)
        upstream = context_up[patches:]
        value, gain_terms = layer_norm_back(latents_in[j].astype(F32), vectors[2:3], upstream)
        sums[2] = sums[2] + fold(gain_terms)
        sums[3] = sums[3] + fold(upstream)
        latents_in[j] = (d_feed[own] + value).astype(BF16)

    pl.loop(0, 2)(input_slot)
    send_off(11)
    pl.loop(2, 3)(input_slot)
    send_off(12)
    own_rows_move.wait()
    up_result[1] = own_rows_land[...].astype(F32)

    def hand_over(numbers):
        for number in numbers:
            value, out = result[number], grads_out[number]
            written.append(locals_.copy(value, out.at[rep]))
            written.append(slots.move(links.device("core"), value, out.at[rep], out.at[1 - rep]))
            written[-1].start()

    hand_over((0, 1))
    pl.loop(3, slot_count)(input_slot)
    written.append(locals_.copy(media_in, media_grad_out))
    written.append(locals_.copy(latents_in, latents_grad_out))
    for number in range(6):
        total[number:number + 1] = jnp.sum(sums[number], axis=0, keepdims=True)
    total[6:] = jnp.zeros_like(total[6:])
    vector_sum = VectorSum(links, slots, total, total_stage, total_lands)
    vector_sum.step(0)
    send_off(13)
    vector_sum.step(1)
    hand_over((2, 4))
    vector_sum.step(2)
    send_off(14)
    hand_over((3,))
    vector_sum.step(3)
    vector_sum.step(4)
    sums_out[...] = total[...]
    for copy in written:
        copy.wait()
    slots.drain(6)
    slots.drain(7)


def layer(length, counts, media, latents, grad_out, packed, shards):
    query_shard, context_shard, output_shard, up_shard, down_shard = shards
    slot_count, patches, width = media.shape
    latent_count = latents.shape[1]
    key_count = patches + latent_count
    rows = slot_count * latent_count
    inner = query_shard.shape[1]
    unit = down_shard.shape[0] // 2
    hidden = up_shard.shape[1] // 4
    blocks = (length, 2, 2)

    def halved(shard):
        return blocks + (2, shard.shape[0] // 2, shard.shape[1])

    up_shape = blocks + (up_shard.shape[0], hidden)
    down_shape = (length, 2, unit, width)
    halves = [halved(s)[4:] for s in shards[:3]]
    results = [(2,) + up_shape[3:], (unit, width)] + halves
    anywhere = pl.BlockSpec(memory_space=pl.ANY)
    vmem = pl.BlockSpec(memory_space=pltpu.VMEM)
    sums_shape = (8, width)
    scratch = [
        pltpu.VMEM(halved(query_shard), BF16),
        pltpu.VMEM(halved(context_shard), BF16),
        pltpu.VMEM(halved(output_shard), BF16),
        pltpu.VMEM(up_shape, BF16),
        pltpu.VMEM(up_shape[3:], BF16),
        pltpu.VMEM(down_shape, BF16),
        pltpu.VMEM(blocks + packed.shape, BF16),
        pltpu.VMEM((8, width), F32),
        pltpu.VMEM(media.shape, BF16),
        pltpu.VMEM(latents.shape, BF16),
        pltpu.VMEM(grad_out.shape, BF16),
        pltpu.VMEM((slot_count, key_count, width), BF16),
        pltpu.VMEM((slot_count, key_count, 2 * inner), BF16),
        pltpu.VMEM((slot_count, latent_count, inner), BF16),
        pltpu.VMEM((slot_count, latent_count, inner), BF16),
        pltpu.VMEM((rows, width), F32),
        pltpu.VMEM((4 * rows, width), BF16),
        pltpu.VMEM((width, 4 * rows), BF16),
        pltpu.VMEM((4 * rows, width), BF16),
        pltpu.VMEM((width, 4 * rows), BF16),
        pltpu.VMEM((max(12 * rows, slot_count * key_count), hidden), BF16),
        pltpu.VMEM((2, rows, width), F32),
        pltpu.VMEM((3, rows, width), BF16),
        pltpu.VMEM((3, rows, width), BF16),
        [pltpu.VMEM((rows, inner), BF16)] * 2,
        pltpu.VMEM(up_shape, BF16),
        pltpu.VMEM((length, 2, width, unit), BF16),
        pltpu.VMEM(halved(query_shard), BF16),
        pltpu.VMEM(halved(output_shard), BF16),
        pltpu.VMEM((latent_count * (GROUP // HEAD_DIM), GROUP), F32),
        pltpu.VMEM((6, 8, width), F32),
        pltpu.VMEM(sums_shape, F32),
        pltpu.VMEM((4,) + sums_shape, F32),
        pltpu.VMEM((2 + length,) + sums_shape, F32),
        pltpu.VMEM(up_shape[3:], BF16),
        pltpu.VMEM(up_shape[3:], BF16),
        [pltpu.VMEM(blocks + h, BF16) for h in halves],
        [pltpu.VMEM((length, 2) + up_shape[3:], BF16), pltpu.VMEM((length, width, unit), BF16)]
        + [pltpu.VMEM((length, 2) + h, BF16) for h in halves],
        [None, None] + [pltpu.VMEM((length,) + h, BF16) for h in halves],
        [pltpu.VMEM((length - 1, 2) + up_shape[3:], BF16), pltpu.VMEM((length - 1, width, unit), BF16)]
        + [pltpu.VMEM((length - 1,) + h, BF16) for h in halves],
        [pltpu.VMEM(r, F32) for r in results],
        pltpu.SemaphoreType.DMA((8,)),
        pltpu.SemaphoreType.DMA((112,)),
        pltpu.SemaphoreType.DMA((24,)),
    ]
    out_shape = (
        jax.ShapeDtypeStruct(latents.shape, BF16), jax.ShapeDtypeStruct(media.shape, BF16),
        jax.ShapeDtypeStruct(latents.shape, BF16), jax.ShapeDtypeStruct(sums_shape, F32),
        [jax.ShapeDtypeStruct((2,) + r, F32) for r in results])
    return pl.pallas_call(
        functools.partial(layer_kernel, length, HEAD_DIM ** (-0.5)),
        out_shape=out_shape,
        in_specs=[pl.BlockSpec(memory_space=pltpu.SMEM)] + [anywhere] * 9,
        out_specs=(anywhere, anywhere, anywhere, vmem, [anywhere] * 5),
        scratch_shapes=scratch,
        compiler_params=pltpu.CompilerParams(
            collective_id=0, has_side_effects=True, vmem_limit_bytes=63 * 2 ** 20),
        name="resampler_layer",
    )(counts, media, latents, grad_out, packed, query_shard, context_shard, output_shard, up_shard, down_shard)


def head_scores(first_heads, second_heads):
    return jnp.einsum(
        "bqhd,bkhd->bhqk", first_heads, second_heads, preferred_element_type=jnp.float32
    )


def collective_body(
    media,
    latents,
    image_counts,
    grad_out,
    media_gain,
    media_bias,
    latent_gain,
    latent_bias,
    feed_gain,
    feed_bias,
    query_weight,
    context_weight,
    output_weight,
    up_weight,
    down_weight,
):
    samples, slots, patches, model_width = media.shape
    latent_count = latents.shape[2]
    inner_width = query_weight.shape[1]
    head_count = inner_width // HEAD_DIM
    blocks = samples * slots
    key_count = patches + latent_count
    latent_total = blocks * latent_count
    scaling = HEAD_DIM ** (-0.5)
    vector_shards = (media_gain, media_bias, latent_gain, latent_bias, feed_gain, feed_bias)
    weight_shards = (query_weight, context_weight, output_weight, up_weight, down_weight)
    gathered = tuple(lax.all_gather(s, "dp", axis=0, tiled=True) for s in vector_shards + weight_shards)
    vectors = [element.astype(jnp.float32) for element in gathered[:6]]
    media_rows = media.reshape(blocks * patches, model_width).astype(jnp.float32)
    latent_rows = latents.reshape(latent_total, model_width).astype(jnp.float32)
    media_normed = layer_norm(media_rows, vectors[0], vectors[1]).astype(jnp.bfloat16)
    latent_normed = layer_norm(latent_rows, vectors[2], vectors[3]).astype(jnp.bfloat16)
    queries = (matmul(latent_normed, gathered[6]) * scaling).astype(jnp.bfloat16)
    context = jnp.concatenate(
        [
            media_normed.reshape(blocks, patches, model_width),
            latent_normed.reshape(blocks, latent_count, model_width),
        ],
        axis=1,
    ).reshape(blocks * key_count, model_width)
    key_value = (
        matmul(context, gathered[7])
        .astype(jnp.bfloat16)
        .reshape(blocks, key_count, 2 * inner_width)
    )
    query_heads = queries.reshape(blocks, latent_count, head_count, HEAD_DIM)
    key_heads = key_value[:, :, :inner_width].reshape(blocks, key_count, head_count, HEAD_DIM)
    value_heads = key_value[:, :, inner_width:].reshape(blocks, key_count, head_count, HEAD_DIM)
    scores = head_scores(query_heads, key_heads)
    row_max = jnp.max(scores, axis=-1, keepdims=True)
    exponent = jnp.exp(scores - row_max)
    row_total = jnp.sum(exponent, axis=-1, keepdims=True)
    log_total = row_max + jnp.log(row_total)
    attention_weights = (exponent / row_total).astype(jnp.bfloat16)
    attended = (
        jnp.einsum(
            "bhqk,bkhd->bqhd", attention_weights, value_heads, preferred_element_type=jnp.float32
        )
        .astype(jnp.bfloat16)
        .reshape(latent_total, inner_width)
    )
    after_attention = latent_rows + matmul(attended, gathered[8])
    feed_input = layer_norm(after_attention, vectors[4], vectors[5]).astype(jnp.bfloat16)
    hidden = matmul(feed_input, gathered[9])
    activated = gelu_exact(hidden).astype(jnp.bfloat16)
    after_feed = after_attention + matmul(activated, gathered[10])
    slot_mask = (
        lax.broadcasted_iota(jnp.int32, (samples, slots), 1) < image_counts[:, None]
    ).astype(jnp.float32)
    row_mask = jnp.broadcast_to(slot_mask[:, :, None], (samples, slots, latent_count)).reshape(
        latent_total, 1
    )
    latents_out = (after_feed * row_mask).astype(jnp.bfloat16).reshape(latents.shape)
    backward_set = gathered
    back_vectors = [element.astype(jnp.float32) for element in backward_set[:6]]
    d_after = grad_out.reshape(latent_total, model_width).astype(jnp.float32) * row_mask
    d_branch = d_after.astype(jnp.bfloat16)
    grad_down = matmul_left(activated, d_branch)
    d_activated = matmul_right(d_branch, backward_set[10])
    d_hidden = jax.vjp(gelu_exact, hidden)[1](d_activated)[0].astype(jnp.bfloat16)
    grad_up = matmul_left(feed_input, d_hidden)
    d_feed = matmul_right(d_hidden, backward_set[9])
    d_feed_norm, grad_feed_gain, grad_feed_bias = jax.vjp(
        layer_norm, after_attention, back_vectors[4], back_vectors[5]
    )[1](d_feed)
    d_middle = d_after + d_feed_norm
    d_out_branch = d_middle.astype(jnp.bfloat16)
    grad_output = matmul_left(attended, d_out_branch)
    d_attended = (
        matmul_right(d_out_branch, backward_set[8])
        .astype(jnp.bfloat16)
        .reshape(blocks, latent_count, head_count, HEAD_DIM)
    )
    recomputed = jnp.exp(head_scores(query_heads, key_heads) - log_total)
    d_weights = head_scores(d_attended, value_heads)
    d_scores = (
        recomputed * (d_weights - jnp.sum(recomputed * d_weights, axis=-1, keepdims=True))
    ).astype(jnp.bfloat16)
    d_queries = (
        jnp.einsum(
            "bhqk,bkhd->bqhd", d_scores, key_heads, preferred_element_type=jnp.float32
        ).astype(jnp.bfloat16)
        * scaling
    ).reshape(latent_total, inner_width)
    d_keys = jnp.einsum(
        "bhqk,bqhd->bkhd", d_scores, query_heads, preferred_element_type=jnp.float32
    ).astype(jnp.bfloat16)
    d_values = jnp.einsum(
        "bhqk,bqhd->bkhd",
        recomputed.astype(jnp.bfloat16),
        d_attended,
        preferred_element_type=jnp.float32,
    ).astype(jnp.bfloat16)
    d_key_value = jnp.concatenate(
        [
            d_keys.reshape(blocks, key_count, inner_width),
            d_values.reshape(blocks, key_count, inner_width),
        ],
        axis=-1,
    ).reshape(blocks * key_count, 2 * inner_width)
    grad_query = matmul_left(latent_normed, d_queries)
    grad_context = matmul_left(context, d_key_value)
    d_context = matmul_right(d_key_value, backward_set[7]).reshape(blocks, key_count, model_width)
    d_latent_normed = matmul_right(d_queries, backward_set[6]) + d_context[:, patches:, :].reshape(
        latent_total, model_width
    )
    d_media_normed = d_context[:, :patches, :].reshape(blocks * patches, model_width)
    d_latent_norm, grad_latent_gain, grad_latent_bias = jax.vjp(
        layer_norm, latent_rows, back_vectors[2], back_vectors[3]
    )[1](d_latent_normed)
    grad_latents = (d_middle + d_latent_norm).astype(jnp.bfloat16).reshape(latents.shape)
    d_media, grad_media_gain, grad_media_bias = jax.vjp(
        layer_norm, media_rows, back_vectors[0], back_vectors[1]
    )[1](d_media_normed)
    grad_media = d_media.astype(jnp.bfloat16).reshape(media.shape)
    vector_grads = jnp.stack([
        grad_media_gain, grad_media_bias, grad_latent_gain, grad_latent_bias, grad_feed_gain, grad_feed_bias])
    weight_grads = [
        g.astype(jnp.bfloat16) for g in (grad_query, grad_context, grad_output, grad_up, grad_down)]
    vector_sums = lax.psum_scatter(vector_grads, "dp", scatter_dimension=1, tiled=True)
    summed = [lax.psum_scatter(g, "dp", scatter_dimension=0, tiled=True) for g in weight_grads]
    owned = tuple(lax.psum(vector_sums, "rep")) + tuple(
        lax.psum(s, "rep").astype(jnp.float32) for s in summed)
    return (
        latents_out,
        grad_media,
        grad_latents,
        owned[0],
        owned[1],
        owned[2],
        owned[3],
        owned[4],
        owned[5],
        owned[6],
        owned[7],
        owned[8],
        owned[9],
        owned[10],
    )


def body(media, latents, image_counts, grad_out, *parameters):
    chips = lax.axis_size("dp")
    weight_shards = parameters[6:]
    tiled = (media.shape[0] == 1 and chips % 4 == 0 and chips > 4 and parameters[0].shape[0] == 64
             and all(s.shape[0] % 32 == 0 for s in weight_shards))
    if not tiled:
        return collective_body(media, latents, image_counts, grad_out, *parameters)
    side = lax.rem(lax.axis_index("dp"), 2)
    stacked = jnp.stack(parameters[:6])
    packed = jnp.pad(
        jnp.concatenate([jnp.where(side == 0, stacked, 0), jnp.where(side == 0, 0, stacked)], axis=1), ((0, 10), (0, 0)))
    latents_out, grad_media, grad_latents, vector_sums, summed = layer(
        chips // 4, image_counts, media[0], latents[0], grad_out[0], packed, weight_shards)
    sums = [s.reshape(-1, s.shape[-1]) for s in summed[2:]]
    rows, hidden = summed[0].shape[2:]
    unit = summed[1].shape[1]
    planes = jnp.where(lax.rem(lax.axis_index("dp"), 2) == 0, summed[0], summed[0][:, ::-1])
    sums.append(planes.reshape(2, 2, rows, hidden // unit, unit).transpose(2, 3, 1, 0, 4).reshape(rows, 4 * hidden))
    sums.append(summed[1].reshape(-1, summed[1].shape[-1]))
    width = parameters[0].shape[0]
    mine = lax.dynamic_slice(vector_sums, (0, lax.axis_index("dp") * width), (6, width))
    return (latents_out[None], grad_media[None], grad_latents[None]) + tuple(mine) + tuple(sums)


def solution(mesh):
    return jax.shard_map(
        body,
        mesh=mesh,
        in_specs=(
            P(("dp", "rep"), None, None, None),
            P(("dp", "rep"), None, None, None),
            P(("dp", "rep")),
            P(("dp", "rep"), None, None, None),
            P("dp"),
            P("dp"),
            P("dp"),
            P("dp"),
            P("dp"),
            P("dp"),
            P("dp", None),
            P("dp", None),
            P("dp", None),
            P("dp", None),
            P("dp", None),
        ),
        out_specs=(
            P(("dp", "rep"), None, None, None),
            P(("dp", "rep"), None, None, None),
            P(("dp", "rep"), None, None, None),
            P("dp"),
            P("dp"),
            P("dp"),
            P("dp"),
            P("dp"),
            P("dp"),
            P("dp", None),
            P("dp", None),
            P("dp", None),
            P("dp", None),
            P("dp", None),
        ),
        check_vma=False,
    )
```

```python
import functools

import jax
import jax.numpy as jnp
from jax import lax
from jax.experimental import pallas as pl
from jax.experimental.pallas import tpu as pltpu
from jax.sharding import PartitionSpec as P

HEAD_DIM = 64
GROUP = 256

epsilon = 1e-05

MESH = pl.DeviceIdType.MESH
ALL = slice(None)
F32 = jnp.float32
BF16 = jnp.bfloat16


class Links:
    def __init__(self, length):
        self.length = length
        self.dp = lax.axis_index("dp")
        self.rep = lax.axis_index("rep")
        self.z = lax.div(self.dp, 4)
        self.y = lax.rem(lax.div(self.dp, 2), 2)
        self.x = lax.rem(self.dp, 2)

    def device(self, axis, way=0):
        if axis == "core":
            return (self.dp, 1 - self.rep)
        if axis == "x":
            return (self.dp + 1 - 2 * self.x, self.rep)
        if axis == "y":
            return (self.dp + 2 - 4 * self.y, self.rep)
        return (self.dp + 4 * (self.along(way) - self.z), self.rep)

    def along(self, way):
        return lax.rem(self.z + way + self.length, self.length)

    def greet(self):
        barrier = pltpu.get_barrier_semaphore()
        peers = [("core", 0), ("x", 0), ("y", 0)] + [("z", way) for way in range(1, self.length)]
        for axis, way in peers:
            pl.semaphore_signal(barrier, inc=1, device_id=self.device(axis, way), device_id_type=MESH)
        pl.semaphore_wait(barrier, len(peers))


class Move:
    def __init__(self, slots, copies, landing):
        send, recv = slots.send.at[slots.group], slots.recv.at[slots.made]
        slots.made += 1
        self.slots, self.group, self.copies = slots, slots.group, [
            pltpu.make_async_remote_copy(
                src_ref=source, dst_ref=target, send_sem=send, recv_sem=recv,
                device_id=device, device_id_type=MESH)
            for device, source, target in copies]
        self.bytes = 0
        for _, source, _ in copies:
            size = jnp.dtype(source.dtype).itemsize
            for extent in source.shape:
                size *= extent
            self.bytes += size
        self.into = pltpu.make_async_remote_copy(
            src_ref=landing, dst_ref=landing, send_sem=send, recv_sem=recv,
            device_id=copies[0][0], device_id_type=MESH)

    def start(self):
        for copy in self.copies:
            copy.start()
        self.slots.sent[self.group] += self.bytes

    def wait(self):
        self.into.wait_recv()


class Slots:
    def __init__(self, send, recv, ruler):
        self.send, self.recv, self.ruler, self.made, self.group = send, recv, ruler, 0, 0
        self.sent = [0] * send.shape[0]

    def move(self, device, source, target, landing):
        return Move(self, [(device, source, target)], landing)

    def drain(self, group, ruler=None):
        ruler = self.ruler if ruler is None else ruler
        row = ruler.shape[-1] * jnp.dtype(ruler.dtype).itemsize
        rows, rest = divmod(self.sent[group], row)
        assert rest == 0 and rows % 16 == 0 and rows <= ruler.shape[0]
        whole = ruler.at[pl.ds(0, rows)]
        pltpu.make_async_copy(whole, whole, self.send.at[group]).wait()


class Locals:
    def __init__(self, semaphores):
        self.semaphores, self.made = semaphores, 0

    def copy(self, source, target):
        return self.fill([(source, target)], target)

    def fill(self, copies, whole):
        semaphore = self.semaphores.at[self.made]
        self.made += 1
        for source, target in copies:
            pltpu.make_async_copy(source, target, semaphore).start()
        return pltpu.make_async_copy(whole, whole, semaphore)


class Gather:
    def __init__(self, links, slots, view, axes, halved):
        here = {"z": links.z, "y": links.y, "x": links.x}
        self.moves = []
        for axis in axes:
            mine = view(here["z"], here["y"], here["x"])
            if axis == "z":
                self.moves.append(Move(
                    slots, [(links.device("z", way), mine, mine) for way in range(1, links.length)],
                    view(pl.ds(0, links.length - 1), here["y"], here["x"])))
            else:
                other = dict(here)
                other[axis] = 1 - here[axis]
                self.moves.append(
                    slots.move(links.device(axis), mine, mine, view(other["z"], other["y"], other["x"])))
            here[axis] = ALL
        if halved:
            mine = view(ALL, ALL, ALL)
            self.moves.append(
                slots.move(links.device("core"), mine, mine, view(ALL, ALL, ALL, 1 - links.rep)))

    def step(self, number):
        if 0 < number <= len(self.moves):
            self.moves[number - 1].wait()
        if 0 <= number < len(self.moves):
            self.moves[number].start()


class Reduce:
    def __init__(self, links, slots, own, axes, lands, lands_z, finish):
        self.own, self.links, self.finish, self.lands_z = own, links, finish, lands_z
        self.moves, self.adds = [], []
        z, y, x = links.z, links.y, links.x
        here = {"z": ALL, "y": ALL, "x": ALL}
        for axis, land in zip(axes, lands):
            away, home = dict(here), dict(here)
            place = {"y": y, "x": x}[axis]
            away[axis], home[axis] = 1 - place, place
            self.moves.append(slots.move(
                links.device(axis), own(away["z"], away["y"], away["x"]), land, land))
            here = home
            self.adds.append(functools.partial(add_into, own(home["z"], home["y"], home["x"]), land))
        self.moves.append(Move(
            slots, [(links.device("z", way), own(links.along(way), here["y"], here["x"]), lands_z.at[way - 1])
                    for way in range(1, links.length)], lands_z))
        self.mine = own(z, here["y"], here["x"])
        self.adds.append(self.end)

    def step(self, number):
        if 0 < number <= len(self.moves):
            self.moves[number - 1].wait()
            self.adds[number - 1]()
        if 0 <= number < len(self.moves):
            self.moves[number].start()

    def end(self):
        total = self.mine[...].astype(F32)
        for way in range(1, self.links.length):
            total = total + self.lands_z[way - 1].astype(F32)
        self.finish(total)


def add_into(target, arrived):
    @pl.loop(0, target.shape[0])
    def _(number):
        target[number] = (target[number].astype(F32) + arrived[number].astype(F32)).astype(target.dtype)


def run(table, tick):
    for item, ticks in table:
        if tick in ticks:
            item.step(ticks.index(tick))


def matmul(left, right):
    return jnp.dot(left, right, preferred_element_type=F32)


def matmul_left(left, right):
    return lax.dot_general(left, right, (((0,), (0,)), ((), ())), preferred_element_type=F32)


def matmul_right(left, right):
    return lax.dot_general(left, right, (((1,), (1,)), ((), ())), preferred_element_type=F32)


def layer_norm(values, gain, offset):
    centre = jnp.mean(values, axis=-1, keepdims=True)
    shifted = values - centre
    spread = jnp.mean(shifted * shifted, axis=-1, keepdims=True)
    return shifted * lax.rsqrt(spread + epsilon) * gain + offset


def layer_norm_back(values, gain, upstream):
    centre = jnp.mean(values, axis=-1, keepdims=True)
    shifted = values - centre
    spread = jnp.mean(shifted * shifted, axis=-1, keepdims=True)
    rate = lax.rsqrt(spread + epsilon)
    normed = shifted * rate
    scaled = upstream * gain
    first = jnp.mean(scaled, axis=-1, keepdims=True)
    second = jnp.mean(scaled * normed, axis=-1, keepdims=True)
    return rate * (scaled - first - normed * second), upstream * normed


def gelu_exact(values):
    return 0.5 * values * (1.0 + jax.scipy.special.erf(values * 0.7071067811865476))


def gelu_parts(values):
    cumulative = 0.5 * (1.0 + lax.erf(values * 0.7071067811865476))
    density = 0.3989422804014327 * jnp.exp(-0.5 * values * values)
    return values * cumulative, cumulative + values * density


def tiles(count, size, action):
    @pl.loop(0, count)
    def _(number):
        action(pl.multiple_of(number * size, size))


def head_mask(rows, columns):
    heads = columns // HEAD_DIM
    row = lax.broadcasted_iota(jnp.int32, (rows * heads, columns), 0)
    column = lax.broadcasted_iota(jnp.int32, (rows * heads, columns), 1)
    head_row = jnp.zeros_like(row)
    head_column = jnp.zeros_like(row)
    for head in range(1, heads):
        head_row = head_row + jnp.where(row >= head * rows, 1, 0)
        head_column = head_column + jnp.where(column >= head * HEAD_DIM, 1, 0)
    return jnp.where(head_row == head_column, 1.0, 0.0)


def spread_heads(rows, mask):
    return jnp.concatenate([rows] * (mask.shape[0] // rows.shape[0]), axis=0) * mask


def pick_heads(stacked, mask, rows):
    kept = stacked * mask
    total = kept[:rows]
    for head in range(1, stacked.shape[0] // rows):
        total = total + kept[head * rows:(head + 1) * rows]
    return total


def softmax(scores):
    exponent = jnp.exp(scores - jnp.max(scores, axis=-1, keepdims=True))
    return exponent / jnp.sum(exponent, axis=-1, keepdims=True)


class VectorSum:
    def __init__(self, links, slots, total, stage, lands):
        self.total, self.stage, self.lands, self.length = total, stage, lands, links.length
        self.moves = [slots.move(links.device(axis), stage.at[number], lands.at[number], lands.at[number])
                      for number, axis in enumerate(("core", "x", "y"))]
        self.moves.append(Move(
            slots, [(links.device("z", way), stage.at[3], lands.at[2 + way]) for way in range(1, links.length)],
            lands.at[pl.ds(3, links.length - 1)]))

    def step(self, number):
        if 0 < number <= 4:
            self.moves[number - 1].wait()
            for land in ([number - 1] if number < 4 else range(3, 2 + self.length)):
                self.total[...] = self.total[...] + self.lands[land]
        if number < 4:
            self.stage[number] = self.total[...]
            self.moves[number].start()


class Rows:
    def __init__(self, links, slots, buffer, count, parts):
        self.moves, self.passed = [], []
        for begin, size in parts:
            def place(owner, begin=begin, size=size):
                return buffer.at[pl.ds(owner * count + begin, size)]

            self.moves.append([
                slots.move(links.device("x"), place(0), place(2), place(2)),
                slots.move(links.device("core"), place(0), place(1), place(1))])
            self.passed.append(slots.move(links.device("core"), place(2), place(3), place(3)))

    def send(self, part):
        for move in self.moves[part]:
            move.start()

    def near(self, part):
        self.moves[part][1].wait()

    def forward(self, part):
        self.moves[part][0].wait()
        self.passed[part].start()

    def far(self, part):
        self.passed[part].wait()


class Partials:
    def __init__(self, links, slots, stage, lands, count):
        def place(owner):
            return stage.at[pl.ds(owner * count, count)]

        self.place, self.lands = place, lands
        self.far = slots.move(links.device("core"), place(3), lands.at[0], lands.at[0])
        self.near = slots.move(links.device("core"), place(1), lands.at[1], lands.at[1])
        self.across = slots.move(links.device("x"), place(2), lands.at[2], lands.at[2])


def layer_kernel(length, scaling, counts, media, latents, grad_out, packed, query_shard, context_shard,
                 output_shard, up_shard, down_shard, latents_out, media_grad_out, latents_grad_out, sums_out, grads_out,
                 query_all, context_all, output_all, up_all, up_stage, down_all,
                 packed_all, vectors, media_in, latents_in, grad_in, context, key_value, query, attended, after,
                 feed, feed_t, branch, branch_t, pool, totals, after_lands, d_feed_lands, upstream_rows,
                 grad_up, grad_down, grad_query, grad_output, mask, sums, total, total_stage, total_lands,
                 own_rows_send, own_rows_land, lands_c, lands_b, lands_a, lands_z, result, send, recv, local):
    links = Links(length)
    z, y, x, rep = links.z, links.y, links.x, links.rep
    slots, locals_ = Slots(send, recv, pool), Locals(local)
    slot_count, patches, width = media.shape
    latent_count = latents.shape[1]
    key_count = patches + latent_count
    rows = slot_count * latent_count
    inner = query.shape[-1]
    chunks = length
    hidden = up_all.shape[-1]
    chunk = hidden // chunks
    unit = down_all.shape[-2]
    xy, yx = ("z", "x", "y"), ("z", "y", "x")

    def unit_columns(half, number):
        return pl.ds(pl.multiple_of(((2 * number + half) * 2 + rep) * unit, unit), unit)

    staged = [locals_.copy(packed, packed_all.at[z, y, x])]
    for shard, whole in ((context_shard, context_all), (query_shard, query_all), (output_shard, output_all)):
        half = whole.shape[-2]
        staged.append(locals_.copy(shard.at[pl.ds(pl.multiple_of(rep * half, 16), half)], whole.at[z, y, x, rep]))
    units = range(hidden // unit)
    staged.append(locals_.fill(
        [(up_shard.at[:, unit_columns(1 - x, n)], up_stage.at[:, pl.ds(n * unit, unit)]) for n in units], up_stage))
    staged.append(locals_.fill(
        [(up_shard.at[:, unit_columns(x, n)], up_all.at[z, y, x, :, pl.ds(n * unit, unit)]) for n in units],
        up_all.at[z, y, x]))
    staged.append(locals_.copy(down_shard.at[pl.ds(pl.multiple_of(rep * unit, 16), unit)], down_all.at[z, y]))
    grad_load = locals_.copy(grad_out, grad_in)
    latents_load = locals_.copy(latents, latents_in)
    media_load = locals_.copy(media, media_in)
    links.greet()

    def halves(whole, begin, size, order):
        def view(zi, yi, xi, half=rep):
            return whole.at[zi, yi, xi, half, :, pl.ds(begin, size)]

        return Gather(links, slots, view, order, True)

    slots.group = 0
    vector_gather = Gather(links, slots, lambda zi, yi, xi: packed_all.at[zi, yi, xi], xy, False)
    slots.group = 1
    gathers = [
        (halves(context_all, 0, width // 2, xy), (0, 1, 2, 3, 4)),
        (halves(context_all, width // 2, width // 2, yx), (0, 1, 2, 3, 4)),
        (halves(query_all, 0, inner, yx), (0, 2, 3, 4, 5)), (halves(output_all, 0, width, yx), (0, 2, 3, 4, 5)),
    ]
    slots.group = 2
    for number in range(2 * chunks):
        window = pl.ds(number % chunks * chunk, chunk)
        if number < chunks:
            def view(zi, yi, xi, window=window):
                return down_all.at[zi, yi, :, window]
        else:
            def view(zi, yi, xi, window=window):
                return up_all.at[zi, yi, ALL, :, window]
        ticks = (max(number - 1, 0), number + 2, number + 4)
        gathers.append((Gather(links, slots, view, ("z", "y"), False), ticks))
    up_across = slots.move(links.device("x"), up_stage, up_all.at[z, y, x], up_all.at[z, y, 1 - x])
    slots.group = 3
    parts = [(0, 2 * latent_count), (2 * latent_count, rows - 2 * latent_count)]
    branch_rows = Rows(links, slots, branch, rows, [(0, rows)])
    feed_rows = Rows(links, slots, feed, rows, parts)

    def pump(tick):
        run(gathers, tick)

    for copy in staged:
        copy.wait()
    vector_gather.step(0)
    pump(0)
    up_across.start()
    grad_load.wait()
    kept = jnp.where(lax.broadcasted_iota(jnp.int32, (rows, 1), 0) < counts[0] * latent_count, 1.0, 0.0)
    branch[:rows] = (grad_in[...].reshape(rows, width).astype(F32) * kept).astype(BF16)
    vector_gather.step(1)
    mask[...] = head_mask(latent_count, GROUP)
    sums[...] = jnp.zeros_like(sums)
    vector_gather.step(2)
    latents_load.wait()
    media_load.wait()
    pump(1)
    vector_gather.step(3)
    lane = packed_all.shape[-1]
    for zi in range(length):
        for yi in range(2):
            place = (zi * 2 + yi) * lane
            vectors[:, place:place + lane] = (packed_all[zi, yi, 0] + packed_all[zi, yi, 1]).astype(F32)[:8]

    def normalise_slot(j):
        context[j, :patches] = layer_norm(media_in[j].astype(F32), vectors[0:1], vectors[1:2]).astype(BF16)
        context[j, patches:] = layer_norm(latents_in[j].astype(F32), vectors[2:3], vectors[3:4]).astype(BF16)

    pl.loop(0, slot_count)(normalise_slot)
    pump(2)
    up_across.wait()
    pump(3)
    pump(4)
    branch_rows.send(0)

    def key_value_slot(j):
        key_value[j] = matmul(context[j], context_all[...].reshape(width, 2 * inner)).astype(BF16)

    pl.loop(0, 3)(key_value_slot)
    pump(5)
    pl.loop(3, slot_count)(key_value_slot)
    latent_normed = context[:, patches:, :].reshape(rows, width)
    query[...] = (matmul(latent_normed, query_all[...].reshape(width, inner)) * scaling).astype(BF16).reshape(
        slot_count, latent_count, inner)
    pump(6)

    def attention_slot(j):
        for begin in range(0, inner, GROUP):
            stacked = spread_heads(query[j, :, begin:begin + GROUP], mask[...].astype(BF16))
            probs = softmax(matmul_right(stacked, key_value[j, :, begin:begin + GROUP])).astype(BF16)
            value = matmul(probs, key_value[j, :, inner + begin:inner + begin + GROUP])
            attended[j, :, begin:begin + GROUP] = pick_heads(value, mask[...], latent_count).astype(BF16)

    for part, (begin, size) in enumerate(parts):
        first, last = begin // latent_count, (begin + size) // latent_count
        pl.loop(first, last)(attention_slot)
        after[begin:begin + size] = latents_in[first:last].reshape(size, width).astype(F32) + matmul(
            attended[first:last].reshape(size, inner), output_all[...].reshape(inner, width))
        feed[begin:begin + size] = layer_norm(
            after[begin:begin + size], vectors[4:5], vectors[5:6]).astype(BF16)
        feed_rows.send(part)
        pump(7 + part)
    slots.drain(0, grad_down.at[0, 0])
    branch_rows.near(0)
    branch_rows.forward(0)

    def turn(source, target, owner):
        def body(at):
            target[pl.ds(at, 256), pl.ds(owner * rows, 2 * rows)] = source[
                pl.ds(owner * rows, 2 * rows), pl.ds(at, 256)].T

        tiles(width // 256, 256, body)

    turn(branch, branch_t, 0)
    branch_rows.far(0)
    tall = rows
    d_active, active, d_hidden = [pool.at[pl.ds(n * 4 * rows, 4 * rows)] for n in range(3)]

    def d_active_tile(at):
        d_active[pl.ds(at, tall)] = matmul_right(
            branch[pl.ds(at, tall)], down_all[...].reshape(hidden, width)).astype(BF16)

    tiles(4, tall, d_active_tile)
    turn(branch, branch_t, 2)

    def hidden_tile(at, begin):
        window = pl.ds(begin, chunk)
        weight = up_all[:, :, :, :, window].reshape(width, chunk)
        value, slope = gelu_parts(matmul(feed[pl.ds(at, tall)], weight))
        active[pl.ds(at, tall), window] = value.astype(BF16)
        d_hidden[pl.ds(at, tall), window] = (d_active[pl.ds(at, tall), window].astype(F32) * slope).astype(BF16)

    def d_feed_of(owner):
        return matmul_right(d_hidden[pl.ds(owner * rows, rows)], up_all[...].reshape(width, hidden))

    def after_feed_of(owner):
        return matmul(active[pl.ds(owner * rows, rows)], down_all[...].reshape(hidden, width))

    def rounded(buffer, owner, value):
        buffer[pl.ds(owner * rows, rows)] = value.astype(BF16)

    def across_tile(back, buffer):
        rounded(buffer, 2, totals[1] + back.lands[0].astype(F32))

    up_result, down_result, query_result, context_result, output_result = result
    reductions = []

    def send_off(tick):
        run(reductions, tick)

    def plane_reduction(own, lands_y, lands, finish):
        return Reduce(links, slots, own, ("y",), [lands_y], lands, finish)

    def keep_up(value, window):
        up_result[0, :, window] = jnp.where(x == 0, value[0], value[1])
        own_rows_send[:, window] = jnp.where(x == 0, value[1], value[0]).astype(BF16)

    feed_rows.near(0)
    feed_rows.near(1)
    slots.group = 6
    for c in range(chunks):
        begin = c * chunk
        window = pl.ds(begin, chunk)
        tiles(2, tall, lambda at, begin=begin: hidden_tile(at, begin))
        if c == 0:
            pump(9)
            turn(feed, feed_t, 0)
            feed_rows.forward(0)
            feed_rows.forward(1)
            feed_rows.far(0)
            feed_rows.far(1)
            turn(feed, feed_t, 2)
        tiles(2, tall, lambda at, begin=begin: hidden_tile(pl.multiple_of(2 * rows + at, tall), begin))
        if c == chunks - 1:
            for group in range(1, 4):
                slots.drain(group)
            slots.group = 4
            d_feed_back = Partials(links, slots, feed, d_feed_lands, rows)
            slots.group = 5
            after_back = Partials(links, slots, branch, after_lands, rows)
            slots.group = 6
            rounded(feed, 3, d_feed_of(3))
            d_feed_back.far.start()
            totals[1] = d_feed_of(2)
            d_feed_back.far.wait()
            across_tile(d_feed_back, feed)
            d_feed_back.across.start()

        def grad_tile(number, window=window, c=c):
            size = width // 2
            place = pl.multiple_of(number * size, size)
            up = matmul(feed_t[pl.ds(place, size)], d_hidden[:, window]).astype(BF16)
            grad_up[pl.ds(number * (length // 2), length // 2), :, :, :, window] = up.reshape(
                length // 2, 2, 2, size // (2 * length), chunk)
            down = matmul(branch_t[pl.ds(place, size)], active[:, window]).astype(BF16)
            for owner in range(2):
                grad_down[c, owner, pl.ds(place, size)] = down[:, owner * unit:(owner + 1) * unit]

        pl.loop(0, 2)(grad_tile)
        reductions.append((plane_reduction(
            lambda zi, yi, xi, window=window: grad_up.at[zi, yi, ALL, :, window],
            lands_b[0].at[:, :, :, window], lands_z[0].at[:, :, :, window],
            functools.partial(keep_up, window=window)), (c, c + 3, c + 5)))
        if c == 0:
            pump(10)
        if c == chunks - 2:
            pump(11)
        send_off(c)
    part_size = width // chunks
    for number in range(chunks):
        window = pl.ds(number * part_size, part_size)

        def keep_down(value, window=window):
            down_result[:, window] = value.T

        reductions.append((plane_reduction(
            lambda zi, yi, xi, window=window: grad_down.at[zi, yi, window],
            lands_b[1].at[:, window], lands_z[1].at[:, window], keep_down),
            (chunks, chunks + 3 + number, chunks + 5 + number)))
    send_off(4)
    rounded(feed, 1, d_feed_of(1))
    d_feed_back.near.start()
    totals[0] = d_feed_of(0)

    rounded(branch, 3, after_feed_of(3))
    after_back.far.start()
    totals[1] = after_feed_of(2)
    after_back.far.wait()
    across_tile(after_back, branch)
    send_off(5)
    rounded(branch, 1, after_feed_of(1))
    after_back.near.start()
    totals[1] = after_feed_of(0)
    d_feed_back.near.wait()
    d_feed_back.across.wait()
    after_back.across.start()
    slots.drain(4)

    def fold(terms):
        return jnp.sum(terms.reshape(-1, 8, width), axis=0)

    d_feed = totals.at[0]
    flat_grad = lambda at, size: grad_in[pl.ds(lax.div(at, latent_count), size // latent_count)].reshape(size, width)

    def middle_tile(at, size=latent_count):
        own = pl.ds(at, size)
        upstream = d_feed[own] + d_feed_lands[1, own].astype(F32) + d_feed_lands[2, own].astype(F32)
        d_norm, gain_terms = layer_norm_back(after[own], vectors[4:5], upstream)
        sums[4] = sums[4] + fold(gain_terms)
        sums[5] = sums[5] + fold(upstream)
        row = lax.broadcasted_iota(jnp.int32, (size, 1), 0) + at
        keep = jnp.where(row < counts[0] * latent_count, 1.0, 0.0)
        d_middle = flat_grad(at, size).astype(F32) * keep + d_norm
        d_feed[own] = d_middle
        feed[own] = d_middle.astype(BF16)

    tiles(slot_count, latent_count, middle_tile)
    send_off(6)

    context_rows, output_rows = context_all.shape[-2], output_all.shape[-2]

    def context_own(zi, yi, xi, half):
        return up_all.at[zi, yi, xi, pl.ds(pl.multiple_of(half * context_rows, 16), context_rows)]

    def query_own(zi, yi, xi, half):
        return grad_query.at[zi, yi, xi, half]

    def output_own(zi, yi, xi, half):
        return grad_output.at[zi, yi, xi, half]

    def to_sibling(own, land):
        move = slots.move(links.device("core"), own(ALL, ALL, ALL, 1 - rep), land, land)
        move.start()

        def settle():
            move.wait()
            add_into(own(ALL, ALL, ALL, rep), land)

        return settle

    def halved_reduction(own, number, target, begin, size, *ticks):
        made = []
        for which, order in enumerate((("y", "x"), ("x", "y"))):
            window = pl.ds(begin + which * (size // 2), size // 2)

            def finish(value, window=window):
                target[:, window] = value

            made.append((Reduce(
                links, slots, lambda zi, yi, xi, window=window: own(zi, yi, xi, rep).at[..., window], order,
                [lands_b[number].at[:, :, :, window], lands_a[number].at[:, :, window]],
                lands_z[number].at[:, :, window], finish), ticks))
        return made

    d_branch = feed.at[pl.ds(0, rows)]
    output_block = inner // 2

    def output_grad_tile(number):
        place = pl.multiple_of(number * output_block, output_block)
        turned = attended[:, :, pl.ds(place, output_block)].reshape(rows, output_block).T
        value = matmul(turned, d_branch[...]).astype(BF16)
        grad_output[pl.ds(number * (length // 2), length // 2)] = value.reshape(
            length // 2, 2, 2, 2, output_rows, width)

    d_attended, d_query = upstream_rows[0], upstream_rows[1]
    d_attended[...] = matmul_right(d_branch[...], output_all[...].reshape(inner, width)).astype(BF16)
    send_off(7)

    def attention_back_slot(j):
        own = pl.ds(pl.multiple_of(j * latent_count, latent_count), latent_count)
        for begin in range(0, inner, GROUP):
            keys = key_value[j, :, begin:begin + GROUP]
            values = key_value[j, :, inner + begin:inner + begin + GROUP]
            low_mask = mask[...].astype(BF16)
            stacked = spread_heads(query[j, :, begin:begin + GROUP], low_mask)
            upstream = spread_heads(d_attended[own, begin:begin + GROUP], low_mask)
            probs = softmax(matmul_right(stacked, keys))
            d_probs = matmul_right(upstream, values)
            d_scores = (probs * (d_probs - jnp.sum(probs * d_probs, axis=-1, keepdims=True))).astype(BF16)
            d_query[own, begin:begin + GROUP] = (
                pick_heads(matmul(d_scores, keys), mask[...], latent_count).astype(BF16).astype(F32) * scaling
            ).astype(BF16)
            at = pl.ds(pl.multiple_of(j * key_count, 16), key_count)
            pool[at, begin:begin + GROUP] = matmul_left(d_scores, stacked).astype(BF16)
            pool[at, inner + begin:inner + begin + GROUP] = matmul_left(probs.astype(BF16), upstream).astype(BF16)

    pl.loop(0, 2)(attention_back_slot)
    pl.loop(0, 2)(output_grad_tile)
    settle_output = to_sibling(output_own, lands_c[2])
    pl.loop(2, 4)(attention_back_slot)
    settle_output()
    reductions.extend(halved_reduction(output_own, 4, output_result, 0, width, 8, 9, 10, 11))
    send_off(8)
    pl.loop(4, slot_count)(attention_back_slot)
    block = width // length

    def query_grad_tile(zi):
        place = pl.multiple_of(zi * block, block)
        turned = context[:, patches:, pl.ds(place, block)].reshape(rows, block).T
        value = matmul(turned, d_query[...]).astype(BF16)
        grad_query[zi] = value.reshape(2, 2, 2, context_rows, inner)

    pl.loop(0, length)(query_grad_tile)
    settle_query = to_sibling(query_own, lands_c[0])

    def context_grad_tile(zi):
        place = pl.multiple_of(zi * block, block)
        value = None
        for j in range(slot_count):
            turned = context[j, :, pl.ds(place, block)].T
            term = matmul(turned, pool[j * key_count:(j + 1) * key_count])
            value = term if value is None else value + term
        up_all[zi] = value.astype(BF16).reshape(2, 2, block // 4, 2 * inner)

    context_moves = []

    def settle_context(zi):
        context_moves[zi].wait()
        add_into(context_own(zi, ALL, ALL, rep), lands_c[1].at[zi])

    for zi in range(length):
        context_grad_tile(zi)
        land = lands_c[1].at[zi]
        context_moves.append(slots.move(links.device("core"), context_own(zi, ALL, ALL, 1 - rep), land, land))
        context_moves[-1].start()
        if zi == 1:
            settle_query()
            reductions.extend(halved_reduction(query_own, 2, query_result, 0, inner, 9, 10, 11, 12))
            send_off(9)
        if zi > 0:
            settle_context(zi - 1)
    settle_context(length - 1)
    reductions.extend(halved_reduction(context_own, 3, context_result, 0, inner, 10, 11, 12, 13))
    reductions.extend(halved_reduction(context_own, 3, context_result, inner, inner, 10, 12, 13, 14))
    send_off(10)
    slots.group = 7
    own_rows_move = slots.move(links.device("x"), own_rows_send, own_rows_land, own_rows_land)
    own_rows_move.start()
    after_back.near.wait()
    after_back.across.wait()
    slots.drain(5)
    branch[:rows] = ((after[...] + totals[1] + after_lands[1].astype(F32) + after_lands[2].astype(F32)) * kept).astype(BF16)
    written = [locals_.fill(
        [(branch.at[pl.ds(j * latent_count, latent_count)], latents_out.at[j]) for j in range(slot_count)], latents_out)]

    context_up = totals.at[1]

    def input_slot(j):
        at = pl.ds(pl.multiple_of(j * key_count, 16), key_count)
        own = pl.ds(pl.multiple_of(j * latent_count, latent_count), latent_count)
        context_up[...] = matmul_right(pool[at], context_all[...].reshape(width, 2 * inner))
        context_up[patches:] = context_up[patches:] + matmul_right(d_query[own], query_all[...].reshape(width, inner))

        def media_tile(at, size=patches // 2):
            tile = pl.ds(at, size)
            upstream = context_up[tile]
            value, gain_terms = layer_norm_back(media_in[j, tile].astype(F32), vectors[0:1], upstream)
            sums[0] = sums[0] + fold(gain_terms)
            sums[1] = sums[1] + fold(upstream)
            media_in[j, tile] = value.astype(BF16)

        tiles(2, patches // 2, media_tile)
        upstream = context_up[patches:]
        value, gain_terms = layer_norm_back(latents_in[j].astype(F32), vectors[2:3], upstream)
        sums[2] = sums[2] + fold(gain_terms)
        sums[3] = sums[3] + fold(upstream)
        latents_in[j] = (d_feed[own] + value).astype(BF16)

    pl.loop(0, 2)(input_slot)
    send_off(11)
    pl.loop(2, 3)(input_slot)
    send_off(12)
    own_rows_move.wait()
    up_result[1] = own_rows_land[...].astype(F32)

    def hand_over(numbers):
        for number in numbers:
            value, out = result[number], grads_out[number]
            written.append(locals_.copy(value, out.at[rep]))
            written.append(slots.move(links.device("core"), value, out.at[rep], out.at[1 - rep]))
            written[-1].start()

    hand_over((0, 1, 2, 4))
    pl.loop(3, slot_count)(input_slot)
    written.append(locals_.copy(media_in, media_grad_out))
    written.append(locals_.copy(latents_in, latents_grad_out))
    for number in range(6):
        total[number:number + 1] = jnp.sum(sums[number], axis=0, keepdims=True)
    total[6:] = jnp.zeros_like(total[6:])
    vector_sum = VectorSum(links, slots, total, total_stage, total_lands)
    vector_sum.step(0)
    send_off(13)
    vector_sum.step(1)
    vector_sum.step(2)
    send_off(14)
    hand_over((3,))
    vector_sum.step(3)
    vector_sum.step(4)
    sums_out[...] = total[...]
    for copy in written:
        copy.wait()
    slots.drain(6)
    slots.drain(7)


def layer(length, counts, media, latents, grad_out, packed, shards):
    query_shard, context_shard, output_shard, up_shard, down_shard = shards
    slot_count, patches, width = media.shape
    latent_count = latents.shape[1]
    key_count = patches + latent_count
    rows = slot_count * latent_count
    inner = query_shard.shape[1]
    unit = down_shard.shape[0] // 2
    hidden = up_shard.shape[1] // 4
    blocks = (length, 2, 2)

    def halved(shard):
        return blocks + (2, shard.shape[0] // 2, shard.shape[1])

    up_shape = blocks + (up_shard.shape[0], hidden)
    down_shape = (length, 2, unit, width)
    halves = [halved(s)[4:] for s in shards[:3]]
    results = [(2,) + up_shape[3:], (unit, width)] + halves
    anywhere = pl.BlockSpec(memory_space=pl.ANY)
    vmem = pl.BlockSpec(memory_space=pltpu.VMEM)
    sums_shape = (8, width)
    scratch = [
        pltpu.VMEM(halved(query_shard), BF16),
        pltpu.VMEM(halved(context_shard), BF16),
        pltpu.VMEM(halved(output_shard), BF16),
        pltpu.VMEM(up_shape, BF16),
        pltpu.VMEM(up_shape[3:], BF16),
        pltpu.VMEM(down_shape, BF16),
        pltpu.VMEM(blocks + packed.shape, BF16),
        pltpu.VMEM((8, width), F32),
        pltpu.VMEM(media.shape, BF16),
        pltpu.VMEM(latents.shape, BF16),
        pltpu.VMEM(grad_out.shape, BF16),
        pltpu.VMEM((slot_count, key_count, width), BF16),
        pltpu.VMEM((slot_count, key_count, 2 * inner), BF16),
        pltpu.VMEM((slot_count, latent_count, inner), BF16),
        pltpu.VMEM((slot_count, latent_count, inner), BF16),
        pltpu.VMEM((rows, width), F32),
        pltpu.VMEM((4 * rows, width), BF16),
        pltpu.VMEM((width, 4 * rows), BF16),
        pltpu.VMEM((4 * rows, width), BF16),
        pltpu.VMEM((width, 4 * rows), BF16),
        pltpu.VMEM((max(12 * rows, slot_count * key_count), hidden), BF16),
        pltpu.VMEM((2, rows, width), F32),
        pltpu.VMEM((3, rows, width), BF16),
        pltpu.VMEM((3, rows, width), BF16),
        [pltpu.VMEM((rows, inner), BF16)] * 2,
        pltpu.VMEM(up_shape, BF16),
        pltpu.VMEM((length, 2, width, unit), BF16),
        pltpu.VMEM(halved(query_shard), BF16),
        pltpu.VMEM(halved(output_shard), BF16),
        pltpu.VMEM((latent_count * (GROUP // HEAD_DIM), GROUP), F32),
        pltpu.VMEM((6, 8, width), F32),
        pltpu.VMEM(sums_shape, F32),
        pltpu.VMEM((4,) + sums_shape, F32),
        pltpu.VMEM((2 + length,) + sums_shape, F32),
        pltpu.VMEM(up_shape[3:], BF16),
        pltpu.VMEM(up_shape[3:], BF16),
        [pltpu.VMEM(blocks + h, BF16) for h in halves],
        [pltpu.VMEM((length, 2) + up_shape[3:], BF16), pltpu.VMEM((length, width, unit), BF16)]
        + [pltpu.VMEM((length, 2) + h, BF16) for h in halves],
        [None, None] + [pltpu.VMEM((length,) + h, BF16) for h in halves],
        [pltpu.VMEM((length - 1, 2) + up_shape[3:], BF16), pltpu.VMEM((length - 1, width, unit), BF16)]
        + [pltpu.VMEM((length - 1,) + h, BF16) for h in halves],
        [pltpu.VMEM(r, F32) for r in results],
        pltpu.SemaphoreType.DMA((8,)),
        pltpu.SemaphoreType.DMA((112,)),
        pltpu.SemaphoreType.DMA((24,)),
    ]
    out_shape = (
        jax.ShapeDtypeStruct(latents.shape, BF16), jax.ShapeDtypeStruct(media.shape, BF16),
        jax.ShapeDtypeStruct(latents.shape, BF16), jax.ShapeDtypeStruct(sums_shape, F32),
        [jax.ShapeDtypeStruct((2,) + r, F32) for r in results])
    return pl.pallas_call(
        functools.partial(layer_kernel, length, HEAD_DIM ** (-0.5)),
        out_shape=out_shape,
        in_specs=[pl.BlockSpec(memory_space=pltpu.SMEM)] + [anywhere] * 9,
        out_specs=(anywhere, anywhere, anywhere, vmem, [anywhere] * 5),
        scratch_shapes=scratch,
        compiler_params=pltpu.CompilerParams(
            collective_id=0, has_side_effects=True, vmem_limit_bytes=63 * 2 ** 20),
        name="resampler_layer",
    )(counts, media, latents, grad_out, packed, query_shard, context_shard, output_shard, up_shard, down_shard)


def finish_kernel(length, latents_raw, media_grad_raw, latents_grad_raw, grads_raw, latents_out, media_grad_out,
                  latents_grad_out, grads_out, local):
    x = Links(length).x
    locals_ = Locals(local)
    count = media_grad_raw.shape[0]
    copies = [locals_.fill([(media_grad_raw.at[j], media_grad_out.at[j]) for j in range(count)], media_grad_out)]
    up, up_out = grads_raw[0], grads_out[0]
    unit = grads_raw[1].shape[1]
    moves = []
    for core in range(2):
        for plane in range(2):
            half = x if plane == 0 else 1 - x
            for owner in range(up.shape[-1] // unit):
                begin = pl.multiple_of(((2 * owner + half) * 2 + core) * unit, unit)
                moves.append((up.at[core, plane, :, pl.ds(owner * unit, unit)], up_out.at[:, pl.ds(begin, unit)]))
    copies.append(locals_.fill(moves, up_out))
    for raw, out in zip((latents_raw, latents_grad_raw) + tuple(grads_raw[1:]),
                        (latents_out, latents_grad_out) + tuple(grads_out[1:])):
        copies.append(locals_.copy(raw, out))
    for copy in copies:
        copy.wait()


def finish(length, latents_raw, media_grad_raw, latents_grad_raw, grads_raw):
    anywhere = pl.BlockSpec(memory_space=pl.ANY)
    up = grads_raw[0]
    shapes = [jax.ShapeDtypeStruct((up.shape[2], 4 * up.shape[3]), up.dtype)]
    shapes += [jax.ShapeDtypeStruct(g.shape, g.dtype) for g in grads_raw[1:]]
    same = [jax.ShapeDtypeStruct(r.shape, r.dtype) for r in (latents_raw, media_grad_raw, latents_grad_raw)]
    return pl.pallas_call(
        functools.partial(finish_kernel, length),
        out_shape=(*same, shapes),
        in_specs=[anywhere, anywhere, anywhere, [anywhere] * 5],
        out_specs=(anywhere, anywhere, anywhere, [anywhere] * 5),
        scratch_shapes=[pltpu.SemaphoreType.DMA((8,))],
        name="finish",
    )(latents_raw, media_grad_raw, latents_grad_raw, grads_raw)


def head_scores(first_heads, second_heads):
    return jnp.einsum(
        "bqhd,bkhd->bhqk", first_heads, second_heads, preferred_element_type=jnp.float32
    )


def collective_body(
    media,
    latents,
    image_counts,
    grad_out,
    media_gain,
    media_bias,
    latent_gain,
    latent_bias,
    feed_gain,
    feed_bias,
    query_weight,
    context_weight,
    output_weight,
    up_weight,
    down_weight,
):
    samples, slots, patches, model_width = media.shape
    latent_count = latents.shape[2]
    inner_width = query_weight.shape[1]
    head_count = inner_width // HEAD_DIM
    blocks = samples * slots
    key_count = patches + latent_count
    latent_total = blocks * latent_count
    scaling = HEAD_DIM ** (-0.5)
    vector_shards = (media_gain, media_bias, latent_gain, latent_bias, feed_gain, feed_bias)
    weight_shards = (query_weight, context_weight, output_weight, up_weight, down_weight)
    gathered = tuple(lax.all_gather(s, "dp", axis=0, tiled=True) for s in vector_shards + weight_shards)
    vectors = [element.astype(jnp.float32) for element in gathered[:6]]
    media_rows = media.reshape(blocks * patches, model_width).astype(jnp.float32)
    latent_rows = latents.reshape(latent_total, model_width).astype(jnp.float32)
    media_normed = layer_norm(media_rows, vectors[0], vectors[1]).astype(jnp.bfloat16)
    latent_normed = layer_norm(latent_rows, vectors[2], vectors[3]).astype(jnp.bfloat16)
    queries = (matmul(latent_normed, gathered[6]) * scaling).astype(jnp.bfloat16)
    context = jnp.concatenate(
        [
            media_normed.reshape(blocks, patches, model_width),
            latent_normed.reshape(blocks, latent_count, model_width),
        ],
        axis=1,
    ).reshape(blocks * key_count, model_width)
    key_value = (
        matmul(context, gathered[7])
        .astype(jnp.bfloat16)
        .reshape(blocks, key_count, 2 * inner_width)
    )
    query_heads = queries.reshape(blocks, latent_count, head_count, HEAD_DIM)
    key_heads = key_value[:, :, :inner_width].reshape(blocks, key_count, head_count, HEAD_DIM)
    value_heads = key_value[:, :, inner_width:].reshape(blocks, key_count, head_count, HEAD_DIM)
    scores = head_scores(query_heads, key_heads)
    row_max = jnp.max(scores, axis=-1, keepdims=True)
    exponent = jnp.exp(scores - row_max)
    row_total = jnp.sum(exponent, axis=-1, keepdims=True)
    log_total = row_max + jnp.log(row_total)
    attention_weights = (exponent / row_total).astype(jnp.bfloat16)
    attended = (
        jnp.einsum(
            "bhqk,bkhd->bqhd", attention_weights, value_heads, preferred_element_type=jnp.float32
        )
        .astype(jnp.bfloat16)
        .reshape(latent_total, inner_width)
    )
    after_attention = latent_rows + matmul(attended, gathered[8])
    feed_input = layer_norm(after_attention, vectors[4], vectors[5]).astype(jnp.bfloat16)
    hidden = matmul(feed_input, gathered[9])
    activated = gelu_exact(hidden).astype(jnp.bfloat16)
    after_feed = after_attention + matmul(activated, gathered[10])
    slot_mask = (
        lax.broadcasted_iota(jnp.int32, (samples, slots), 1) < image_counts[:, None]
    ).astype(jnp.float32)
    row_mask = jnp.broadcast_to(slot_mask[:, :, None], (samples, slots, latent_count)).reshape(
        latent_total, 1
    )
    latents_out = (after_feed * row_mask).astype(jnp.bfloat16).reshape(latents.shape)
    backward_set = gathered
    back_vectors = [element.astype(jnp.float32) for element in backward_set[:6]]
    d_after = grad_out.reshape(latent_total, model_width).astype(jnp.float32) * row_mask
    d_branch = d_after.astype(jnp.bfloat16)
    grad_down = matmul_left(activated, d_branch)
    d_activated = matmul_right(d_branch, backward_set[10])
    d_hidden = jax.vjp(gelu_exact, hidden)[1](d_activated)[0].astype(jnp.bfloat16)
    grad_up = matmul_left(feed_input, d_hidden)
    d_feed = matmul_right(d_hidden, backward_set[9])
    d_feed_norm, grad_feed_gain, grad_feed_bias = jax.vjp(
        layer_norm, after_attention, back_vectors[4], back_vectors[5]
    )[1](d_feed)
    d_middle = d_after + d_feed_norm
    d_out_branch = d_middle.astype(jnp.bfloat16)
    grad_output = matmul_left(attended, d_out_branch)
    d_attended = (
        matmul_right(d_out_branch, backward_set[8])
        .astype(jnp.bfloat16)
        .reshape(blocks, latent_count, head_count, HEAD_DIM)
    )
    recomputed = jnp.exp(head_scores(query_heads, key_heads) - log_total)
    d_weights = head_scores(d_attended, value_heads)
    d_scores = (
        recomputed * (d_weights - jnp.sum(recomputed * d_weights, axis=-1, keepdims=True))
    ).astype(jnp.bfloat16)
    d_queries = (
        jnp.einsum(
            "bhqk,bkhd->bqhd", d_scores, key_heads, preferred_element_type=jnp.float32
        ).astype(jnp.bfloat16)
        * scaling
    ).reshape(latent_total, inner_width)
    d_keys = jnp.einsum(
        "bhqk,bqhd->bkhd", d_scores, query_heads, preferred_element_type=jnp.float32
    ).astype(jnp.bfloat16)
    d_values = jnp.einsum(
        "bhqk,bqhd->bkhd",
        recomputed.astype(jnp.bfloat16),
        d_attended,
        preferred_element_type=jnp.float32,
    ).astype(jnp.bfloat16)
    d_key_value = jnp.concatenate(
        [
            d_keys.reshape(blocks, key_count, inner_width),
            d_values.reshape(blocks, key_count, inner_width),
        ],
        axis=-1,
    ).reshape(blocks * key_count, 2 * inner_width)
    grad_query = matmul_left(latent_normed, d_queries)
    grad_context = matmul_left(context, d_key_value)
    d_context = matmul_right(d_key_value, backward_set[7]).reshape(blocks, key_count, model_width)
    d_latent_normed = matmul_right(d_queries, backward_set[6]) + d_context[:, patches:, :].reshape(
        latent_total, model_width
    )
    d_media_normed = d_context[:, :patches, :].reshape(blocks * patches, model_width)
    d_latent_norm, grad_latent_gain, grad_latent_bias = jax.vjp(
        layer_norm, latent_rows, back_vectors[2], back_vectors[3]
    )[1](d_latent_normed)
    grad_latents = (d_middle + d_latent_norm).astype(jnp.bfloat16).reshape(latents.shape)
    d_media, grad_media_gain, grad_media_bias = jax.vjp(
        layer_norm, media_rows, back_vectors[0], back_vectors[1]
    )[1](d_media_normed)
    grad_media = d_media.astype(jnp.bfloat16).reshape(media.shape)
    vector_grads = jnp.stack([
        grad_media_gain, grad_media_bias, grad_latent_gain, grad_latent_bias, grad_feed_gain, grad_feed_bias])
    weight_grads = [
        g.astype(jnp.bfloat16) for g in (grad_query, grad_context, grad_output, grad_up, grad_down)]
    vector_sums = lax.psum_scatter(vector_grads, "dp", scatter_dimension=1, tiled=True)
    summed = [lax.psum_scatter(g, "dp", scatter_dimension=0, tiled=True) for g in weight_grads]
    owned = tuple(lax.psum(vector_sums, "rep")) + tuple(
        lax.psum(s, "rep").astype(jnp.float32) for s in summed)
    return (
        latents_out,
        grad_media,
        grad_latents,
        owned[0],
        owned[1],
        owned[2],
        owned[3],
        owned[4],
        owned[5],
        owned[6],
        owned[7],
        owned[8],
        owned[9],
        owned[10],
    )


def body(media, latents, image_counts, grad_out, *parameters):
    chips = lax.axis_size("dp")
    weight_shards = parameters[6:]
    tiled = (media.shape[0] == 1 and chips % 4 == 0 and chips > 4 and parameters[0].shape[0] == 64
             and all(s.shape[0] % 32 == 0 for s in weight_shards))
    if not tiled:
        return collective_body(media, latents, image_counts, grad_out, *parameters)
    side = lax.rem(lax.axis_index("dp"), 2)
    stacked = jnp.stack(parameters[:6])
    packed = jnp.pad(
        jnp.concatenate([jnp.where(side == 0, stacked, 0), jnp.where(side == 0, 0, stacked)], axis=1), ((0, 10), (0, 0)))
    latents_out, grad_media, grad_latents, vector_sums, summed = layer(
        chips // 4, image_counts, media[0], latents[0], grad_out[0], packed, weight_shards)
    latents_out, grad_media, grad_latents, summed = finish(
        chips // 4, latents_out, grad_media, grad_latents, summed)
    sums = [s.reshape(-1, s.shape[-1]) for s in summed[2:] + summed[:2]]
    width = parameters[0].shape[0]
    mine = lax.dynamic_slice(vector_sums, (0, lax.axis_index("dp") * width), (6, width))
    return (latents_out[None], grad_media[None], grad_latents[None]) + tuple(mine) + tuple(sums)


def solution(mesh):
    return jax.shard_map(
        body,
        mesh=mesh,
        in_specs=(
            P(("dp", "rep"), None, None, None),
            P(("dp", "rep"), None, None, None),
            P(("dp", "rep")),
            P(("dp", "rep"), None, None, None),
            P("dp"),
            P("dp"),
            P("dp"),
            P("dp"),
            P("dp"),
            P("dp"),
            P("dp", None),
            P("dp", None),
            P("dp", None),
            P("dp", None),
            P("dp", None),
        ),
        out_specs=(
            P(("dp", "rep"), None, None, None),
            P(("dp", "rep"), None, None, None),
            P(("dp", "rep"), None, None, None),
            P("dp"),
            P("dp"),
            P("dp"),
            P("dp"),
            P("dp"),
            P("dp"),
            P("dp", None),
            P("dp", None),
            P("dp", None),
            P("dp", None),
            P("dp", None),
        ),
        check_vma=False,
    )
```

```python
import functools

import jax
import jax.numpy as jnp
from jax import lax
from jax.experimental import pallas as pl
from jax.experimental.pallas import tpu as pltpu
from jax.sharding import PartitionSpec as P

HEAD_DIM = 64
GROUP = 256

epsilon = 1e-05

MESH = pl.DeviceIdType.MESH
ALL = slice(None)
F32 = jnp.float32
BF16 = jnp.bfloat16


class Links:
    def __init__(self, length):
        self.length = length
        self.dp = lax.axis_index("dp")
        self.rep = lax.axis_index("rep")
        self.z = lax.div(self.dp, 4)
        self.y = lax.rem(lax.div(self.dp, 2), 2)
        self.x = lax.rem(self.dp, 2)

    def device(self, axis, way=0):
        if axis == "core":
            return (self.dp, 1 - self.rep)
        if axis == "x":
            return (self.dp + 1 - 2 * self.x, self.rep)
        if axis == "y":
            return (self.dp + 2 - 4 * self.y, self.rep)
        return (self.dp + 4 * (self.along(way) - self.z), self.rep)

    def along(self, way):
        return lax.rem(self.z + way + self.length, self.length)

    def greet(self):
        barrier = pltpu.get_barrier_semaphore()
        peers = [("core", 0), ("x", 0), ("y", 0)] + [("z", way) for way in range(1, self.length)]
        for axis, way in peers:
            pl.semaphore_signal(barrier, inc=1, device_id=self.device(axis, way), device_id_type=MESH)
        pl.semaphore_wait(barrier, len(peers))


class Move:
    def __init__(self, slots, copies, landing):
        send, recv = slots.send.at[slots.group], slots.recv.at[slots.made]
        slots.made += 1
        self.slots, self.group, self.copies = slots, slots.group, [
            pltpu.make_async_remote_copy(
                src_ref=source, dst_ref=target, send_sem=send, recv_sem=recv,
                device_id=device, device_id_type=MESH)
            for device, source, target in copies]
        self.bytes = 0
        for _, source, _ in copies:
            size = jnp.dtype(source.dtype).itemsize
            for extent in source.shape:
                size *= extent
            self.bytes += size
        self.into = pltpu.make_async_remote_copy(
            src_ref=landing, dst_ref=landing, send_sem=send, recv_sem=recv,
            device_id=copies[0][0], device_id_type=MESH)

    def start(self):
        for copy in self.copies:
            copy.start()
        self.slots.sent[self.group] += self.bytes

    def wait(self):
        self.into.wait_recv()


class Slots:
    def __init__(self, send, recv, ruler):
        self.send, self.recv, self.ruler, self.made, self.group = send, recv, ruler, 0, 0
        self.sent = [0] * send.shape[0]

    def move(self, device, source, target, landing):
        return Move(self, [(device, source, target)], landing)

    def drain(self, group, ruler=None):
        ruler = self.ruler if ruler is None else ruler
        row = ruler.shape[-1] * jnp.dtype(ruler.dtype).itemsize
        rows, rest = divmod(self.sent[group], row)
        assert rest == 0 and rows % 16 == 0 and rows <= ruler.shape[0]
        whole = ruler.at[pl.ds(0, rows)]
        pltpu.make_async_copy(whole, whole, self.send.at[group]).wait()


class Locals:
    def __init__(self, semaphores):
        self.semaphores, self.made = semaphores, 0

    def copy(self, source, target):
        return self.fill([(source, target)], target)

    def fill(self, copies, whole):
        semaphore = self.semaphores.at[self.made]
        self.made += 1
        for source, target in copies:
            pltpu.make_async_copy(source, target, semaphore).start()
        return pltpu.make_async_copy(whole, whole, semaphore)


class Gather:
    def __init__(self, links, slots, view, axes, halved):
        here = {"z": links.z, "y": links.y, "x": links.x}
        self.moves = []
        for axis in axes:
            mine = view(here["z"], here["y"], here["x"])
            if axis == "z":
                self.moves.append(Move(
                    slots, [(links.device("z", way), mine, mine) for way in range(1, links.length)],
                    view(pl.ds(0, links.length - 1), here["y"], here["x"])))
            else:
                other = dict(here)
                other[axis] = 1 - here[axis]
                self.moves.append(
                    slots.move(links.device(axis), mine, mine, view(other["z"], other["y"], other["x"])))
            here[axis] = ALL
        if halved:
            mine = view(ALL, ALL, ALL)
            self.moves.append(
                slots.move(links.device("core"), mine, mine, view(ALL, ALL, ALL, 1 - links.rep)))

    def step(self, number):
        if 0 < number <= len(self.moves):
            self.moves[number - 1].wait()
        if 0 <= number < len(self.moves):
            self.moves[number].start()


class Reduce:
    def __init__(self, links, slots, own, axes, lands, lands_z, finish):
        self.own, self.links, self.finish, self.lands_z = own, links, finish, lands_z
        self.moves, self.adds = [], []
        z, y, x = links.z, links.y, links.x
        here = {"z": ALL, "y": ALL, "x": ALL}
        for axis, land in zip(axes, lands):
            away, home = dict(here), dict(here)
            place = {"y": y, "x": x}[axis]
            away[axis], home[axis] = 1 - place, place
            self.moves.append(slots.move(
                links.device(axis), own(away["z"], away["y"], away["x"]), land, land))
            here = home
            self.adds.append(functools.partial(add_into, own(home["z"], home["y"], home["x"]), land))
        self.moves.append(Move(
            slots, [(links.device("z", way), own(links.along(way), here["y"], here["x"]), lands_z.at[way - 1])
                    for way in range(1, links.length)], lands_z))
        self.mine = own(z, here["y"], here["x"])
        self.adds.append(self.end)

    def step(self, number):
        if 0 < number <= len(self.moves):
            self.moves[number - 1].wait()
            self.adds[number - 1]()
        if 0 <= number < len(self.moves):
            self.moves[number].start()

    def end(self):
        total = self.mine[...].astype(F32)
        for way in range(1, self.links.length):
            total = total + self.lands_z[way - 1].astype(F32)
        self.finish(total)


def add_into(target, arrived):
    @pl.loop(0, target.shape[0])
    def _(number):
        target[number] = (target[number].astype(F32) + arrived[number].astype(F32)).astype(target.dtype)


def run(table, tick):
    for item, ticks in table:
        if tick in ticks:
            item.step(ticks.index(tick))


def matmul(left, right):
    return jnp.dot(left, right, preferred_element_type=F32)


def matmul_left(left, right):
    return lax.dot_general(left, right, (((0,), (0,)), ((), ())), preferred_element_type=F32)


def matmul_right(left, right):
    return lax.dot_general(left, right, (((1,), (1,)), ((), ())), preferred_element_type=F32)


def layer_norm(values, gain, offset):
    centre = jnp.mean(values, axis=-1, keepdims=True)
    shifted = values - centre
    spread = jnp.mean(shifted * shifted, axis=-1, keepdims=True)
    return shifted * lax.rsqrt(spread + epsilon) * gain + offset


def layer_norm_back(values, gain, upstream):
    centre = jnp.mean(values, axis=-1, keepdims=True)
    shifted = values - centre
    spread = jnp.mean(shifted * shifted, axis=-1, keepdims=True)
    rate = lax.rsqrt(spread + epsilon)
    normed = shifted * rate
    scaled = upstream * gain
    first = jnp.mean(scaled, axis=-1, keepdims=True)
    second = jnp.mean(scaled * normed, axis=-1, keepdims=True)
    return rate * (scaled - first - normed * second), upstream * normed


def gelu_exact(values):
    return 0.5 * values * (1.0 + jax.scipy.special.erf(values * 0.7071067811865476))


def gelu_parts(values):
    cumulative = 0.5 * (1.0 + lax.erf(values * 0.7071067811865476))
    density = 0.3989422804014327 * jnp.exp(-0.5 * values * values)
    return values * cumulative, cumulative + values * density


def tiles(count, size, action):
    @pl.loop(0, count)
    def _(number):
        action(pl.multiple_of(number * size, size))


def head_mask(rows, columns):
    heads = columns // HEAD_DIM
    row = lax.broadcasted_iota(jnp.int32, (rows * heads, columns), 0)
    column = lax.broadcasted_iota(jnp.int32, (rows * heads, columns), 1)
    head_row = jnp.zeros_like(row)
    head_column = jnp.zeros_like(row)
    for head in range(1, heads):
        head_row = head_row + jnp.where(row >= head * rows, 1, 0)
        head_column = head_column + jnp.where(column >= head * HEAD_DIM, 1, 0)
    return jnp.where(head_row == head_column, 1.0, 0.0)


def spread_heads(rows, mask):
    return jnp.concatenate([rows] * (mask.shape[0] // rows.shape[0]), axis=0) * mask


def pick_heads(stacked, mask, rows):
    kept = stacked * mask
    total = kept[:rows]
    for head in range(1, stacked.shape[0] // rows):
        total = total + kept[head * rows:(head + 1) * rows]
    return total


def softmax(scores):
    exponent = jnp.exp(scores - jnp.max(scores, axis=-1, keepdims=True))
    return exponent / jnp.sum(exponent, axis=-1, keepdims=True)


class VectorSum:
    def __init__(self, links, slots, total, stage, lands):
        self.total, self.stage, self.lands, self.length = total, stage, lands, links.length
        self.moves = [slots.move(links.device(axis), stage.at[number], lands.at[number], lands.at[number])
                      for number, axis in enumerate(("core", "x", "y"))]
        self.moves.append(Move(
            slots, [(links.device("z", way), stage.at[3], lands.at[2 + way]) for way in range(1, links.length)],
            lands.at[pl.ds(3, links.length - 1)]))

    def step(self, number):
        if 0 < number <= 4:
            self.moves[number - 1].wait()
            for land in ([number - 1] if number < 4 else range(3, 2 + self.length)):
                self.total[...] = self.total[...] + self.lands[land]
        if number < 4:
            self.stage[number] = self.total[...]
            self.moves[number].start()


class Rows:
    def __init__(self, links, slots, buffer, count, parts):
        self.moves, self.passed = [], []
        for begin, size in parts:
            def place(owner, begin=begin, size=size):
                return buffer.at[pl.ds(owner * count + begin, size)]

            self.moves.append([
                slots.move(links.device("x"), place(0), place(2), place(2)),
                slots.move(links.device("core"), place(0), place(1), place(1))])
            self.passed.append(slots.move(links.device("core"), place(2), place(3), place(3)))

    def send(self, part):
        for move in self.moves[part]:
            move.start()

    def near(self, part):
        self.moves[part][1].wait()

    def forward(self, part):
        self.moves[part][0].wait()
        self.passed[part].start()

    def far(self, part):
        self.passed[part].wait()


class Partials:
    def __init__(self, links, slots, stage, lands, count):
        def place(owner):
            return stage.at[pl.ds(owner * count, count)]

        self.place, self.lands = place, lands
        self.far = slots.move(links.device("core"), place(3), lands.at[0], lands.at[0])
        self.near = slots.move(links.device("core"), place(1), lands.at[1], lands.at[1])
        self.across = slots.move(links.device("x"), place(2), lands.at[2], lands.at[2])


def layer_kernel(length, scaling, counts, media, latents, grad_out, packed, query_shard, context_shard,
                 output_shard, up_shard, down_shard, latents_out, media_grad_out, latents_grad_out, sums_out, grads_out,
                 query_all, context_all, output_all, up_all, up_stage, down_all,
                 packed_all, vectors, media_in, latents_in, grad_in, context, key_value, query, attended, after,
                 feed, feed_t, branch, branch_t, pool, totals, after_lands, d_feed_lands, upstream_rows,
                 grad_up, grad_down, grad_query, grad_output, mask, sums, total, total_stage, total_lands,
                 own_rows_send, own_rows_land, lands_c, lands_b, lands_a, lands_z, result, send, recv, local):
    links = Links(length)
    z, y, x, rep = links.z, links.y, links.x, links.rep
    slots, locals_ = Slots(send, recv, pool), Locals(local)
    slot_count, patches, width = media.shape
    latent_count = latents.shape[1]
    key_count = patches + latent_count
    rows = slot_count * latent_count
    inner = query.shape[-1]
    chunks = length
    hidden = up_all.shape[-1]
    chunk = hidden // chunks
    unit = down_all.shape[-2]
    xy, yx = ("z", "x", "y"), ("z", "y", "x")

    def unit_columns(half, number):
        return pl.ds(pl.multiple_of(((2 * number + half) * 2 + rep) * unit, unit), unit)

    staged = [locals_.copy(packed, packed_all.at[z, y, x])]
    for shard, whole in ((context_shard, context_all), (query_shard, query_all), (output_shard, output_all)):
        half = whole.shape[-2]
        staged.append(locals_.copy(shard.at[pl.ds(pl.multiple_of(rep * half, 16), half)], whole.at[z, y, x, rep]))
    units = range(hidden // unit)
    staged.append(locals_.fill(
        [(up_shard.at[:, unit_columns(1 - x, n)], up_stage.at[:, pl.ds(n * unit, unit)]) for n in units], up_stage))
    staged.append(locals_.fill(
        [(up_shard.at[:, unit_columns(x, n)], up_all.at[z, y, x, :, pl.ds(n * unit, unit)]) for n in units],
        up_all.at[z, y, x]))
    staged.append(locals_.copy(down_shard.at[pl.ds(pl.multiple_of(rep * unit, 16), unit)], down_all.at[z, y]))
    grad_load = locals_.copy(grad_out, grad_in)
    latents_load = locals_.copy(latents, latents_in)
    media_load = locals_.copy(media, media_in)
    links.greet()

    def halves(whole, begin, size, order):
        def view(zi, yi, xi, half=rep):
            return whole.at[zi, yi, xi, half, :, pl.ds(begin, size)]

        return Gather(links, slots, view, order, True)

    slots.group = 0
    vector_gather = Gather(links, slots, lambda zi, yi, xi: packed_all.at[zi, yi, xi], xy, False)
    slots.group = 1
    gathers = [
        (halves(context_all, 0, width // 2, xy), (0, 1, 2, 3, 4)),
        (halves(context_all, width // 2, width // 2, yx), (0, 1, 2, 3, 4)),
        (halves(query_all, 0, inner, yx), (0, 2, 3, 4, 5)), (halves(output_all, 0, width, yx), (0, 2, 3, 4, 5)),
    ]
    slots.group = 2
    for number in range(2 * chunks):
        window = pl.ds(number % chunks * chunk, chunk)
        if number < chunks:
            def view(zi, yi, xi, window=window):
                return down_all.at[zi, yi, :, window]
        else:
            def view(zi, yi, xi, window=window):
                return up_all.at[zi, yi, ALL, :, window]
        ticks = (max(number - 1, 0), number + 2, number + 4)
        gathers.append((Gather(links, slots, view, ("z", "y"), False), ticks))
    up_across = slots.move(links.device("x"), up_stage, up_all.at[z, y, x], up_all.at[z, y, 1 - x])
    slots.group = 3
    parts = [(0, 2 * latent_count), (2 * latent_count, rows - 2 * latent_count)]
    branch_rows = Rows(links, slots, branch, rows, [(0, rows)])
    feed_rows = Rows(links, slots, feed, rows, parts)

    def pump(tick):
        run(gathers, tick)

    for copy in staged:
        copy.wait()
    vector_gather.step(0)
    pump(0)
    up_across.start()
    grad_load.wait()
    kept = jnp.where(lax.broadcasted_iota(jnp.int32, (rows, 1), 0) < counts[0] * latent_count, 1.0, 0.0)
    branch[:rows] = (grad_in[...].reshape(rows, width).astype(F32) * kept).astype(BF16)
    vector_gather.step(1)
    mask[...] = head_mask(latent_count, GROUP)
    sums[...] = jnp.zeros_like(sums)
    vector_gather.step(2)
    latents_load.wait()
    media_load.wait()
    pump(1)
    vector_gather.step(3)
    lane = packed_all.shape[-1]
    for zi in range(length):
        for yi in range(2):
            place = (zi * 2 + yi) * lane
            vectors[:, place:place + lane] = (packed_all[zi, yi, 0] + packed_all[zi, yi, 1]).astype(F32)[:8]

    def normalise_slot(j):
        context[j, :patches] = layer_norm(media_in[j].astype(F32), vectors[0:1], vectors[1:2]).astype(BF16)
        context[j, patches:] = layer_norm(latents_in[j].astype(F32), vectors[2:3], vectors[3:4]).astype(BF16)

    pl.loop(0, slot_count)(normalise_slot)
    pump(2)
    up_across.wait()
    pump(3)
    pump(4)
    branch_rows.send(0)

    def key_value_slot(j):
        key_value[j] = matmul(context[j], context_all[...].reshape(width, 2 * inner)).astype(BF16)

    pl.loop(0, 3)(key_value_slot)
    pump(5)
    pl.loop(3, slot_count)(key_value_slot)
    latent_normed = context[:, patches:, :].reshape(rows, width)
    query[...] = (matmul(latent_normed, query_all[...].reshape(width, inner)) * scaling).astype(BF16).reshape(
        slot_count, latent_count, inner)
    pump(6)

    def attention_slot(j):
        for begin in range(0, inner, GROUP):
            stacked = spread_heads(query[j, :, begin:begin + GROUP], mask[...].astype(BF16))
            probs = softmax(matmul_right(stacked, key_value[j, :, begin:begin + GROUP])).astype(BF16)
            value = matmul(probs, key_value[j, :, inner + begin:inner + begin + GROUP])
            attended[j, :, begin:begin + GROUP] = pick_heads(value, mask[...], latent_count).astype(BF16)

    for part, (begin, size) in enumerate(parts):
        first, last = begin // latent_count, (begin + size) // latent_count
        pl.loop(first, last)(attention_slot)
        after[begin:begin + size] = latents_in[first:last].reshape(size, width).astype(F32) + matmul(
            attended[first:last].reshape(size, inner), output_all[...].reshape(inner, width))
        feed[begin:begin + size] = layer_norm(
            after[begin:begin + size], vectors[4:5], vectors[5:6]).astype(BF16)
        feed_rows.send(part)
        pump(7 + part)
    slots.drain(0, grad_down.at[0, 0])
    branch_rows.near(0)
    branch_rows.forward(0)

    def turn(source, target, owner):
        def body(at):
            target[pl.ds(at, 256), pl.ds(owner * rows, 2 * rows)] = source[
                pl.ds(owner * rows, 2 * rows), pl.ds(at, 256)].T

        tiles(width // 256, 256, body)

    turn(branch, branch_t, 0)
    branch_rows.far(0)
    tall = rows
    d_active, active, d_hidden = [pool.at[pl.ds(n * 4 * rows, 4 * rows)] for n in range(3)]

    def d_active_tile(at):
        d_active[pl.ds(at, tall)] = matmul_right(
            branch[pl.ds(at, tall)], down_all[...].reshape(hidden, width)).astype(BF16)

    tiles(4, tall, d_active_tile)
    turn(branch, branch_t, 2)

    def hidden_tile(at, begin):
        window = pl.ds(begin, chunk)
        weight = up_all[:, :, :, :, window].reshape(width, chunk)
        value, slope = gelu_parts(matmul(feed[pl.ds(at, tall)], weight))
        active[pl.ds(at, tall), window] = value.astype(BF16)
        d_hidden[pl.ds(at, tall), window] = (d_active[pl.ds(at, tall), window].astype(F32) * slope).astype(BF16)

    def d_feed_of(owner):
        return matmul_right(d_hidden[pl.ds(owner * rows, rows)], up_all[...].reshape(width, hidden))

    def after_feed_of(owner):
        return matmul(active[pl.ds(owner * rows, rows)], down_all[...].reshape(hidden, width))

    def rounded(buffer, owner, value):
        buffer[pl.ds(owner * rows, rows)] = value.astype(BF16)

    def across_tile(back, buffer):
        rounded(buffer, 2, totals[1] + back.lands[0].astype(F32))

    up_result, down_result, query_result, context_result, output_result = result
    reductions = []

    def send_off(tick):
        run(reductions, tick)

    def plane_reduction(own, lands_y, lands, finish):
        return Reduce(links, slots, own, ("y",), [lands_y], lands, finish)

    def keep_up(value, window):
        up_result[0, :, window] = jnp.where(x == 0, value[0], value[1])
        own_rows_send[:, window] = jnp.where(x == 0, value[1], value[0]).astype(BF16)

    feed_rows.near(0)
    feed_rows.near(1)
    slots.group = 6
    for c in range(chunks):
        begin = c * chunk
        window = pl.ds(begin, chunk)
        tiles(2, tall, lambda at, begin=begin: hidden_tile(at, begin))
        if c == 0:
            pump(9)
            turn(feed, feed_t, 0)
            feed_rows.forward(0)
            feed_rows.forward(1)
            feed_rows.far(0)
            feed_rows.far(1)
            turn(feed, feed_t, 2)
        tiles(2, tall, lambda at, begin=begin: hidden_tile(pl.multiple_of(2 * rows + at, tall), begin))
        if c == chunks - 1:
            for group in range(1, 4):
                slots.drain(group)
            slots.group = 4
            d_feed_back = Partials(links, slots, feed, d_feed_lands, rows)
            slots.group = 5
            after_back = Partials(links, slots, branch, after_lands, rows)
            slots.group = 6
            rounded(feed, 3, d_feed_of(3))
            d_feed_back.far.start()
            totals[1] = d_feed_of(2)
            d_feed_back.far.wait()
            across_tile(d_feed_back, feed)
            d_feed_back.across.start()

        def grad_tile(number, window=window, c=c):
            size = width // 2
            place = pl.multiple_of(number * size, size)
            up = matmul(feed_t[pl.ds(place, size)], d_hidden[:, window]).astype(BF16)
            grad_up[pl.ds(number * (length // 2), length // 2), :, :, :, window] = up.reshape(
                length // 2, 2, 2, size // (2 * length), chunk)
            down = matmul(branch_t[pl.ds(place, size)], active[:, window]).astype(BF16)
            for owner in range(2):
                grad_down[c, owner, pl.ds(place, size)] = down[:, owner * unit:(owner + 1) * unit]

        pl.loop(0, 2)(grad_tile)
        reductions.append((plane_reduction(
            lambda zi, yi, xi, window=window: grad_up.at[zi, yi, ALL, :, window],
            lands_b[0].at[:, :, :, window], lands_z[0].at[:, :, :, window],
            functools.partial(keep_up, window=window)), (c, c + 3, c + 5)))
        if c == 0:
            pump(10)
        if c == chunks - 2:
            pump(11)
        send_off(c)
    part_size = width // chunks
    for number in range(chunks):
        window = pl.ds(number * part_size, part_size)

        def keep_down(value, window=window):
            down_result[:, window] = value.T

        reductions.append((plane_reduction(
            lambda zi, yi, xi, window=window: grad_down.at[zi, yi, window],
            lands_b[1].at[:, window], lands_z[1].at[:, window], keep_down),
            (chunks, chunks + 3 + number, chunks + 5 + number)))
    send_off(4)
    rounded(feed, 1, d_feed_of(1))
    d_feed_back.near.start()
    totals[0] = d_feed_of(0)

    rounded(branch, 3, after_feed_of(3))
    after_back.far.start()
    totals[1] = after_feed_of(2)
    after_back.far.wait()
    across_tile(after_back, branch)
    send_off(5)
    rounded(branch, 1, after_feed_of(1))
    after_back.near.start()
    totals[1] = after_feed_of(0)
    d_feed_back.near.wait()
    d_feed_back.across.wait()
    after_back.across.start()
    slots.drain(4)

    def fold(terms):
        return jnp.sum(terms.reshape(-1, 8, width), axis=0)

    d_feed = totals.at[0]
    flat_grad = lambda at, size: grad_in[pl.ds(lax.div(at, latent_count), size // latent_count)].reshape(size, width)

    def middle_tile(at, size=latent_count):
        own = pl.ds(at, size)
        upstream = d_feed[own] + d_feed_lands[1, own].astype(F32) + d_feed_lands[2, own].astype(F32)
        d_norm, gain_terms = layer_norm_back(after[own], vectors[4:5], upstream)
        sums[4] = sums[4] + fold(gain_terms)
        sums[5] = sums[5] + fold(upstream)
        row = lax.broadcasted_iota(jnp.int32, (size, 1), 0) + at
        keep = jnp.where(row < counts[0] * latent_count, 1.0, 0.0)
        d_middle = flat_grad(at, size).astype(F32) * keep + d_norm
        d_feed[own] = d_middle
        feed[own] = d_middle.astype(BF16)

    tiles(slot_count, latent_count, middle_tile)
    send_off(6)

    context_rows, output_rows = context_all.shape[-2], output_all.shape[-2]

    def context_own(zi, yi, xi, half):
        return up_all.at[zi, yi, xi, pl.ds(pl.multiple_of(half * context_rows, 16), context_rows)]

    def query_own(zi, yi, xi, half):
        return grad_query.at[zi, yi, xi, half]

    def output_own(zi, yi, xi, half):
        return grad_output.at[zi, yi, xi, half]

    def to_sibling(own, land):
        move = slots.move(links.device("core"), own(ALL, ALL, ALL, 1 - rep), land, land)
        move.start()

        def settle():
            move.wait()
            add_into(own(ALL, ALL, ALL, rep), land)

        return settle

    def halved_reduction(own, number, target, begin, size, *ticks):
        made = []
        for which, order in enumerate((("y", "x"), ("x", "y"))):
            window = pl.ds(begin + which * (size // 2), size // 2)

            def finish(value, window=window):
                target[:, window] = value

            made.append((Reduce(
                links, slots, lambda zi, yi, xi, window=window: own(zi, yi, xi, rep).at[..., window], order,
                [lands_b[number].at[:, :, :, window], lands_a[number].at[:, :, window]],
                lands_z[number].at[:, :, window], finish), ticks))
        return made

    d_branch = feed.at[pl.ds(0, rows)]
    output_block = inner // 2

    def output_grad_tile(number):
        place = pl.multiple_of(number * output_block, output_block)
        turned = attended[:, :, pl.ds(place, output_block)].reshape(rows, output_block).T
        value = matmul(turned, d_branch[...]).astype(BF16)
        grad_output[pl.ds(number * (length // 2), length // 2)] = value.reshape(
            length // 2, 2, 2, 2, output_rows, width)

    d_attended, d_query = upstream_rows[0], upstream_rows[1]
    d_attended[...] = matmul_right(d_branch[...], output_all[...].reshape(inner, width)).astype(BF16)
    send_off(7)

    def attention_back_slot(j):
        own = pl.ds(pl.multiple_of(j * latent_count, latent_count), latent_count)
        for begin in range(0, inner, GROUP):
            keys = key_value[j, :, begin:begin + GROUP]
            values = key_value[j, :, inner + begin:inner + begin + GROUP]
            low_mask = mask[...].astype(BF16)
            stacked = spread_heads(query[j, :, begin:begin + GROUP], low_mask)
            upstream = spread_heads(d_attended[own, begin:begin + GROUP], low_mask)
            probs = softmax(matmul_right(stacked, keys))
            d_probs = matmul_right(upstream, values)
            d_scores = (probs * (d_probs - jnp.sum(probs * d_probs, axis=-1, keepdims=True))).astype(BF16)
            d_query[own, begin:begin + GROUP] = (
                pick_heads(matmul(d_scores, keys), mask[...], latent_count).astype(BF16).astype(F32) * scaling
            ).astype(BF16)
            at = pl.ds(pl.multiple_of(j * key_count, 16), key_count)
            pool[at, begin:begin + GROUP] = matmul_left(d_scores, stacked).astype(BF16)
            pool[at, inner + begin:inner + begin + GROUP] = matmul_left(probs.astype(BF16), upstream).astype(BF16)

    pl.loop(0, 2)(attention_back_slot)
    pl.loop(0, 2)(output_grad_tile)
    settle_output = to_sibling(output_own, lands_c[2])
    pl.loop(2, 4)(attention_back_slot)
    settle_output()
    reductions.extend(halved_reduction(output_own, 4, output_result, 0, width, 8, 9, 10, 11))
    send_off(8)
    pl.loop(4, slot_count)(attention_back_slot)
    block = width // length

    def query_grad_tile(zi):
        place = pl.multiple_of(zi * block, block)
        turned = context[:, patches:, pl.ds(place, block)].reshape(rows, block).T
        value = matmul(turned, d_query[...]).astype(BF16)
        grad_query[zi] = value.reshape(2, 2, 2, context_rows, inner)

    pl.loop(0, length)(query_grad_tile)
    settle_query = to_sibling(query_own, lands_c[0])

    def context_grad_tile(zi):
        place = pl.multiple_of(zi * block, block)
        value = None
        for j in range(slot_count):
            turned = context[j, :, pl.ds(place, block)].T
            term = matmul(turned, pool[j * key_count:(j + 1) * key_count])
            value = term if value is None else value + term
        up_all[zi] = value.astype(BF16).reshape(2, 2, block // 4, 2 * inner)

    context_moves = []

    def settle_context(zi):
        context_moves[zi].wait()
        add_into(context_own(zi, ALL, ALL, rep), lands_c[1].at[zi])

    for zi in range(length):
        context_grad_tile(zi)
        land = lands_c[1].at[zi]
        context_moves.append(slots.move(links.device("core"), context_own(zi, ALL, ALL, 1 - rep), land, land))
        context_moves[-1].start()
        if zi == 1:
            settle_query()
            reductions.extend(halved_reduction(query_own, 2, query_result, 0, inner, 9, 10, 11, 12))
            send_off(9)
        if zi > 0:
            settle_context(zi - 1)
    settle_context(length - 1)
    reductions.extend(halved_reduction(context_own, 3, context_result, 0, inner, 10, 11, 12, 13))
    reductions.extend(halved_reduction(context_own, 3, context_result, inner, inner, 10, 12, 13, 14))
    send_off(10)
    slots.group = 7
    own_rows_move = slots.move(links.device("x"), own_rows_send, own_rows_land, own_rows_land)
    own_rows_move.start()
    after_back.near.wait()
    after_back.across.wait()
    slots.drain(5)
    branch[:rows] = ((after[...] + totals[1] + after_lands[1].astype(F32) + after_lands[2].astype(F32)) * kept).astype(BF16)
    written = [locals_.fill(
        [(branch.at[pl.ds(j * latent_count, latent_count)], latents_out.at[j]) for j in range(slot_count)], latents_out)]

    context_up = totals.at[1]

    def input_slot(j):
        at = pl.ds(pl.multiple_of(j * key_count, 16), key_count)
        own = pl.ds(pl.multiple_of(j * latent_count, latent_count), latent_count)
        context_up[...] = matmul_right(pool[at], context_all[...].reshape(width, 2 * inner))
        context_up[patches:] = context_up[patches:] + matmul_right(d_query[own], query_all[...].reshape(width, inner))

        def media_tile(at, size=patches // 2):
            tile = pl.ds(at, size)
            upstream = context_up[tile]
            value, gain_terms = layer_norm_back(media_in[j, tile].astype(F32), vectors[0:1], upstream)
            sums[0] = sums[0] + fold(gain_terms)
            sums[1] = sums[1] + fold(upstream)
            media_in[j, tile] = value.astype(BF16)

        tiles(2, patches // 2, media_tile)
        upstream = context_up[patches:]
        value, gain_terms = layer_norm_back(latents_in[j].astype(F32), vectors[2:3], upstream)
        sums[2] = sums[2] + fold(gain_terms)
        sums[3] = sums[3] + fold(upstream)
        latents_in[j] = (d_feed[own] + value).astype(BF16)

    pl.loop(0, 2)(input_slot)
    send_off(11)
    pl.loop(2, 3)(input_slot)
    send_off(12)
    own_rows_move.wait()
    up_result[1] = own_rows_land[...].astype(F32)

    def hand_over(numbers):
        for number in numbers:
            value, out = result[number], grads_out[number]
            written.append(locals_.copy(value, out.at[rep]))
            written.append(slots.move(links.device("core"), value, out.at[rep], out.at[1 - rep]))
            written[-1].start()

    hand_over((0, 1, 2, 4))
    pl.loop(3, slot_count)(input_slot)
    written.append(locals_.copy(media_in, media_grad_out))
    written.append(locals_.copy(latents_in, latents_grad_out))
    for number in range(6):
        total[number:number + 1] = jnp.sum(sums[number], axis=0, keepdims=True)
    total[6:] = jnp.zeros_like(total[6:])
    vector_sum = VectorSum(links, slots, total, total_stage, total_lands)
    vector_sum.step(0)
    send_off(13)
    vector_sum.step(1)
    vector_sum.step(2)
    send_off(14)
    hand_over((3,))
    vector_sum.step(3)
    vector_sum.step(4)
    sums_out[...] = total[...]
    for copy in written:
        copy.wait()
    slots.drain(6)
    slots.drain(7)


def layer(length, counts, media, latents, grad_out, packed, shards):
    query_shard, context_shard, output_shard, up_shard, down_shard = shards
    slot_count, patches, width = media.shape
    latent_count = latents.shape[1]
    key_count = patches + latent_count
    rows = slot_count * latent_count
    inner = query_shard.shape[1]
    unit = down_shard.shape[0] // 2
    hidden = up_shard.shape[1] // 4
    blocks = (length, 2, 2)

    def halved(shard):
        return blocks + (2, shard.shape[0] // 2, shard.shape[1])

    up_shape = blocks + (up_shard.shape[0], hidden)
    down_shape = (length, 2, unit, width)
    halves = [halved(s)[4:] for s in shards[:3]]
    results = [(2,) + up_shape[3:], (unit, width)] + halves
    anywhere = pl.BlockSpec(memory_space=pl.ANY)
    vmem = pl.BlockSpec(memory_space=pltpu.VMEM)
    sums_shape = (8, width)
    scratch = [
        pltpu.VMEM(halved(query_shard), BF16),
        pltpu.VMEM(halved(context_shard), BF16),
        pltpu.VMEM(halved(output_shard), BF16),
        pltpu.VMEM(up_shape, BF16),
        pltpu.VMEM(up_shape[3:], BF16),
        pltpu.VMEM(down_shape, BF16),
        pltpu.VMEM(blocks + packed.shape, BF16),
        pltpu.VMEM((8, width), F32),
        pltpu.VMEM(media.shape, BF16),
        pltpu.VMEM(latents.shape, BF16),
        pltpu.VMEM(grad_out.shape, BF16),
        pltpu.VMEM((slot_count, key_count, width), BF16),
        pltpu.VMEM((slot_count, key_count, 2 * inner), BF16),
        pltpu.VMEM((slot_count, latent_count, inner), BF16),
        pltpu.VMEM((slot_count, latent_count, inner), BF16),
        pltpu.VMEM((rows, width), F32),
        pltpu.VMEM((4 * rows, width), BF16),
        pltpu.VMEM((width, 4 * rows), BF16),
        pltpu.VMEM((4 * rows, width), BF16),
        pltpu.VMEM((width, 4 * rows), BF16),
        pltpu.VMEM((max(12 * rows, slot_count * key_count), hidden), BF16),
        pltpu.VMEM((2, rows, width), F32),
        pltpu.VMEM((3, rows, width), BF16),
        pltpu.VMEM((3, rows, width), BF16),
        [pltpu.VMEM((rows, inner), BF16)] * 2,
        pltpu.VMEM(up_shape, BF16),
        pltpu.VMEM((length, 2, width, unit), BF16),
        pltpu.VMEM(halved(query_shard), BF16),
        pltpu.VMEM(halved(output_shard), BF16),
        pltpu.VMEM((latent_count * (GROUP // HEAD_DIM), GROUP), F32),
        pltpu.VMEM((6, 8, width), F32),
        pltpu.VMEM(sums_shape, F32),
        pltpu.VMEM((4,) + sums_shape, F32),
        pltpu.VMEM((2 + length,) + sums_shape, F32),
        pltpu.VMEM(up_shape[3:], BF16),
        pltpu.VMEM(up_shape[3:], BF16),
        [pltpu.VMEM(blocks + h, BF16) for h in halves],
        [pltpu.VMEM((length, 2) + up_shape[3:], BF16), pltpu.VMEM((length, width, unit), BF16)]
        + [pltpu.VMEM((length, 2) + h, BF16) for h in halves],
        [None, None] + [pltpu.VMEM((length,) + h, BF16) for h in halves],
        [pltpu.VMEM((length - 1, 2) + up_shape[3:], BF16), pltpu.VMEM((length - 1, width, unit), BF16)]
        + [pltpu.VMEM((length - 1,) + h, BF16) for h in halves],
        [pltpu.VMEM(r, F32) for r in results],
        pltpu.SemaphoreType.DMA((8,)),
        pltpu.SemaphoreType.DMA((112,)),
        pltpu.SemaphoreType.DMA((24,)),
    ]
    out_shape = (
        jax.ShapeDtypeStruct(latents.shape, BF16), jax.ShapeDtypeStruct(media.shape, BF16),
        jax.ShapeDtypeStruct(latents.shape, BF16), jax.ShapeDtypeStruct(sums_shape, F32),
        [jax.ShapeDtypeStruct((2,) + r, F32) for r in results])
    return pl.pallas_call(
        functools.partial(layer_kernel, length, HEAD_DIM ** (-0.5)),
        out_shape=out_shape,
        in_specs=[pl.BlockSpec(memory_space=pltpu.SMEM)] + [anywhere] * 9,
        out_specs=(anywhere, anywhere, anywhere, vmem, [anywhere] * 5),
        scratch_shapes=scratch,
        compiler_params=pltpu.CompilerParams(
            collective_id=0, has_side_effects=True, vmem_limit_bytes=63 * 2 ** 20),
        name="resampler_layer",
    )(counts, media, latents, grad_out, packed, query_shard, context_shard, output_shard, up_shard, down_shard)


def finish_kernel(length, latents_raw, media_grad_raw, latents_grad_raw, grads_raw, latents_out, media_grad_out,
                  latents_grad_out, grads_out, held, held_grads, local):
    x = Links(length).x
    locals_ = Locals(local)
    raws = [latents_raw, latents_grad_raw, *grads_raw]
    stages = [held[0], held[1], *held_grads]
    outs = [latents_out, latents_grad_out, *grads_out]
    count = media_grad_raw.shape[0]
    for j in range(count):
        raws.append(media_grad_raw.at[j])
        stages.append(held[2].at[j])
        outs.append(media_grad_out.at[j])
    loads = [locals_.copy(raw, stage) for raw, stage in zip(raws, stages)]
    unit = grads_raw[1].shape[1]
    copies = []
    for number, (load, stage, out) in enumerate(zip(loads, stages, outs)):
        load.wait()
        if number != 2:
            copies.append(locals_.copy(stage, out))
            continue
        moves = []
        for core in range(2):
            for plane in range(2):
                half = x if plane == 0 else 1 - x
                for owner in range(stage.shape[-1] // unit):
                    begin = pl.multiple_of(((2 * owner + half) * 2 + core) * unit, unit)
                    moves.append((stage.at[core, plane, :, pl.ds(owner * unit, unit)], out.at[:, pl.ds(begin, unit)]))
        copies.append(locals_.fill(moves, out))
    for copy in copies:
        copy.wait()


def finish(length, latents_raw, media_grad_raw, latents_grad_raw, grads_raw):
    anywhere = pl.BlockSpec(memory_space=pl.ANY)
    up = grads_raw[0]
    shapes = [jax.ShapeDtypeStruct((up.shape[2], 4 * up.shape[3]), up.dtype)]
    shapes += [jax.ShapeDtypeStruct(g.shape, g.dtype) for g in grads_raw[1:]]
    same = [jax.ShapeDtypeStruct(r.shape, r.dtype) for r in (latents_raw, media_grad_raw, latents_grad_raw)]
    return pl.pallas_call(
        functools.partial(finish_kernel, length),
        out_shape=(*same, shapes),
        in_specs=[anywhere, anywhere, anywhere, [anywhere] * 5],
        out_specs=(anywhere, anywhere, anywhere, [anywhere] * 5),
        scratch_shapes=[
            [pltpu.VMEM(r.shape, r.dtype) for r in (latents_raw, latents_grad_raw, media_grad_raw)],
            [pltpu.VMEM(g.shape, g.dtype) for g in grads_raw],
            pltpu.SemaphoreType.DMA((2 * (7 + media_grad_raw.shape[0]),)),
        ],
        compiler_params=pltpu.CompilerParams(vmem_limit_bytes=60 * 2 ** 20),
        name="finish",
    )(latents_raw, media_grad_raw, latents_grad_raw, grads_raw)


def head_scores(first_heads, second_heads):
    return jnp.einsum(
        "bqhd,bkhd->bhqk", first_heads, second_heads, preferred_element_type=jnp.float32
    )


def collective_body(
    media,
    latents,
    image_counts,
    grad_out,
    media_gain,
    media_bias,
    latent_gain,
    latent_bias,
    feed_gain,
    feed_bias,
    query_weight,
    context_weight,
    output_weight,
    up_weight,
    down_weight,
):
    samples, slots, patches, model_width = media.shape
    latent_count = latents.shape[2]
    inner_width = query_weight.shape[1]
    head_count = inner_width // HEAD_DIM
    blocks = samples * slots
    key_count = patches + latent_count
    latent_total = blocks * latent_count
    scaling = HEAD_DIM ** (-0.5)
    vector_shards = (media_gain, media_bias, latent_gain, latent_bias, feed_gain, feed_bias)
    weight_shards = (query_weight, context_weight, output_weight, up_weight, down_weight)
    gathered = tuple(lax.all_gather(s, "dp", axis=0, tiled=True) for s in vector_shards + weight_shards)
    vectors = [element.astype(jnp.float32) for element in gathered[:6]]
    media_rows = media.reshape(blocks * patches, model_width).astype(jnp.float32)
    latent_rows = latents.reshape(latent_total, model_width).astype(jnp.float32)
    media_normed = layer_norm(media_rows, vectors[0], vectors[1]).astype(jnp.bfloat16)
    latent_normed = layer_norm(latent_rows, vectors[2], vectors[3]).astype(jnp.bfloat16)
    queries = (matmul(latent_normed, gathered[6]) * scaling).astype(jnp.bfloat16)
    context = jnp.concatenate(
        [
            media_normed.reshape(blocks, patches, model_width),
            latent_normed.reshape(blocks, latent_count, model_width),
        ],
        axis=1,
    ).reshape(blocks * key_count, model_width)
    key_value = (
        matmul(context, gathered[7])
        .astype(jnp.bfloat16)
        .reshape(blocks, key_count, 2 * inner_width)
    )
    query_heads = queries.reshape(blocks, latent_count, head_count, HEAD_DIM)
    key_heads = key_value[:, :, :inner_width].reshape(blocks, key_count, head_count, HEAD_DIM)
    value_heads = key_value[:, :, inner_width:].reshape(blocks, key_count, head_count, HEAD_DIM)
    scores = head_scores(query_heads, key_heads)
    row_max = jnp.max(scores, axis=-1, keepdims=True)
    exponent = jnp.exp(scores - row_max)
    row_total = jnp.sum(exponent, axis=-1, keepdims=True)
    log_total = row_max + jnp.log(row_total)
    attention_weights = (exponent / row_total).astype(jnp.bfloat16)
    attended = (
        jnp.einsum(
            "bhqk,bkhd->bqhd", attention_weights, value_heads, preferred_element_type=jnp.float32
        )
        .astype(jnp.bfloat16)
        .reshape(latent_total, inner_width)
    )
    after_attention = latent_rows + matmul(attended, gathered[8])
    feed_input = layer_norm(after_attention, vectors[4], vectors[5]).astype(jnp.bfloat16)
    hidden = matmul(feed_input, gathered[9])
    activated = gelu_exact(hidden).astype(jnp.bfloat16)
    after_feed = after_attention + matmul(activated, gathered[10])
    slot_mask = (
        lax.broadcasted_iota(jnp.int32, (samples, slots), 1) < image_counts[:, None]
    ).astype(jnp.float32)
    row_mask = jnp.broadcast_to(slot_mask[:, :, None], (samples, slots, latent_count)).reshape(
        latent_total, 1
    )
    latents_out = (after_feed * row_mask).astype(jnp.bfloat16).reshape(latents.shape)
    backward_set = gathered
    back_vectors = [element.astype(jnp.float32) for element in backward_set[:6]]
    d_after = grad_out.reshape(latent_total, model_width).astype(jnp.float32) * row_mask
    d_branch = d_after.astype(jnp.bfloat16)
    grad_down = matmul_left(activated, d_branch)
    d_activated = matmul_right(d_branch, backward_set[10])
    d_hidden = jax.vjp(gelu_exact, hidden)[1](d_activated)[0].astype(jnp.bfloat16)
    grad_up = matmul_left(feed_input, d_hidden)
    d_feed = matmul_right(d_hidden, backward_set[9])
    d_feed_norm, grad_feed_gain, grad_feed_bias = jax.vjp(
        layer_norm, after_attention, back_vectors[4], back_vectors[5]
    )[1](d_feed)
    d_middle = d_after + d_feed_norm
    d_out_branch = d_middle.astype(jnp.bfloat16)
    grad_output = matmul_left(attended, d_out_branch)
    d_attended = (
        matmul_right(d_out_branch, backward_set[8])
        .astype(jnp.bfloat16)
        .reshape(blocks, latent_count, head_count, HEAD_DIM)
    )
    recomputed = jnp.exp(head_scores(query_heads, key_heads) - log_total)
    d_weights = head_scores(d_attended, value_heads)
    d_scores = (
        recomputed * (d_weights - jnp.sum(recomputed * d_weights, axis=-1, keepdims=True))
    ).astype(jnp.bfloat16)
    d_queries = (
        jnp.einsum(
            "bhqk,bkhd->bqhd", d_scores, key_heads, preferred_element_type=jnp.float32
        ).astype(jnp.bfloat16)
        * scaling
    ).reshape(latent_total, inner_width)
    d_keys = jnp.einsum(
        "bhqk,bqhd->bkhd", d_scores, query_heads, preferred_element_type=jnp.float32
    ).astype(jnp.bfloat16)
    d_values = jnp.einsum(
        "bhqk,bqhd->bkhd",
        recomputed.astype(jnp.bfloat16),
        d_attended,
        preferred_element_type=jnp.float32,
    ).astype(jnp.bfloat16)
    d_key_value = jnp.concatenate(
        [
            d_keys.reshape(blocks, key_count, inner_width),
            d_values.reshape(blocks, key_count, inner_width),
        ],
        axis=-1,
    ).reshape(blocks * key_count, 2 * inner_width)
    grad_query = matmul_left(latent_normed, d_queries)
    grad_context = matmul_left(context, d_key_value)
    d_context = matmul_right(d_key_value, backward_set[7]).reshape(blocks, key_count, model_width)
    d_latent_normed = matmul_right(d_queries, backward_set[6]) + d_context[:, patches:, :].reshape(
        latent_total, model_width
    )
    d_media_normed = d_context[:, :patches, :].reshape(blocks * patches, model_width)
    d_latent_norm, grad_latent_gain, grad_latent_bias = jax.vjp(
        layer_norm, latent_rows, back_vectors[2], back_vectors[3]
    )[1](d_latent_normed)
    grad_latents = (d_middle + d_latent_norm).astype(jnp.bfloat16).reshape(latents.shape)
    d_media, grad_media_gain, grad_media_bias = jax.vjp(
        layer_norm, media_rows, back_vectors[0], back_vectors[1]
    )[1](d_media_normed)
    grad_media = d_media.astype(jnp.bfloat16).reshape(media.shape)
    vector_grads = jnp.stack([
        grad_media_gain, grad_media_bias, grad_latent_gain, grad_latent_bias, grad_feed_gain, grad_feed_bias])
    weight_grads = [
        g.astype(jnp.bfloat16) for g in (grad_query, grad_context, grad_output, grad_up, grad_down)]
    vector_sums = lax.psum_scatter(vector_grads, "dp", scatter_dimension=1, tiled=True)
    summed = [lax.psum_scatter(g, "dp", scatter_dimension=0, tiled=True) for g in weight_grads]
    owned = tuple(lax.psum(vector_sums, "rep")) + tuple(
        lax.psum(s, "rep").astype(jnp.float32) for s in summed)
    return (
        latents_out,
        grad_media,
        grad_latents,
        owned[0],
        owned[1],
        owned[2],
        owned[3],
        owned[4],
        owned[5],
        owned[6],
        owned[7],
        owned[8],
        owned[9],
        owned[10],
    )


def body(media, latents, image_counts, grad_out, *parameters):
    chips = lax.axis_size("dp")
    weight_shards = parameters[6:]
    tiled = (media.shape[0] == 1 and chips % 4 == 0 and chips > 4 and parameters[0].shape[0] == 64
             and all(s.shape[0] % 32 == 0 for s in weight_shards))
    if not tiled:
        return collective_body(media, latents, image_counts, grad_out, *parameters)
    side = lax.rem(lax.axis_index("dp"), 2)
    stacked = jnp.stack(parameters[:6])
    packed = jnp.pad(
        jnp.concatenate([jnp.where(side == 0, stacked, 0), jnp.where(side == 0, 0, stacked)], axis=1), ((0, 10), (0, 0)))
    latents_out, grad_media, grad_latents, vector_sums, summed = layer(
        chips // 4, image_counts, media[0], latents[0], grad_out[0], packed, weight_shards)
    latents_out, grad_media, grad_latents, summed = finish(
        chips // 4, latents_out, grad_media, grad_latents, summed)
    sums = [s.reshape(-1, s.shape[-1]) for s in summed[2:] + summed[:2]]
    width = parameters[0].shape[0]
    mine = lax.dynamic_slice(vector_sums, (0, lax.axis_index("dp") * width), (6, width))
    return (latents_out[None], grad_media[None], grad_latents[None]) + tuple(mine) + tuple(sums)


def solution(mesh):
    return jax.shard_map(
        body,
        mesh=mesh,
        in_specs=(
            P(("dp", "rep"), None, None, None),
            P(("dp", "rep"), None, None, None),
            P(("dp", "rep")),
            P(("dp", "rep"), None, None, None),
            P("dp"),
            P("dp"),
            P("dp"),
            P("dp"),
            P("dp"),
            P("dp"),
            P("dp", None),
            P("dp", None),
            P("dp", None),
            P("dp", None),
            P("dp", None),
        ),
        out_specs=(
            P(("dp", "rep"), None, None, None),
            P(("dp", "rep"), None, None, None),
            P(("dp", "rep"), None, None, None),
            P("dp"),
            P("dp"),
            P("dp"),
            P("dp"),
            P("dp"),
            P("dp"),
            P("dp", None),
            P("dp", None),
            P("dp", None),
            P("dp", None),
            P("dp", None),
        ),
        check_vma=False,
    )
```

```python
import functools

import jax
import jax.numpy as jnp
from jax import lax
from jax.experimental import pallas as pl
from jax.experimental.pallas import tpu as pltpu
from jax.sharding import PartitionSpec as P

HEAD_DIM = 64
GROUP = 256

epsilon = 1e-05

MESH = pl.DeviceIdType.MESH
ALL = slice(None)
F32 = jnp.float32
BF16 = jnp.bfloat16


class Links:
    def __init__(self, length):
        self.length = length
        self.dp = lax.axis_index("dp")
        self.rep = lax.axis_index("rep")
        self.z = lax.div(self.dp, 4)
        self.y = lax.rem(lax.div(self.dp, 2), 2)
        self.x = lax.rem(self.dp, 2)

    def device(self, axis, way=0):
        if axis == "core":
            return (self.dp, 1 - self.rep)
        if axis == "x":
            return (self.dp + 1 - 2 * self.x, self.rep)
        if axis == "y":
            return (self.dp + 2 - 4 * self.y, self.rep)
        return (self.dp + 4 * (self.along(way) - self.z), self.rep)

    def along(self, way):
        return lax.rem(self.z + way + self.length, self.length)

    def greet(self):
        barrier = pltpu.get_barrier_semaphore()
        peers = [("core", 0), ("x", 0), ("y", 0)] + [("z", way) for way in range(1, self.length)]
        for axis, way in peers:
            pl.semaphore_signal(barrier, inc=1, device_id=self.device(axis, way), device_id_type=MESH)
        pl.semaphore_wait(barrier, len(peers))


class Move:
    def __init__(self, slots, copies, landing):
        send, recv = slots.send.at[slots.group], slots.recv.at[slots.made]
        slots.made += 1
        self.slots, self.group, self.copies = slots, slots.group, [
            pltpu.make_async_remote_copy(
                src_ref=source, dst_ref=target, send_sem=send, recv_sem=recv,
                device_id=device, device_id_type=MESH)
            for device, source, target in copies]
        self.bytes = 0
        for _, source, _ in copies:
            size = jnp.dtype(source.dtype).itemsize
            for extent in source.shape:
                size *= extent
            self.bytes += size
        self.into = pltpu.make_async_remote_copy(
            src_ref=landing, dst_ref=landing, send_sem=send, recv_sem=recv,
            device_id=copies[0][0], device_id_type=MESH)

    def start(self):
        for copy in self.copies:
            copy.start()
        self.slots.sent[self.group] += self.bytes

    def wait(self):
        self.into.wait_recv()


class Slots:
    def __init__(self, send, recv, ruler):
        self.send, self.recv, self.ruler, self.made, self.group = send, recv, ruler, 0, 0
        self.sent = [0] * send.shape[0]

    def move(self, device, source, target, landing):
        return Move(self, [(device, source, target)], landing)

    def drain(self, group, ruler=None):
        ruler = self.ruler if ruler is None else ruler
        row = ruler.shape[-1] * jnp.dtype(ruler.dtype).itemsize
        rows, rest = divmod(self.sent[group], row)
        assert rest == 0 and rows % 16 == 0 and rows <= ruler.shape[0]
        whole = ruler.at[pl.ds(0, rows)]
        pltpu.make_async_copy(whole, whole, self.send.at[group]).wait()


class Locals:
    def __init__(self, semaphores):
        self.semaphores, self.made = semaphores, 0

    def copy(self, source, target):
        return self.fill([(source, target)], target)

    def fill(self, copies, whole):
        semaphore = self.semaphores.at[self.made]
        self.made += 1
        for source, target in copies:
            pltpu.make_async_copy(source, target, semaphore).start()
        return pltpu.make_async_copy(whole, whole, semaphore)


class Gather:
    def __init__(self, links, slots, view, axes, halved):
        here = {"z": links.z, "y": links.y, "x": links.x}
        self.moves = []
        for axis in axes:
            mine = view(here["z"], here["y"], here["x"])
            if axis == "z":
                self.moves.append(Move(
                    slots, [(links.device("z", way), mine, mine) for way in range(1, links.length)],
                    view(pl.ds(0, links.length - 1), here["y"], here["x"])))
            else:
                other = dict(here)
                other[axis] = 1 - here[axis]
                self.moves.append(
                    slots.move(links.device(axis), mine, mine, view(other["z"], other["y"], other["x"])))
            here[axis] = ALL
        if halved:
            mine = view(ALL, ALL, ALL)
            self.moves.append(
                slots.move(links.device("core"), mine, mine, view(ALL, ALL, ALL, 1 - links.rep)))

    def step(self, number):
        if 0 < number <= len(self.moves):
            self.moves[number - 1].wait()
        if 0 <= number < len(self.moves):
            self.moves[number].start()


class Reduce:
    def __init__(self, links, slots, own, axes, lands, lands_z, finish):
        self.own, self.links, self.finish, self.lands_z = own, links, finish, lands_z
        self.moves, self.adds = [], []
        z, y, x = links.z, links.y, links.x
        here = {"z": ALL, "y": ALL, "x": ALL}
        for axis, land in zip(axes, lands):
            away, home = dict(here), dict(here)
            place = {"y": y, "x": x}[axis]
            away[axis], home[axis] = 1 - place, place
            self.moves.append(slots.move(
                links.device(axis), own(away["z"], away["y"], away["x"]), land, land))
            here = home
            self.adds.append(functools.partial(add_into, own(home["z"], home["y"], home["x"]), land))
        self.moves.append(Move(
            slots, [(links.device("z", way), own(links.along(way), here["y"], here["x"]), lands_z.at[way - 1])
                    for way in range(1, links.length)], lands_z))
        self.mine = own(z, here["y"], here["x"])
        self.adds.append(self.end)

    def step(self, number):
        if 0 < number <= len(self.moves):
            self.moves[number - 1].wait()
            self.adds[number - 1]()
        if 0 <= number < len(self.moves):
            self.moves[number].start()

    def end(self):
        total = self.mine[...].astype(F32)
        for way in range(1, self.links.length):
            total = total + self.lands_z[way - 1].astype(F32)
        self.finish(total)


def add_into(target, arrived):
    @pl.loop(0, target.shape[0])
    def _(number):
        target[number] = (target[number].astype(F32) + arrived[number].astype(F32)).astype(target.dtype)


def run(table, tick):
    for item, ticks in table:
        if tick in ticks:
            item.step(ticks.index(tick))


def matmul(left, right):
    return jnp.dot(left, right, preferred_element_type=F32)


def matmul_left(left, right):
    return lax.dot_general(left, right, (((0,), (0,)), ((), ())), preferred_element_type=F32)


def matmul_right(left, right):
    return lax.dot_general(left, right, (((1,), (1,)), ((), ())), preferred_element_type=F32)


def layer_norm(values, gain, offset):
    centre = jnp.mean(values, axis=-1, keepdims=True)
    shifted = values - centre
    spread = jnp.mean(shifted * shifted, axis=-1, keepdims=True)
    return shifted * lax.rsqrt(spread + epsilon) * gain + offset


def layer_norm_back(values, gain, upstream):
    centre = jnp.mean(values, axis=-1, keepdims=True)
    shifted = values - centre
    spread = jnp.mean(shifted * shifted, axis=-1, keepdims=True)
    rate = lax.rsqrt(spread + epsilon)
    normed = shifted * rate
    scaled = upstream * gain
    first = jnp.mean(scaled, axis=-1, keepdims=True)
    second = jnp.mean(scaled * normed, axis=-1, keepdims=True)
    return rate * (scaled - first - normed * second), upstream * normed


def gelu_exact(values):
    return 0.5 * values * (1.0 + jax.scipy.special.erf(values * 0.7071067811865476))


def gelu_parts(values):
    cumulative = 0.5 * (1.0 + lax.erf(values * 0.7071067811865476))
    density = 0.3989422804014327 * jnp.exp(-0.5 * values * values)
    return values * cumulative, cumulative + values * density


def tiles(count, size, action):
    @pl.loop(0, count)
    def _(number):
        action(pl.multiple_of(number * size, size))


def head_mask(rows, columns):
    heads = columns // HEAD_DIM
    row = lax.broadcasted_iota(jnp.int32, (rows * heads, columns), 0)
    column = lax.broadcasted_iota(jnp.int32, (rows * heads, columns), 1)
    head_row = jnp.zeros_like(row)
    head_column = jnp.zeros_like(row)
    for head in range(1, heads):
        head_row = head_row + jnp.where(row >= head * rows, 1, 0)
        head_column = head_column + jnp.where(column >= head * HEAD_DIM, 1, 0)
    return jnp.where(head_row == head_column, 1.0, 0.0)


def spread_heads(rows, mask):
    return jnp.concatenate([rows] * (mask.shape[0] // rows.shape[0]), axis=0) * mask


def pick_heads(stacked, mask, rows):
    kept = stacked * mask
    total = kept[:rows]
    for head in range(1, stacked.shape[0] // rows):
        total = total + kept[head * rows:(head + 1) * rows]
    return total


def softmax(scores):
    exponent = jnp.exp(scores - jnp.max(scores, axis=-1, keepdims=True))
    return exponent / jnp.sum(exponent, axis=-1, keepdims=True)


class VectorSum:
    def __init__(self, links, slots, total, stage, lands):
        self.total, self.stage, self.lands, self.length = total, stage, lands, links.length
        self.moves = [slots.move(links.device(axis), stage.at[number], lands.at[number], lands.at[number])
                      for number, axis in enumerate(("core", "x", "y"))]
        self.moves.append(Move(
            slots, [(links.device("z", way), stage.at[3], lands.at[2 + way]) for way in range(1, links.length)],
            lands.at[pl.ds(3, links.length - 1)]))

    def step(self, number):
        if 0 < number <= 4:
            self.moves[number - 1].wait()
            for land in ([number - 1] if number < 4 else range(3, 2 + self.length)):
                self.total[...] = self.total[...] + self.lands[land]
        if number < 4:
            self.stage[number] = self.total[...]
            self.moves[number].start()


class Rows:
    def __init__(self, links, slots, buffer, count, parts):
        self.moves, self.passed = [], []
        for begin, size in parts:
            def place(owner, begin=begin, size=size):
                return buffer.at[pl.ds(owner * count + begin, size)]

            self.moves.append([
                slots.move(links.device("x"), place(0), place(2), place(2)),
                slots.move(links.device("core"), place(0), place(1), place(1))])
            self.passed.append(slots.move(links.device("core"), place(2), place(3), place(3)))

    def send(self, part):
        for move in self.moves[part]:
            move.start()

    def near(self, part):
        self.moves[part][1].wait()

    def forward(self, part):
        self.moves[part][0].wait()
        self.passed[part].start()

    def far(self, part):
        self.passed[part].wait()


class Partials:
    def __init__(self, links, slots, stage, lands, count):
        def place(owner):
            return stage.at[pl.ds(owner * count, count)]

        self.place, self.lands = place, lands
        self.far = slots.move(links.device("core"), place(3), lands.at[0], lands.at[0])
        self.near = slots.move(links.device("core"), place(1), lands.at[1], lands.at[1])
        self.across = slots.move(links.device("x"), place(2), lands.at[2], lands.at[2])


def layer_kernel(length, scaling, counts, media, latents, grad_out, packed, query_shard, context_shard,
                 output_shard, up_shard, down_shard, latents_out, media_grad_out, latents_grad_out, sums_out, grads_out,
                 query_all, context_all, output_all, up_all, down_all,
                 packed_all, vectors, media_in, latents_in, grad_in, context, key_value, query, attended, after,
                 feed, feed_t, branch, branch_t, pool, totals, after_lands, d_feed_lands,
                 grad_up, grad_down, grad_query, grad_output, mask, sums, total, total_stage, total_lands,
                 own_rows_send, own_rows_land, lands_c, lands_b, lands_a, lands_z, result, send, recv, local):
    links = Links(length)
    z, y, x, rep = links.z, links.y, links.x, links.rep
    slots, locals_ = Slots(send, recv, pool), Locals(local)
    slot_count, patches, width = media.shape
    latent_count = latents.shape[1]
    key_count = patches + latent_count
    rows = slot_count * latent_count
    inner = query.shape[-1]
    chunks = length
    hidden = up_all.shape[-1]
    chunk = hidden // chunks
    unit = down_all.shape[-2]
    xy, yx = ("z", "x", "y"), ("z", "y", "x")

    def unit_columns(half, number):
        return pl.ds(pl.multiple_of(((2 * number + half) * 2 + rep) * unit, unit), unit)

    staged = [locals_.copy(packed, packed_all.at[z, y, x])]
    for shard, whole in ((context_shard, context_all), (query_shard, query_all), (output_shard, output_all)):
        half = whole.shape[-2]
        staged.append(locals_.copy(shard.at[pl.ds(pl.multiple_of(rep * half, 16), half)], whole.at[z, y, x, rep]))
    units = range(hidden // unit)
    staged.append(locals_.fill(
        [(up_shard.at[:, unit_columns(1 - x, n)], own_rows_send.at[:, pl.ds(n * unit, unit)]) for n in units],
        own_rows_send))
    staged.append(locals_.fill(
        [(up_shard.at[:, unit_columns(x, n)], up_all.at[z, y, x, :, pl.ds(n * unit, unit)]) for n in units],
        up_all.at[z, y, x]))
    staged.append(locals_.copy(down_shard.at[pl.ds(pl.multiple_of(rep * unit, 16), unit)], down_all.at[z, y]))
    grad_load = locals_.copy(grad_out, grad_in)
    latents_load = locals_.copy(latents, latents_in)
    media_load = locals_.copy(media, media_in)
    links.greet()

    def halves(whole, begin, size, order):
        def view(zi, yi, xi, half=rep):
            return whole.at[zi, yi, xi, half, :, pl.ds(begin, size)]

        return Gather(links, slots, view, order, True)

    slots.group = 0
    vector_gather = Gather(links, slots, lambda zi, yi, xi: packed_all.at[zi, yi, xi], xy, False)
    slots.group = 1
    gathers = [
        (halves(context_all, 0, width // 2, xy), (0, 1, 2, 3, 4)),
        (halves(context_all, width // 2, width // 2, yx), (0, 1, 2, 3, 4)),
        (halves(query_all, 0, inner, yx), (0, 2, 3, 4, 5)), (halves(output_all, 0, width, yx), (0, 2, 3, 4, 5)),
    ]
    slots.group = 2
    for number in range(2 * chunks):
        window = pl.ds(number % chunks * chunk, chunk)
        if number < chunks:
            def view(zi, yi, xi, window=window):
                return down_all.at[zi, yi, :, window]
        else:
            def view(zi, yi, xi, window=window):
                return up_all.at[zi, yi, ALL, :, window]
        ticks = (max(number - 1, 0), number + 2, number + 4)
        gathers.append((Gather(links, slots, view, ("z", "y"), False), ticks))
    up_across = slots.move(links.device("x"), own_rows_send, up_all.at[z, y, x], up_all.at[z, y, 1 - x])
    slots.group = 3
    parts = [(0, 2 * latent_count), (2 * latent_count, rows - 2 * latent_count)]
    branch_rows = Rows(links, slots, branch, rows, [(0, rows)])
    feed_rows = Rows(links, slots, feed, rows, parts)

    def pump(tick):
        run(gathers, tick)

    for copy in staged:
        copy.wait()
    vector_gather.step(0)
    pump(0)
    up_across.start()
    grad_load.wait()
    kept = jnp.where(lax.broadcasted_iota(jnp.int32, (rows, 1), 0) < counts[0] * latent_count, 1.0, 0.0)
    branch[:rows] = (grad_in[...].reshape(rows, width).astype(F32) * kept).astype(BF16)
    vector_gather.step(1)
    mask[...] = head_mask(latent_count, GROUP)
    sums[...] = jnp.zeros_like(sums)
    vector_gather.step(2)
    latents_load.wait()
    media_load.wait()
    pump(1)
    vector_gather.step(3)
    lane = packed_all.shape[-1]
    for zi in range(length):
        for yi in range(2):
            place = (zi * 2 + yi) * lane
            vectors[:, place:place + lane] = (packed_all[zi, yi, 0] + packed_all[zi, yi, 1]).astype(F32)[:8]

    def normalise_slot(j):
        context[j, :patches] = layer_norm(media_in[j].astype(F32), vectors[0:1], vectors[1:2]).astype(BF16)
        context[j, patches:] = layer_norm(latents_in[j].astype(F32), vectors[2:3], vectors[3:4]).astype(BF16)

    pl.loop(0, slot_count)(normalise_slot)
    pump(2)
    up_across.wait()
    pump(3)
    pump(4)
    branch_rows.send(0)

    def key_value_slot(j):
        key_value[j] = matmul(context[j], context_all[...].reshape(width, 2 * inner)).astype(BF16)

    pl.loop(0, 3)(key_value_slot)
    pump(5)
    pl.loop(3, slot_count)(key_value_slot)
    latent_normed = context[:, patches:, :].reshape(rows, width)
    query[...] = (matmul(latent_normed, query_all[...].reshape(width, inner)) * scaling).astype(BF16).reshape(
        slot_count, latent_count, inner)
    pump(6)

    def attention_slot(j):
        for begin in range(0, inner, GROUP):
            stacked = spread_heads(query[j, :, begin:begin + GROUP], mask[...].astype(BF16))
            probs = softmax(matmul_right(stacked, key_value[j, :, begin:begin + GROUP])).astype(BF16)
            value = matmul(probs, key_value[j, :, inner + begin:inner + begin + GROUP])
            attended[j, :, begin:begin + GROUP] = pick_heads(value, mask[...], latent_count).astype(BF16)

    for part, (begin, size) in enumerate(parts):
        first, last = begin // latent_count, (begin + size) // latent_count
        pl.loop(first, last)(attention_slot)
        after[begin:begin + size] = latents_in[first:last].reshape(size, width).astype(F32) + matmul(
            attended[first:last].reshape(size, inner), output_all[...].reshape(inner, width))
        feed[begin:begin + size] = layer_norm(
            after[begin:begin + size], vectors[4:5], vectors[5:6]).astype(BF16)
        feed_rows.send(part)
        pump(7 + part)
    slots.drain(0, grad_down.at[0, 0])
    branch_rows.near(0)
    branch_rows.forward(0)

    def turn(source, target, owner):
        def body(at):
            target[pl.ds(at, 256), pl.ds(owner * rows, 2 * rows)] = source[
                pl.ds(owner * rows, 2 * rows), pl.ds(at, 256)].T

        tiles(width // 256, 256, body)

    turn(branch, branch_t, 0)
    branch_rows.far(0)
    tall = rows
    d_active, active, d_hidden = [pool.at[pl.ds(n * 4 * rows, 4 * rows)] for n in range(3)]

    def d_active_tile(at):
        d_active[pl.ds(at, tall)] = matmul_right(
            branch[pl.ds(at, tall)], down_all[...].reshape(hidden, width)).astype(BF16)

    tiles(4, tall, d_active_tile)
    turn(branch, branch_t, 2)

    def hidden_tile(at, begin):
        window = pl.ds(begin, chunk)
        weight = up_all[:, :, :, :, window].reshape(width, chunk)
        value, slope = gelu_parts(matmul(feed[pl.ds(at, tall)], weight))
        active[pl.ds(at, tall), window] = value.astype(BF16)
        d_hidden[pl.ds(at, tall), window] = (d_active[pl.ds(at, tall), window].astype(F32) * slope).astype(BF16)

    def d_feed_of(owner):
        return matmul_right(d_hidden[pl.ds(owner * rows, rows)], up_all[...].reshape(width, hidden))

    def after_feed_of(owner):
        return matmul(active[pl.ds(owner * rows, rows)], down_all[...].reshape(hidden, width))

    def rounded(buffer, owner, value):
        buffer[pl.ds(owner * rows, rows)] = value.astype(BF16)

    def across_tile(back, buffer):
        rounded(buffer, 2, totals[1] + back.lands[0].astype(F32))

    up_result, down_result, query_result, context_result, output_result = result
    reductions = []

    def send_off(tick):
        run(reductions, tick)

    def plane_reduction(own, lands_y, lands, finish):
        return Reduce(links, slots, own, ("y",), [lands_y], lands, finish)

    def keep_up(value, window):
        up_result[0, :, window] = jnp.where(x == 0, value[0], value[1])
        own_rows_send[:, window] = jnp.where(x == 0, value[1], value[0]).astype(BF16)

    feed_rows.near(0)
    feed_rows.near(1)
    slots.group = 6

    def near_hidden(c):
        tiles(2, tall, lambda at: hidden_tile(at, c * chunk))

    def far_hidden(c):
        tiles(2, tall, lambda at: hidden_tile(pl.multiple_of(2 * rows + at, tall), c * chunk))

    def grads(c):
        window = pl.ds(c * chunk, chunk)

        def grad_tile(number):
            size = width // 2
            place = pl.multiple_of(number * size, size)
            up = matmul(feed_t[pl.ds(place, size)], d_hidden[:, window]).astype(BF16)
            grad_up[pl.ds(number * (length // 2), length // 2), :, :, :, window] = up.reshape(
                length // 2, 2, 2, size // (2 * length), chunk)
            down = matmul(branch_t[pl.ds(place, size)], active[:, window]).astype(BF16)
            for owner in range(2):
                grad_down[c, owner, pl.ds(place, size)] = down[:, owner * unit:(owner + 1) * unit]

        pl.loop(0, 2)(grad_tile)
        reductions.append((plane_reduction(
            lambda zi, yi, xi: grad_up.at[zi, yi, ALL, :, window],
            lands_b[0].at[:, :, :, window], lands_z[0].at[:, :, :, window],
            functools.partial(keep_up, window=window)), (c, c + 2, c + 4)))
        send_off(c)

    near_hidden(0)
    pump(9)
    turn(feed, feed_t, 0)
    feed_rows.forward(0)
    feed_rows.forward(1)
    feed_rows.far(0)
    feed_rows.far(1)
    turn(feed, feed_t, 2)
    far_hidden(0)
    grads(0)
    near_hidden(1)
    far_hidden(1)
    pump(10)
    near_hidden(2)
    far_hidden(2)
    grads(1)
    for c in range(3, chunks):
        pump(8 + c)
        near_hidden(c)
        far_hidden(c)
    for group in range(1, 4):
        slots.drain(group)
    slots.group = 4
    d_feed_back = Partials(links, slots, feed, d_feed_lands, rows)
    slots.group = 5
    after_back = Partials(links, slots, branch, after_lands, rows)
    slots.group = 6
    rounded(feed, 3, d_feed_of(3))
    d_feed_back.far.start()
    totals[1] = d_feed_of(2)
    d_feed_back.far.wait()
    across_tile(d_feed_back, feed)
    d_feed_back.across.start()
    for c in range(2, chunks):
        grads(c)
    part_size = width // chunks
    for number in range(chunks):
        window = pl.ds(number * part_size, part_size)

        def keep_down(value, window=window):
            down_result[:, window] = value.T

        reductions.append((plane_reduction(
            lambda zi, yi, xi, window=window: grad_down.at[zi, yi, window],
            lands_b[1].at[:, window], lands_z[1].at[:, window], keep_down),
            (chunks, chunks + 2 + number, chunks + 4 + number) if number < chunks - 1 else (chunks, 10, 12)))
    send_off(4)
    rounded(feed, 1, d_feed_of(1))
    d_feed_back.near.start()
    totals[0] = d_feed_of(0)

    rounded(branch, 3, after_feed_of(3))
    after_back.far.start()
    totals[1] = after_feed_of(2)
    after_back.far.wait()
    across_tile(after_back, branch)
    send_off(5)
    rounded(branch, 1, after_feed_of(1))
    after_back.near.start()
    totals[1] = after_feed_of(0)
    d_feed_back.near.wait()
    d_feed_back.across.wait()
    after_back.across.start()
    slots.drain(4)

    def fold(terms):
        return jnp.sum(terms.reshape(-1, 8, width), axis=0)

    d_feed = totals.at[0]
    flat_grad = lambda at, size: grad_in[pl.ds(lax.div(at, latent_count), size // latent_count)].reshape(size, width)

    def middle_tile(at, size=latent_count):
        own = pl.ds(at, size)
        upstream = d_feed[own] + d_feed_lands[1, own].astype(F32) + d_feed_lands[2, own].astype(F32)
        d_norm, gain_terms = layer_norm_back(after[own], vectors[4:5], upstream)
        sums[4] = sums[4] + fold(gain_terms)
        sums[5] = sums[5] + fold(upstream)
        row = lax.broadcasted_iota(jnp.int32, (size, 1), 0) + at
        keep = jnp.where(row < counts[0] * latent_count, 1.0, 0.0)
        d_middle = flat_grad(at, size).astype(F32) * keep + d_norm
        d_feed[own] = d_middle
        feed[own] = d_middle.astype(BF16)

    tiles(slot_count, latent_count, middle_tile)

    context_rows, output_rows = context_all.shape[-2], output_all.shape[-2]

    def context_own(zi, yi, xi, half):
        return up_all.at[zi, yi, xi, pl.ds(pl.multiple_of(half * context_rows, 16), context_rows)]

    def query_own(zi, yi, xi, half):
        return grad_query.at[zi, yi, xi, half]

    def output_own(zi, yi, xi, half):
        return grad_output.at[zi, yi, xi, half]

    def to_sibling(own, land):
        move = slots.move(links.device("core"), own(ALL, ALL, ALL, 1 - rep), land, land)
        move.start()

        def settle():
            move.wait()
            add_into(own(ALL, ALL, ALL, rep), land)

        return settle

    def halved_reduction(own, number, target, begin, size, first, *ticks):
        made = []
        for which, order in enumerate((first, ("x", "y"))):
            window = pl.ds(begin + which * (size // 2), size // 2)

            def finish(value, window=window):
                target[:, window] = value

            made.append((Reduce(
                links, slots, lambda zi, yi, xi, window=window: own(zi, yi, xi, rep).at[..., window], order,
                [lands_b[number].at[:, :, :, window], lands_a[number].at[:, :, window]],
                lands_z[number].at[:, :, window], finish), ticks))
        return made

    d_branch = feed.at[pl.ds(0, rows)]
    output_block = inner // 2

    def output_grad_tile(number):
        place = pl.multiple_of(number * output_block, output_block)
        turned = attended[:, :, pl.ds(place, output_block)].reshape(rows, output_block).T
        value = matmul(turned, d_branch[...]).astype(BF16)
        grad_output[pl.ds(number * (length // 2), length // 2)] = value.reshape(
            length // 2, 2, 2, 2, output_rows, width)

    d_attended, d_query = grad_in.at[:, :, pl.ds(0, inner)], grad_in.at[:, :, pl.ds(inner, inner)]
    d_attended[...] = matmul_right(d_branch[...], output_all[...].reshape(inner, width)).astype(BF16).reshape(
        slot_count, latent_count, inner)

    def attention_back_slot(j):
        own = pl.ds(pl.multiple_of(j * latent_count, latent_count), latent_count)
        for begin in range(0, inner, GROUP):
            keys = key_value[j, :, begin:begin + GROUP]
            values = key_value[j, :, inner + begin:inner + begin + GROUP]
            low_mask = mask[...].astype(BF16)
            stacked = spread_heads(query[j, :, begin:begin + GROUP], low_mask)
            upstream = spread_heads(d_attended[j, :, begin:begin + GROUP], low_mask)
            probs = softmax(matmul_right(stacked, keys))
            d_probs = matmul_right(upstream, values)
            d_scores = (probs * (d_probs - jnp.sum(probs * d_probs, axis=-1, keepdims=True))).astype(BF16)
            d_query[j, :, begin:begin + GROUP] = (
                pick_heads(matmul(d_scores, keys), mask[...], latent_count).astype(BF16).astype(F32) * scaling
            ).astype(BF16)
            at = pl.ds(pl.multiple_of(j * key_count, 16), key_count)
            pool[at, begin:begin + GROUP] = matmul_left(d_scores, stacked).astype(BF16)
            pool[at, inner + begin:inner + begin + GROUP] = matmul_left(probs.astype(BF16), upstream).astype(BF16)

    pl.loop(0, 2)(attention_back_slot)
    send_off(6)
    pl.loop(0, 2)(output_grad_tile)
    settle_output = to_sibling(output_own, lands_c[2])
    pl.loop(2, 4)(attention_back_slot)
    settle_output()
    reductions.extend(halved_reduction(output_own, 4, output_result, 0, width, ("x", "y"), 7, 9, 10, 11))
    send_off(7)
    pl.loop(4, slot_count)(attention_back_slot)
    block = width // length

    def query_grad_tile(zi):
        place = pl.multiple_of(zi * block, block)
        turned = context[:, patches:, pl.ds(place, block)].reshape(rows, block).T
        value = matmul(turned, d_query[...].reshape(rows, inner)).astype(BF16)
        grad_query[zi] = value.reshape(2, 2, 2, context_rows, inner)

    pl.loop(0, length)(query_grad_tile)
    settle_query = to_sibling(query_own, lands_c[0])

    def context_grad_tile(zi):
        place = pl.multiple_of(zi * block, block)
        value = None
        for j in range(slot_count):
            turned = context[j, :, pl.ds(place, block)].T
            term = matmul(turned, pool[j * key_count:(j + 1) * key_count])
            value = term if value is None else value + term
        up_all[zi] = value.astype(BF16).reshape(2, 2, block // 4, 2 * inner)

    context_moves = []

    def settle_context(zi):
        context_moves[zi].wait()
        add_into(context_own(zi, ALL, ALL, rep), lands_c[1].at[zi])

    for zi in range(length):
        context_grad_tile(zi)
        land = lands_c[1].at[zi]
        context_moves.append(slots.move(links.device("core"), context_own(zi, ALL, ALL, 1 - rep), land, land))
        context_moves[-1].start()
        if zi == 1:
            settle_query()
            reductions.extend(halved_reduction(query_own, 2, query_result, 0, inner, ("x", "y"), 8, 10, 11, 12))
            send_off(8)
        if zi > 0:
            settle_context(zi - 1)
    settle_context(length - 1)
    reductions.extend(halved_reduction(context_own, 3, context_result, 0, inner, ("y", "x"), 9, 11, 12, 13))
    reductions.extend(halved_reduction(context_own, 3, context_result, inner, inner, ("y", "x"), 9, 12, 13, 14))
    send_off(9)
    slots.group = 7
    own_rows_move = slots.move(links.device("x"), own_rows_send, own_rows_land, own_rows_land)
    own_rows_move.start()
    after_back.near.wait()
    after_back.across.wait()
    slots.drain(5)
    branch[:rows] = ((after[...] + totals[1] + after_lands[1].astype(F32) + after_lands[2].astype(F32)) * kept).astype(BF16)
    written = [locals_.fill(
        [(branch.at[pl.ds(j * latent_count, latent_count)], latents_out.at[j]) for j in range(slot_count)], latents_out)]

    context_up = totals.at[1]

    def input_slot(j):
        at = pl.ds(pl.multiple_of(j * key_count, 16), key_count)
        own = pl.ds(pl.multiple_of(j * latent_count, latent_count), latent_count)
        context_up[...] = matmul_right(pool[at], context_all[...].reshape(width, 2 * inner))
        context_up[patches:] = context_up[patches:] + matmul_right(d_query[j], query_all[...].reshape(width, inner))

        def media_tile(at, size=patches // 2):
            tile = pl.ds(at, size)
            upstream = context_up[tile]
            value, gain_terms = layer_norm_back(media_in[j, tile].astype(F32), vectors[0:1], upstream)
            sums[0] = sums[0] + fold(gain_terms)
            sums[1] = sums[1] + fold(upstream)
            media_in[j, tile] = value.astype(BF16)

        tiles(2, patches // 2, media_tile)
        upstream = context_up[patches:]
        value, gain_terms = layer_norm_back(latents_in[j].astype(F32), vectors[2:3], upstream)
        sums[2] = sums[2] + fold(gain_terms)
        sums[3] = sums[3] + fold(upstream)
        latents_in[j] = (d_feed[own] + value).astype(BF16)

    pl.loop(0, 1)(input_slot)
    send_off(10)
    pl.loop(1, 3)(input_slot)
    send_off(11)
    pl.loop(3, 4)(input_slot)
    send_off(12)
    pl.loop(4, slot_count)(input_slot)
    for number in range(6):
        total[number:number + 1] = jnp.sum(sums[number], axis=0, keepdims=True)
    total[6:] = jnp.zeros_like(total[6:])
    vector_sum = VectorSum(links, slots, total, total_stage, total_lands)
    vector_sum.step(0)
    send_off(13)
    written.append(locals_.copy(media_in, media_grad_out))
    written.append(locals_.copy(latents_in, latents_grad_out))
    own_rows_move.wait()
    up_result[1] = own_rows_land[...].astype(F32)
    vector_sum.step(1)

    def hand_over(numbers):
        for number in numbers:
            value, out = result[number], grads_out[number]
            written.append(locals_.copy(value, out.at[rep]))
            written.append(slots.move(links.device("core"), value, out.at[rep], out.at[1 - rep]))
            written[-1].start()

    hand_over((0, 1, 2, 4))
    vector_sum.step(2)
    vector_sum.step(3)
    vector_sum.step(4)
    send_off(14)
    hand_over((3,))
    sums_out[...] = total[...]
    for copy in written:
        copy.wait()
    slots.drain(6)
    slots.drain(7)


def layer(length, counts, media, latents, grad_out, packed, shards):
    query_shard, context_shard, output_shard, up_shard, down_shard = shards
    slot_count, patches, width = media.shape
    latent_count = latents.shape[1]
    key_count = patches + latent_count
    rows = slot_count * latent_count
    inner = query_shard.shape[1]
    unit = down_shard.shape[0] // 2
    hidden = up_shard.shape[1] // 4
    blocks = (length, 2, 2)

    def halved(shard):
        return blocks + (2, shard.shape[0] // 2, shard.shape[1])

    up_shape = blocks + (up_shard.shape[0], hidden)
    down_shape = (length, 2, unit, width)
    halves = [halved(s)[4:] for s in shards[:3]]
    results = [(2,) + up_shape[3:], (unit, width)] + halves
    anywhere = pl.BlockSpec(memory_space=pl.ANY)
    vmem = pl.BlockSpec(memory_space=pltpu.VMEM)
    sums_shape = (8, width)
    scratch = [
        pltpu.VMEM(halved(query_shard), BF16),
        pltpu.VMEM(halved(context_shard), BF16),
        pltpu.VMEM(halved(output_shard), BF16),
        pltpu.VMEM(up_shape, BF16),
        pltpu.VMEM(down_shape, BF16),
        pltpu.VMEM(blocks + packed.shape, BF16),
        pltpu.VMEM((8, width), F32),
        pltpu.VMEM(media.shape, BF16),
        pltpu.VMEM(latents.shape, BF16),
        pltpu.VMEM(grad_out.shape, BF16),
        pltpu.VMEM((slot_count, key_count, width), BF16),
        pltpu.VMEM((slot_count, key_count, 2 * inner), BF16),
        pltpu.VMEM((slot_count, latent_count, inner), BF16),
        pltpu.VMEM((slot_count, latent_count, inner), BF16),
        pltpu.VMEM((rows, width), F32),
        pltpu.VMEM((4 * rows, width), BF16),
        pltpu.VMEM((width, 4 * rows), BF16),
        pltpu.VMEM((4 * rows, width), BF16),
        pltpu.VMEM((width, 4 * rows), BF16),
        pltpu.VMEM((max(12 * rows, slot_count * key_count), hidden), BF16),
        pltpu.VMEM((2, rows, width), F32),
        pltpu.VMEM((3, rows, width), BF16),
        pltpu.VMEM((3, rows, width), BF16),
        pltpu.VMEM(up_shape, BF16),
        pltpu.VMEM((length, 2, width, unit), BF16),
        pltpu.VMEM(halved(query_shard), BF16),
        pltpu.VMEM(halved(output_shard), BF16),
        pltpu.VMEM((latent_count * (GROUP // HEAD_DIM), GROUP), F32),
        pltpu.VMEM((6, 8, width), F32),
        pltpu.VMEM(sums_shape, F32),
        pltpu.VMEM((4,) + sums_shape, F32),
        pltpu.VMEM((2 + length,) + sums_shape, F32),
        pltpu.VMEM(up_shape[3:], BF16),
        pltpu.VMEM(up_shape[3:], BF16),
        [pltpu.VMEM(blocks + h, BF16) for h in halves],
        [pltpu.VMEM((length, 2) + up_shape[3:], BF16), pltpu.VMEM((length, width, unit), BF16)]
        + [pltpu.VMEM((length, 2) + h, BF16) for h in halves],
        [None, None] + [pltpu.VMEM((length,) + h, BF16) for h in halves],
        [pltpu.VMEM((length - 1, 2) + up_shape[3:], BF16), pltpu.VMEM((length - 1, width, unit), BF16)]
        + [pltpu.VMEM((length - 1,) + h, BF16) for h in halves],
        [pltpu.VMEM(r, F32) for r in results],
        pltpu.SemaphoreType.DMA((8,)),
        pltpu.SemaphoreType.DMA((112,)),
        pltpu.SemaphoreType.DMA((24,)),
    ]
    out_shape = (
        jax.ShapeDtypeStruct(latents.shape, BF16), jax.ShapeDtypeStruct(media.shape, BF16),
        jax.ShapeDtypeStruct(latents.shape, BF16), jax.ShapeDtypeStruct(sums_shape, F32),
        [jax.ShapeDtypeStruct((2,) + r, F32) for r in results])
    return pl.pallas_call(
        functools.partial(layer_kernel, length, HEAD_DIM ** (-0.5)),
        out_shape=out_shape,
        in_specs=[pl.BlockSpec(memory_space=pltpu.SMEM)] + [anywhere] * 9,
        out_specs=(anywhere, anywhere, anywhere, vmem, [anywhere] * 5),
        scratch_shapes=scratch,
        compiler_params=pltpu.CompilerParams(
            collective_id=0, has_side_effects=True, vmem_limit_bytes=127 * 2 ** 19),
        name="resampler_layer",
    )(counts, media, latents, grad_out, packed, query_shard, context_shard, output_shard, up_shard, down_shard)


def finish_kernel(length, latents_raw, media_grad_raw, latents_grad_raw, grads_raw, latents_out, media_grad_out,
                  latents_grad_out, grads_out, held, held_grads, local):
    x = Links(length).x
    locals_ = Locals(local)
    raws = [latents_raw, latents_grad_raw, *grads_raw]
    stages = [held[0], held[1], *held_grads]
    outs = [latents_out, latents_grad_out, *grads_out]
    count = media_grad_raw.shape[0]
    for j in range(count):
        raws.append(media_grad_raw.at[j])
        stages.append(held[2].at[j])
        outs.append(media_grad_out.at[j])
    loads = [locals_.copy(raw, stage) for raw, stage in zip(raws, stages)]
    unit = grads_raw[1].shape[1]
    copies = []
    for number, (load, stage, out) in enumerate(zip(loads, stages, outs)):
        load.wait()
        if number != 2:
            copies.append(locals_.copy(stage, out))
            continue
        moves = []
        for core in range(2):
            for plane in range(2):
                half = x if plane == 0 else 1 - x
                for owner in range(stage.shape[-1] // unit):
                    begin = pl.multiple_of(((2 * owner + half) * 2 + core) * unit, unit)
                    moves.append((stage.at[core, plane, :, pl.ds(owner * unit, unit)], out.at[:, pl.ds(begin, unit)]))
        copies.append(locals_.fill(moves, out))
    for copy in copies:
        copy.wait()


def finish(length, latents_raw, media_grad_raw, latents_grad_raw, grads_raw):
    anywhere = pl.BlockSpec(memory_space=pl.ANY)
    up = grads_raw[0]
    shapes = [jax.ShapeDtypeStruct((up.shape[2], 4 * up.shape[3]), up.dtype)]
    shapes += [jax.ShapeDtypeStruct(g.shape, g.dtype) for g in grads_raw[1:]]
    same = [jax.ShapeDtypeStruct(r.shape, r.dtype) for r in (latents_raw, media_grad_raw, latents_grad_raw)]
    return pl.pallas_call(
        functools.partial(finish_kernel, length),
        out_shape=(*same, shapes),
        in_specs=[anywhere, anywhere, anywhere, [anywhere] * 5],
        out_specs=(anywhere, anywhere, anywhere, [anywhere] * 5),
        scratch_shapes=[
            [pltpu.VMEM(r.shape, r.dtype) for r in (latents_raw, latents_grad_raw, media_grad_raw)],
            [pltpu.VMEM(g.shape, g.dtype) for g in grads_raw],
            pltpu.SemaphoreType.DMA((2 * (7 + media_grad_raw.shape[0]),)),
        ],
        compiler_params=pltpu.CompilerParams(vmem_limit_bytes=60 * 2 ** 20),
        name="finish",
    )(latents_raw, media_grad_raw, latents_grad_raw, grads_raw)


def head_scores(first_heads, second_heads):
    return jnp.einsum(
        "bqhd,bkhd->bhqk", first_heads, second_heads, preferred_element_type=jnp.float32
    )


def collective_body(
    media,
    latents,
    image_counts,
    grad_out,
    media_gain,
    media_bias,
    latent_gain,
    latent_bias,
    feed_gain,
    feed_bias,
    query_weight,
    context_weight,
    output_weight,
    up_weight,
    down_weight,
):
    samples, slots, patches, model_width = media.shape
    latent_count = latents.shape[2]
    inner_width = query_weight.shape[1]
    head_count = inner_width // HEAD_DIM
    blocks = samples * slots
    key_count = patches + latent_count
    latent_total = blocks * latent_count
    scaling = HEAD_DIM ** (-0.5)
    vector_shards = (media_gain, media_bias, latent_gain, latent_bias, feed_gain, feed_bias)
    weight_shards = (query_weight, context_weight, output_weight, up_weight, down_weight)
    gathered = tuple(lax.all_gather(s, "dp", axis=0, tiled=True) for s in vector_shards + weight_shards)
    vectors = [element.astype(jnp.float32) for element in gathered[:6]]
    media_rows = media.reshape(blocks * patches, model_width).astype(jnp.float32)
    latent_rows = latents.reshape(latent_total, model_width).astype(jnp.float32)
    media_normed = layer_norm(media_rows, vectors[0], vectors[1]).astype(jnp.bfloat16)
    latent_normed = layer_norm(latent_rows, vectors[2], vectors[3]).astype(jnp.bfloat16)
    queries = (matmul(latent_normed, gathered[6]) * scaling).astype(jnp.bfloat16)
    context = jnp.concatenate(
        [
            media_normed.reshape(blocks, patches, model_width),
            latent_normed.reshape(blocks, latent_count, model_width),
        ],
        axis=1,
    ).reshape(blocks * key_count, model_width)
    key_value = (
        matmul(context, gathered[7])
        .astype(jnp.bfloat16)
        .reshape(blocks, key_count, 2 * inner_width)
    )
    query_heads = queries.reshape(blocks, latent_count, head_count, HEAD_DIM)
    key_heads = key_value[:, :, :inner_width].reshape(blocks, key_count, head_count, HEAD_DIM)
    value_heads = key_value[:, :, inner_width:].reshape(blocks, key_count, head_count, HEAD_DIM)
    scores = head_scores(query_heads, key_heads)
    row_max = jnp.max(scores, axis=-1, keepdims=True)
    exponent = jnp.exp(scores - row_max)
    row_total = jnp.sum(exponent, axis=-1, keepdims=True)
    log_total = row_max + jnp.log(row_total)
    attention_weights = (exponent / row_total).astype(jnp.bfloat16)
    attended = (
        jnp.einsum(
            "bhqk,bkhd->bqhd", attention_weights, value_heads, preferred_element_type=jnp.float32
        )
        .astype(jnp.bfloat16)
        .reshape(latent_total, inner_width)
    )
    after_attention = latent_rows + matmul(attended, gathered[8])
    feed_input = layer_norm(after_attention, vectors[4], vectors[5]).astype(jnp.bfloat16)
    hidden = matmul(feed_input, gathered[9])
    activated = gelu_exact(hidden).astype(jnp.bfloat16)
    after_feed = after_attention + matmul(activated, gathered[10])
    slot_mask = (
        lax.broadcasted_iota(jnp.int32, (samples, slots), 1) < image_counts[:, None]
    ).astype(jnp.float32)
    row_mask = jnp.broadcast_to(slot_mask[:, :, None], (samples, slots, latent_count)).reshape(
        latent_total, 1
    )
    latents_out = (after_feed * row_mask).astype(jnp.bfloat16).reshape(latents.shape)
    backward_set = gathered
    back_vectors = [element.astype(jnp.float32) for element in backward_set[:6]]
    d_after = grad_out.reshape(latent_total, model_width).astype(jnp.float32) * row_mask
    d_branch = d_after.astype(jnp.bfloat16)
    grad_down = matmul_left(activated, d_branch)
    d_activated = matmul_right(d_branch, backward_set[10])
    d_hidden = jax.vjp(gelu_exact, hidden)[1](d_activated)[0].astype(jnp.bfloat16)
    grad_up = matmul_left(feed_input, d_hidden)
    d_feed = matmul_right(d_hidden, backward_set[9])
    d_feed_norm, grad_feed_gain, grad_feed_bias = jax.vjp(
        layer_norm, after_attention, back_vectors[4], back_vectors[5]
    )[1](d_feed)
    d_middle = d_after + d_feed_norm
    d_out_branch = d_middle.astype(jnp.bfloat16)
    grad_output = matmul_left(attended, d_out_branch)
    d_attended = (
        matmul_right(d_out_branch, backward_set[8])
        .astype(jnp.bfloat16)
        .reshape(blocks, latent_count, head_count, HEAD_DIM)
    )
    recomputed = jnp.exp(head_scores(query_heads, key_heads) - log_total)
    d_weights = head_scores(d_attended, value_heads)
    d_scores = (
        recomputed * (d_weights - jnp.sum(recomputed * d_weights, axis=-1, keepdims=True))
    ).astype(jnp.bfloat16)
    d_queries = (
        jnp.einsum(
            "bhqk,bkhd->bqhd", d_scores, key_heads, preferred_element_type=jnp.float32
        ).astype(jnp.bfloat16)
        * scaling
    ).reshape(latent_total, inner_width)
    d_keys = jnp.einsum(
        "bhqk,bqhd->bkhd", d_scores, query_heads, preferred_element_type=jnp.float32
    ).astype(jnp.bfloat16)
    d_values = jnp.einsum(
        "bhqk,bqhd->bkhd",
        recomputed.astype(jnp.bfloat16),
        d_attended,
        preferred_element_type=jnp.float32,
    ).astype(jnp.bfloat16)
    d_key_value = jnp.concatenate(
        [
            d_keys.reshape(blocks, key_count, inner_width),
            d_values.reshape(blocks, key_count, inner_width),
        ],
        axis=-1,
    ).reshape(blocks * key_count, 2 * inner_width)
    grad_query = matmul_left(latent_normed, d_queries)
    grad_context = matmul_left(context, d_key_value)
    d_context = matmul_right(d_key_value, backward_set[7]).reshape(blocks, key_count, model_width)
    d_latent_normed = matmul_right(d_queries, backward_set[6]) + d_context[:, patches:, :].reshape(
        latent_total, model_width
    )
    d_media_normed = d_context[:, :patches, :].reshape(blocks * patches, model_width)
    d_latent_norm, grad_latent_gain, grad_latent_bias = jax.vjp(
        layer_norm, latent_rows, back_vectors[2], back_vectors[3]
    )[1](d_latent_normed)
    grad_latents = (d_middle + d_latent_norm).astype(jnp.bfloat16).reshape(latents.shape)
    d_media, grad_media_gain, grad_media_bias = jax.vjp(
        layer_norm, media_rows, back_vectors[0], back_vectors[1]
    )[1](d_media_normed)
    grad_media = d_media.astype(jnp.bfloat16).reshape(media.shape)
    vector_grads = jnp.stack([
        grad_media_gain, grad_media_bias, grad_latent_gain, grad_latent_bias, grad_feed_gain, grad_feed_bias])
    weight_grads = [
        g.astype(jnp.bfloat16) for g in (grad_query, grad_context, grad_output, grad_up, grad_down)]
    vector_sums = lax.psum_scatter(vector_grads, "dp", scatter_dimension=1, tiled=True)
    summed = [lax.psum_scatter(g, "dp", scatter_dimension=0, tiled=True) for g in weight_grads]
    owned = tuple(lax.psum(vector_sums, "rep")) + tuple(
        lax.psum(s, "rep").astype(jnp.float32) for s in summed)
    return (
        latents_out,
        grad_media,
        grad_latents,
        owned[0],
        owned[1],
        owned[2],
        owned[3],
        owned[4],
        owned[5],
        owned[6],
        owned[7],
        owned[8],
        owned[9],
        owned[10],
    )


def body(media, latents, image_counts, grad_out, *parameters):
    chips = lax.axis_size("dp")
    weight_shards = parameters[6:]
    tiled = (media.shape[0] == 1 and chips % 4 == 0 and chips > 4 and parameters[0].shape[0] == 64
             and all(s.shape[0] % 32 == 0 for s in weight_shards))
    if not tiled:
        return collective_body(media, latents, image_counts, grad_out, *parameters)
    side = lax.rem(lax.axis_index("dp"), 2)
    stacked = jnp.stack(parameters[:6])
    packed = jnp.pad(
        jnp.concatenate([jnp.where(side == 0, stacked, 0), jnp.where(side == 0, 0, stacked)], axis=1), ((0, 10), (0, 0)))
    latents_out, grad_media, grad_latents, vector_sums, summed = layer(
        chips // 4, image_counts, media[0], latents[0], grad_out[0], packed, weight_shards)
    latents_out, grad_media, grad_latents, summed = finish(
        chips // 4, latents_out, grad_media, grad_latents, summed)
    sums = [s.reshape(-1, s.shape[-1]) for s in summed[2:] + summed[:2]]
    width = parameters[0].shape[0]
    mine = lax.dynamic_slice(vector_sums, (0, lax.axis_index("dp") * width), (6, width))
    return (latents_out[None], grad_media[None], grad_latents[None]) + tuple(mine) + tuple(sums)


def solution(mesh):
    return jax.shard_map(
        body,
        mesh=mesh,
        in_specs=(
            P(("dp", "rep"), None, None, None),
            P(("dp", "rep"), None, None, None),
            P(("dp", "rep")),
            P(("dp", "rep"), None, None, None),
            P("dp"),
            P("dp"),
            P("dp"),
            P("dp"),
            P("dp"),
            P("dp"),
            P("dp", None),
            P("dp", None),
            P("dp", None),
            P("dp", None),
            P("dp", None),
        ),
        out_specs=(
            P(("dp", "rep"), None, None, None),
            P(("dp", "rep"), None, None, None),
            P(("dp", "rep"), None, None, None),
            P("dp"),
            P("dp"),
            P("dp"),
            P("dp"),
            P("dp"),
            P("dp"),
            P("dp", None),
            P("dp", None),
            P("dp", None),
            P("dp", None),
            P("dp", None),
        ),
        check_vma=False,
    )
```

```python
import functools

import jax
import jax.numpy as jnp
from jax import lax
from jax.experimental import pallas as pl
from jax.experimental.pallas import tpu as pltpu
from jax.sharding import PartitionSpec as P

HEAD_DIM = 64
GROUP = 256

epsilon = 1e-05

MESH = pl.DeviceIdType.MESH
ALL = slice(None)
F32 = jnp.float32
BF16 = jnp.bfloat16


class Links:
    def __init__(self, length):
        self.length = length
        self.dp = lax.axis_index("dp")
        self.rep = lax.axis_index("rep")
        self.z = lax.div(self.dp, 4)
        self.y = lax.rem(lax.div(self.dp, 2), 2)
        self.x = lax.rem(self.dp, 2)

    def device(self, axis, way=0):
        if axis == "core":
            return (self.dp, 1 - self.rep)
        if axis == "x":
            return (self.dp + 1 - 2 * self.x, self.rep)
        if axis == "y":
            return (self.dp + 2 - 4 * self.y, self.rep)
        return (self.dp + 4 * (self.along(way) - self.z), self.rep)

    def along(self, way):
        return lax.rem(self.z + way + self.length, self.length)

    def greet(self):
        barrier = pltpu.get_barrier_semaphore()
        peers = [("core", 0), ("x", 0), ("y", 0)] + [("z", way) for way in range(1, self.length)]
        for axis, way in peers:
            pl.semaphore_signal(barrier, inc=1, device_id=self.device(axis, way), device_id_type=MESH)
        pl.semaphore_wait(barrier, len(peers))


class Move:
    def __init__(self, slots, copies, landing):
        send, recv = slots.send.at[slots.group], slots.recv.at[slots.made]
        slots.made += 1
        self.slots, self.group, self.copies = slots, slots.group, [
            pltpu.make_async_remote_copy(
                src_ref=source, dst_ref=target, send_sem=send, recv_sem=recv,
                device_id=device, device_id_type=MESH)
            for device, source, target in copies]
        self.bytes = 0
        for _, source, _ in copies:
            size = jnp.dtype(source.dtype).itemsize
            for extent in source.shape:
                size *= extent
            self.bytes += size
        self.into = pltpu.make_async_remote_copy(
            src_ref=landing, dst_ref=landing, send_sem=send, recv_sem=recv,
            device_id=copies[0][0], device_id_type=MESH)

    def start(self):
        for copy in self.copies:
            copy.start()
        self.slots.sent[self.group] += self.bytes

    def wait(self):
        self.into.wait_recv()


class Slots:
    def __init__(self, send, recv, ruler):
        self.send, self.recv, self.ruler, self.made, self.group = send, recv, ruler, 0, 0
        self.sent = [0] * send.shape[0]

    def move(self, device, source, target, landing):
        return Move(self, [(device, source, target)], landing)

    def drain(self, group, ruler=None):
        ruler = self.ruler if ruler is None else ruler
        row = ruler.shape[-1] * jnp.dtype(ruler.dtype).itemsize
        rows, rest = divmod(self.sent[group], row)
        assert rest == 0 and rows % 16 == 0 and rows <= ruler.shape[0]
        whole = ruler.at[pl.ds(0, rows)]
        pltpu.make_async_copy(whole, whole, self.send.at[group]).wait()


class Locals:
    def __init__(self, semaphores):
        self.semaphores, self.made = semaphores, 0

    def copy(self, source, target):
        return self.fill([(source, target)], target)

    def fill(self, copies, whole):
        semaphore = self.semaphores.at[self.made]
        self.made += 1
        for source, target in copies:
            pltpu.make_async_copy(source, target, semaphore).start()
        return pltpu.make_async_copy(whole, whole, semaphore)


class Gather:
    def __init__(self, links, slots, view, axes, halved):
        here = {"z": links.z, "y": links.y, "x": links.x}
        self.moves = []
        for axis in axes:
            mine = view(here["z"], here["y"], here["x"])
            if axis == "z":
                self.moves.append(Move(
                    slots, [(links.device("z", way), mine, mine) for way in range(1, links.length)],
                    view(pl.ds(0, links.length - 1), here["y"], here["x"])))
            else:
                other = dict(here)
                other[axis] = 1 - here[axis]
                self.moves.append(
                    slots.move(links.device(axis), mine, mine, view(other["z"], other["y"], other["x"])))
            here[axis] = ALL
        if halved:
            mine = view(ALL, ALL, ALL)
            self.moves.append(
                slots.move(links.device("core"), mine, mine, view(ALL, ALL, ALL, 1 - links.rep)))

    def step(self, number):
        if 0 < number <= len(self.moves):
            self.moves[number - 1].wait()
        if 0 <= number < len(self.moves):
            self.moves[number].start()


class Reduce:
    def __init__(self, links, slots, own, axes, lands, lands_z, finish):
        self.own, self.links, self.finish, self.lands_z = own, links, finish, lands_z
        self.moves, self.adds = [], []
        z, y, x = links.z, links.y, links.x
        here = {"z": ALL, "y": ALL, "x": ALL}
        for axis, land in zip(axes, lands):
            away, home = dict(here), dict(here)
            place = {"y": y, "x": x}[axis]
            away[axis], home[axis] = 1 - place, place
            self.moves.append(slots.move(
                links.device(axis), own(away["z"], away["y"], away["x"]), land, land))
            here = home
            self.adds.append(functools.partial(add_into, own(home["z"], home["y"], home["x"]), land))
        self.moves.append(Move(
            slots, [(links.device("z", way), own(links.along(way), here["y"], here["x"]), lands_z.at[way - 1])
                    for way in range(1, links.length)], lands_z))
        self.mine = own(z, here["y"], here["x"])
        self.adds.append(self.end)

    def step(self, number):
        if 0 < number <= len(self.moves):
            self.moves[number - 1].wait()
            self.adds[number - 1]()
        if 0 <= number < len(self.moves):
            self.moves[number].start()

    def end(self):
        total = self.mine[...].astype(F32)
        for way in range(1, self.links.length):
            total = total + self.lands_z[way - 1].astype(F32)
        self.finish(total)


def add_into(target, arrived):
    @pl.loop(0, target.shape[0])
    def _(number):
        target[number] = (target[number].astype(F32) + arrived[number].astype(F32)).astype(target.dtype)


def run(table, tick):
    for item, ticks in table:
        if tick in ticks:
            item.step(ticks.index(tick))


def matmul(left, right):
    return jnp.dot(left, right, preferred_element_type=F32)


def matmul_left(left, right):
    return lax.dot_general(left, right, (((0,), (0,)), ((), ())), preferred_element_type=F32)


def matmul_right(left, right):
    return lax.dot_general(left, right, (((1,), (1,)), ((), ())), preferred_element_type=F32)


def layer_norm(values, gain, offset):
    centre = jnp.mean(values, axis=-1, keepdims=True)
    shifted = values - centre
    spread = jnp.mean(shifted * shifted, axis=-1, keepdims=True)
    return shifted * lax.rsqrt(spread + epsilon) * gain + offset


def layer_norm_back(values, gain, upstream):
    centre = jnp.mean(values, axis=-1, keepdims=True)
    shifted = values - centre
    spread = jnp.mean(shifted * shifted, axis=-1, keepdims=True)
    rate = lax.rsqrt(spread + epsilon)
    normed = shifted * rate
    scaled = upstream * gain
    first = jnp.mean(scaled, axis=-1, keepdims=True)
    second = jnp.mean(scaled * normed, axis=-1, keepdims=True)
    return rate * (scaled - first - normed * second), upstream * normed


def gelu_exact(values):
    return 0.5 * values * (1.0 + jax.scipy.special.erf(values * 0.7071067811865476))


def gelu_parts(values):
    cumulative = 0.5 * (1.0 + lax.erf(values * 0.7071067811865476))
    density = 0.3989422804014327 * jnp.exp(-0.5 * values * values)
    return values * cumulative, cumulative + values * density


def tiles(count, size, action):
    @pl.loop(0, count)
    def _(number):
        action(pl.multiple_of(number * size, size))


def head_mask(rows, columns):
    heads = columns // HEAD_DIM
    row = lax.broadcasted_iota(jnp.int32, (rows * heads, columns), 0)
    column = lax.broadcasted_iota(jnp.int32, (rows * heads, columns), 1)
    head_row = jnp.zeros_like(row)
    head_column = jnp.zeros_like(row)
    for head in range(1, heads):
        head_row = head_row + jnp.where(row >= head * rows, 1, 0)
        head_column = head_column + jnp.where(column >= head * HEAD_DIM, 1, 0)
    return jnp.where(head_row == head_column, 1.0, 0.0)


def spread_heads(rows, mask):
    return jnp.concatenate([rows] * (mask.shape[0] // rows.shape[0]), axis=0) * mask


def pick_heads(stacked, mask, rows):
    kept = stacked * mask
    total = kept[:rows]
    for head in range(1, stacked.shape[0] // rows):
        total = total + kept[head * rows:(head + 1) * rows]
    return total


def softmax(scores):
    exponent = jnp.exp(scores - jnp.max(scores, axis=-1, keepdims=True))
    return exponent / jnp.sum(exponent, axis=-1, keepdims=True)


class VectorSum:
    def __init__(self, links, slots, total, stage, lands):
        self.total, self.stage, self.lands, self.length = total, stage, lands, links.length
        self.moves = [slots.move(links.device(axis), stage.at[number], lands.at[number], lands.at[number])
                      for number, axis in enumerate(("core", "x", "y"))]
        self.moves.append(Move(
            slots, [(links.device("z", way), stage.at[3], lands.at[2 + way]) for way in range(1, links.length)],
            lands.at[pl.ds(3, links.length - 1)]))

    def step(self, number):
        if 0 < number <= 4:
            self.moves[number - 1].wait()
            for land in ([number - 1] if number < 4 else range(3, 2 + self.length)):
                self.total[...] = self.total[...] + self.lands[land]
        if number < 4:
            self.stage[number] = self.total[...]
            self.moves[number].start()


class Rows:
    def __init__(self, links, slots, buffer, count, parts):
        self.moves, self.passed = [], []
        for begin, size in parts:
            def place(owner, begin=begin, size=size):
                return buffer.at[pl.ds(owner * count + begin, size)]

            self.moves.append([
                slots.move(links.device("x"), place(0), place(2), place(2)),
                slots.move(links.device("core"), place(0), place(1), place(1))])
            self.passed.append(slots.move(links.device("core"), place(2), place(3), place(3)))

    def send(self, part):
        for move in self.moves[part]:
            move.start()

    def near(self, part):
        self.moves[part][1].wait()

    def forward(self, part):
        self.moves[part][0].wait()
        self.passed[part].start()

    def far(self, part):
        self.passed[part].wait()


class Partials:
    def __init__(self, links, slots, stage, lands, count):
        def place(owner):
            return stage.at[pl.ds(owner * count, count)]

        self.place, self.lands = place, lands
        self.far = slots.move(links.device("core"), place(3), lands.at[0], lands.at[0])
        self.near = slots.move(links.device("core"), place(1), lands.at[1], lands.at[1])
        self.across = slots.move(links.device("x"), place(2), lands.at[2], lands.at[2])


def layer_kernel(length, scaling, counts, media, latents, grad_out, packed, query_shard, context_shard,
                 output_shard, up_shard, down_shard, latents_out, media_grad_out, latents_grad_out, sums_out, grads_out,
                 query_all, context_all, output_all, up_all, down_all,
                 packed_all, vectors, media_in, latents_in, grad_in, context, key_value, query, attended, after,
                 feed, feed_t, branch, branch_t, pool, totals, after_lands, d_feed_lands,
                 grad_up, grad_down, grad_query, grad_output, mask, sums, total, total_stage, total_lands,
                 own_rows_send, own_rows_land, lands_c, lands_b, lands_a, lands_z, result, send, recv, local):
    links = Links(length)
    z, y, x, rep = links.z, links.y, links.x, links.rep
    slots, locals_ = Slots(send, recv, pool), Locals(local)
    slot_count, patches, width = media.shape
    latent_count = latents.shape[1]
    key_count = patches + latent_count
    rows = slot_count * latent_count
    inner = query.shape[-1]
    chunks = length
    hidden = up_all.shape[-1]
    chunk = hidden // chunks
    unit = down_all.shape[-2]
    xy, yx = ("z", "x", "y"), ("z", "y", "x")

    def unit_columns(half, number):
        return pl.ds(pl.multiple_of(((2 * number + half) * 2 + rep) * unit, unit), unit)

    staged = [locals_.copy(packed, packed_all.at[z, y, x])]
    for shard, whole in ((context_shard, context_all), (query_shard, query_all), (output_shard, output_all)):
        half = whole.shape[-2]
        staged.append(locals_.copy(shard.at[pl.ds(pl.multiple_of(rep * half, 16), half)], whole.at[z, y, x, rep]))
    units = range(hidden // unit)
    staged.append(locals_.fill(
        [(up_shard.at[:, unit_columns(1 - x, n)], own_rows_send.at[:, pl.ds(n * unit, unit)]) for n in units],
        own_rows_send))
    staged.append(locals_.fill(
        [(up_shard.at[:, unit_columns(x, n)], up_all.at[z, y, x, :, pl.ds(n * unit, unit)]) for n in units],
        up_all.at[z, y, x]))
    staged.append(locals_.copy(down_shard.at[pl.ds(pl.multiple_of(rep * unit, 16), unit)], down_all.at[z, y]))
    grad_load = locals_.copy(grad_out, grad_in)
    latents_load = locals_.copy(latents, latents_in)
    media_load = locals_.copy(media, media_in)
    links.greet()

    def halves(whole, begin, size, order):
        def view(zi, yi, xi, half=rep):
            return whole.at[zi, yi, xi, half, :, pl.ds(begin, size)]

        return Gather(links, slots, view, order, True)

    slots.group = 0
    vector_gather = Gather(links, slots, lambda zi, yi, xi: packed_all.at[zi, yi, xi], xy, False)
    slots.group = 1
    gathers = [
        (halves(context_all, 0, width // 2, xy), (0, 1, 2, 3, 4)),
        (halves(context_all, width // 2, width // 2, yx), (0, 1, 2, 3, 4)),
        (halves(query_all, 0, inner, yx), (0, 2, 3, 4, 5)), (halves(output_all, 0, width, yx), (0, 2, 3, 4, 5)),
    ]
    slots.group = 2
    for number in range(2 * chunks):
        window = pl.ds(number % chunks * chunk, chunk)
        if number < chunks:
            def view(zi, yi, xi, window=window):
                return down_all.at[zi, yi, :, window]
        else:
            def view(zi, yi, xi, window=window):
                return up_all.at[zi, yi, ALL, :, window]
        ticks = (max(number - 1, 0), number + 2, number + 4)
        gathers.append((Gather(links, slots, view, ("z", "y"), False), ticks))
    up_across = slots.move(links.device("x"), own_rows_send, up_all.at[z, y, x], up_all.at[z, y, 1 - x])
    slots.group = 3
    parts = [(0, 2 * latent_count), (2 * latent_count, rows - 2 * latent_count)]
    branch_rows = Rows(links, slots, branch, rows, [(0, rows)])
    feed_rows = Rows(links, slots, feed, rows, parts)

    def pump(tick):
        run(gathers, tick)

    for copy in staged:
        copy.wait()
    vector_gather.step(0)
    pump(0)
    up_across.start()
    grad_load.wait()
    kept = jnp.where(lax.broadcasted_iota(jnp.int32, (rows, 1), 0) < counts[0] * latent_count, 1.0, 0.0)
    branch[:rows] = (grad_in[...].reshape(rows, width).astype(F32) * kept).astype(BF16)
    vector_gather.step(1)
    mask[...] = head_mask(latent_count, GROUP)
    sums[...] = jnp.zeros_like(sums)
    vector_gather.step(2)
    latents_load.wait()
    media_load.wait()
    pump(1)
    vector_gather.step(3)
    lane = packed_all.shape[-1]
    for zi in range(length):
        for yi in range(2):
            place = (zi * 2 + yi) * lane
            vectors[:, place:place + lane] = (packed_all[zi, yi, 0] + packed_all[zi, yi, 1]).astype(F32)[:8]

    def normalise_slot(j):
        context[j, :patches] = layer_norm(media_in[j].astype(F32), vectors[0:1], vectors[1:2]).astype(BF16)
        context[j, patches:] = layer_norm(latents_in[j].astype(F32), vectors[2:3], vectors[3:4]).astype(BF16)

    pl.loop(0, slot_count)(normalise_slot)
    pump(2)
    up_across.wait()
    pump(3)
    pump(4)
    branch_rows.send(0)

    def key_value_slot(j):
        key_value[j] = matmul(context[j], context_all[...].reshape(width, 2 * inner)).astype(BF16)

    pl.loop(0, 3)(key_value_slot)
    pump(5)
    pl.loop(3, slot_count)(key_value_slot)
    latent_normed = context[:, patches:, :].reshape(rows, width)
    query[...] = (matmul(latent_normed, query_all[...].reshape(width, inner)) * scaling).astype(BF16).reshape(
        slot_count, latent_count, inner)
    pump(6)

    def attention_slot(j):
        for begin in range(0, inner, GROUP):
            stacked = spread_heads(query[j, :, begin:begin + GROUP], mask[...].astype(BF16))
            probs = softmax(matmul_right(stacked, key_value[j, :, begin:begin + GROUP])).astype(BF16)
            value = matmul(probs, key_value[j, :, inner + begin:inner + begin + GROUP])
            attended[j, :, begin:begin + GROUP] = pick_heads(value, mask[...], latent_count).astype(BF16)

    for part, (begin, size) in enumerate(parts):
        first, last = begin // latent_count, (begin + size) // latent_count
        pl.loop(first, last)(attention_slot)
        after[begin:begin + size] = latents_in[first:last].reshape(size, width).astype(F32) + matmul(
            attended[first:last].reshape(size, inner), output_all[...].reshape(inner, width))
        feed[begin:begin + size] = layer_norm(
            after[begin:begin + size], vectors[4:5], vectors[5:6]).astype(BF16)
        feed_rows.send(part)
        pump(7 + part)
    slots.drain(0, grad_down.at[0, 0])
    branch_rows.near(0)
    branch_rows.forward(0)

    def turn(source, target, owner):
        def body(at):
            target[pl.ds(at, 256), pl.ds(owner * rows, 2 * rows)] = source[
                pl.ds(owner * rows, 2 * rows), pl.ds(at, 256)].T

        tiles(width // 256, 256, body)

    turn(branch, branch_t, 0)
    branch_rows.far(0)
    tall = rows
    d_active, active, d_hidden = [pool.at[pl.ds(n * 4 * rows, 4 * rows)] for n in range(3)]

    def d_active_tile(at):
        d_active[pl.ds(at, tall)] = matmul_right(
            branch[pl.ds(at, tall)], down_all[...].reshape(hidden, width)).astype(BF16)

    tiles(4, tall, d_active_tile)
    turn(branch, branch_t, 2)

    def hidden_tile(at, begin):
        window = pl.ds(begin, chunk)
        weight = up_all[:, :, :, :, window].reshape(width, chunk)
        value, slope = gelu_parts(matmul(feed[pl.ds(at, tall)], weight))
        active[pl.ds(at, tall), window] = value.astype(BF16)
        d_hidden[pl.ds(at, tall), window] = (d_active[pl.ds(at, tall), window].astype(F32) * slope).astype(BF16)

    def d_feed_of(owner):
        return matmul_right(d_hidden[pl.ds(owner * rows, rows)], up_all[...].reshape(width, hidden))

    def after_feed_of(owner):
        return matmul(active[pl.ds(owner * rows, rows)], down_all[...].reshape(hidden, width))

    def rounded(buffer, owner, value):
        buffer[pl.ds(owner * rows, rows)] = value.astype(BF16)

    def across_tile(back, buffer):
        rounded(buffer, 2, totals[1] + back.lands[0].astype(F32))

    up_result, down_result, query_result, context_result, output_result = result
    reductions = []

    def send_off(tick):
        run(reductions, tick)

    def plane_reduction(own, lands_y, lands, finish):
        return Reduce(links, slots, own, ("y",), [lands_y], lands, finish)

    def keep_up(value, window):
        up_result[0, :, window] = jnp.where(x == 0, value[0], value[1])
        own_rows_send[:, window] = jnp.where(x == 0, value[1], value[0]).astype(BF16)

    feed_rows.near(0)
    feed_rows.near(1)
    slots.group = 6

    def near_hidden(c):
        tiles(2, tall, lambda at: hidden_tile(at, c * chunk))

    def far_hidden(c):
        tiles(2, tall, lambda at: hidden_tile(pl.multiple_of(2 * rows + at, tall), c * chunk))

    def grads(c):
        window = pl.ds(c * chunk, chunk)

        def grad_tile(number):
            size = width // 2
            place = pl.multiple_of(number * size, size)
            up = matmul(feed_t[pl.ds(place, size)], d_hidden[:, window]).astype(BF16)
            grad_up[pl.ds(number * (length // 2), length // 2), :, :, :, window] = up.reshape(
                length // 2, 2, 2, size // (2 * length), chunk)
            down = matmul(branch_t[pl.ds(place, size)], active[:, window]).astype(BF16)
            for owner in range(2):
                grad_down[c, owner, pl.ds(place, size)] = down[:, owner * unit:(owner + 1) * unit]

        pl.loop(0, 2)(grad_tile)
        reductions.append((plane_reduction(
            lambda zi, yi, xi: grad_up.at[zi, yi, ALL, :, window],
            lands_b[0].at[:, :, :, window], lands_z[0].at[:, :, :, window],
            functools.partial(keep_up, window=window)), (c, c + 2, c + 4)))
        send_off(c)

    near_hidden(0)
    pump(9)
    turn(feed, feed_t, 0)
    feed_rows.forward(0)
    feed_rows.forward(1)
    feed_rows.far(0)
    feed_rows.far(1)
    turn(feed, feed_t, 2)
    far_hidden(0)
    grads(0)
    near_hidden(1)
    far_hidden(1)
    pump(10)
    near_hidden(2)
    far_hidden(2)
    grads(1)
    for c in range(3, chunks):
        pump(8 + c)
        near_hidden(c)
        far_hidden(c)
    for group in range(1, 4):
        slots.drain(group)
    slots.group = 4
    d_feed_back = Partials(links, slots, feed, d_feed_lands, rows)
    slots.group = 5
    after_back = Partials(links, slots, branch, after_lands, rows)
    slots.group = 6
    rounded(feed, 3, d_feed_of(3))
    d_feed_back.far.start()
    totals[1] = d_feed_of(2)
    d_feed_back.far.wait()
    across_tile(d_feed_back, feed)
    d_feed_back.across.start()
    for c in range(2, chunks):
        grads(c)
    part_size = width // chunks
    for number in range(chunks):
        window = pl.ds(number * part_size, part_size)

        def keep_down(value, window=window):
            down_result[:, window] = value.T

        reductions.append((plane_reduction(
            lambda zi, yi, xi, window=window: grad_down.at[zi, yi, window],
            lands_b[1].at[:, window], lands_z[1].at[:, window], keep_down),
            (chunks, chunks + 2 + number, chunks + 4 + number) if number < chunks - 1 else (chunks, 10, 12)))
    send_off(4)
    rounded(feed, 1, d_feed_of(1))
    d_feed_back.near.start()
    totals[0] = d_feed_of(0)

    rounded(branch, 3, after_feed_of(3))
    after_back.far.start()
    totals[1] = after_feed_of(2)
    after_back.far.wait()
    across_tile(after_back, branch)
    send_off(5)
    rounded(branch, 1, after_feed_of(1))
    after_back.near.start()
    totals[1] = after_feed_of(0)
    d_feed_back.near.wait()
    d_feed_back.across.wait()
    after_back.across.start()
    slots.drain(4)

    def fold(terms):
        return jnp.sum(terms.reshape(-1, 8, width), axis=0)

    d_feed = totals.at[0]
    flat_grad = lambda at, size: grad_in[pl.ds(lax.div(at, latent_count), size // latent_count)].reshape(size, width)

    def middle_tile(at, size=latent_count):
        own = pl.ds(at, size)
        upstream = d_feed[own] + d_feed_lands[1, own].astype(F32) + d_feed_lands[2, own].astype(F32)
        d_norm, gain_terms = layer_norm_back(after[own], vectors[4:5], upstream)
        sums[4] = sums[4] + fold(gain_terms)
        sums[5] = sums[5] + fold(upstream)
        row = lax.broadcasted_iota(jnp.int32, (size, 1), 0) + at
        keep = jnp.where(row < counts[0] * latent_count, 1.0, 0.0)
        d_middle = flat_grad(at, size).astype(F32) * keep + d_norm
        d_feed[own] = d_middle
        feed[own] = d_middle.astype(BF16)

    tiles(slot_count, latent_count, middle_tile)

    context_rows, output_rows = context_all.shape[-2], output_all.shape[-2]

    def context_own(zi, yi, xi, half):
        return up_all.at[zi, yi, xi, pl.ds(pl.multiple_of(half * context_rows, 16), context_rows)]

    def query_own(zi, yi, xi, half):
        return grad_query.at[zi, yi, xi, half]

    def output_own(zi, yi, xi, half):
        return grad_output.at[zi, yi, xi, half]

    def to_sibling(own, land):
        move = slots.move(links.device("core"), own(ALL, ALL, ALL, 1 - rep), land, land)
        move.start()

        def settle():
            move.wait()
            add_into(own(ALL, ALL, ALL, rep), land)

        return settle

    def halved_reduction(own, number, target, begin, size, first, *ticks):
        made = []
        for which, order in enumerate((first, ("x", "y"))):
            window = pl.ds(begin + which * (size // 2), size // 2)

            def finish(value, window=window):
                target[:, window] = value

            made.append((Reduce(
                links, slots, lambda zi, yi, xi, window=window: own(zi, yi, xi, rep).at[..., window], order,
                [lands_b[number].at[:, :, :, window], lands_a[number].at[:, :, window]],
                lands_z[number].at[:, :, window], finish), ticks))
        return made

    d_branch = feed.at[pl.ds(0, rows)]
    output_block = inner // 2

    def output_grad_tile(number):
        place = pl.multiple_of(number * output_block, output_block)
        turned = attended[:, :, pl.ds(place, output_block)].reshape(rows, output_block).T
        value = matmul(turned, d_branch[...]).astype(BF16)
        grad_output[pl.ds(number * (length // 2), length // 2)] = value.reshape(
            length // 2, 2, 2, 2, output_rows, width)

    d_attended, d_query = grad_in.at[:, :, pl.ds(0, inner)], grad_in.at[:, :, pl.ds(inner, inner)]
    d_attended[...] = matmul_right(d_branch[...], output_all[...].reshape(inner, width)).astype(BF16).reshape(
        slot_count, latent_count, inner)

    def attention_back_slot(j):
        own = pl.ds(pl.multiple_of(j * latent_count, latent_count), latent_count)
        for begin in range(0, inner, GROUP):
            keys = key_value[j, :, begin:begin + GROUP]
            values = key_value[j, :, inner + begin:inner + begin + GROUP]
            low_mask = mask[...].astype(BF16)
            stacked = spread_heads(query[j, :, begin:begin + GROUP], low_mask)
            upstream = spread_heads(d_attended[j, :, begin:begin + GROUP], low_mask)
            probs = softmax(matmul_right(stacked, keys))
            d_probs = matmul_right(upstream, values)
            d_scores = (probs * (d_probs - jnp.sum(probs * d_probs, axis=-1, keepdims=True))).astype(BF16)
            d_query[j, :, begin:begin + GROUP] = (
                pick_heads(matmul(d_scores, keys), mask[...], latent_count).astype(BF16).astype(F32) * scaling
            ).astype(BF16)
            at = pl.ds(pl.multiple_of(j * key_count, 16), key_count)
            pool[at, begin:begin + GROUP] = matmul_left(d_scores, stacked).astype(BF16)
            pool[at, inner + begin:inner + begin + GROUP] = matmul_left(probs.astype(BF16), upstream).astype(BF16)

    pl.loop(0, 2)(attention_back_slot)
    send_off(6)
    pl.loop(0, 2)(output_grad_tile)
    settle_output = to_sibling(output_own, lands_c[2])
    pl.loop(2, 4)(attention_back_slot)
    settle_output()
    reductions.extend(halved_reduction(output_own, 4, output_result, 0, width, ("x", "y"), 7, 9, 10, 11))
    send_off(7)
    pl.loop(4, slot_count)(attention_back_slot)
    block = width // length

    def query_grad_tile(zi):
        place = pl.multiple_of(zi * block, block)
        turned = context[:, patches:, pl.ds(place, block)].reshape(rows, block).T
        value = matmul(turned, d_query[...].reshape(rows, inner)).astype(BF16)
        grad_query[zi] = value.reshape(2, 2, 2, context_rows, inner)

    pl.loop(0, length)(query_grad_tile)
    settle_query = to_sibling(query_own, lands_c[0])

    def context_grad_tile(zi):
        place = pl.multiple_of(zi * block, block)
        value = None
        for j in range(slot_count):
            turned = context[j, :, pl.ds(place, block)].T
            term = matmul(turned, pool[j * key_count:(j + 1) * key_count])
            value = term if value is None else value + term
        up_all[zi] = value.astype(BF16).reshape(2, 2, block // 4, 2 * inner)

    context_moves = []

    def settle_context(zi):
        context_moves[zi].wait()
        add_into(context_own(zi, ALL, ALL, rep), lands_c[1].at[zi])

    for zi in range(length):
        context_grad_tile(zi)
        land = lands_c[1].at[zi]
        context_moves.append(slots.move(links.device("core"), context_own(zi, ALL, ALL, 1 - rep), land, land))
        context_moves[-1].start()
        if zi == 1:
            settle_query()
            reductions.extend(halved_reduction(query_own, 2, query_result, 0, inner, ("y", "x"), 8, 10, 11, 12))
            send_off(8)
        if zi > 0:
            settle_context(zi - 1)
    settle_context(length - 1)
    reductions.extend(halved_reduction(context_own, 3, context_result, 0, inner, ("y", "x"), 9, 11, 12, 13))
    reductions.extend(halved_reduction(context_own, 3, context_result, inner, inner, ("y", "x"), 9, 12, 13, 14))
    send_off(9)
    slots.group = 7
    own_rows_move = slots.move(links.device("x"), own_rows_send, own_rows_land, own_rows_land)
    own_rows_move.start()
    after_back.near.wait()
    after_back.across.wait()
    slots.drain(5)
    branch[:rows] = ((after[...] + totals[1] + after_lands[1].astype(F32) + after_lands[2].astype(F32)) * kept).astype(BF16)
    written = [locals_.fill(
        [(branch.at[pl.ds(j * latent_count, latent_count)], latents_out.at[j]) for j in range(slot_count)], latents_out)]

    context_up = totals.at[1]

    def input_slot(j):
        at = pl.ds(pl.multiple_of(j * key_count, 16), key_count)
        own = pl.ds(pl.multiple_of(j * latent_count, latent_count), latent_count)
        context_up[...] = matmul_right(pool[at], context_all[...].reshape(width, 2 * inner))
        context_up[patches:] = context_up[patches:] + matmul_right(d_query[j], query_all[...].reshape(width, inner))

        def media_tile(at, size=patches // 2):
            tile = pl.ds(at, size)
            upstream = context_up[tile]
            value, gain_terms = layer_norm_back(media_in[j, tile].astype(F32), vectors[0:1], upstream)
            sums[0] = sums[0] + fold(gain_terms)
            sums[1] = sums[1] + fold(upstream)
            media_in[j, tile] = value.astype(BF16)

        tiles(2, patches // 2, media_tile)
        upstream = context_up[patches:]
        value, gain_terms = layer_norm_back(latents_in[j].astype(F32), vectors[2:3], upstream)
        sums[2] = sums[2] + fold(gain_terms)
        sums[3] = sums[3] + fold(upstream)
        latents_in[j] = (d_feed[own] + value).astype(BF16)

    pl.loop(0, 1)(input_slot)
    send_off(10)
    pl.loop(1, 3)(input_slot)
    send_off(11)
    pl.loop(3, 4)(input_slot)
    send_off(12)
    pl.loop(4, slot_count)(input_slot)
    for number in range(6):
        total[number:number + 1] = jnp.sum(sums[number], axis=0, keepdims=True)
    total[6:] = jnp.zeros_like(total[6:])
    vector_sum = VectorSum(links, slots, total, total_stage, total_lands)
    vector_sum.step(0)
    send_off(13)
    written.append(locals_.copy(media_in, media_grad_out))
    written.append(locals_.copy(latents_in, latents_grad_out))
    own_rows_move.wait()
    up_result[1] = own_rows_land[...].astype(F32)
    vector_sum.step(1)

    def hand_over(numbers):
        for number in numbers:
            value, out = result[number], grads_out[number]
            written.append(locals_.copy(value, out.at[rep]))
            written.append(slots.move(links.device("core"), value, out.at[rep], out.at[1 - rep]))
            written[-1].start()

    hand_over((0, 1, 2, 4))
    vector_sum.step(2)
    send_off(14)
    hand_over((3,))
    vector_sum.step(3)
    vector_sum.step(4)
    sums_out[...] = total[...]
    for copy in written:
        copy.wait()
    slots.drain(6)
    slots.drain(7)


def layer(length, counts, media, latents, grad_out, packed, shards):
    query_shard, context_shard, output_shard, up_shard, down_shard = shards
    slot_count, patches, width = media.shape
    latent_count = latents.shape[1]
    key_count = patches + latent_count
    rows = slot_count * latent_count
    inner = query_shard.shape[1]
    unit = down_shard.shape[0] // 2
    hidden = up_shard.shape[1] // 4
    blocks = (length, 2, 2)

    def halved(shard):
        return blocks + (2, shard.shape[0] // 2, shard.shape[1])

    up_shape = blocks + (up_shard.shape[0], hidden)
    down_shape = (length, 2, unit, width)
    halves = [halved(s)[4:] for s in shards[:3]]
    results = [(2,) + up_shape[3:], (unit, width)] + halves
    anywhere = pl.BlockSpec(memory_space=pl.ANY)
    vmem = pl.BlockSpec(memory_space=pltpu.VMEM)
    sums_shape = (8, width)
    scratch = [
        pltpu.VMEM(halved(query_shard), BF16),
        pltpu.VMEM(halved(context_shard), BF16),
        pltpu.VMEM(halved(output_shard), BF16),
        pltpu.VMEM(up_shape, BF16),
        pltpu.VMEM(down_shape, BF16),
        pltpu.VMEM(blocks + packed.shape, BF16),
        pltpu.VMEM((8, width), F32),
        pltpu.VMEM(media.shape, BF16),
        pltpu.VMEM(latents.shape, BF16),
        pltpu.VMEM(grad_out.shape, BF16),
        pltpu.VMEM((slot_count, key_count, width), BF16),
        pltpu.VMEM((slot_count, key_count, 2 * inner), BF16),
        pltpu.VMEM((slot_count, latent_count, inner), BF16),
        pltpu.VMEM((slot_count, latent_count, inner), BF16),
        pltpu.VMEM((rows, width), F32),
        pltpu.VMEM((4 * rows, width), BF16),
        pltpu.VMEM((width, 4 * rows), BF16),
        pltpu.VMEM((4 * rows, width), BF16),
        pltpu.VMEM((width, 4 * rows), BF16),
        pltpu.VMEM((max(12 * rows, slot_count * key_count), hidden), BF16),
        pltpu.VMEM((2, rows, width), F32),
        pltpu.VMEM((3, rows, width), BF16),
        pltpu.VMEM((3, rows, width), BF16),
        pltpu.VMEM(up_shape, BF16),
        pltpu.VMEM((length, 2, width, unit), BF16),
        pltpu.VMEM(halved(query_shard), BF16),
        pltpu.VMEM(halved(output_shard), BF16),
        pltpu.VMEM((latent_count * (GROUP // HEAD_DIM), GROUP), F32),
        pltpu.VMEM((6, 8, width), F32),
        pltpu.VMEM(sums_shape, F32),
        pltpu.VMEM((4,) + sums_shape, F32),
        pltpu.VMEM((2 + length,) + sums_shape, F32),
        pltpu.VMEM(up_shape[3:], BF16),
        pltpu.VMEM(up_shape[3:], BF16),
        [pltpu.VMEM(blocks + h, BF16) for h in halves],
        [pltpu.VMEM((length, 2) + up_shape[3:], BF16), pltpu.VMEM((length, width, unit), BF16)]
        + [pltpu.VMEM((length, 2) + h, BF16) for h in halves],
        [None, None] + [pltpu.VMEM((length,) + h, BF16) for h in halves],
        [pltpu.VMEM((length - 1, 2) + up_shape[3:], BF16), pltpu.VMEM((length - 1, width, unit), BF16)]
        + [pltpu.VMEM((length - 1,) + h, BF16) for h in halves],
        [pltpu.VMEM(r, F32) for r in results],
        pltpu.SemaphoreType.DMA((8,)),
        pltpu.SemaphoreType.DMA((112,)),
        pltpu.SemaphoreType.DMA((24,)),
    ]
    out_shape = (
        jax.ShapeDtypeStruct(latents.shape, BF16), jax.ShapeDtypeStruct(media.shape, BF16),
        jax.ShapeDtypeStruct(latents.shape, BF16), jax.ShapeDtypeStruct(sums_shape, F32),
        [jax.ShapeDtypeStruct((2,) + r, F32) for r in results])
    return pl.pallas_call(
        functools.partial(layer_kernel, length, HEAD_DIM ** (-0.5)),
        out_shape=out_shape,
        in_specs=[pl.BlockSpec(memory_space=pltpu.SMEM)] + [anywhere] * 9,
        out_specs=(anywhere, anywhere, anywhere, vmem, [anywhere] * 5),
        scratch_shapes=scratch,
        compiler_params=pltpu.CompilerParams(
            collective_id=0, has_side_effects=True, vmem_limit_bytes=127 * 2 ** 19),
        name="resampler_layer",
    )(counts, media, latents, grad_out, packed, query_shard, context_shard, output_shard, up_shard, down_shard)


def finish_kernel(length, latents_raw, media_grad_raw, latents_grad_raw, grads_raw, latents_out, media_grad_out,
                  latents_grad_out, grads_out, held, held_grads, local):
    x = Links(length).x
    locals_ = Locals(local)
    raws = [latents_raw, latents_grad_raw, *grads_raw]
    stages = [held[0], held[1], *held_grads]
    outs = [latents_out, latents_grad_out, *grads_out]
    count = media_grad_raw.shape[0]
    for j in range(count):
        raws.append(media_grad_raw.at[j])
        stages.append(held[2].at[j])
        outs.append(media_grad_out.at[j])
    loads = [locals_.copy(raw, stage) for raw, stage in zip(raws, stages)]
    unit = grads_raw[1].shape[1]
    copies = []
    for number, (load, stage, out) in enumerate(zip(loads, stages, outs)):
        load.wait()
        if number != 2:
            copies.append(locals_.copy(stage, out))
            continue
        moves = []
        for core in range(2):
            for plane in range(2):
                half = x if plane == 0 else 1 - x
                for owner in range(stage.shape[-1] // unit):
                    begin = pl.multiple_of(((2 * owner + half) * 2 + core) * unit, unit)
                    moves.append((stage.at[core, plane, :, pl.ds(owner * unit, unit)], out.at[:, pl.ds(begin, unit)]))
        copies.append(locals_.fill(moves, out))
    for copy in copies:
        copy.wait()


def finish(length, latents_raw, media_grad_raw, latents_grad_raw, grads_raw):
    anywhere = pl.BlockSpec(memory_space=pl.ANY)
    up = grads_raw[0]
    shapes = [jax.ShapeDtypeStruct((up.shape[2], 4 * up.shape[3]), up.dtype)]
    shapes += [jax.ShapeDtypeStruct(g.shape, g.dtype) for g in grads_raw[1:]]
    same = [jax.ShapeDtypeStruct(r.shape, r.dtype) for r in (latents_raw, media_grad_raw, latents_grad_raw)]
    return pl.pallas_call(
        functools.partial(finish_kernel, length),
        out_shape=(*same, shapes),
        in_specs=[anywhere, anywhere, anywhere, [anywhere] * 5],
        out_specs=(anywhere, anywhere, anywhere, [anywhere] * 5),
        scratch_shapes=[
            [pltpu.VMEM(r.shape, r.dtype) for r in (latents_raw, latents_grad_raw, media_grad_raw)],
            [pltpu.VMEM(g.shape, g.dtype) for g in grads_raw],
            pltpu.SemaphoreType.DMA((2 * (7 + media_grad_raw.shape[0]),)),
        ],
        compiler_params=pltpu.CompilerParams(vmem_limit_bytes=60 * 2 ** 20),
        name="finish",
    )(latents_raw, media_grad_raw, latents_grad_raw, grads_raw)


def head_scores(first_heads, second_heads):
    return jnp.einsum(
        "bqhd,bkhd->bhqk", first_heads, second_heads, preferred_element_type=jnp.float32
    )


def collective_body(
    media,
    latents,
    image_counts,
    grad_out,
    media_gain,
    media_bias,
    latent_gain,
    latent_bias,
    feed_gain,
    feed_bias,
    query_weight,
    context_weight,
    output_weight,
    up_weight,
    down_weight,
):
    samples, slots, patches, model_width = media.shape
    latent_count = latents.shape[2]
    inner_width = query_weight.shape[1]
    head_count = inner_width // HEAD_DIM
    blocks = samples * slots
    key_count = patches + latent_count
    latent_total = blocks * latent_count
    scaling = HEAD_DIM ** (-0.5)
    vector_shards = (media_gain, media_bias, latent_gain, latent_bias, feed_gain, feed_bias)
    weight_shards = (query_weight, context_weight, output_weight, up_weight, down_weight)
    gathered = tuple(lax.all_gather(s, "dp", axis=0, tiled=True) for s in vector_shards + weight_shards)
    vectors = [element.astype(jnp.float32) for element in gathered[:6]]
    media_rows = media.reshape(blocks * patches, model_width).astype(jnp.float32)
    latent_rows = latents.reshape(latent_total, model_width).astype(jnp.float32)
    media_normed = layer_norm(media_rows, vectors[0], vectors[1]).astype(jnp.bfloat16)
    latent_normed = layer_norm(latent_rows, vectors[2], vectors[3]).astype(jnp.bfloat16)
    queries = (matmul(latent_normed, gathered[6]) * scaling).astype(jnp.bfloat16)
    context = jnp.concatenate(
        [
            media_normed.reshape(blocks, patches, model_width),
            latent_normed.reshape(blocks, latent_count, model_width),
        ],
        axis=1,
    ).reshape(blocks * key_count, model_width)
    key_value = (
        matmul(context, gathered[7])
        .astype(jnp.bfloat16)
        .reshape(blocks, key_count, 2 * inner_width)
    )
    query_heads = queries.reshape(blocks, latent_count, head_count, HEAD_DIM)
    key_heads = key_value[:, :, :inner_width].reshape(blocks, key_count, head_count, HEAD_DIM)
    value_heads = key_value[:, :, inner_width:].reshape(blocks, key_count, head_count, HEAD_DIM)
    scores = head_scores(query_heads, key_heads)
    row_max = jnp.max(scores, axis=-1, keepdims=True)
    exponent = jnp.exp(scores - row_max)
    row_total = jnp.sum(exponent, axis=-1, keepdims=True)
    log_total = row_max + jnp.log(row_total)
    attention_weights = (exponent / row_total).astype(jnp.bfloat16)
    attended = (
        jnp.einsum(
            "bhqk,bkhd->bqhd", attention_weights, value_heads, preferred_element_type=jnp.float32
        )
        .astype(jnp.bfloat16)
        .reshape(latent_total, inner_width)
    )
    after_attention = latent_rows + matmul(attended, gathered[8])
    feed_input = layer_norm(after_attention, vectors[4], vectors[5]).astype(jnp.bfloat16)
    hidden = matmul(feed_input, gathered[9])
    activated = gelu_exact(hidden).astype(jnp.bfloat16)
    after_feed = after_attention + matmul(activated, gathered[10])
    slot_mask = (
        lax.broadcasted_iota(jnp.int32, (samples, slots), 1) < image_counts[:, None]
    ).astype(jnp.float32)
    row_mask = jnp.broadcast_to(slot_mask[:, :, None], (samples, slots, latent_count)).reshape(
        latent_total, 1
    )
    latents_out = (after_feed * row_mask).astype(jnp.bfloat16).reshape(latents.shape)
    backward_set = gathered
    back_vectors = [element.astype(jnp.float32) for element in backward_set[:6]]
    d_after = grad_out.reshape(latent_total, model_width).astype(jnp.float32) * row_mask
    d_branch = d_after.astype(jnp.bfloat16)
    grad_down = matmul_left(activated, d_branch)
    d_activated = matmul_right(d_branch, backward_set[10])
    d_hidden = jax.vjp(gelu_exact, hidden)[1](d_activated)[0].astype(jnp.bfloat16)
    grad_up = matmul_left(feed_input, d_hidden)
    d_feed = matmul_right(d_hidden, backward_set[9])
    d_feed_norm, grad_feed_gain, grad_feed_bias = jax.vjp(
        layer_norm, after_attention, back_vectors[4], back_vectors[5]
    )[1](d_feed)
    d_middle = d_after + d_feed_norm
    d_out_branch = d_middle.astype(jnp.bfloat16)
    grad_output = matmul_left(attended, d_out_branch)
    d_attended = (
        matmul_right(d_out_branch, backward_set[8])
        .astype(jnp.bfloat16)
        .reshape(blocks, latent_count, head_count, HEAD_DIM)
    )
    recomputed = jnp.exp(head_scores(query_heads, key_heads) - log_total)
    d_weights = head_scores(d_attended, value_heads)
    d_scores = (
        recomputed * (d_weights - jnp.sum(recomputed * d_weights, axis=-1, keepdims=True))
    ).astype(jnp.bfloat16)
    d_queries = (
        jnp.einsum(
            "bhqk,bkhd->bqhd", d_scores, key_heads, preferred_element_type=jnp.float32
        ).astype(jnp.bfloat16)
        * scaling
    ).reshape(latent_total, inner_width)
    d_keys = jnp.einsum(
        "bhqk,bqhd->bkhd", d_scores, query_heads, preferred_element_type=jnp.float32
    ).astype(jnp.bfloat16)
    d_values = jnp.einsum(
        "bhqk,bqhd->bkhd",
        recomputed.astype(jnp.bfloat16),
        d_attended,
        preferred_element_type=jnp.float32,
    ).astype(jnp.bfloat16)
    d_key_value = jnp.concatenate(
        [
            d_keys.reshape(blocks, key_count, inner_width),
            d_values.reshape(blocks, key_count, inner_width),
        ],
        axis=-1,
    ).reshape(blocks * key_count, 2 * inner_width)
    grad_query = matmul_left(latent_normed, d_queries)
    grad_context = matmul_left(context, d_key_value)
    d_context = matmul_right(d_key_value, backward_set[7]).reshape(blocks, key_count, model_width)
    d_latent_normed = matmul_right(d_queries, backward_set[6]) + d_context[:, patches:, :].reshape(
        latent_total, model_width
    )
    d_media_normed = d_context[:, :patches, :].reshape(blocks * patches, model_width)
    d_latent_norm, grad_latent_gain, grad_latent_bias = jax.vjp(
        layer_norm, latent_rows, back_vectors[2], back_vectors[3]
    )[1](d_latent_normed)
    grad_latents = (d_middle + d_latent_norm).astype(jnp.bfloat16).reshape(latents.shape)
    d_media, grad_media_gain, grad_media_bias = jax.vjp(
        layer_norm, media_rows, back_vectors[0], back_vectors[1]
    )[1](d_media_normed)
    grad_media = d_media.astype(jnp.bfloat16).reshape(media.shape)
    vector_grads = jnp.stack([
        grad_media_gain, grad_media_bias, grad_latent_gain, grad_latent_bias, grad_feed_gain, grad_feed_bias])
    weight_grads = [
        g.astype(jnp.bfloat16) for g in (grad_query, grad_context, grad_output, grad_up, grad_down)]
    vector_sums = lax.psum_scatter(vector_grads, "dp", scatter_dimension=1, tiled=True)
    summed = [lax.psum_scatter(g, "dp", scatter_dimension=0, tiled=True) for g in weight_grads]
    owned = tuple(lax.psum(vector_sums, "rep")) + tuple(
        lax.psum(s, "rep").astype(jnp.float32) for s in summed)
    return (
        latents_out,
        grad_media,
        grad_latents,
        owned[0],
        owned[1],
        owned[2],
        owned[3],
        owned[4],
        owned[5],
        owned[6],
        owned[7],
        owned[8],
        owned[9],
        owned[10],
    )


def body(media, latents, image_counts, grad_out, *parameters):
    chips = lax.axis_size("dp")
    weight_shards = parameters[6:]
    tiled = (media.shape[0] == 1 and chips % 4 == 0 and chips > 4 and parameters[0].shape[0] == 64
             and all(s.shape[0] % 32 == 0 for s in weight_shards))
    if not tiled:
        return collective_body(media, latents, image_counts, grad_out, *parameters)
    side = lax.rem(lax.axis_index("dp"), 2)
    stacked = jnp.stack(parameters[:6])
    packed = jnp.pad(
        jnp.concatenate([jnp.where(side == 0, stacked, 0), jnp.where(side == 0, 0, stacked)], axis=1), ((0, 10), (0, 0)))
    latents_out, grad_media, grad_latents, vector_sums, summed = layer(
        chips // 4, image_counts, media[0], latents[0], grad_out[0], packed, weight_shards)
    latents_out, grad_media, grad_latents, summed = finish(
        chips // 4, latents_out, grad_media, grad_latents, summed)
    sums = [s.reshape(-1, s.shape[-1]) for s in summed[2:] + summed[:2]]
    width = parameters[0].shape[0]
    mine = lax.dynamic_slice(vector_sums, (0, lax.axis_index("dp") * width), (6, width))
    return (latents_out[None], grad_media[None], grad_latents[None]) + tuple(mine) + tuple(sums)


def solution(mesh):
    return jax.shard_map(
        body,
        mesh=mesh,
        in_specs=(
            P(("dp", "rep"), None, None, None),
            P(("dp", "rep"), None, None, None),
            P(("dp", "rep")),
            P(("dp", "rep"), None, None, None),
            P("dp"),
            P("dp"),
            P("dp"),
            P("dp"),
            P("dp"),
            P("dp"),
            P("dp", None),
            P("dp", None),
            P("dp", None),
            P("dp", None),
            P("dp", None),
        ),
        out_specs=(
            P(("dp", "rep"), None, None, None),
            P(("dp", "rep"), None, None, None),
            P(("dp", "rep"), None, None, None),
            P("dp"),
            P("dp"),
            P("dp"),
            P("dp"),
            P("dp"),
            P("dp"),
            P("dp", None),
            P("dp", None),
            P("dp", None),
            P("dp", None),
            P("dp", None),
        ),
        check_vma=False,
    )
```

```python
import functools

import jax
import jax.numpy as jnp
from jax import lax
from jax.experimental import pallas as pl
from jax.experimental.pallas import tpu as pltpu
from jax.sharding import PartitionSpec as P

HEAD_DIM = 64
GROUP = 256

epsilon = 1e-05

MESH = pl.DeviceIdType.MESH
ALL = slice(None)
F32 = jnp.float32
BF16 = jnp.bfloat16


class Links:
    def __init__(self, length):
        self.length = length
        self.dp = lax.axis_index("dp")
        self.rep = lax.axis_index("rep")
        self.z = lax.div(self.dp, 4)
        self.y = lax.rem(lax.div(self.dp, 2), 2)
        self.x = lax.rem(self.dp, 2)

    def device(self, axis, way=0):
        if axis == "core":
            return (self.dp, 1 - self.rep)
        if axis == "x":
            return (self.dp + 1 - 2 * self.x, self.rep)
        if axis == "y":
            return (self.dp + 2 - 4 * self.y, self.rep)
        return (self.dp + 4 * (self.along(way) - self.z), self.rep)

    def along(self, way):
        return lax.rem(self.z + way + self.length, self.length)

    def greet(self):
        barrier = pltpu.get_barrier_semaphore()
        peers = [("core", 0), ("x", 0), ("y", 0)] + [("z", way) for way in range(1, self.length)]
        for axis, way in peers:
            pl.semaphore_signal(barrier, inc=1, device_id=self.device(axis, way), device_id_type=MESH)
        pl.semaphore_wait(barrier, len(peers))


class Move:
    def __init__(self, slots, copies, landing):
        send, recv = slots.send.at[slots.group], slots.recv.at[slots.made]
        slots.made += 1
        self.slots, self.group, self.copies = slots, slots.group, [
            pltpu.make_async_remote_copy(
                src_ref=source, dst_ref=target, send_sem=send, recv_sem=recv,
                device_id=device, device_id_type=MESH)
            for device, source, target in copies]
        self.bytes = 0
        for _, source, _ in copies:
            size = jnp.dtype(source.dtype).itemsize
            for extent in source.shape:
                size *= extent
            self.bytes += size
        self.into = pltpu.make_async_remote_copy(
            src_ref=landing, dst_ref=landing, send_sem=send, recv_sem=recv,
            device_id=copies[0][0], device_id_type=MESH)

    def start(self):
        for copy in self.copies:
            copy.start()
        self.slots.sent[self.group] += self.bytes

    def wait(self):
        self.into.wait_recv()


class Slots:
    def __init__(self, send, recv, ruler):
        self.send, self.recv, self.ruler, self.made, self.group = send, recv, ruler, 0, 0
        self.sent = [0] * send.shape[0]

    def move(self, device, source, target, landing):
        return Move(self, [(device, source, target)], landing)

    def drain(self, group, ruler=None):
        ruler = self.ruler if ruler is None else ruler
        row = ruler.shape[-1] * jnp.dtype(ruler.dtype).itemsize
        rows, rest = divmod(self.sent[group], row)
        assert rest == 0 and rows % 16 == 0 and rows <= ruler.shape[0]
        whole = ruler.at[pl.ds(0, rows)]
        pltpu.make_async_copy(whole, whole, self.send.at[group]).wait()


class Locals:
    def __init__(self, semaphores):
        self.semaphores, self.made = semaphores, 0

    def copy(self, source, target):
        return self.fill([(source, target)], target)

    def fill(self, copies, whole):
        semaphore = self.semaphores.at[self.made]
        self.made += 1
        for source, target in copies:
            pltpu.make_async_copy(source, target, semaphore).start()
        return pltpu.make_async_copy(whole, whole, semaphore)


class Gather:
    def __init__(self, links, slots, view, axes, halved):
        here = {"z": links.z, "y": links.y, "x": links.x}
        self.moves = []
        for axis in axes:
            mine = view(here["z"], here["y"], here["x"])
            if axis == "z":
                self.moves.append(Move(
                    slots, [(links.device("z", way), mine, mine) for way in range(1, links.length)],
                    view(pl.ds(0, links.length - 1), here["y"], here["x"])))
            else:
                other = dict(here)
                other[axis] = 1 - here[axis]
                self.moves.append(
                    slots.move(links.device(axis), mine, mine, view(other["z"], other["y"], other["x"])))
            here[axis] = ALL
        if halved:
            mine = view(ALL, ALL, ALL)
            self.moves.append(
                slots.move(links.device("core"), mine, mine, view(ALL, ALL, ALL, 1 - links.rep)))

    def step(self, number):
        if 0 < number <= len(self.moves):
            self.moves[number - 1].wait()
        if 0 <= number < len(self.moves):
            self.moves[number].start()


class Reduce:
    def __init__(self, links, slots, own, axes, lands, lands_z, finish):
        self.own, self.links, self.finish, self.lands_z = own, links, finish, lands_z
        self.moves, self.adds = [], []
        z, y, x = links.z, links.y, links.x
        here = {"z": ALL, "y": ALL, "x": ALL}
        for axis, land in zip(axes, lands):
            away, home = dict(here), dict(here)
            place = {"y": y, "x": x}[axis]
            away[axis], home[axis] = 1 - place, place
            self.moves.append(slots.move(
                links.device(axis), own(away["z"], away["y"], away["x"]), land, land))
            here = home
            self.adds.append(functools.partial(add_into, own(home["z"], home["y"], home["x"]), land))
        self.moves.append(Move(
            slots, [(links.device("z", way), own(links.along(way), here["y"], here["x"]), lands_z.at[way - 1])
                    for way in range(1, links.length)], lands_z))
        self.mine = own(z, here["y"], here["x"])
        self.adds.append(self.end)

    def step(self, number):
        if 0 < number <= len(self.moves):
            self.moves[number - 1].wait()
            self.adds[number - 1]()
        if 0 <= number < len(self.moves):
            self.moves[number].start()

    def end(self):
        total = self.mine[...].astype(F32)
        for way in range(1, self.links.length):
            total = total + self.lands_z[way - 1].astype(F32)
        self.finish(total)


def add_into(target, arrived):
    @pl.loop(0, target.shape[0])
    def _(number):
        target[number] = (target[number].astype(F32) + arrived[number].astype(F32)).astype(target.dtype)


def run(table, tick):
    for item, ticks in table:
        if tick in ticks:
            item.step(ticks.index(tick))


def matmul(left, right):
    return jnp.dot(left, right, preferred_element_type=F32)


def matmul_left(left, right):
    return lax.dot_general(left, right, (((0,), (0,)), ((), ())), preferred_element_type=F32)


def matmul_right(left, right):
    return lax.dot_general(left, right, (((1,), (1,)), ((), ())), preferred_element_type=F32)


def layer_norm(values, gain, offset):
    centre = jnp.mean(values, axis=-1, keepdims=True)
    shifted = values - centre
    spread = jnp.mean(shifted * shifted, axis=-1, keepdims=True)
    return shifted * lax.rsqrt(spread + epsilon) * gain + offset


def layer_norm_back(values, gain, upstream):
    centre = jnp.mean(values, axis=-1, keepdims=True)
    shifted = values - centre
    spread = jnp.mean(shifted * shifted, axis=-1, keepdims=True)
    rate = lax.rsqrt(spread + epsilon)
    normed = shifted * rate
    scaled = upstream * gain
    first = jnp.mean(scaled, axis=-1, keepdims=True)
    second = jnp.mean(scaled * normed, axis=-1, keepdims=True)
    return rate * (scaled - first - normed * second), upstream * normed


def gelu_exact(values):
    return 0.5 * values * (1.0 + jax.scipy.special.erf(values * 0.7071067811865476))


def gelu_parts(values):
    cumulative = 0.5 * (1.0 + lax.erf(values * 0.7071067811865476))
    density = 0.3989422804014327 * jnp.exp(-0.5 * values * values)
    return values * cumulative, cumulative + values * density


def tiles(count, size, action):
    @pl.loop(0, count)
    def _(number):
        action(pl.multiple_of(number * size, size))


def head_mask(rows, columns):
    heads = columns // HEAD_DIM
    row = lax.broadcasted_iota(jnp.int32, (rows * heads, columns), 0)
    column = lax.broadcasted_iota(jnp.int32, (rows * heads, columns), 1)
    head_row = jnp.zeros_like(row)
    head_column = jnp.zeros_like(row)
    for head in range(1, heads):
        head_row = head_row + jnp.where(row >= head * rows, 1, 0)
        head_column = head_column + jnp.where(column >= head * HEAD_DIM, 1, 0)
    return jnp.where(head_row == head_column, 1.0, 0.0)


def spread_heads(rows, mask):
    return jnp.concatenate([rows] * (mask.shape[0] // rows.shape[0]), axis=0) * mask


def pick_heads(stacked, mask, rows):
    kept = stacked * mask
    total = kept[:rows]
    for head in range(1, stacked.shape[0] // rows):
        total = total + kept[head * rows:(head + 1) * rows]
    return total


def softmax(scores):
    exponent = jnp.exp(scores - jnp.max(scores, axis=-1, keepdims=True))
    return exponent / jnp.sum(exponent, axis=-1, keepdims=True)


class VectorSum:
    def __init__(self, links, slots, total, stage, lands):
        self.total, self.stage, self.lands, self.length = total, stage, lands, links.length
        self.moves = [slots.move(links.device(axis), stage.at[number], lands.at[number], lands.at[number])
                      for number, axis in enumerate(("core", "x", "y"))]
        self.moves.append(Move(
            slots, [(links.device("z", way), stage.at[3], lands.at[2 + way]) for way in range(1, links.length)],
            lands.at[pl.ds(3, links.length - 1)]))

    def step(self, number):
        if 0 < number <= 4:
            self.moves[number - 1].wait()
            for land in ([number - 1] if number < 4 else range(3, 2 + self.length)):
                self.total[...] = self.total[...] + self.lands[land]
        if number < 4:
            self.stage[number] = self.total[...]
            self.moves[number].start()


class Rows:
    def __init__(self, links, slots, buffer, count, parts):
        self.moves, self.passed = [], []
        for begin, size in parts:
            def place(owner, begin=begin, size=size):
                return buffer.at[pl.ds(owner * count + begin, size)]

            self.moves.append([
                slots.move(links.device("x"), place(0), place(2), place(2)),
                slots.move(links.device("core"), place(0), place(1), place(1))])
            self.passed.append(slots.move(links.device("core"), place(2), place(3), place(3)))

    def send(self, part):
        for move in self.moves[part]:
            move.start()

    def near(self, part):
        self.moves[part][1].wait()

    def forward(self, part):
        self.moves[part][0].wait()
        self.passed[part].start()

    def far(self, part):
        self.passed[part].wait()


class Partials:
    def __init__(self, links, slots, stage, lands, count):
        def place(owner):
            return stage.at[pl.ds(owner * count, count)]

        self.place, self.lands = place, lands
        self.far = slots.move(links.device("core"), place(3), lands.at[0], lands.at[0])
        self.near = slots.move(links.device("core"), place(1), lands.at[1], lands.at[1])
        self.across = slots.move(links.device("x"), place(2), lands.at[2], lands.at[2])


def layer_kernel(length, scaling, counts, media, latents, grad_out, packed, query_shard, context_shard,
                 output_shard, up_shard, down_shard, latents_out, media_grad_out, latents_grad_out, sums_out, grads_out,
                 query_all, context_all, output_all, up_all, down_all,
                 packed_all, vectors, media_in, latents_in, grad_in, context, key_value, query, attended, after,
                 feed, feed_t, branch, branch_t, pool, totals, after_lands, d_feed_lands,
                 grad_up, grad_down, grad_query, grad_output, mask, sums, total, total_stage, total_lands,
                 own_rows_send, own_rows_land, lands_c, lands_b, lands_a, lands_z, result, send, recv, local):
    links = Links(length)
    z, y, x, rep = links.z, links.y, links.x, links.rep
    slots, locals_ = Slots(send, recv, pool), Locals(local)
    slot_count, patches, width = media.shape
    latent_count = latents.shape[1]
    key_count = patches + latent_count
    rows = slot_count * latent_count
    inner = query.shape[-1]
    chunks = length
    hidden = up_all.shape[-1]
    chunk = hidden // chunks
    unit = down_all.shape[-2]
    xy, yx = ("z", "x", "y"), ("z", "y", "x")

    def unit_columns(half, number):
        return pl.ds(pl.multiple_of(((2 * number + half) * 2 + rep) * unit, unit), unit)

    staged = [locals_.copy(packed, packed_all.at[z, y, x])]
    for shard, whole in ((context_shard, context_all), (query_shard, query_all), (output_shard, output_all)):
        half = whole.shape[-2]
        staged.append(locals_.copy(shard.at[pl.ds(pl.multiple_of(rep * half, 16), half)], whole.at[z, y, x, rep]))
    units = range(hidden // unit)
    staged.append(locals_.fill(
        [(up_shard.at[:, unit_columns(1 - x, n)], own_rows_send.at[:, pl.ds(n * unit, unit)]) for n in units],
        own_rows_send))
    staged.append(locals_.fill(
        [(up_shard.at[:, unit_columns(x, n)], up_all.at[z, y, x, :, pl.ds(n * unit, unit)]) for n in units],
        up_all.at[z, y, x]))
    staged.append(locals_.copy(down_shard.at[pl.ds(pl.multiple_of(rep * unit, 16), unit)], down_all.at[z, y]))
    grad_load = locals_.copy(grad_out, grad_in)
    latents_load = locals_.copy(latents, latents_in)
    media_load = locals_.copy(media, media_in)
    links.greet()

    def halves(whole, begin, size, order):
        def view(zi, yi, xi, half=rep):
            return whole.at[zi, yi, xi, half, :, pl.ds(begin, size)]

        return Gather(links, slots, view, order, True)

    slots.group = 0
    vector_gather = Gather(links, slots, lambda zi, yi, xi: packed_all.at[zi, yi, xi], xy, False)
    slots.group = 1
    gathers = [
        (halves(context_all, 0, width // 2, xy), (0, 1, 2, 3, 4)),
        (halves(context_all, width // 2, width // 2, yx), (0, 1, 2, 3, 4)),
        (halves(query_all, 0, inner, yx), (0, 2, 3, 4, 5)), (halves(output_all, 0, width, yx), (0, 2, 3, 4, 5)),
    ]
    slots.group = 2
    for number in range(2 * chunks):
        window = pl.ds(number % chunks * chunk, chunk)
        if number < chunks:
            def view(zi, yi, xi, window=window):
                return down_all.at[zi, yi, :, window]
        else:
            def view(zi, yi, xi, window=window):
                return up_all.at[zi, yi, ALL, :, window]
        ticks = (max(number - 1, 0), number + 2, number + 4)
        gathers.append((Gather(links, slots, view, ("z", "y"), False), ticks))
    up_across = slots.move(links.device("x"), own_rows_send, up_all.at[z, y, x], up_all.at[z, y, 1 - x])
    slots.group = 3
    parts = [(0, 2 * latent_count), (2 * latent_count, rows - 2 * latent_count)]
    branch_rows = Rows(links, slots, branch, rows, [(0, rows)])
    feed_rows = Rows(links, slots, feed, rows, parts)

    def pump(tick):
        run(gathers, tick)

    for copy in staged:
        copy.wait()
    vector_gather.step(0)
    pump(0)
    up_across.start()
    grad_load.wait()
    kept = jnp.where(lax.broadcasted_iota(jnp.int32, (rows, 1), 0) < counts[0] * latent_count, 1.0, 0.0)
    branch[:rows] = (grad_in[...].reshape(rows, width).astype(F32) * kept).astype(BF16)
    vector_gather.step(1)
    mask[...] = head_mask(latent_count, GROUP)
    sums[...] = jnp.zeros_like(sums)
    vector_gather.step(2)
    latents_load.wait()
    media_load.wait()
    pump(1)
    vector_gather.step(3)
    lane = packed_all.shape[-1]
    for zi in range(length):
        for yi in range(2):
            place = (zi * 2 + yi) * lane
            vectors[:, place:place + lane] = (packed_all[zi, yi, 0] + packed_all[zi, yi, 1]).astype(F32)[:8]

    def normalise_slot(j):
        context[j, :patches] = layer_norm(media_in[j].astype(F32), vectors[0:1], vectors[1:2]).astype(BF16)
        context[j, patches:] = layer_norm(latents_in[j].astype(F32), vectors[2:3], vectors[3:4]).astype(BF16)

    pl.loop(0, slot_count)(normalise_slot)
    pump(2)
    up_across.wait()
    pump(3)
    pump(4)
    branch_rows.send(0)

    def key_value_slot(j):
        key_value[j] = matmul(context[j], context_all[...].reshape(width, 2 * inner)).astype(BF16)

    pl.loop(0, 3)(key_value_slot)
    pump(5)
    pl.loop(3, slot_count)(key_value_slot)
    latent_normed = context[:, patches:, :].reshape(rows, width)
    query[...] = (matmul(latent_normed, query_all[...].reshape(width, inner)) * scaling).astype(BF16).reshape(
        slot_count, latent_count, inner)
    pump(6)

    def attention_slot(j):
        for begin in range(0, inner, GROUP):
            stacked = spread_heads(query[j, :, begin:begin + GROUP], mask[...].astype(BF16))
            probs = softmax(matmul_right(stacked, key_value[j, :, begin:begin + GROUP])).astype(BF16)
            value = matmul(probs, key_value[j, :, inner + begin:inner + begin + GROUP])
            attended[j, :, begin:begin + GROUP] = pick_heads(value, mask[...], latent_count).astype(BF16)

    for part, (begin, size) in enumerate(parts):
        first, last = begin // latent_count, (begin + size) // latent_count
        pl.loop(first, last)(attention_slot)
        after[begin:begin + size] = latents_in[first:last].reshape(size, width).astype(F32) + matmul(
            attended[first:last].reshape(size, inner), output_all[...].reshape(inner, width))
        feed[begin:begin + size] = layer_norm(
            after[begin:begin + size], vectors[4:5], vectors[5:6]).astype(BF16)
        feed_rows.send(part)
        pump(7 + part)
    slots.drain(0, grad_down.at[0, 0])
    branch_rows.near(0)
    branch_rows.forward(0)

    def turn(source, target, owner):
        def body(at):
            target[pl.ds(at, 256), pl.ds(owner * rows, 2 * rows)] = source[
                pl.ds(owner * rows, 2 * rows), pl.ds(at, 256)].T

        tiles(width // 256, 256, body)

    turn(branch, branch_t, 0)
    branch_rows.far(0)
    tall = rows
    d_active, active, d_hidden = [pool.at[pl.ds(n * 4 * rows, 4 * rows)] for n in range(3)]

    def d_active_tile(at):
        d_active[pl.ds(at, tall)] = matmul_right(
            branch[pl.ds(at, tall)], down_all[...].reshape(hidden, width)).astype(BF16)

    tiles(4, tall, d_active_tile)
    turn(branch, branch_t, 2)

    def hidden_tile(at, begin):
        window = pl.ds(begin, chunk)
        weight = up_all[:, :, :, :, window].reshape(width, chunk)
        value, slope = gelu_parts(matmul(feed[pl.ds(at, tall)], weight))
        active[pl.ds(at, tall), window] = value.astype(BF16)
        d_hidden[pl.ds(at, tall), window] = (d_active[pl.ds(at, tall), window].astype(F32) * slope).astype(BF16)

    def d_feed_of(owner):
        return matmul_right(d_hidden[pl.ds(owner * rows, rows)], up_all[...].reshape(width, hidden))

    def after_feed_of(owner):
        return matmul(active[pl.ds(owner * rows, rows)], down_all[...].reshape(hidden, width))

    def rounded(buffer, owner, value):
        buffer[pl.ds(owner * rows, rows)] = value.astype(BF16)

    def across_tile(back, buffer):
        rounded(buffer, 2, totals[1] + back.lands[0].astype(F32))

    up_result, down_result, query_result, context_result, output_result = result
    reductions = []

    def send_off(tick):
        run(reductions, tick)

    def plane_reduction(own, lands_y, lands, finish):
        return Reduce(links, slots, own, ("y",), [lands_y], lands, finish)

    def keep_up(value, window):
        up_result[0, :, window] = jnp.where(x == 0, value[0], value[1])
        own_rows_send[:, window] = jnp.where(x == 0, value[1], value[0]).astype(BF16)

    feed_rows.near(0)
    feed_rows.near(1)
    slots.group = 6

    def near_hidden(c):
        tiles(2, tall, lambda at: hidden_tile(at, c * chunk))

    def far_hidden(c):
        tiles(2, tall, lambda at: hidden_tile(pl.multiple_of(2 * rows + at, tall), c * chunk))

    def grads(c):
        window = pl.ds(c * chunk, chunk)

        def grad_tile(number):
            size = width // 2
            place = pl.multiple_of(number * size, size)
            up = matmul(feed_t[pl.ds(place, size)], d_hidden[:, window]).astype(BF16)
            grad_up[pl.ds(number * (length // 2), length // 2), :, :, :, window] = up.reshape(
                length // 2, 2, 2, size // (2 * length), chunk)
            down = matmul(branch_t[pl.ds(place, size)], active[:, window]).astype(BF16)
            for owner in range(2):
                grad_down[c, owner, pl.ds(place, size)] = down[:, owner * unit:(owner + 1) * unit]

        pl.loop(0, 2)(grad_tile)
        reductions.append((plane_reduction(
            lambda zi, yi, xi: grad_up.at[zi, yi, ALL, :, window],
            lands_b[0].at[:, :, :, window], lands_z[0].at[:, :, :, window],
            functools.partial(keep_up, window=window)), (c, c + 2, c + 4)))
        send_off(c)

    near_hidden(0)
    pump(9)
    turn(feed, feed_t, 0)
    feed_rows.forward(0)
    feed_rows.forward(1)
    feed_rows.far(0)
    feed_rows.far(1)
    turn(feed, feed_t, 2)
    far_hidden(0)
    grads(0)
    near_hidden(1)
    far_hidden(1)
    pump(10)
    near_hidden(2)
    far_hidden(2)
    grads(1)
    for c in range(3, chunks):
        pump(8 + c)
        near_hidden(c)
        far_hidden(c)
    for group in range(1, 4):
        slots.drain(group)
    slots.group = 4
    d_feed_back = Partials(links, slots, feed, d_feed_lands, rows)
    slots.group = 5
    after_back = Partials(links, slots, branch, after_lands, rows)
    slots.group = 6
    rounded(feed, 3, d_feed_of(3))
    d_feed_back.far.start()
    totals[1] = d_feed_of(2)
    d_feed_back.far.wait()
    across_tile(d_feed_back, feed)
    d_feed_back.across.start()
    for c in range(2, chunks):
        grads(c)
    part_size = width // chunks
    for number in range(chunks):
        window = pl.ds(number * part_size, part_size)

        def keep_down(value, window=window):
            down_result[:, window] = value.T

        reductions.append((plane_reduction(
            lambda zi, yi, xi, window=window: grad_down.at[zi, yi, window],
            lands_b[1].at[:, window], lands_z[1].at[:, window], keep_down),
            (chunks, chunks + 2 + number, chunks + 4 + number) if number < chunks - 1 else (chunks, 10, 12)))
    send_off(4)
    rounded(feed, 1, d_feed_of(1))
    d_feed_back.near.start()
    totals[0] = d_feed_of(0)

    rounded(branch, 3, after_feed_of(3))
    after_back.far.start()
    totals[1] = after_feed_of(2)
    after_back.far.wait()
    across_tile(after_back, branch)
    send_off(5)
    rounded(branch, 1, after_feed_of(1))
    after_back.near.start()
    totals[1] = after_feed_of(0)
    d_feed_back.near.wait()
    d_feed_back.across.wait()
    after_back.across.start()
    slots.drain(4)

    def fold(terms):
        return jnp.sum(terms.reshape(-1, 8, width), axis=0)

    d_feed = totals.at[0]
    flat_grad = lambda at, size: grad_in[pl.ds(lax.div(at, latent_count), size // latent_count)].reshape(size, width)

    def middle_tile(at, size=latent_count):
        own = pl.ds(at, size)
        upstream = d_feed[own] + d_feed_lands[1, own].astype(F32) + d_feed_lands[2, own].astype(F32)
        d_norm, gain_terms = layer_norm_back(after[own], vectors[4:5], upstream)
        sums[4] = sums[4] + fold(gain_terms)
        sums[5] = sums[5] + fold(upstream)
        row = lax.broadcasted_iota(jnp.int32, (size, 1), 0) + at
        keep = jnp.where(row < counts[0] * latent_count, 1.0, 0.0)
        d_middle = flat_grad(at, size).astype(F32) * keep + d_norm
        d_feed[own] = d_middle
        feed[own] = d_middle.astype(BF16)

    tiles(slot_count, latent_count, middle_tile)

    context_rows, output_rows = context_all.shape[-2], output_all.shape[-2]

    def context_own(zi, yi, xi, half):
        return up_all.at[zi, yi, xi, pl.ds(pl.multiple_of(half * context_rows, 16), context_rows)]

    def query_own(zi, yi, xi, half):
        return grad_query.at[zi, yi, xi, half]

    def output_own(zi, yi, xi, half):
        return grad_output.at[zi, yi, xi, half]

    def to_sibling(own, land):
        move = slots.move(links.device("core"), own(ALL, ALL, ALL, 1 - rep), land, land)
        move.start()

        def settle():
            move.wait()
            add_into(own(ALL, ALL, ALL, rep), land)

        return settle

    def halved_reduction(own, number, target, begin, size, first, *ticks):
        made = []
        for which, order in enumerate((first, ("x", "y"))):
            window = pl.ds(begin + which * (size // 2), size // 2)

            def finish(value, window=window):
                target[:, window] = value

            made.append((Reduce(
                links, slots, lambda zi, yi, xi, window=window: own(zi, yi, xi, rep).at[..., window], order,
                [lands_b[number].at[:, :, :, window], lands_a[number].at[:, :, window]],
                lands_z[number].at[:, :, window], finish), ticks))
        return made

    d_branch = feed.at[pl.ds(0, rows)]
    output_block = inner // 2

    def output_grad_tile(number):
        place = pl.multiple_of(number * output_block, output_block)
        turned = attended[:, :, pl.ds(place, output_block)].reshape(rows, output_block).T
        value = matmul(turned, d_branch[...]).astype(BF16)
        grad_output[pl.ds(number * (length // 2), length // 2)] = value.reshape(
            length // 2, 2, 2, 2, output_rows, width)

    d_attended, d_query = grad_in.at[:, :, pl.ds(0, inner)], grad_in.at[:, :, pl.ds(inner, inner)]
    d_attended[...] = matmul_right(d_branch[...], output_all[...].reshape(inner, width)).astype(BF16).reshape(
        slot_count, latent_count, inner)

    def attention_back_slot(j):
        own = pl.ds(pl.multiple_of(j * latent_count, latent_count), latent_count)
        for begin in range(0, inner, GROUP):
            keys = key_value[j, :, begin:begin + GROUP]
            values = key_value[j, :, inner + begin:inner + begin + GROUP]
            low_mask = mask[...].astype(BF16)
            stacked = spread_heads(query[j, :, begin:begin + GROUP], low_mask)
            upstream = spread_heads(d_attended[j, :, begin:begin + GROUP], low_mask)
            probs = softmax(matmul_right(stacked, keys))
            d_probs = matmul_right(upstream, values)
            d_scores = (probs * (d_probs - jnp.sum(probs * d_probs, axis=-1, keepdims=True))).astype(BF16)
            d_query[j, :, begin:begin + GROUP] = (
                pick_heads(matmul(d_scores, keys), mask[...], latent_count).astype(BF16).astype(F32) * scaling
            ).astype(BF16)
            at = pl.ds(pl.multiple_of(j * key_count, 16), key_count)
            pool[at, begin:begin + GROUP] = matmul_left(d_scores, stacked).astype(BF16)
            pool[at, inner + begin:inner + begin + GROUP] = matmul_left(probs.astype(BF16), upstream).astype(BF16)

    pl.loop(0, 2)(attention_back_slot)
    send_off(6)
    pl.loop(0, 2)(output_grad_tile)
    settle_output = to_sibling(output_own, lands_c[2])
    pl.loop(2, 4)(attention_back_slot)
    settle_output()
    reductions.extend(halved_reduction(output_own, 4, output_result, 0, width, ("x", "y"), 7, 9, 10, 11))
    send_off(7)
    pl.loop(4, slot_count)(attention_back_slot)
    block = width // length

    def query_grad_tile(zi):
        place = pl.multiple_of(zi * block, block)
        turned = context[:, patches:, pl.ds(place, block)].reshape(rows, block).T
        value = matmul(turned, d_query[...].reshape(rows, inner)).astype(BF16)
        grad_query[zi] = value.reshape(2, 2, 2, context_rows, inner)

    pl.loop(0, length)(query_grad_tile)
    settle_query = to_sibling(query_own, lands_c[0])

    def context_grad_tile(zi):
        place = pl.multiple_of(zi * block, block)
        value = None
        for j in range(slot_count):
            turned = context[j, :, pl.ds(place, block)].T
            term = matmul(turned, pool[j * key_count:(j + 1) * key_count])
            value = term if value is None else value + term
        up_all[zi] = value.astype(BF16).reshape(2, 2, block // 4, 2 * inner)

    context_moves = []

    def settle_context(zi):
        context_moves[zi].wait()
        add_into(context_own(zi, ALL, ALL, rep), lands_c[1].at[zi])

    for zi in range(length):
        context_grad_tile(zi)
        land = lands_c[1].at[zi]
        context_moves.append(slots.move(links.device("core"), context_own(zi, ALL, ALL, 1 - rep), land, land))
        context_moves[-1].start()
        if zi == 1:
            settle_query()
            reductions.extend(halved_reduction(query_own, 2, query_result, 0, inner, ("y", "x"), 8, 10, 11, 12))
            send_off(8)
        if zi > 0:
            settle_context(zi - 1)
    settle_context(length - 1)
    reductions.extend(halved_reduction(context_own, 3, context_result, 0, inner, ("y", "x"), 9, 11, 12, 13))
    reductions.extend(halved_reduction(context_own, 3, context_result, inner, inner, ("y", "x"), 9, 11, 12, 13))
    send_off(9)
    slots.group = 7
    own_rows_move = slots.move(links.device("x"), own_rows_send, own_rows_land, own_rows_land)
    own_rows_move.start()
    after_back.near.wait()
    after_back.across.wait()
    slots.drain(5)
    branch[:rows] = ((after[...] + totals[1] + after_lands[1].astype(F32) + after_lands[2].astype(F32)) * kept).astype(BF16)
    written = [locals_.fill(
        [(branch.at[pl.ds(j * latent_count, latent_count)], latents_out.at[j]) for j in range(slot_count)], latents_out)]

    context_up = totals.at[1]

    def input_slot(j):
        at = pl.ds(pl.multiple_of(j * key_count, 16), key_count)
        own = pl.ds(pl.multiple_of(j * latent_count, latent_count), latent_count)
        context_up[...] = matmul_right(pool[at], context_all[...].reshape(width, 2 * inner))
        context_up[patches:] = context_up[patches:] + matmul_right(d_query[j], query_all[...].reshape(width, inner))

        def media_tile(at, size=patches // 2):
            tile = pl.ds(at, size)
            upstream = context_up[tile]
            value, gain_terms = layer_norm_back(media_in[j, tile].astype(F32), vectors[0:1], upstream)
            sums[0] = sums[0] + fold(gain_terms)
            sums[1] = sums[1] + fold(upstream)
            media_in[j, tile] = value.astype(BF16)

        tiles(2, patches // 2, media_tile)
        upstream = context_up[patches:]
        value, gain_terms = layer_norm_back(latents_in[j].astype(F32), vectors[2:3], upstream)
        sums[2] = sums[2] + fold(gain_terms)
        sums[3] = sums[3] + fold(upstream)
        latents_in[j] = (d_feed[own] + value).astype(BF16)

    pl.loop(0, 1)(input_slot)
    send_off(10)
    pl.loop(1, 3)(input_slot)
    send_off(11)
    pl.loop(3, 4)(input_slot)
    send_off(12)
    pl.loop(4, slot_count)(input_slot)
    for number in range(6):
        total[number:number + 1] = jnp.sum(sums[number], axis=0, keepdims=True)
    total[6:] = jnp.zeros_like(total[6:])
    vector_sum = VectorSum(links, slots, total, total_stage, total_lands)
    vector_sum.step(0)
    send_off(13)
    written.append(locals_.copy(media_in, media_grad_out))
    written.append(locals_.copy(latents_in, latents_grad_out))
    own_rows_move.wait()
    up_result[1] = own_rows_land[...].astype(F32)
    vector_sum.step(1)

    def hand_over(numbers):
        for number in numbers:
            value, out = result[number], grads_out[number]
            written.append(locals_.copy(value, out.at[rep]))
            written.append(slots.move(links.device("core"), value, out.at[rep], out.at[1 - rep]))
            written[-1].start()

    hand_over((0, 1, 2, 4))
    vector_sum.step(2)
    send_off(14)
    hand_over((3,))
    vector_sum.step(3)
    vector_sum.step(4)
    sums_out[...] = total[...]
    for copy in written:
        copy.wait()
    slots.drain(6)
    slots.drain(7)


def layer(length, counts, media, latents, grad_out, packed, shards):
    query_shard, context_shard, output_shard, up_shard, down_shard = shards
    slot_count, patches, width = media.shape
    latent_count = latents.shape[1]
    key_count = patches + latent_count
    rows = slot_count * latent_count
    inner = query_shard.shape[1]
    unit = down_shard.shape[0] // 2
    hidden = up_shard.shape[1] // 4
    blocks = (length, 2, 2)

    def halved(shard):
        return blocks + (2, shard.shape[0] // 2, shard.shape[1])

    up_shape = blocks + (up_shard.shape[0], hidden)
    down_shape = (length, 2, unit, width)
    halves = [halved(s)[4:] for s in shards[:3]]
    results = [(2,) + up_shape[3:], (unit, width)] + halves
    anywhere = pl.BlockSpec(memory_space=pl.ANY)
    vmem = pl.BlockSpec(memory_space=pltpu.VMEM)
    sums_shape = (8, width)
    scratch = [
        pltpu.VMEM(halved(query_shard), BF16),
        pltpu.VMEM(halved(context_shard), BF16),
        pltpu.VMEM(halved(output_shard), BF16),
        pltpu.VMEM(up_shape, BF16),
        pltpu.VMEM(down_shape, BF16),
        pltpu.VMEM(blocks + packed.shape, BF16),
        pltpu.VMEM((8, width), F32),
        pltpu.VMEM(media.shape, BF16),
        pltpu.VMEM(latents.shape, BF16),
        pltpu.VMEM(grad_out.shape, BF16),
        pltpu.VMEM((slot_count, key_count, width), BF16),
        pltpu.VMEM((slot_count, key_count, 2 * inner), BF16),
        pltpu.VMEM((slot_count, latent_count, inner), BF16),
        pltpu.VMEM((slot_count, latent_count, inner), BF16),
        pltpu.VMEM((rows, width), F32),
        pltpu.VMEM((4 * rows, width), BF16),
        pltpu.VMEM((width, 4 * rows), BF16),
        pltpu.VMEM((4 * rows, width), BF16),
        pltpu.VMEM((width, 4 * rows), BF16),
        pltpu.VMEM((max(12 * rows, slot_count * key_count), hidden), BF16),
        pltpu.VMEM((2, rows, width), F32),
        pltpu.VMEM((3, rows, width), BF16),
        pltpu.VMEM((3, rows, width), BF16),
        pltpu.VMEM(up_shape, BF16),
        pltpu.VMEM((length, 2, width, unit), BF16),
        pltpu.VMEM(halved(query_shard), BF16),
        pltpu.VMEM(halved(output_shard), BF16),
        pltpu.VMEM((latent_count * (GROUP // HEAD_DIM), GROUP), F32),
        pltpu.VMEM((6, 8, width), F32),
        pltpu.VMEM(sums_shape, F32),
        pltpu.VMEM((4,) + sums_shape, F32),
        pltpu.VMEM((2 + length,) + sums_shape, F32),
        pltpu.VMEM(up_shape[3:], BF16),
        pltpu.VMEM(up_shape[3:], BF16),
        [pltpu.VMEM(blocks + h, BF16) for h in halves],
        [pltpu.VMEM((length, 2) + up_shape[3:], BF16), pltpu.VMEM((length, width, unit), BF16)]
        + [pltpu.VMEM((length, 2) + h, BF16) for h in halves],
        [None, None] + [pltpu.VMEM((length,) + h, BF16) for h in halves],
        [pltpu.VMEM((length - 1, 2) + up_shape[3:], BF16), pltpu.VMEM((length - 1, width, unit), BF16)]
        + [pltpu.VMEM((length - 1,) + h, BF16) for h in halves],
        [pltpu.VMEM(r, F32) for r in results],
        pltpu.SemaphoreType.DMA((8,)),
        pltpu.SemaphoreType.DMA((112,)),
        pltpu.SemaphoreType.DMA((24,)),
    ]
    out_shape = (
        jax.ShapeDtypeStruct(latents.shape, BF16), jax.ShapeDtypeStruct(media.shape, BF16),
        jax.ShapeDtypeStruct(latents.shape, BF16), jax.ShapeDtypeStruct(sums_shape, F32),
        [jax.ShapeDtypeStruct((2,) + r, F32) for r in results])
    return pl.pallas_call(
        functools.partial(layer_kernel, length, HEAD_DIM ** (-0.5)),
        out_shape=out_shape,
        in_specs=[pl.BlockSpec(memory_space=pltpu.SMEM)] + [anywhere] * 9,
        out_specs=(anywhere, anywhere, anywhere, vmem, [anywhere] * 5),
        scratch_shapes=scratch,
        compiler_params=pltpu.CompilerParams(
            collective_id=0, has_side_effects=True, vmem_limit_bytes=127 * 2 ** 19),
        name="resampler_layer",
    )(counts, media, latents, grad_out, packed, query_shard, context_shard, output_shard, up_shard, down_shard)


def finish_kernel(length, latents_raw, media_grad_raw, latents_grad_raw, grads_raw, latents_out, media_grad_out,
                  latents_grad_out, grads_out, held, held_grads, local):
    x = Links(length).x
    locals_ = Locals(local)
    raws = [latents_raw, latents_grad_raw, *grads_raw]
    stages = [held[0], held[1], *held_grads]
    outs = [latents_out, latents_grad_out, *grads_out]
    count = media_grad_raw.shape[0]
    for j in range(count):
        raws.append(media_grad_raw.at[j])
        stages.append(held[2].at[j])
        outs.append(media_grad_out.at[j])
    loads = [locals_.copy(raw, stage) for raw, stage in zip(raws, stages)]
    unit = grads_raw[1].shape[1]
    copies = []
    for number, (load, stage, out) in enumerate(zip(loads, stages, outs)):
        load.wait()
        if number != 2:
            copies.append(locals_.copy(stage, out))
            continue
        moves = []
        for core in range(2):
            for plane in range(2):
                half = x if plane == 0 else 1 - x
                for owner in range(stage.shape[-1] // unit):
                    begin = pl.multiple_of(((2 * owner + half) * 2 + core) * unit, unit)
                    moves.append((stage.at[core, plane, :, pl.ds(owner * unit, unit)], out.at[:, pl.ds(begin, unit)]))
        copies.append(locals_.fill(moves, out))
    for copy in copies:
        copy.wait()


def finish(length, latents_raw, media_grad_raw, latents_grad_raw, grads_raw):
    anywhere = pl.BlockSpec(memory_space=pl.ANY)
    up = grads_raw[0]
    shapes = [jax.ShapeDtypeStruct((up.shape[2], 4 * up.shape[3]), up.dtype)]
    shapes += [jax.ShapeDtypeStruct(g.shape, g.dtype) for g in grads_raw[1:]]
    same = [jax.ShapeDtypeStruct(r.shape, r.dtype) for r in (latents_raw, media_grad_raw, latents_grad_raw)]
    return pl.pallas_call(
        functools.partial(finish_kernel, length),
        out_shape=(*same, shapes),
        in_specs=[anywhere, anywhere, anywhere, [anywhere] * 5],
        out_specs=(anywhere, anywhere, anywhere, [anywhere] * 5),
        scratch_shapes=[
            [pltpu.VMEM(r.shape, r.dtype) for r in (latents_raw, latents_grad_raw, media_grad_raw)],
            [pltpu.VMEM(g.shape, g.dtype) for g in grads_raw],
            pltpu.SemaphoreType.DMA((2 * (7 + media_grad_raw.shape[0]),)),
        ],
        compiler_params=pltpu.CompilerParams(vmem_limit_bytes=60 * 2 ** 20),
        name="finish",
    )(latents_raw, media_grad_raw, latents_grad_raw, grads_raw)


def head_scores(first_heads, second_heads):
    return jnp.einsum(
        "bqhd,bkhd->bhqk", first_heads, second_heads, preferred_element_type=jnp.float32
    )


def collective_body(
    media,
    latents,
    image_counts,
    grad_out,
    media_gain,
    media_bias,
    latent_gain,
    latent_bias,
    feed_gain,
    feed_bias,
    query_weight,
    context_weight,
    output_weight,
    up_weight,
    down_weight,
):
    samples, slots, patches, model_width = media.shape
    latent_count = latents.shape[2]
    inner_width = query_weight.shape[1]
    head_count = inner_width // HEAD_DIM
    blocks = samples * slots
    key_count = patches + latent_count
    latent_total = blocks * latent_count
    scaling = HEAD_DIM ** (-0.5)
    vector_shards = (media_gain, media_bias, latent_gain, latent_bias, feed_gain, feed_bias)
    weight_shards = (query_weight, context_weight, output_weight, up_weight, down_weight)
    gathered = tuple(lax.all_gather(s, "dp", axis=0, tiled=True) for s in vector_shards + weight_shards)
    vectors = [element.astype(jnp.float32) for element in gathered[:6]]
    media_rows = media.reshape(blocks * patches, model_width).astype(jnp.float32)
    latent_rows = latents.reshape(latent_total, model_width).astype(jnp.float32)
    media_normed = layer_norm(media_rows, vectors[0], vectors[1]).astype(jnp.bfloat16)
    latent_normed = layer_norm(latent_rows, vectors[2], vectors[3]).astype(jnp.bfloat16)
    queries = (matmul(latent_normed, gathered[6]) * scaling).astype(jnp.bfloat16)
    context = jnp.concatenate(
        [
            media_normed.reshape(blocks, patches, model_width),
            latent_normed.reshape(blocks, latent_count, model_width),
        ],
        axis=1,
    ).reshape(blocks * key_count, model_width)
    key_value = (
        matmul(context, gathered[7])
        .astype(jnp.bfloat16)
        .reshape(blocks, key_count, 2 * inner_width)
    )
    query_heads = queries.reshape(blocks, latent_count, head_count, HEAD_DIM)
    key_heads = key_value[:, :, :inner_width].reshape(blocks, key_count, head_count, HEAD_DIM)
    value_heads = key_value[:, :, inner_width:].reshape(blocks, key_count, head_count, HEAD_DIM)
    scores = head_scores(query_heads, key_heads)
    row_max = jnp.max(scores, axis=-1, keepdims=True)
    exponent = jnp.exp(scores - row_max)
    row_total = jnp.sum(exponent, axis=-1, keepdims=True)
    log_total = row_max + jnp.log(row_total)
    attention_weights = (exponent / row_total).astype(jnp.bfloat16)
    attended = (
        jnp.einsum(
            "bhqk,bkhd->bqhd", attention_weights, value_heads, preferred_element_type=jnp.float32
        )
        .astype(jnp.bfloat16)
        .reshape(latent_total, inner_width)
    )
    after_attention = latent_rows + matmul(attended, gathered[8])
    feed_input = layer_norm(after_attention, vectors[4], vectors[5]).astype(jnp.bfloat16)
    hidden = matmul(feed_input, gathered[9])
    activated = gelu_exact(hidden).astype(jnp.bfloat16)
    after_feed = after_attention + matmul(activated, gathered[10])
    slot_mask = (
        lax.broadcasted_iota(jnp.int32, (samples, slots), 1) < image_counts[:, None]
    ).astype(jnp.float32)
    row_mask = jnp.broadcast_to(slot_mask[:, :, None], (samples, slots, latent_count)).reshape(
        latent_total, 1
    )
    latents_out = (after_feed * row_mask).astype(jnp.bfloat16).reshape(latents.shape)
    backward_set = gathered
    back_vectors = [element.astype(jnp.float32) for element in backward_set[:6]]
    d_after = grad_out.reshape(latent_total, model_width).astype(jnp.float32) * row_mask
    d_branch = d_after.astype(jnp.bfloat16)
    grad_down = matmul_left(activated, d_branch)
    d_activated = matmul_right(d_branch, backward_set[10])
    d_hidden = jax.vjp(gelu_exact, hidden)[1](d_activated)[0].astype(jnp.bfloat16)
    grad_up = matmul_left(feed_input, d_hidden)
    d_feed = matmul_right(d_hidden, backward_set[9])
    d_feed_norm, grad_feed_gain, grad_feed_bias = jax.vjp(
        layer_norm, after_attention, back_vectors[4], back_vectors[5]
    )[1](d_feed)
    d_middle = d_after + d_feed_norm
    d_out_branch = d_middle.astype(jnp.bfloat16)
    grad_output = matmul_left(attended, d_out_branch)
    d_attended = (
        matmul_right(d_out_branch, backward_set[8])
        .astype(jnp.bfloat16)
        .reshape(blocks, latent_count, head_count, HEAD_DIM)
    )
    recomputed = jnp.exp(head_scores(query_heads, key_heads) - log_total)
    d_weights = head_scores(d_attended, value_heads)
    d_scores = (
        recomputed * (d_weights - jnp.sum(recomputed * d_weights, axis=-1, keepdims=True))
    ).astype(jnp.bfloat16)
    d_queries = (
        jnp.einsum(
            "bhqk,bkhd->bqhd", d_scores, key_heads, preferred_element_type=jnp.float32
        ).astype(jnp.bfloat16)
        * scaling
    ).reshape(latent_total, inner_width)
    d_keys = jnp.einsum(
        "bhqk,bqhd->bkhd", d_scores, query_heads, preferred_element_type=jnp.float32
    ).astype(jnp.bfloat16)
    d_values = jnp.einsum(
        "bhqk,bqhd->bkhd",
        recomputed.astype(jnp.bfloat16),
        d_attended,
        preferred_element_type=jnp.float32,
    ).astype(jnp.bfloat16)
    d_key_value = jnp.concatenate(
        [
            d_keys.reshape(blocks, key_count, inner_width),
            d_values.reshape(blocks, key_count, inner_width),
        ],
        axis=-1,
    ).reshape(blocks * key_count, 2 * inner_width)
    grad_query = matmul_left(latent_normed, d_queries)
    grad_context = matmul_left(context, d_key_value)
    d_context = matmul_right(d_key_value, backward_set[7]).reshape(blocks, key_count, model_width)
    d_latent_normed = matmul_right(d_queries, backward_set[6]) + d_context[:, patches:, :].reshape(
        latent_total, model_width
    )
    d_media_normed = d_context[:, :patches, :].reshape(blocks * patches, model_width)
    d_latent_norm, grad_latent_gain, grad_latent_bias = jax.vjp(
        layer_norm, latent_rows, back_vectors[2], back_vectors[3]
    )[1](d_latent_normed)
    grad_latents = (d_middle + d_latent_norm).astype(jnp.bfloat16).reshape(latents.shape)
    d_media, grad_media_gain, grad_media_bias = jax.vjp(
        layer_norm, media_rows, back_vectors[0], back_vectors[1]
    )[1](d_media_normed)
    grad_media = d_media.astype(jnp.bfloat16).reshape(media.shape)
    vector_grads = jnp.stack([
        grad_media_gain, grad_media_bias, grad_latent_gain, grad_latent_bias, grad_feed_gain, grad_feed_bias])
    weight_grads = [
        g.astype(jnp.bfloat16) for g in (grad_query, grad_context, grad_output, grad_up, grad_down)]
    vector_sums = lax.psum_scatter(vector_grads, "dp", scatter_dimension=1, tiled=True)
    summed = [lax.psum_scatter(g, "dp", scatter_dimension=0, tiled=True) for g in weight_grads]
    owned = tuple(lax.psum(vector_sums, "rep")) + tuple(
        lax.psum(s, "rep").astype(jnp.float32) for s in summed)
    return (
        latents_out,
        grad_media,
        grad_latents,
        owned[0],
        owned[1],
        owned[2],
        owned[3],
        owned[4],
        owned[5],
        owned[6],
        owned[7],
        owned[8],
        owned[9],
        owned[10],
    )


def body(media, latents, image_counts, grad_out, *parameters):
    chips = lax.axis_size("dp")
    weight_shards = parameters[6:]
    tiled = (media.shape[0] == 1 and chips % 4 == 0 and chips > 4 and parameters[0].shape[0] == 64
             and all(s.shape[0] % 32 == 0 for s in weight_shards))
    if not tiled:
        return collective_body(media, latents, image_counts, grad_out, *parameters)
    side = lax.rem(lax.axis_index("dp"), 2)
    stacked = jnp.stack(parameters[:6])
    packed = jnp.pad(
        jnp.concatenate([jnp.where(side == 0, stacked, 0), jnp.where(side == 0, 0, stacked)], axis=1), ((0, 10), (0, 0)))
    latents_out, grad_media, grad_latents, vector_sums, summed = layer(
        chips // 4, image_counts, media[0], latents[0], grad_out[0], packed, weight_shards)
    latents_out, grad_media, grad_latents, summed = finish(
        chips // 4, latents_out, grad_media, grad_latents, summed)
    sums = [s.reshape(-1, s.shape[-1]) for s in summed[2:] + summed[:2]]
    width = parameters[0].shape[0]
    mine = lax.dynamic_slice(vector_sums, (0, lax.axis_index("dp") * width), (6, width))
    return (latents_out[None], grad_media[None], grad_latents[None]) + tuple(mine) + tuple(sums)


def solution(mesh):
    return jax.shard_map(
        body,
        mesh=mesh,
        in_specs=(
            P(("dp", "rep"), None, None, None),
            P(("dp", "rep"), None, None, None),
            P(("dp", "rep")),
            P(("dp", "rep"), None, None, None),
            P("dp"),
            P("dp"),
            P("dp"),
            P("dp"),
            P("dp"),
            P("dp"),
            P("dp", None),
            P("dp", None),
            P("dp", None),
            P("dp", None),
            P("dp", None),
        ),
        out_specs=(
            P(("dp", "rep"), None, None, None),
            P(("dp", "rep"), None, None, None),
            P(("dp", "rep"), None, None, None),
            P("dp"),
            P("dp"),
            P("dp"),
            P("dp"),
            P("dp"),
            P("dp"),
            P("dp", None),
            P("dp", None),
            P("dp", None),
            P("dp", None),
            P("dp", None),
        ),
        check_vma=False,
    )
```
